32 devices in a mesh: dp: 2 (over y), seq: 16 (over z, x, core).
Axes of the slice: x: 2, y: 2, z: 4, core: 2. Of those that a mesh axis runs over, the one named last changes fastest.
Arguments:
- tokens: bfloat16 [2, 4096, 768], P('dp', 'seq'), may hold values from -6 to 6
- qkv_weight: bfloat16 [1769472], P(('dp', 'seq')), may hold values from -0.21875 to 0.21875
- out_weight: bfloat16 [589824], P(('dp', 'seq')), may hold values from -0.875 to 0.875
- expand_weight: bfloat16 [2359296], P(('dp', 'seq')), may hold values from -0.21875 to 0.21875
- contract_weight: bfloat16 [2359296], P(('dp', 'seq')), may hold values from -0.109375 to 0.109375
- bias_vectors: bfloat16 [4608], P(('dp', 'seq')), may hold values from -3 to 3
- gain_vectors: bfloat16 [1536], P(('dp', 'seq')), may hold values from 0.5 to 1.5
- ffn_bias: bfloat16 [3072], P(('dp', 'seq')), may hold values from -3 to 3
- random_blocks: int32 [2, 12, 64, 3], P('dp', None, 'seq'), may hold values from 0 to 63, as said below
- cotangent: bfloat16 [2, 4096, 768], P('dp', 'seq'), may hold values from -6 to 6
Outputs:
- output: float32 [2, 4096, 768], P('dp', 'seq')
- grad_tokens: float32 [2, 4096, 768], P('dp', 'seq')
- grad_qkv: float32 [1769472], P(('dp', 'seq'))
- grad_out: float32 [589824], P(('dp', 'seq'))
- grad_expand: float32 [2359296], P(('dp', 'seq'))
- grad_contract: float32 [2359296], P(('dp', 'seq'))
- grad_biases: float32 [4608], P(('dp', 'seq'))
- grad_gains: float32 [1536], P(('dp', 'seq'))
- grad_ffn_bias: float32 [3072], P(('dp', 'seq'))
The draws below stay inside these ranges and needn't reach their ends.
Inputs may be any that keep to these rules, and one draw needn't show every extreme that they name: `random_blocks`: over the 1 sequence of one index of dp, all 12 heads and the three picks, the (head, query block, pick) entries of the query blocks held by one seq device, counted with repeats, name blocks held by any single seq device at most 9 times (each device holds 4 consecutive blocks of every sequence), and exactly 9 for some device.
All inputs are finite; a program needn't handle non-finite values.
Results may differ from the reference program's by a relative error of at most 0.014.
Values may be sent and summed in bfloat16 or wider, within the bound.
A program may use at most 192 MiB of HBM per device.

```python
import jax
import jax.numpy as jnp
from jax import lax

D = 768
FF = 3072
H = 12
HD = 64
BLOCK = 64
SEQ_GRP = 1
SHARDS = 16
BATCH = 2
LEN = 4096
NB = 64
BPD = 4


def draw_random_blocks(key, part):
    key = jax.random.fold_in(key, 11)
    groups = BATCH // SEQ_GRP
    count = SEQ_GRP * H * BPD * 3
    owners = groups * SHARDS
    perm_keys = jax.random.split(jax.random.fold_in(key, 1), owners)

    def shuffle(sub):
        return jax.random.permutation(sub, count)
    ranks = jax.vmap(shuffle)(perm_keys).astype(jnp.int32)
    shift = jax.random.randint(jax.random.fold_in(key, 2), (owners, 1), 0, SHARDS).astype(jnp.int32)
    offset = jax.random.randint(jax.random.fold_in(key, 3), (owners, count), 0, BPD).astype(jnp.int32)
    blocks = (ranks + shift) % SHARDS * BPD + offset
    blocks = blocks.reshape(groups, SHARDS, SEQ_GRP, H, BPD, 3).transpose(0, 2, 3, 1, 4, 5)
    return blocks.reshape(BATCH, H, NB, 3).astype(jnp.int32)


def block_levels(key, extent, cuts, low, top_value):
    factor_of = 1.0
    for dim, blocks in cuts:
        steps = jax.random.uniform(jax.random.fold_in(jax.random.fold_in(key, 6), dim), (blocks,), jnp.float32, low / len(cuts), top_value / len(cuts))
        factor_of = factor_of * jnp.repeat(jnp.exp(steps), extent[dim] // blocks).reshape((-1,) + (1,) * (len(extent) - 1 - dim))
    return factor_of


def scatter_about(own_key, extent, deviation, reach, cuts=(), kind=jnp.bfloat16):
    array = jax.random.normal(own_key, extent, jnp.float32) * deviation
    if len(cuts) > 0:
        array = block_levels(own_key, extent, cuts, -0.22, 0.18) * array
    return jnp.clip(array, min=-reach, max=reach).astype(kind)


def setup_inputs(seed: int = 0) -> dict:
    splits = jax.random.split(jax.random.key(seed), 11)
    tokens = scatter_about(splits[0], (BATCH, LEN, D), 1.0, 6.0, ((0, 2), (1, 16)))
    qkv_weight = scatter_about(splits[1], (3 * D * D,), D ** -0.5, 0.21875, ((0, 32),))
    out_weight = scatter_about(splits[2], (D * D,), (D // 16) ** -0.5, 0.875, ((0, 32),))
    expand_weight = scatter_about(splits[3], (D * FF,), D ** -0.5, 0.21875, ((0, 32),))
    contract_weight = scatter_about(splits[4], (FF * D,), FF ** -0.5, 0.109375, ((0, 32),))
    bias_vectors = scatter_about(splits[5], (6 * D,), 0.5, 3.0, ((0, 32),))
    gain_vectors = jnp.clip(1.0 + 0.1 * jax.random.normal(splits[6], (2 * D,), jnp.float32), 0.5, 1.5).astype(jnp.bfloat16)
    ffn_bias = scatter_about(splits[7], (FF,), 0.5, 3.0, ((0, 32),))
    random_blocks = draw_random_blocks(jax.random.fold_in(splits[10], 71), 0)
    cotangent = scatter_about(splits[9], (BATCH, LEN, D), 1.0, 6.0, ((0, 2), (1, 16)))
    return {"tokens": tokens, "qkv_weight": qkv_weight, "out_weight": out_weight, "expand_weight": expand_weight, "contract_weight": contract_weight, "bias_vectors": bias_vectors, "gain_vectors": gain_vectors, "ffn_bias": ffn_bias, "random_blocks": random_blocks, "cotangent": cotangent}


@jax.custom_vjp
def low(v):
    return lax.optimization_barrier(v.astype(jnp.bfloat16)).astype(jnp.float32)

@jax.custom_vjp
def low_back(v):
    return v

def low_keep(v):
    return (low(v), None)

def low_pass(kept, grad):
    return (grad,)

def back_keep(v):
    return (v, None)

def back_low(kept, grad):
    return (low(grad),)
low.defvjp(low_keep, low_pass)
low_back.defvjp(back_keep, back_low)
norm_eps = 1e-12
masked_score = -1e+30
highest = lax.Precision.HIGHEST

def product(left, right):
    return jnp.matmul(left, right, precision=highest)

def layer_norm(value, gain, shift):
    mean = lax.optimization_barrier(jnp.mean(value, axis=-1, keepdims=True))
    centred = value - mean
    inverse = lax.rsqrt(lax.optimization_barrier(jnp.mean(centred * centred, axis=-1, keepdims=True)) + norm_eps)
    return centred * inverse * gain + shift

def layer(tokens, qkv_weight, out_weight, expand_weight, contract_weight, bias_vectors, gain_vectors, ffn_bias, picks):
    qkv = qkv_weight.reshape(3, D, D)
    biases = bias_vectors.reshape(6, D)
    gains = gain_vectors.reshape(2, D)
    query = low_back(low(product(tokens, qkv[0]) + biases[0]))
    key = low_back(low(product(tokens, qkv[1])))
    value = low_back(low(product(tokens, qkv[2]) + biases[1]))
    query_heads = query.reshape(NB // 8, 8, BLOCK, H, HD).transpose(0, 1, 3, 2, 4)
    key_heads = key.reshape(NB, BLOCK, H, HD).transpose(2, 0, 1, 3)
    value_heads = value.reshape(NB, BLOCK, H, HD).transpose(2, 0, 1, 3)
    place = jnp.arange(NB, dtype=jnp.int32)
    fixed = jnp.stack([jnp.maximum(place - 1, 0), place, jnp.minimum(place + 1, NB - 1), jnp.zeros_like(place), jnp.full_like(place, NB - 1)], axis=1)
    listed = jnp.concatenate([jnp.broadcast_to(fixed[:, None, :], (NB, H, 5)), picks.transpose(1, 0, 2).astype(jnp.int32)], axis=2).astype(jnp.int32)
    always = jnp.ones((NB,), dtype=bool)
    valid = jnp.stack([place >= 1, always, place + 1 < NB, always, always, always, always, always], axis=1)
    valid = jnp.broadcast_to(valid[:, :, None], (NB, 8, BLOCK)).reshape(NB // 8, 8, 8 * BLOCK)
    heads = jnp.arange(H, dtype=jnp.int32)[None, :, None]
    scale = HD ** (-0.5)

    def group(items):
        group_query, group_list, group_valid = items
        keys = key_heads[heads, group_list].reshape(8, H, 8 * BLOCK, HD)
        values = value_heads[heads, group_list].reshape(8, H, 8 * BLOCK, HD)
        scores = low_back(jnp.einsum('ghqd,ghkd->ghqk', group_query, keys, precision=highest) * scale)
        scores = jnp.where(group_valid[:, None, None, :], scores, masked_score)
        top = lax.optimization_barrier(jnp.max(scores, axis=-1, keepdims=True))
        weights = jnp.exp(scores - top)
        probs = weights / lax.optimization_barrier(jnp.sum(weights, axis=-1, keepdims=True))
        return jnp.einsum('ghqk,ghkd->ghqd', low(probs), values, precision=highest)
    attended = lax.map(jax.checkpoint(group), (query_heads, listed.reshape(NB // 8, 8, H, 8), valid))
    mixed = low_back(low(attended.transpose(0, 1, 3, 2, 4).reshape(LEN, D)))
    attn = low_back(product(mixed, out_weight.reshape(D, D)) + biases[2])
    normed1 = layer_norm(tokens + attn, gains[0], biases[3])
    up = low_back(product(low(normed1), expand_weight.reshape(D, FF)) + ffn_bias)
    active = low(jax.nn.gelu(up, approximate=True))
    down = low_back(product(active, contract_weight.reshape(FF, D)) + biases[4])
    return layer_norm(normed1 + down, gains[1], biases[5])

def reference(tokens, qkv_weight, out_weight, expand_weight, contract_weight, bias_vectors, gain_vectors, ffn_bias, random_blocks, cotangent):
    weights = tuple((w.astype(jnp.float32) for w in (qkv_weight, out_weight, expand_weight, contract_weight, bias_vectors, gain_vectors, ffn_bias)))

    def one_sequence(totals, items):
        seq_tokens, picks, seq_grad = items

        def run(inputs, *params):
            return layer(inputs, *params, picks)
        result, pull = jax.vjp(run, seq_tokens.astype(jnp.float32), *weights)
        grads = pull(seq_grad.astype(jnp.float32))
        totals = tuple((t + g for t, g in zip(totals, grads[1:])))
        return (totals, (result, grads[0]))
    start = tuple((jnp.zeros_like(w) for w in weights))
    totals, (results, grad_tokens) = lax.scan(one_sequence, start, (tokens, random_blocks, cotangent))
    return (results, grad_tokens, totals[0], totals[1], totals[2], totals[3], totals[4], totals[5], totals[6])
```

```python
import functools

import jax
import jax.numpy as jnp
from jax import lax
from jax.experimental import pallas as pl
from jax.experimental.pallas import tpu as pltpu
from jax.sharding import PartitionSpec as P

MESH = pl.DeviceIdType.MESH

D = 768
FF = 3072
H = 12
HD = 64
BLOCK = 64
TOK_SEQ = 256
SEQ_GRP = 1
BPD = 4


norm_eps = 1e-12
masked_score = -1e30


def with_halo(cells, sides, width):
    for axis, dim in sides:
        count = lax.axis_size(axis)
        ends = count - 1
        head = lax.slice_in_dim(cells, 0, width, axis=dim)
        tail = lax.slice_in_dim(cells, cells.shape[dim] - width, cells.shape[dim], axis=dim)
        cells = jnp.concatenate(
            [
                lax.ppermute(tail, axis, [(i, (i + 1) % count) for i in range(ends)]),
                cells,
                lax.ppermute(head, axis, [((i + 1) % count, i) for i in range(ends)]),
            ],
            axis=dim,
        )
    return cells


def spread(block, axis, source):
    block = jnp.where(lax.axis_index(axis) == source, block, jnp.zeros_like(block))
    return lax.psum(block, axis)


def matmul(left, right):
    return jnp.dot(left, right, preferred_element_type=jnp.float32)


def inner_rows(left, right):
    return lax.dot_general(
        left, right, (((0,), (0,)), ((), ())), preferred_element_type=jnp.float32
    )


def outer_cols(left, right):
    return lax.dot_general(
        left, right, (((1,), (1,)), ((), ())), preferred_element_type=jnp.float32
    )


def gelu_tanh(value):
    return jax.nn.gelu(value, approximate=True)


def normalize(value, gain, shift):
    mean = jnp.mean(value, axis=-1, keepdims=True)
    centred = value - mean
    inverse = lax.rsqrt(jnp.mean(centred * centred, axis=-1, keepdims=True) + norm_eps)
    normed = centred * inverse
    return (normed * gain + shift, normed, inverse)


def normalize_back(grad, normed, inverse, gain):
    scaled = grad * gain
    centred = scaled - jnp.mean(scaled, axis=-1, keepdims=True)
    return inverse * (centred - normed * jnp.mean(scaled * normed, axis=-1, keepdims=True))


def place(nz):
    y = lax.axis_index("dp")
    s = lax.axis_index("seq")
    return {"y": y, "z": s // 4, "x": (s // 2) % 2, "c": s % 2}

def device(p):
    return (p["y"], p["z"] * 4 + p["x"] * 2 + p["c"])

def chip(p, nz):
    return (p["y"] * nz + p["z"]) * 2 + p["x"]

def index(p, nz):
    return chip(p, nz) * 2 + p["c"]

def nearest(m, n, j):
    if n == 2:
        return m if j == 0 else 1 - m
    out = 0
    for i in range(n):
        rank = sorted(range(n), key=lambda s: (abs(s - i), s))
        out = jnp.where(m == i, rank[j], out)
    return out

ORDERS = (("z", "x", "y"), ("z", "y", "x"), ("x", "y", "z"))

def gather_kernel(nz, *refs):
    k = len(ORDERS)
    xs, gs = refs[:k], refs[k:2 * k]
    own_sem, send_sem, recv_sem, csend, crecv = refs[2 * k:]
    me = place(nz)
    size = {"y": 2, "z": nz, "x": 2}
    sib = dict(me, c=1 - me["c"])
    bar = pltpu.get_barrier_semaphore()
    for d in ("x", "y", "c"):
        pl.semaphore_signal(bar, inc=1, device_id=device(dict(me, **{d: 1 - me[d]})), device_id_type=MESH)
    @pl.when(me["z"] > 0)
    def _():
        pl.semaphore_signal(bar, inc=1, device_id=device(dict(me, z=me["z"] - 1)), device_id_type=MESH)
    @pl.when(me["z"] < nz - 1)
    def _():
        pl.semaphore_signal(bar, inc=1, device_id=device(dict(me, z=me["z"] + 1)), device_id_type=MESH)
    inside = jnp.where(me["z"] > 0, 1, 0) + jnp.where(me["z"] < nz - 1, 1, 0)
    pl.semaphore_wait(bar, 3 + inside)

    pending = []
    def remote(item, src_ref, slot, sem_slot, way, to, cond=None):
        cp = pltpu.make_async_remote_copy(src_ref=src_ref, dst_ref=gs[item].at[slot], send_sem=send_sem.at[item, sem_slot, way],
            recv_sem=recv_sem.at[item, sem_slot], device_id=device(to), device_id_type=MESH)
        if cond is None:
            cp.start()
        else:
            pl.when(cond)(cp.start)
        pending.append((cp, cond))

    work = []
    for item in range(k):
        order = ORDERS[item]
        n0, n1, n2 = (size[d] for d in order)
        for i2 in range(n2):
            for i1 in range(n1):
                for i0 in range(n0):
                    work.append((i0 + i1 + i2, item, i0, i1, i2))
    work.sort(key=lambda w: w[0])
    local = []
    for depth, item, i0, i1, i2 in work:
        order = ORDERS[item]
        src = dict(me)
        for d, i in zip(order, (i0, i1, i2)):
            src[d] = nearest(me[d], size[d], i)
        c = chip(src, nz)
        slot = c * 2 + me["c"]
        own = depth == 0
        ref = xs[item] if own else gs[item].at[slot]
        if not own:
            pltpu.make_async_remote_copy(src_ref=ref, dst_ref=ref, send_sem=send_sem.at[item, c, 0], recv_sem=recv_sem.at[item, c],
                device_id=device(sib), device_id_type=MESH).wait_recv()
        stage = 2 if i2 else (1 if i1 else 0)
        for t in range(stage, 3):
            d = order[t]
            onward = t == stage and not own
            if d == "z":
                if nz > 1:
                    up = me["z"] < nz - 1
                    dn = me["z"] > 0
                    if onward:
                        up = jnp.logical_and(up, src["z"] <= me["z"])
                        dn = jnp.logical_and(dn, src["z"] >= me["z"])
                    remote(item, ref, slot, c, 0, dict(me, z=jnp.minimum(me["z"] + 1, nz - 1)), up)
                    remote(item, ref, slot, c, 1, dict(me, z=jnp.maximum(me["z"] - 1, 0)), dn)
            elif not (onward and (i0, i1, i2)[t]):
                remote(item, ref, slot, c, 2 if d == "x" else 3, dict(me, **{d: 1 - me[d]}))
        cp = pltpu.make_async_remote_copy(src_ref=ref, dst_ref=gs[item].at[slot], send_sem=csend.at[item, c],
            recv_sem=crecv.at[item, c], device_id=device(sib), device_id_type=MESH)
        cp.start()
        pending.append((cp, None))
        if own:
            lc = pltpu.make_async_copy(xs[item], gs[item].at[slot], own_sem.at[item])
            lc.start()
            local.append(lc)
    for lc in local:
        lc.wait()
    for item in range(k):
        def body(c, _):
            ref = gs[item].at[c * 2 + 1 - me["c"]]
            pltpu.make_async_remote_copy(src_ref=ref, dst_ref=ref, send_sem=csend.at[item, c], recv_sem=crecv.at[item, c],
                device_id=device(sib), device_id_type=MESH).wait_recv()
            return 0
        lax.fori_loop(0, 4 * nz, body, 0)
    for cp, cond in pending:
        if cond is None:
            cp.wait_send()
        else:
            pl.when(cond)(cp.wait_send)

def gather_all(xs, nz):
    n = 8 * nz
    k = len(xs)
    chips = 4 * nz
    return pl.pallas_call(
        functools.partial(gather_kernel, nz),
        out_shape=[jax.ShapeDtypeStruct((n,) + x.shape, x.dtype) for x in xs],
        in_specs=[pl.BlockSpec(memory_space=pl.ANY)] * k,
        out_specs=[pl.BlockSpec(memory_space=pl.ANY)] * k,
        scratch_shapes=[pltpu.SemaphoreType.DMA((k,)), pltpu.SemaphoreType.DMA((k, chips, 4)), pltpu.SemaphoreType.DMA((k, chips)),
            pltpu.SemaphoreType.DMA((k, chips)), pltpu.SemaphoreType.DMA((k, chips))],
        compiler_params=pltpu.CompilerParams(collective_id=0, has_side_effects=True),
        name="gather_weights",
    )(*xs)


CHAIN_FIRST = (False, False, False, True, False)
LINKS = (("x", "y"), ("x", "y"), ("y", "x"), ("x", "y"), ("x", "y"))

def combine(dst, srcs):
    rows, cols = dst.shape
    step = min(cols, max(128, (24 * 1024 // rows) // 128 * 128))
    while cols % step:
        step -= 128
    def part(sl):
        total = srcs[0][:, sl].astype(jnp.float32)
        for s in srcs[1:]:
            total = total + s[:, sl].astype(jnp.float32)
        dst[:, sl] = total.astype(dst.dtype)
    if cols == step:
        part(slice(None))
    else:
        def body(i, _):
            part(pl.ds(pl.multiple_of(i * step, 128), step))
            return 0
        lax.fori_loop(0, cols // step, body, 0)

def scatter_kernel(nz, k, *refs):
    xs, outs = refs[:k], refs[k:2 * k]
    scr = refs[2 * k:]
    acc, rc, ra, rb, below, above = (scr[i * k:(i + 1) * k] for i in range(6))
    csend, crecv, send_sem, recv_sem = scr[6 * k:]
    me = place(nz)
    mz = me["z"]
    sib = dict(me, c=1 - me["c"])
    bar = pltpu.get_barrier_semaphore()
    for d in ("x", "y", "c"):
        pl.semaphore_signal(bar, inc=1, device_id=device(dict(me, **{d: 1 - me[d]})), device_id_type=MESH)
    @pl.when(mz > 0)
    def _():
        pl.semaphore_signal(bar, inc=1, device_id=device(dict(me, z=mz - 1)), device_id_type=MESH)
    @pl.when(mz < nz - 1)
    def _():
        pl.semaphore_signal(bar, inc=1, device_id=device(dict(me, z=mz + 1)), device_id_type=MESH)
    pl.semaphore_wait(bar, 3 + jnp.where(mz > 0, 1, 0) + jnp.where(mz < nz - 1, 1, 0))

    pending = []
    up_to = dict(me, z=jnp.minimum(mz + 1, nz - 1))
    dn_to = dict(me, z=jnp.maximum(mz - 1, 0))

    def copy(item, src, dst, ss, rs, to):
        return pltpu.make_async_remote_copy(src_ref=src, dst_ref=dst, send_sem=ss, recv_sem=rs, device_id=device(to), device_id_type=MESH)

    def start(cp, cond=None):
        if cond is None:
            cp.start()
        else:
            pl.when(cond)(cp.start)
        pending.append((cp, cond))

    def arrived(item, ref, sem):
        copy(item, ref, ref, send_sem.at[item, 0], sem, sib).wait_recv()

    def piece(z, x, y):
        return (y * nz + z) * 2 + x

    def coords(a, b, item):
        la, lb = LINKS[item]
        return {la: a, lb: b}

    def wanted(item):
        la, lb = LINKS[item]
        out = []
        zs = [0, nz - 1, 1, nz - 2][:nz] if nz == 4 else list(range(nz))
        if CHAIN_FIRST[item]:
            for z in zs:
                for fa in (1, 0):
                    for fb in (1, 0):
                        out.append((z, fa, fb))
        else:
            for fb in (1, 0):
                for fa in (1, 0):
                    for z in zs:
                        out.append((z, fa, fb))
        return out

    def flip(d, f):
        return 1 - me[d] if f else me[d]

    order_items = (1, 2, 3, 4, 0)
    lists = {i: wanted(i) for i in range(k)}
    for n in range(4 * nz):
        for item in order_items:
            z, fa, fb = lists[item][n]
            la, lb = LINKS[item]
            p = piece(z, **{la: flip(la, fa), lb: flip(lb, fb)})
            start(copy(item, xs[item].at[p * 2 + 1 - me["c"]], rc[item].at[p], csend.at[item, p], crecv.at[item, p], sib))

    steps = []
    def tail(item):
        la, lb = LINKS[item]
        def own(p):
            arrived(item, rc[item].at[p], crecv.at[item, p])
            return [xs[item].at[p * 2 + me["c"]], rc[item].at[p]]
        zs = [nz - 1, 0, nz - 2, 1] if nz == 4 else list(reversed(range(nz)))
        if not CHAIN_FIRST[item]:
            def stage_b(z, fa):
                def run():
                    a = flip(la, fa)
                    p = piece(z, **{la: a, lb: 1 - me[lb]})
                    combine(acc[item].at[p], own(p))
                    s = z * 2 + a
                    start(copy(item, acc[item].at[p], rb[item].at[s], send_sem.at[item, s], recv_sem.at[item, s], dict(me, **{lb: 1 - me[lb]})))
                return run
            def stage_a(z):
                def run():
                    a = 1 - me[la]
                    p = piece(z, **{la: a, lb: me[lb]})
                    s = z * 2 + a
                    srcs = own(p)
                    arrived(item, rb[item].at[s], recv_sem.at[item, s])
                    combine(acc[item].at[p], srcs + [rb[item].at[s]])
                    s2 = 2 * nz + z
                    start(copy(item, acc[item].at[p], ra[item].at[z], send_sem.at[item, s2], recv_sem.at[item, s2], dict(me, **{la: 1 - me[la]})))
                return run
            def base(z):
                p = piece(z, **{la: me[la], lb: me[lb]})
                s = z * 2 + me[la]
                srcs = own(p)
                arrived(item, rb[item].at[s], recv_sem.at[item, s])
                arrived(item, ra[item].at[z], recv_sem.at[item, 2 * nz + z])
                return p, srcs + [rb[item].at[s], ra[item].at[z]]
            def chain(z):
                def run():
                    p, srcs = base(z)
                    sb, sa = 3 * nz + z, 4 * nz + z
                    @pl.when(jnp.logical_and(mz == 0, z > 0))
                    def _():
                        combine(acc[item].at[p], srcs)
                    @pl.when(jnp.logical_and(mz > 0, mz < z))
                    def _():
                        arrived(item, below[item].at[z], recv_sem.at[item, sb])
                        combine(acc[item].at[p], srcs + [below[item].at[z]])
                    if z > 0:
                        start(copy(item, acc[item].at[p], below[item].at[z], send_sem.at[item, sb], recv_sem.at[item, sb], up_to), mz < z)
                    @pl.when(jnp.logical_and(mz == nz - 1, z < nz - 1))
                    def _():
                        combine(acc[item].at[p], srcs)
                    @pl.when(jnp.logical_and(mz < nz - 1, mz > z))
                    def _():
                        arrived(item, above[item].at[z], recv_sem.at[item, sa])
                        combine(acc[item].at[p], srcs + [above[item].at[z]])
                    if z < nz - 1:
                        start(copy(item, acc[item].at[p], above[item].at[z], send_sem.at[item, sa], recv_sem.at[item, sa], dn_to), mz > z)
                return run
            def last():
                for z in range(nz):
                    @pl.when(mz == z)
                    def _():
                        p, srcs = piece(z, **{la: me[la], lb: me[lb]}), None
                        s = z * 2 + me[la]
                        srcs = [xs[item].at[p * 2 + me["c"]], rc[item].at[p], rb[item].at[s], ra[item].at[z]]
                        if z > 0:
                            arrived(item, below[item].at[z], recv_sem.at[item, 3 * nz + z])
                            srcs.append(below[item].at[z])
                        if z < nz - 1:
                            arrived(item, above[item].at[z], recv_sem.at[item, 4 * nz + z])
                            srcs.append(above[item].at[z])
                        combine(outs[item], srcs)
            out = []
            for n, z in enumerate(zs):
                out.append((1 + n, stage_b(z, 1)))
            for n, z in enumerate(zs):
                out.append((5 + n, stage_b(z, 0)))
                out.append((5.5 + n, stage_a(z)))
            for n, z in enumerate(zs):
                out.append((9.5 + n, chain(z)))
            out.append((20, last))
            return out
        def chain(z, fa, fb):
            def run():
                a, b = flip(la, fa), flip(lb, fb)
                p = piece(z, **{la: a, lb: b})
                q = a * 2 + b
                srcs = own(p)
                sb, sa = z * 4 + q, 4 * nz + z * 4 + q
                bref, aref = below[item].at[z * 4 + q], above[item].at[z * 4 + q]
                if z > 0:
                    @pl.when(mz == 0)
                    def _():
                        combine(acc[item].at[p], srcs)
                    @pl.when(jnp.logical_and(mz > 0, mz < z))
                    def _():
                        arrived(item, bref, recv_sem.at[item, sb])
                        combine(acc[item].at[p], srcs + [bref])
                    start(copy(item, acc[item].at[p], bref, send_sem.at[item, sb], recv_sem.at[item, sb], up_to), mz < z)
                if z < nz - 1:
                    @pl.when(mz == nz - 1)
                    def _():
                        combine(acc[item].at[p], srcs)
                    @pl.when(jnp.logical_and(mz < nz - 1, mz > z))
                    def _():
                        arrived(item, aref, recv_sem.at[item, sa])
                        combine(acc[item].at[p], srcs + [aref])
                    start(copy(item, acc[item].at[p], aref, send_sem.at[item, sa], recv_sem.at[item, sa], dn_to), mz > z)
            return run
        def settle(fa, fb):
            a, b = flip(la, fa), flip(lb, fb)
            q = a * 2 + b
            for z in range(nz):
                @pl.when(mz == z)
                def _():
                    p = piece(z, **{la: a, lb: b})
                    srcs = [xs[item].at[p * 2 + me["c"]], rc[item].at[p]]
                    if z > 0:
                        arrived(item, below[item].at[z * 4 + q], recv_sem.at[item, z * 4 + q])
                        srcs.append(below[item].at[z * 4 + q])
                    if z < nz - 1:
                        arrived(item, above[item].at[z * 4 + q], recv_sem.at[item, 4 * nz + z * 4 + q])
                        srcs.append(above[item].at[z * 4 + q])
                    combine(acc[item].at[p], srcs)
            return piece(mz, **{la: a, lb: b})
        s0 = 8 * nz
        def to_b(fa):
            def run():
                p = settle(fa, 1)
                start(copy(item, acc[item].at[p], rb[item].at[fa], send_sem.at[item, s0 + fa], recv_sem.at[item, s0 + fa], dict(me, **{lb: 1 - me[lb]})))
            return run
        def to_a():
            p = settle(1, 0)
            arrived(item, rb[item].at[1], recv_sem.at[item, s0 + 1])
            combine(ra[item].at[0], [acc[item].at[p], rb[item].at[1]])
            start(copy(item, ra[item].at[0], ra[item].at[1], send_sem.at[item, s0 + 2], recv_sem.at[item, s0 + 2], dict(me, **{la: 1 - me[la]})))
        def last():
            p = settle(0, 0)
            arrived(item, rb[item].at[0], recv_sem.at[item, s0])
            arrived(item, ra[item].at[1], recv_sem.at[item, s0 + 2])
            combine(outs[item], [acc[item].at[p], rb[item].at[0], ra[item].at[1]])
        out = []
        for n, z in enumerate(zs):
            for m, (fa, fb) in enumerate(((1, 1), (0, 1), (1, 0), (0, 0))):
                out.append((1 + n * 3 + m * 0.5, chain(z, fa, fb)))
        out.append((12.6, to_b(1)))
        out.append((12.7, to_b(0)))
        out.append((14, to_a))
        out.append((21, last))
        return out

    for n, item in enumerate(order_items):
        steps += [(w + 0.01 * n, f) for w, f in tail(item)]
    for _, f in sorted(steps, key=lambda s: s[0]):
        f()
    for cp, cond in pending:
        if cond is None:
            cp.wait_send()
        else:
            pl.when(cond)(cp.wait_send)

def scatter_all(xs, nz):
    k = len(xs)
    chips = 4 * nz
    slab = [x.shape[1:] for x in xs]
    dt = [x.dtype for x in xs]
    def buf(counts):
        return [pltpu.VMEM((n,) + s, d) for n, s, d in zip(counts, slab, dt)]
    scr = buf([chips] * k) + buf([chips] * k)
    scr += buf([2 if CHAIN_FIRST[i] else nz for i in range(k)])
    scr += buf([2 if CHAIN_FIRST[i] else 2 * nz for i in range(k)])
    scr += buf([4 * nz if CHAIN_FIRST[i] else nz for i in range(k)]) * 2
    sems = 8 * nz + 3
    scr += [pltpu.SemaphoreType.DMA((k, chips)), pltpu.SemaphoreType.DMA((k, chips)), pltpu.SemaphoreType.DMA((k, sems)), pltpu.SemaphoreType.DMA((k, sems))]
    return pl.pallas_call(
        functools.partial(scatter_kernel, nz, k),
        out_shape=[jax.ShapeDtypeStruct(s, jnp.float32) for s in slab],
        in_specs=[pl.BlockSpec(memory_space=pltpu.VMEM)] * k,
        out_specs=[pl.BlockSpec(memory_space=pltpu.VMEM)] * k,
        scratch_shapes=scr,
        compiler_params=pltpu.CompilerParams(collective_id=1, has_side_effects=True, vmem_limit_bytes=60 << 20),
        name="scatter_grads",
    )(*xs)


def kernel_planes(arrays):
    seq = lax.axis_size("seq")
    if lax.axis_size("dp") != 2 or seq % 4 or seq > 16:
        return 0
    rows = [a.size % c for a, c in zip(arrays, (D, D, FF, D))]
    return 0 if any(rows) else seq // 4


def gather_weights(
    qkv_weight, out_weight, expand_weight, contract_weight, bias_vectors, gain_vectors, ffn_bias
):
    vectors = jnp.concatenate([bias_vectors, gain_vectors, ffn_bias])
    planes = kernel_planes((qkv_weight, out_weight, expand_weight, contract_weight))
    if planes:
        shards = 8 * planes
        depth = expand_weight.size // FF
        tail = jnp.pad(vectors, (0, depth * 128 - vectors.size)).reshape(depth, 128)
        first = jnp.concatenate(
            [expand_weight.reshape(depth, FF), out_weight.reshape(depth, D), tail], axis=1
        )
        first, contract, qkv = gather_all(
            (first, contract_weight.reshape(-1, D), qkv_weight.reshape(-1, D)), planes
        )
        rows = first.reshape(D, FF + D + 128)
        expand, out = rows[:, :FF], rows[:, FF : FF + D]
        vectors = rows[:, FF + D :].reshape(shards, depth * 128)
        contract = contract.reshape(FF, D)
        qkv = qkv.reshape(3, D, D)
    else:
        gather = functools.partial(lax.all_gather, axis_name=("dp", "seq"), axis=0, tiled=True)
        qkv = gather(qkv_weight).reshape(3, D, D)
        out = gather(out_weight).reshape(D, D)
        expand = gather(expand_weight).reshape(D, FF)
        contract = gather(contract_weight).reshape(FF, D)
        vectors = gather(vectors[None])
    a, b, c = bias_vectors.size, gain_vectors.size, ffn_bias.size
    vectors = vectors.astype(jnp.float32)
    return (
        qkv,
        out,
        expand,
        contract,
        vectors[:, :a].reshape(6, D),
        vectors[:, a : a + b].reshape(2, D),
        vectors[:, a + b : a + b + c].reshape(FF),
    )


def scatter_grads(grads, planes):
    d_qkv, d_out, d_expand, d_contract, d_biases, d_gains, d_ffn_bias = grads
    shards = lax.axis_size("dp") * lax.axis_size("seq")
    vectors = jnp.concatenate(
        [v.reshape(shards, -1) for v in (d_biases, d_gains, d_ffn_bias)], axis=1
    )
    if planes:
        low = [g.astype(jnp.bfloat16) for g in (d_expand, d_contract, d_qkv, d_out)]
        width = vectors.shape[1]
        padded = jnp.pad(vectors, ((0, 0), (0, -width % 1024)))
        parts = [padded.reshape(shards, -1, 128)]
        parts += [g.reshape(shards, -1, g.shape[-1]) for g in low]
        vectors, d_expand, d_contract, d_qkv, d_out = scatter_all(parts, planes)
        vectors = vectors.reshape(-1)[:width]
    else:
        d_expand, d_contract, d_qkv, d_out = [
            lax.psum_scatter(g.reshape(-1), ("dp", "seq"), scatter_dimension=0, tiled=True)
            for g in (d_expand, d_contract, d_qkv, d_out)
        ]
        vectors = lax.psum_scatter(vectors, ("dp", "seq"), scatter_dimension=0, tiled=True)[0]
    a, b = d_biases.size // shards, d_gains.size // shards
    return (
        d_qkv.reshape(-1),
        d_out.reshape(-1),
        d_expand.reshape(-1),
        d_contract.reshape(-1),
        vectors[:a],
        vectors[a : a + b],
        vectors[a + b :],
    )


def to_heads(rows):
    return rows.reshape(SEQ_GRP, BPD, BLOCK, H, HD).transpose(0, 1, 3, 2, 4)


def from_heads(heads):
    return heads.transpose(0, 1, 3, 2, 4).reshape(SEQ_GRP * TOK_SEQ, D)


def key_blocks(pair, picks):
    shards = lax.axis_size("seq")
    place = lax.axis_index("seq")
    nblocks = BPD * shards
    rims = with_halo(pair, (("seq", 2),), BLOCK)
    wide = rims.reshape(2, SEQ_GRP, BPD + 2, BLOCK, D)
    window = jnp.stack(
        [wide[:, :, 0:BPD], wide[:, :, 1 : BPD + 1], wide[:, :, 2 : BPD + 2]], axis=3
    )
    window = window.reshape(2, SEQ_GRP, BPD, 3, BLOCK, H, HD).transpose(0, 1, 2, 5, 3, 4, 6)
    first = spread(pair[:, :, :BLOCK], "seq", 0)
    last = spread(pair[:, :, TOK_SEQ - BLOCK :], "seq", shards - 1)
    ends = (
        jnp.stack([first, last], axis=2)
        .reshape(2, SEQ_GRP, 2, BLOCK, H, HD)
        .transpose(0, 1, 4, 2, 3, 5)
    )
    ends = jnp.broadcast_to(ends[:, :, None], (2, SEQ_GRP, BPD, H, 2, BLOCK, HD))
    count = SEQ_GRP * H * BPD * 3
    cap = (count + shards - 1) // shards
    flat = picks.reshape(count)
    holder = flat // BPD
    within = flat % BPD
    order = jnp.arange(count, dtype=jnp.int32)
    seq_of = order // (H * BPD * 3)
    head_of = order // (BPD * 3) % H
    tile_id = (seq_of * BPD + within) * H + head_of
    owners = (holder[:, None] == jnp.arange(shards, dtype=jnp.int32)[None, :]).astype(jnp.int32)
    rank = jnp.sum((jnp.cumsum(owners, axis=0) - owners) * owners, axis=1)
    slot = holder * cap + rank
    asked = jnp.zeros((shards * cap,), jnp.int32).at[slot].set(tile_id).reshape(shards, cap)
    tiles = (
        pair.reshape(2, SEQ_GRP, BPD, BLOCK, H, HD)
        .transpose(1, 2, 4, 0, 3, 5)
        .reshape(SEQ_GRP * BPD * H, 2, BLOCK * HD)
    )
    wanted = lax.all_to_all(asked, "seq", split_axis=0, concat_axis=0, tiled=True)
    picked = tiles[wanted]
    returned = lax.all_to_all(picked, "seq", split_axis=0, concat_axis=0, tiled=True)
    mine = returned.reshape(shards * cap, 2, BLOCK * HD)[slot]
    mine = mine.reshape(SEQ_GRP, H, BPD, 3, 2, BLOCK, HD).transpose(4, 0, 2, 1, 3, 5, 6)
    listing = jnp.concatenate([window, ends, mine], axis=4).reshape(
        2, SEQ_GRP, BPD, H, 8 * BLOCK, HD
    )
    position = place * BPD + jnp.arange(BPD, dtype=jnp.int32)
    always = jnp.ones((BPD,), dtype=bool)
    valid = jnp.stack(
        [position >= 1, always, position + 1 < nblocks, always, always, always, always, always],
        axis=1,
    )
    valid = jnp.broadcast_to(valid[:, :, None], (BPD, 8, BLOCK)).reshape(BPD, 8 * BLOCK)
    return (listing, valid, slot, wanted, cap)


def score(query, keys, valid):
    scores = jnp.einsum(
        "sbhqd,sbhkd->sbhqk", query, keys, preferred_element_type=jnp.float32
    ) * HD ** (-0.5)
    return jnp.where(valid[None, :, None, None, :], scores, masked_score)


def attend(query, listing, valid):
    scores = score(query, listing[0], valid)
    top = jnp.max(scores, axis=-1, keepdims=True)
    weights = jnp.exp(scores - top)
    total = jnp.sum(weights, axis=-1, keepdims=True)
    probs = (weights / total).astype(jnp.bfloat16)
    attended = jnp.einsum(
        "sbhqk,sbhkd->sbhqd", probs, listing[1], preferred_element_type=jnp.float32
    )
    return (attended, top + jnp.log(total))


def attend_back(query, listing, valid, lse, grad_out):
    probs = jnp.exp(score(query, listing[0], valid) - lse)
    d_probs = jnp.einsum(
        "sbhqd,sbhkd->sbhqk", grad_out, listing[1], preferred_element_type=jnp.float32
    )
    d_values = jnp.einsum(
        "sbhqk,sbhqd->sbhkd",
        probs.astype(jnp.bfloat16),
        grad_out,
        preferred_element_type=jnp.float32,
    )
    d_scores = (probs * (d_probs - jnp.sum(probs * d_probs, axis=-1, keepdims=True))).astype(
        jnp.bfloat16
    )
    d_query = jnp.einsum(
        "sbhqk,sbhkd->sbhqd", d_scores, listing[0], preferred_element_type=jnp.float32
    ) * HD ** (-0.5)
    d_keys = jnp.einsum(
        "sbhqk,sbhqd->sbhkd", d_scores, query, preferred_element_type=jnp.float32
    ) * HD ** (-0.5)
    return (d_query, jnp.stack([d_keys, d_values]))


def return_grads(grads, slot, served, cap):
    shards = lax.axis_size("seq")
    place = lax.axis_index("seq")
    count = SEQ_GRP * H * BPD * 3
    parts = grads.reshape(2, SEQ_GRP, BPD, H, 8, BLOCK, HD)
    window = (
        parts[:, :, :, :, 0:3].transpose(0, 1, 2, 4, 5, 3, 6).reshape(2, SEQ_GRP, BPD, 3, BLOCK, D)
    )
    wide = sum(
        (
            jnp.pad(window[:, :, :, w], ((0, 0), (0, 0), (w, 2 - w), (0, 0), (0, 0)))
            for w in range(3)
        )
    )
    edges = jnp.concatenate([wide[:, :, 0], wide[:, :, BPD + 1]], axis=2)
    arrived = with_halo(edges.astype(jnp.bfloat16), (("seq", 2),), BLOCK).astype(edges.dtype)
    local = wide[:, :, 1 : BPD + 1].reshape(2, SEQ_GRP, TOK_SEQ, D)
    local = local.at[:, :, :BLOCK].add(arrived[:, :, :BLOCK])
    local = local.at[:, :, TOK_SEQ - BLOCK :].add(arrived[:, :, 3 * BLOCK :])
    ends = (
        jnp.sum(parts[:, :, :, :, 3:5], axis=2)
        .transpose(0, 1, 3, 4, 2, 5)
        .reshape(2, SEQ_GRP, 2, BLOCK, D)
    )
    ends = lax.psum(ends.astype(jnp.bfloat16), "seq").astype(jnp.float32)
    local = local.at[:, :, :BLOCK].add(jnp.where(place == 0, ends[:, :, 0], 0.0))
    local = local.at[:, :, TOK_SEQ - BLOCK :].add(
        jnp.where(place == shards - 1, ends[:, :, 1], 0.0)
    )
    picked = parts[:, :, :, :, 5:8].transpose(1, 3, 2, 4, 0, 5, 6).reshape(count, 2, BLOCK * HD)
    outbox = jnp.zeros((shards * cap, 2, BLOCK * HD), jnp.float32).at[slot].set(picked)
    inbox = lax.all_to_all(
        outbox.reshape(shards, cap, 2, BLOCK * HD).astype(jnp.bfloat16),
        "seq",
        split_axis=0,
        concat_axis=0,
        tiled=True,
    ).astype(jnp.float32)
    table = jnp.zeros((SEQ_GRP * BPD * H, 2, BLOCK * HD), jnp.float32)
    table = table.at[served.reshape(shards * cap)].add(inbox.reshape(shards * cap, 2, BLOCK * HD))
    table = (
        table.reshape(SEQ_GRP, BPD, H, 2, BLOCK, HD)
        .transpose(3, 0, 1, 4, 2, 5)
        .reshape(2, SEQ_GRP, TOK_SEQ, D)
    )
    return local + table


def layer_forward(tokens, picks, weights):
    qkv, out_w, expand, contract, biases, gains, ffn_bias = weights
    rows = tokens.reshape(SEQ_GRP * TOK_SEQ, D)
    projected = jnp.einsum("rd,edf->erf", rows, qkv, preferred_element_type=jnp.float32)
    query = (projected[0] + biases[0]).astype(jnp.bfloat16)
    pair = (
        jnp.stack([projected[1], projected[2] + biases[1]])
        .astype(jnp.bfloat16)
        .reshape(2, SEQ_GRP, TOK_SEQ, D)
    )
    listing, valid, slot, served, cap = key_blocks(pair, picks)
    query_heads = to_heads(query)
    attended, lse = attend(query_heads, listing, valid)
    mixed = from_heads(attended.astype(jnp.bfloat16))
    hidden1 = rows.astype(jnp.float32) + matmul(mixed, out_w) + biases[2]
    normed_out1, normed1, inverse1 = normalize(hidden1, gains[0], biases[3])
    lowered = normed_out1.astype(jnp.bfloat16)
    up = matmul(lowered, expand) + ffn_bias
    active = gelu_tanh(up).astype(jnp.bfloat16)
    hidden2 = normed_out1 + matmul(active, contract) + biases[4]
    result, normed2, inverse2 = normalize(hidden2, gains[1], biases[5])
    saved = (
        query_heads,
        listing,
        valid,
        lse,
        mixed,
        normed1,
        inverse1,
        lowered,
        up,
        active,
        normed2,
        inverse2,
        slot,
        served,
        cap,
    )
    return (result, saved)


def layer_backward(tokens, cotangent, weights, saved, planes):
    qkv, out_w, expand, contract, biases, gains, ffn_bias = weights
    (
        query_heads,
        listing,
        valid,
        lse,
        mixed,
        normed1,
        inverse1,
        lowered,
        up,
        active,
        normed2,
        inverse2,
        slot,
        served,
        cap,
    ) = saved
    rows = tokens.reshape(SEQ_GRP * TOK_SEQ, D)
    grad = cotangent.reshape(SEQ_GRP * TOK_SEQ, D).astype(jnp.float32)
    d_gain2 = jnp.sum(grad * normed2, axis=0)
    d_shift2 = jnp.sum(grad, axis=0)
    d_sum2 = normalize_back(grad, normed2, inverse2, gains[1])
    d_down = d_sum2.astype(jnp.bfloat16)
    d_bias2 = jnp.sum(d_down.astype(jnp.float32), axis=0)
    d_contract = inner_rows(active, d_down)
    d_active = outer_cols(d_down, contract)
    gelu_value, gelu_pull = jax.vjp(gelu_tanh, up)
    d_up = gelu_pull(d_active)[0].astype(jnp.bfloat16)
    d_ffn_bias = jnp.sum(d_up.astype(jnp.float32), axis=0)
    d_expand = inner_rows(lowered, d_up)
    d_norm1 = d_sum2 + outer_cols(d_up, expand)
    d_gain1 = jnp.sum(d_norm1 * normed1, axis=0)
    d_shift1 = jnp.sum(d_norm1, axis=0)
    d_sum1 = normalize_back(d_norm1, normed1, inverse1, gains[0])
    d_attn = d_sum1.astype(jnp.bfloat16)
    d_bias_out = jnp.sum(d_attn.astype(jnp.float32), axis=0)
    d_out_w = inner_rows(mixed, d_attn)
    d_mixed = outer_cols(d_attn, out_w).astype(jnp.bfloat16)
    d_query_heads, d_list = attend_back(query_heads, listing, valid, lse, to_heads(d_mixed))
    d_pair = (
        return_grads(d_list, slot, served, cap)
        .astype(jnp.bfloat16)
        .reshape(2, SEQ_GRP * TOK_SEQ, D)
    )
    d_query = from_heads(d_query_heads).astype(jnp.bfloat16)
    d_proj = jnp.concatenate([d_query[None], d_pair], axis=0)
    d_qkv = jnp.einsum("rd,erf->edf", rows, d_proj, preferred_element_type=jnp.float32).reshape(3 * D, D)
    d_tokens = d_sum1 + jnp.einsum("erf,edf->rd", d_proj, qkv, preferred_element_type=jnp.float32)
    d_bias_q = jnp.sum(d_query.astype(jnp.float32), axis=0)
    d_bias_v = jnp.sum(d_pair[1].astype(jnp.float32), axis=0)
    d_biases = jnp.stack([d_bias_q, d_bias_v, d_bias_out, d_shift1, d_bias2, d_shift2]).reshape(
        6 * D
    )
    d_gains = jnp.stack([d_gain1, d_gain2]).reshape(2 * D)
    shares = scatter_grads(
        (d_qkv, d_out_w, d_expand, d_contract, d_biases, d_gains, d_ffn_bias), planes
    )
    return (d_tokens, shares)


def on_device(
    tokens,
    qkv_weight,
    out_weight,
    expand_weight,
    contract_weight,
    bias_vectors,
    gain_vectors,
    ffn_bias,
    random_blocks,
    cotangent,
):
    weights = gather_weights(
        qkv_weight, out_weight, expand_weight, contract_weight, bias_vectors, gain_vectors, ffn_bias
    )
    result, saved = layer_forward(tokens, random_blocks, weights)
    planes = kernel_planes((qkv_weight, out_weight, expand_weight, contract_weight))
    d_tokens, shares = layer_backward(tokens, cotangent, weights, saved, planes)
    return (
        result.reshape(SEQ_GRP, TOK_SEQ, D),
        d_tokens.reshape(SEQ_GRP, TOK_SEQ, D),
        shares[0],
        shares[1],
        shares[2],
        shares[3],
        shares[4],
        shares[5],
        shares[6],
    )


def solution(mesh):
    return jax.shard_map(
        on_device,
        mesh=mesh,
        in_specs=(
            P("dp", "seq", None),
            P(("dp", "seq")),
            P(("dp", "seq")),
            P(("dp", "seq")),
            P(("dp", "seq")),
            P(("dp", "seq")),
            P(("dp", "seq")),
            P(("dp", "seq")),
            P("dp", None, "seq", None),
            P("dp", "seq", None),
        ),
        out_specs=(
            P("dp", "seq", None),
            P("dp", "seq", None),
            P(("dp", "seq")),
            P(("dp", "seq")),
            P(("dp", "seq")),
            P(("dp", "seq")),
            P(("dp", "seq")),
            P(("dp", "seq")),
            P(("dp", "seq")),
        ),
        check_vma=False,
    )
```

```python
import functools

import jax
import jax.numpy as jnp
from jax import lax
from jax.experimental import pallas as pl
from jax.experimental.pallas import tpu as pltpu
from jax.sharding import PartitionSpec as P

MESH = pl.DeviceIdType.MESH

D = 768
FF = 3072
H = 12
HD = 64
BLOCK = 64
TOK_SEQ = 256
SEQ_GRP = 1
BPD = 4


norm_eps = 1e-12
masked_score = -1e30


def matmul(left, right):
    return jnp.dot(left, right, preferred_element_type=jnp.float32)


def inner_rows(left, right):
    return lax.dot_general(
        left, right, (((0,), (0,)), ((), ())), preferred_element_type=jnp.float32
    )


def outer_cols(left, right):
    return lax.dot_general(
        left, right, (((1,), (1,)), ((), ())), preferred_element_type=jnp.float32
    )


def gelu_tanh(value):
    return jax.nn.gelu(value, approximate=True)


def normalize(value, gain, shift):
    mean = jnp.mean(value, axis=-1, keepdims=True)
    centred = value - mean
    inverse = lax.rsqrt(jnp.mean(centred * centred, axis=-1, keepdims=True) + norm_eps)
    normed = centred * inverse
    return (normed * gain + shift, normed, inverse)


def normalize_back(grad, normed, inverse, gain):
    scaled = grad * gain
    centred = scaled - jnp.mean(scaled, axis=-1, keepdims=True)
    return inverse * (centred - normed * jnp.mean(scaled * normed, axis=-1, keepdims=True))


def place(nz):
    y = lax.axis_index("dp")
    s = lax.axis_index("seq")
    return {"y": y, "z": s // 4, "x": (s // 2) % 2, "c": s % 2}

def device(p):
    return (p["y"], p["z"] * 4 + p["x"] * 2 + p["c"])

def chip(p, nz):
    return (p["y"] * nz + p["z"]) * 2 + p["x"]

def index(p, nz):
    return chip(p, nz) * 2 + p["c"]

def nearest(m, n, j):
    if n == 2:
        return m if j == 0 else 1 - m
    out = 0
    for i in range(n):
        rank = sorted(range(n), key=lambda s: (abs(s - i), s))
        out = jnp.where(m == i, rank[j], out)
    return out

ORDERS = (("z", "x", "y"), ("z", "y", "x"), ("x", "y", "z"))

def gather_kernel(nz, *refs):
    k = len(ORDERS)
    xs, gs = refs[:k], refs[k:2 * k]
    own_sem, send_sem, recv_sem, csend, crecv = refs[2 * k:]
    me = place(nz)
    size = {"y": 2, "z": nz, "x": 2}
    sib = dict(me, c=1 - me["c"])
    bar = pltpu.get_barrier_semaphore()
    for d in ("x", "y", "c"):
        pl.semaphore_signal(bar, inc=1, device_id=device(dict(me, **{d: 1 - me[d]})), device_id_type=MESH)
    @pl.when(me["z"] > 0)
    def _():
        pl.semaphore_signal(bar, inc=1, device_id=device(dict(me, z=me["z"] - 1)), device_id_type=MESH)
    @pl.when(me["z"] < nz - 1)
    def _():
        pl.semaphore_signal(bar, inc=1, device_id=device(dict(me, z=me["z"] + 1)), device_id_type=MESH)
    inside = jnp.where(me["z"] > 0, 1, 0) + jnp.where(me["z"] < nz - 1, 1, 0)
    pl.semaphore_wait(bar, 3 + inside)

    pending = []
    def remote(item, src_ref, slot, sem_slot, way, to, cond=None):
        cp = pltpu.make_async_remote_copy(src_ref=src_ref, dst_ref=gs[item].at[slot], send_sem=send_sem.at[item, sem_slot, way],
            recv_sem=recv_sem.at[item, sem_slot], device_id=device(to), device_id_type=MESH)
        if cond is None:
            cp.start()
        else:
            pl.when(cond)(cp.start)
        pending.append((cp, cond))

    work = []
    for item in range(k):
        order = ORDERS[item]
        n0, n1, n2 = (size[d] for d in order)
        for i2 in range(n2):
            for i1 in range(n1):
                for i0 in range(n0):
                    work.append((i0 + i1 + i2, item, i0, i1, i2))
    work.sort(key=lambda w: w[0])
    local = []
    for depth, item, i0, i1, i2 in work:
        order = ORDERS[item]
        src = dict(me)
        for d, i in zip(order, (i0, i1, i2)):
            src[d] = nearest(me[d], size[d], i)
        c = chip(src, nz)
        slot = c * 2 + me["c"]
        own = depth == 0
        ref = xs[item] if own else gs[item].at[slot]
        if not own:
            pltpu.make_async_remote_copy(src_ref=ref, dst_ref=ref, send_sem=send_sem.at[item, c, 0], recv_sem=recv_sem.at[item, c],
                device_id=device(sib), device_id_type=MESH).wait_recv()
        stage = 2 if i2 else (1 if i1 else 0)
        for t in range(stage, 3):
            d = order[t]
            onward = t == stage and not own
            if d == "z":
                if nz > 1:
                    up = me["z"] < nz - 1
                    dn = me["z"] > 0
                    if onward:
                        up = jnp.logical_and(up, src["z"] <= me["z"])
                        dn = jnp.logical_and(dn, src["z"] >= me["z"])
                    remote(item, ref, slot, c, 0, dict(me, z=jnp.minimum(me["z"] + 1, nz - 1)), up)
                    remote(item, ref, slot, c, 1, dict(me, z=jnp.maximum(me["z"] - 1, 0)), dn)
            elif not (onward and (i0, i1, i2)[t]):
                remote(item, ref, slot, c, 2 if d == "x" else 3, dict(me, **{d: 1 - me[d]}))
        cp = pltpu.make_async_remote_copy(src_ref=ref, dst_ref=gs[item].at[slot], send_sem=csend.at[item, c],
            recv_sem=crecv.at[item, c], device_id=device(sib), device_id_type=MESH)
        cp.start()
        pending.append((cp, None))
        if own:
            lc = pltpu.make_async_copy(xs[item], gs[item].at[slot], own_sem.at[item])
            lc.start()
            local.append(lc)
    for lc in local:
        lc.wait()
    for item in range(k):
        def body(c, _):
            ref = gs[item].at[c * 2 + 1 - me["c"]]
            pltpu.make_async_remote_copy(src_ref=ref, dst_ref=ref, send_sem=csend.at[item, c], recv_sem=crecv.at[item, c],
                device_id=device(sib), device_id_type=MESH).wait_recv()
            return 0
        lax.fori_loop(0, 4 * nz, body, 0)
    for cp, cond in pending:
        if cond is None:
            cp.wait_send()
        else:
            pl.when(cond)(cp.wait_send)

def gather_all(xs, nz):
    n = 8 * nz
    k = len(xs)
    chips = 4 * nz
    return pl.pallas_call(
        functools.partial(gather_kernel, nz),
        out_shape=[jax.ShapeDtypeStruct((n,) + x.shape, x.dtype) for x in xs],
        in_specs=[pl.BlockSpec(memory_space=pl.ANY)] * k,
        out_specs=[pl.BlockSpec(memory_space=pl.ANY)] * k,
        scratch_shapes=[pltpu.SemaphoreType.DMA((k,)), pltpu.SemaphoreType.DMA((k, chips, 4)), pltpu.SemaphoreType.DMA((k, chips)),
            pltpu.SemaphoreType.DMA((k, chips)), pltpu.SemaphoreType.DMA((k, chips))],
        compiler_params=pltpu.CompilerParams(collective_id=0, has_side_effects=True),
        name="gather_weights",
    )(*xs)


CHAIN_FIRST = (False, False, False, True, False)
LINKS = (("x", "y"), ("x", "y"), ("y", "x"), ("x", "y"), ("x", "y"))

def combine(dst, srcs):
    rows, cols = dst.shape
    step = min(cols, max(128, (24 * 1024 // rows) // 128 * 128))
    while cols % step:
        step -= 128
    def part(sl):
        total = srcs[0][:, sl].astype(jnp.float32)
        for s in srcs[1:]:
            total = total + s[:, sl].astype(jnp.float32)
        dst[:, sl] = total.astype(dst.dtype)
    if cols == step:
        part(slice(None))
    else:
        def body(i, _):
            part(pl.ds(pl.multiple_of(i * step, 128), step))
            return 0
        lax.fori_loop(0, cols // step, body, 0)

def scatter_kernel(nz, k, *refs):
    xs, outs = refs[:k], refs[k:2 * k]
    scr = refs[2 * k:]
    acc, rc, ra, rb, below, above = (scr[i * k:(i + 1) * k] for i in range(6))
    csend, crecv, send_sem, recv_sem = scr[6 * k:]
    me = place(nz)
    mz = me["z"]
    sib = dict(me, c=1 - me["c"])
    bar = pltpu.get_barrier_semaphore()
    for d in ("x", "y", "c"):
        pl.semaphore_signal(bar, inc=1, device_id=device(dict(me, **{d: 1 - me[d]})), device_id_type=MESH)
    @pl.when(mz > 0)
    def _():
        pl.semaphore_signal(bar, inc=1, device_id=device(dict(me, z=mz - 1)), device_id_type=MESH)
    @pl.when(mz < nz - 1)
    def _():
        pl.semaphore_signal(bar, inc=1, device_id=device(dict(me, z=mz + 1)), device_id_type=MESH)
    pl.semaphore_wait(bar, 3 + jnp.where(mz > 0, 1, 0) + jnp.where(mz < nz - 1, 1, 0))

    pending = []
    up_to = dict(me, z=jnp.minimum(mz + 1, nz - 1))
    dn_to = dict(me, z=jnp.maximum(mz - 1, 0))

    def copy(item, src, dst, ss, rs, to):
        return pltpu.make_async_remote_copy(src_ref=src, dst_ref=dst, send_sem=ss, recv_sem=rs, device_id=device(to), device_id_type=MESH)

    def start(cp, cond=None):
        if cond is None:
            cp.start()
        else:
            pl.when(cond)(cp.start)
        pending.append((cp, cond))

    def arrived(item, ref, sem):
        copy(item, ref, ref, send_sem.at[item, 0], sem, sib).wait_recv()

    def piece(z, x, y):
        return (y * nz + z) * 2 + x

    def coords(a, b, item):
        la, lb = LINKS[item]
        return {la: a, lb: b}

    def wanted(item):
        la, lb = LINKS[item]
        out = []
        zs = [0, nz - 1, 1, nz - 2][:nz] if nz == 4 else list(range(nz))
        if CHAIN_FIRST[item]:
            for z in zs:
                for fa in (1, 0):
                    for fb in (1, 0):
                        out.append((z, fa, fb))
        else:
            for fb in (1, 0):
                for fa in (1, 0):
                    for z in zs:
                        out.append((z, fa, fb))
        return out

    def flip(d, f):
        return 1 - me[d] if f else me[d]

    order_items = (1, 2, 3, 4, 0)
    lists = {i: wanted(i) for i in range(k)}
    for n in range(4 * nz):
        for item in order_items:
            z, fa, fb = lists[item][n]
            la, lb = LINKS[item]
            p = piece(z, **{la: flip(la, fa), lb: flip(lb, fb)})
            start(copy(item, xs[item].at[p * 2 + 1 - me["c"]], rc[item].at[p], csend.at[item, p], crecv.at[item, p], sib))

    steps = []
    def tail(item):
        la, lb = LINKS[item]
        def own(p):
            arrived(item, rc[item].at[p], crecv.at[item, p])
            return [xs[item].at[p * 2 + me["c"]], rc[item].at[p]]
        zs = [nz - 1, 0, nz - 2, 1] if nz == 4 else list(reversed(range(nz)))
        if not CHAIN_FIRST[item]:
            def stage_b(z, fa):
                def run():
                    a = flip(la, fa)
                    p = piece(z, **{la: a, lb: 1 - me[lb]})
                    combine(acc[item].at[p], own(p))
                    s = z * 2 + a
                    start(copy(item, acc[item].at[p], rb[item].at[s], send_sem.at[item, s], recv_sem.at[item, s], dict(me, **{lb: 1 - me[lb]})))
                return run
            def stage_a(z):
                def run():
                    a = 1 - me[la]
                    p = piece(z, **{la: a, lb: me[lb]})
                    s = z * 2 + a
                    srcs = own(p)
                    arrived(item, rb[item].at[s], recv_sem.at[item, s])
                    combine(acc[item].at[p], srcs + [rb[item].at[s]])
                    s2 = 2 * nz + z
                    start(copy(item, acc[item].at[p], ra[item].at[z], send_sem.at[item, s2], recv_sem.at[item, s2], dict(me, **{la: 1 - me[la]})))
                return run
            def base(z):
                p = piece(z, **{la: me[la], lb: me[lb]})
                s = z * 2 + me[la]
                srcs = own(p)
                arrived(item, rb[item].at[s], recv_sem.at[item, s])
                arrived(item, ra[item].at[z], recv_sem.at[item, 2 * nz + z])
                return p, srcs + [rb[item].at[s], ra[item].at[z]]
            def chain(z):
                def run():
                    p, srcs = base(z)
                    sb, sa = 3 * nz + z, 4 * nz + z
                    @pl.when(jnp.logical_and(mz == 0, z > 0))
                    def _():
                        combine(acc[item].at[p], srcs)
                    @pl.when(jnp.logical_and(mz > 0, mz < z))
                    def _():
                        arrived(item, below[item].at[z], recv_sem.at[item, sb])
                        combine(acc[item].at[p], srcs + [below[item].at[z]])
                    if z > 0:
                        start(copy(item, acc[item].at[p], below[item].at[z], send_sem.at[item, sb], recv_sem.at[item, sb], up_to), mz < z)
                    @pl.when(jnp.logical_and(mz == nz - 1, z < nz - 1))
                    def _():
                        combine(acc[item].at[p], srcs)
                    @pl.when(jnp.logical_and(mz < nz - 1, mz > z))
                    def _():
                        arrived(item, above[item].at[z], recv_sem.at[item, sa])
                        combine(acc[item].at[p], srcs + [above[item].at[z]])
                    if z < nz - 1:
                        start(copy(item, acc[item].at[p], above[item].at[z], send_sem.at[item, sa], recv_sem.at[item, sa], dn_to), mz > z)
                return run
            def last():
                for z in range(nz):
                    @pl.when(mz == z)
                    def _():
                        p, srcs = piece(z, **{la: me[la], lb: me[lb]}), None
                        s = z * 2 + me[la]
                        srcs = [xs[item].at[p * 2 + me["c"]], rc[item].at[p], rb[item].at[s], ra[item].at[z]]
                        if z > 0:
                            arrived(item, below[item].at[z], recv_sem.at[item, 3 * nz + z])
                            srcs.append(below[item].at[z])
                        if z < nz - 1:
                            arrived(item, above[item].at[z], recv_sem.at[item, 4 * nz + z])
                            srcs.append(above[item].at[z])
                        combine(outs[item], srcs)
            out = []
            for n, z in enumerate(zs):
                out.append((1 + n, stage_b(z, 1)))
            for n, z in enumerate(zs):
                out.append((5 + n, stage_b(z, 0)))
                out.append((5.5 + n, stage_a(z)))
            for n, z in enumerate(zs):
                out.append((9.5 + n, chain(z)))
            out.append((20, last))
            return out
        def chain(z, fa, fb):
            def run():
                a, b = flip(la, fa), flip(lb, fb)
                p = piece(z, **{la: a, lb: b})
                q = a * 2 + b
                srcs = own(p)
                sb, sa = z * 4 + q, 4 * nz + z * 4 + q
                bref, aref = below[item].at[z * 4 + q], above[item].at[z * 4 + q]
                if z > 0:
                    @pl.when(mz == 0)
                    def _():
                        combine(acc[item].at[p], srcs)
                    @pl.when(jnp.logical_and(mz > 0, mz < z))
                    def _():
                        arrived(item, bref, recv_sem.at[item, sb])
                        combine(acc[item].at[p], srcs + [bref])
                    start(copy(item, acc[item].at[p], bref, send_sem.at[item, sb], recv_sem.at[item, sb], up_to), mz < z)
                if z < nz - 1:
                    @pl.when(mz == nz - 1)
                    def _():
                        combine(acc[item].at[p], srcs)
                    @pl.when(jnp.logical_and(mz < nz - 1, mz > z))
                    def _():
                        arrived(item, aref, recv_sem.at[item, sa])
                        combine(acc[item].at[p], srcs + [aref])
                    start(copy(item, acc[item].at[p], aref, send_sem.at[item, sa], recv_sem.at[item, sa], dn_to), mz > z)
            return run
        def settle(fa, fb):
            a, b = flip(la, fa), flip(lb, fb)
            q = a * 2 + b
            for z in range(nz):
                @pl.when(mz == z)
                def _():
                    p = piece(z, **{la: a, lb: b})
                    srcs = [xs[item].at[p * 2 + me["c"]], rc[item].at[p]]
                    if z > 0:
                        arrived(item, below[item].at[z * 4 + q], recv_sem.at[item, z * 4 + q])
                        srcs.append(below[item].at[z * 4 + q])
                    if z < nz - 1:
                        arrived(item, above[item].at[z * 4 + q], recv_sem.at[item, 4 * nz + z * 4 + q])
                        srcs.append(above[item].at[z * 4 + q])
                    combine(acc[item].at[p], srcs)
            return piece(mz, **{la: a, lb: b})
        s0 = 8 * nz
        def to_b(fa):
            def run():
                p = settle(fa, 1)
                start(copy(item, acc[item].at[p], rb[item].at[fa], send_sem.at[item, s0 + fa], recv_sem.at[item, s0 + fa], dict(me, **{lb: 1 - me[lb]})))
            return run
        def to_a():
            p = settle(1, 0)
            arrived(item, rb[item].at[1], recv_sem.at[item, s0 + 1])
            combine(ra[item].at[0], [acc[item].at[p], rb[item].at[1]])
            start(copy(item, ra[item].at[0], ra[item].at[1], send_sem.at[item, s0 + 2], recv_sem.at[item, s0 + 2], dict(me, **{la: 1 - me[la]})))
        def last():
            p = settle(0, 0)
            arrived(item, rb[item].at[0], recv_sem.at[item, s0])
            arrived(item, ra[item].at[1], recv_sem.at[item, s0 + 2])
            combine(outs[item], [acc[item].at[p], rb[item].at[0], ra[item].at[1]])
        out = []
        for n, z in enumerate(zs):
            for m, (fa, fb) in enumerate(((1, 1), (0, 1), (1, 0), (0, 0))):
                out.append((1 + n * 3 + m * 0.5, chain(z, fa, fb)))
        out.append((12.6, to_b(1)))
        out.append((12.7, to_b(0)))
        out.append((14, to_a))
        out.append((21, last))
        return out

    for n, item in enumerate(order_items):
        steps += [(w + 0.01 * n, f) for w, f in tail(item)]
    for _, f in sorted(steps, key=lambda s: s[0]):
        f()
    for cp, cond in pending:
        if cond is None:
            cp.wait_send()
        else:
            pl.when(cond)(cp.wait_send)

def scatter_all(xs, nz):
    k = len(xs)
    chips = 4 * nz
    slab = [x.shape[1:] for x in xs]
    dt = [x.dtype for x in xs]
    def buf(counts):
        return [pltpu.VMEM((n,) + s, d) for n, s, d in zip(counts, slab, dt)]
    scr = buf([chips] * k) + buf([chips] * k)
    scr += buf([2 if CHAIN_FIRST[i] else nz for i in range(k)])
    scr += buf([2 if CHAIN_FIRST[i] else 2 * nz for i in range(k)])
    scr += buf([4 * nz if CHAIN_FIRST[i] else nz for i in range(k)]) * 2
    sems = 8 * nz + 3
    scr += [pltpu.SemaphoreType.DMA((k, chips)), pltpu.SemaphoreType.DMA((k, chips)), pltpu.SemaphoreType.DMA((k, sems)), pltpu.SemaphoreType.DMA((k, sems))]
    return pl.pallas_call(
        functools.partial(scatter_kernel, nz, k),
        out_shape=[jax.ShapeDtypeStruct(s, jnp.float32) for s in slab],
        in_specs=[pl.BlockSpec(memory_space=pltpu.VMEM)] * k,
        out_specs=[pl.BlockSpec(memory_space=pltpu.VMEM)] * k,
        scratch_shapes=scr,
        compiler_params=pltpu.CompilerParams(collective_id=1, has_side_effects=True, vmem_limit_bytes=60 << 20),
        name="scatter_grads",
    )(*xs)


def kernel_planes(arrays):
    seq = lax.axis_size("seq")
    if lax.axis_size("dp") != 2 or seq % 4 or seq > 16:
        return 0
    rows = [a.size % c for a, c in zip(arrays, (D, D, FF, D))]
    return 0 if any(rows) else seq // 4


def gather_weights(
    qkv_weight, out_weight, expand_weight, contract_weight, bias_vectors, gain_vectors, ffn_bias
):
    vectors = jnp.concatenate([bias_vectors, gain_vectors, ffn_bias])
    planes = kernel_planes((qkv_weight, out_weight, expand_weight, contract_weight))
    if planes:
        shards = 8 * planes
        depth = expand_weight.size // FF
        tail = jnp.pad(vectors, (0, depth * 128 - vectors.size)).reshape(depth, 128)
        first = jnp.concatenate(
            [expand_weight.reshape(depth, FF), out_weight.reshape(depth, D), tail], axis=1
        )
        first, contract, qkv = gather_all(
            (first, contract_weight.reshape(-1, D), qkv_weight.reshape(-1, D)), planes
        )
        rows = first.reshape(D, FF + D + 128)
        expand, out = rows[:, :FF], rows[:, FF : FF + D]
        vectors = rows[:, FF + D :].reshape(shards, depth * 128)
        contract = contract.reshape(FF, D)
        qkv = qkv.reshape(3, D, D)
    else:
        gather = functools.partial(lax.all_gather, axis_name=("dp", "seq"), axis=0, tiled=True)
        qkv = gather(qkv_weight).reshape(3, D, D)
        out = gather(out_weight).reshape(D, D)
        expand = gather(expand_weight).reshape(D, FF)
        contract = gather(contract_weight).reshape(FF, D)
        vectors = gather(vectors[None])
    a, b, c = bias_vectors.size, gain_vectors.size, ffn_bias.size
    vectors = vectors.astype(jnp.float32)
    return (
        qkv,
        out,
        expand,
        contract,
        vectors[:, :a].reshape(6, D),
        vectors[:, a : a + b].reshape(2, D),
        vectors[:, a + b : a + b + c].reshape(FF),
    )


def scatter_grads(grads, planes):
    d_qkv, d_out, d_expand, d_contract, d_biases, d_gains, d_ffn_bias = grads
    shards = lax.axis_size("dp") * lax.axis_size("seq")
    vectors = jnp.concatenate(
        [v.reshape(shards, -1) for v in (d_biases, d_gains, d_ffn_bias)], axis=1
    )
    if planes:
        low = [g.astype(jnp.bfloat16) for g in (d_expand, d_contract, d_qkv, d_out)]
        width = vectors.shape[1]
        padded = jnp.pad(vectors, ((0, 0), (0, -width % 1024)))
        parts = [padded.reshape(shards, -1, 128)]
        parts += [g.reshape(shards, -1, g.shape[-1]) for g in low]
        vectors, d_expand, d_contract, d_qkv, d_out = scatter_all(parts, planes)
        vectors = vectors.reshape(-1)[:width]
    else:
        d_expand, d_contract, d_qkv, d_out = [
            lax.psum_scatter(g.reshape(-1), ("dp", "seq"), scatter_dimension=0, tiled=True)
            for g in (d_expand, d_contract, d_qkv, d_out)
        ]
        vectors = lax.psum_scatter(vectors, ("dp", "seq"), scatter_dimension=0, tiled=True)[0]
    a, b = d_biases.size // shards, d_gains.size // shards
    return (
        d_qkv.reshape(-1),
        d_out.reshape(-1),
        d_expand.reshape(-1),
        d_contract.reshape(-1),
        vectors[:a],
        vectors[a : a + b],
        vectors[a + b :],
    )


def owner(head, n):
    return head * n // H


def owned(place, n):
    head = (place * H + n - 1) // n
    return jnp.minimum(head, H - 1), jnp.logical_and(head < H, owner(head, n) == place)


def greet_senders(n, place, mine, to_owners):
    row = lax.axis_index("dp")
    bar = pltpu.get_barrier_semaphore()

    def signal(to):
        @pl.when(to != place)
        def _():
            pl.semaphore_signal(bar, inc=1, device_id=(row, to), device_id_type=MESH)

    if to_owners:

        @pl.when(mine)
        def _():
            lax.fori_loop(0, n, lambda s, _: (signal(s), 0)[1], 0)

        pl.semaphore_wait(bar, H - jnp.where(mine, 1, 0))
    else:
        lax.fori_loop(0, H, lambda h, _: (signal(owner(h, n)), 0)[1], 0)

        @pl.when(mine)
        def _():
            pl.semaphore_wait(bar, n - 1)


def send_to_owners(n, place, head, mine, pairs, sems):
    row = lax.axis_index("dp")
    send_sem, recv_sem, own_sem = sems
    first = head + 1

    def walk(act):
        def body(k, _):
            h = (first + k) % H
            to = owner(h, n)
            for i, (src, dst) in enumerate(pairs):

                @pl.when(to != place)
                def _():
                    act(
                        pltpu.make_async_remote_copy(
                            src_ref=src.at[h],
                            dst_ref=dst.at[place],
                            send_sem=send_sem.at[i, h],
                            recv_sem=recv_sem.at[i, place],
                            device_id=(row, to),
                            device_id_type=MESH,
                        )
                    )

            return 0

        lax.fori_loop(0, H, body, 0)

    walk(lambda cp: cp.start())

    @pl.when(mine)
    def _():
        for i, (src, dst) in enumerate(pairs):
            cp = pltpu.make_async_copy(src.at[head], dst.at[place], own_sem.at[i])
            cp.start()
            cp.wait()

        def body(k, _):
            s = (place + 1 + k) % n
            for i, (src, dst) in enumerate(pairs):
                pltpu.make_async_remote_copy(
                    src_ref=src.at[0],
                    dst_ref=dst.at[s],
                    send_sem=send_sem.at[i, 0],
                    recv_sem=recv_sem.at[i, s],
                    device_id=(row, place),
                    device_id_type=MESH,
                ).wait_recv()
            return 0

        lax.fori_loop(0, n - 1, body, 0)

    walk(lambda cp: cp.wait_send())


def send_from_owners(n, place, head, mine, src, dst, sems):
    row = lax.axis_index("dp")
    send_sem, recv_sem, own_sem = sems

    def walk(act):
        def body(k, _):
            to = (place + 1 + k) % n
            act(
                pltpu.make_async_remote_copy(
                    src_ref=src.at[to],
                    dst_ref=dst.at[head],
                    send_sem=send_sem.at[0, to],
                    recv_sem=recv_sem.at[0, head],
                    device_id=(row, to),
                    device_id_type=MESH,
                )
            )
            return 0

        lax.fori_loop(0, n - 1, body, 0)

    @pl.when(mine)
    def _():
        walk(lambda cp: cp.start())
        cp = pltpu.make_async_copy(src.at[place], dst.at[head], own_sem.at[0])
        cp.start()
        cp.wait()

    def body(k, _):
        h = (head + k) % H

        @pl.when(owner(h, n) != place)
        def _():
            pltpu.make_async_remote_copy(
                src_ref=src.at[0],
                dst_ref=dst.at[h],
                send_sem=send_sem.at[0, 0],
                recv_sem=recv_sem.at[0, h],
                device_id=(row, place),
                device_id_type=MESH,
            ).wait_recv()

        return 0

    lax.fori_loop(0, H, body, 0)

    @pl.when(mine)
    def _():
        walk(lambda cp: cp.wait_send())


def swap_halves(tile):
    return pltpu.roll(tile, HD, tile.ndim - 1)


def low_lanes(shape):
    return lax.broadcasted_iota(jnp.int32, shape, len(shape) - 1) < HD


def project_kernel(n, rows_ref, w_ref, bias_ref, picks_ref, out_ref, out_picks_ref, box, *sems):
    place = lax.axis_index("seq")
    head, mine = owned(place, n)
    greet_senders(n, place, mine, True)
    rows = rows_ref[...]
    left = low_lanes((TOK_SEQ, 128))
    left_q = low_lanes((BLOCK, 128))
    wide = 256
    for g in range(D // wide):
        cols = slice(g * wide, (g + 1) * wide)
        q = (matmul(rows, w_ref[0, :, cols]) + bias_ref[0:1, cols]) * HD ** (-0.5)
        k = matmul(rows, w_ref[1, :, cols])
        v = matmul(rows, w_ref[2, :, cols]) + bias_ref[1:2, cols]
        for p in range(wide // 128):
            h = (g * wide + p * 128) // HD
            lanes = slice(p * 128, (p + 1) * 128)
            kp, vp, qp = k[:, lanes], v[:, lanes], q[:, lanes]
            box[h, 0:TOK_SEQ, :] = jnp.where(left, kp, swap_halves(vp)).astype(jnp.bfloat16)
            box[h + 1, 0:TOK_SEQ, :] = jnp.where(left, swap_halves(kp), vp).astype(jnp.bfloat16)
            turned = swap_halves(qp)
            for t in range(BPD // 2):
                a = slice(2 * t * BLOCK, (2 * t + 1) * BLOCK)
                b = slice((2 * t + 1) * BLOCK, (2 * t + 2) * BLOCK)
                to = slice(TOK_SEQ + t * BLOCK, TOK_SEQ + (t + 1) * BLOCK)
                box[h, to, :] = jnp.where(left_q, qp[a], turned[b]).astype(jnp.bfloat16)
                box[h + 1, to, :] = jnp.where(left_q, turned[a], qp[b]).astype(jnp.bfloat16)
    send_to_owners(
        n, place, head, mine, ((box, out_ref), (picks_ref, out_picks_ref)), sems
    )


def exchange_sems(n, pairs=1):
    return [
        pltpu.SemaphoreType.DMA((pairs, max(n, H))),
        pltpu.SemaphoreType.DMA((pairs, max(n, H))),
        pltpu.SemaphoreType.DMA((pairs,)),
    ]


ANY = pl.BlockSpec(memory_space=pl.ANY)
VMEM = pl.BlockSpec(memory_space=pltpu.VMEM)
SMEM = pl.BlockSpec(memory_space=pltpu.SMEM)
MSG = TOK_SEQ + TOK_SEQ // 2


def project_and_send(rows, qkv, biases, picks):
    n = lax.axis_size("seq")
    picks = jnp.pad(picks.reshape(H, 1, BPD * 3), ((0, 0), (0, 7), (0, 128 - BPD * 3)))
    return pl.pallas_call(
        functools.partial(project_kernel, n),
        out_shape=(
            jax.ShapeDtypeStruct((n, MSG, 128), jnp.bfloat16),
            jax.ShapeDtypeStruct((n, 8, 128), jnp.int32),
        ),
        in_specs=[VMEM, VMEM, VMEM, ANY],
        out_specs=(ANY, ANY),
        scratch_shapes=[pltpu.VMEM((H, MSG, 128), jnp.bfloat16)] + exchange_sems(n, 2),
        compiler_params=pltpu.CompilerParams(
            collective_id=2, has_side_effects=True, vmem_limit_bytes=48 << 20
        ),
        name="project_and_send",
    )(rows, qkv, biases, picks)


def to_owners_kernel(n, src, dst, *sems):
    place = lax.axis_index("seq")
    head, mine = owned(place, n)
    greet_senders(n, place, mine, True)
    send_to_owners(n, place, head, mine, ((src, dst),), sems)


def from_owners_kernel(n, src, dst, *sems):
    place = lax.axis_index("seq")
    head, mine = owned(place, n)
    greet_senders(n, place, mine, False)
    send_from_owners(n, place, head, mine, src, dst, sems)


def exchange(kernel, slots, messages, ident, name):
    n = lax.axis_size("seq")
    return pl.pallas_call(
        functools.partial(kernel, n),
        out_shape=jax.ShapeDtypeStruct((slots,) + messages.shape[1:], messages.dtype),
        in_specs=[ANY],
        out_specs=ANY,
        scratch_shapes=exchange_sems(n),
        compiler_params=pltpu.CompilerParams(collective_id=ident, has_side_effects=True),
        name=name,
    )(messages)


def key_list(i, n, picks_ref):
    last = n * BPD - 1

    def of(b):
        s, r = b // BPD, b % BPD
        picked = [picks_ref[s, 0, r * 3 + j] for j in range(3)]
        return [jnp.maximum(b - 1, 0), b, jnp.minimum(b + 1, last), 0, last] + picked

    return [
        [(b // BPD, pl.multiple_of(b % BPD * BLOCK, BLOCK)) for b in of(2 * i + t)]
        for t in range(2)
    ]


def fill_pair(lists, kv_ref, vk_ref, keys, values):
    for j in range(8):
        (sa, ra), (sb, rb) = lists[0][j], lists[1][j]
        to = slice(j * BLOCK, (j + 1) * BLOCK)
        keys[to, 0:HD] = kv_ref[sa, pl.ds(ra, BLOCK), 0:HD]
        keys[to, HD:128] = vk_ref[sb, pl.ds(rb, BLOCK), HD:128]
        values[to, 0:HD] = vk_ref[sa, pl.ds(ra, BLOCK), 0:HD]
        values[to, HD:128] = kv_ref[sb, pl.ds(rb, BLOCK), HD:128]


def two_blocks(tile):
    left = low_lanes(tile.shape)
    zero = jnp.zeros_like(tile)
    return jnp.concatenate([jnp.where(left, tile, zero), jnp.where(left, zero, tile)], axis=0)


def pair_scores(i, n, keys, query):
    scores = outer_cols(keys, query)
    left = low_lanes((BLOCK, 128))
    right = jnp.logical_not(left)
    end = n * BPD // 2 - 1
    hide_first = jnp.logical_and(left, i == 0)
    hide_last = jnp.logical_and(right, i == end)
    return jnp.concatenate(
        [
            jnp.where(hide_first, masked_score, scores[0:BLOCK]),
            scores[BLOCK : 2 * BLOCK],
            jnp.where(hide_last, masked_score, scores[2 * BLOCK : 3 * BLOCK]),
            scores[3 * BLOCK :],
        ],
        axis=0,
    )


def pair_place(i):
    return i // (BPD // 2), pl.multiple_of(i % (BPD // 2) * BLOCK, BLOCK)


def turn_pairs(n, kv_ref, vk_ref):
    def body(s, _):
        tile = kv_ref[s, 0:TOK_SEQ, :].astype(jnp.float32)
        vk_ref[s] = swap_halves(tile).astype(jnp.bfloat16)
        return 0

    lax.fori_loop(0, n, body, 0)


def attend_kernel(n, kvq_ref, picks_ref, out_ref, lse_ref, vk_ref, keys, values):
    place = lax.axis_index("seq")
    head, mine = owned(place, n)

    @pl.when(mine)
    def _():
        turn_pairs(n, kvq_ref, vk_ref)

        def body(i, _):
            fill_pair(key_list(i, n, picks_ref), kvq_ref, vk_ref, keys, values)
            s, r = pair_place(i)
            query = two_blocks(kvq_ref[s, pl.ds(TOK_SEQ + r, BLOCK), :])
            scores = pair_scores(i, n, keys[...], query)
            top = jnp.max(scores, axis=0, keepdims=True)
            weights = jnp.exp(scores - top)
            total = jnp.sum(weights, axis=0, keepdims=True)
            probs = (weights * (1.0 / total)).astype(jnp.bfloat16)
            full = inner_rows(probs, values[...])
            left = low_lanes((BLOCK, 128))
            out_ref[s, pl.ds(r, BLOCK), :] = jnp.where(left, full[:BLOCK], full[BLOCK:]).astype(
                jnp.bfloat16
            )
            lse_ref[i] = top + jnp.log(total)
            return 0

        lax.fori_loop(0, n * BPD // 2, body, 0)


def attend_heads(kvq, picks):
    n = lax.axis_size("seq")
    return pl.pallas_call(
        functools.partial(attend_kernel, n),
        out_shape=(
            jax.ShapeDtypeStruct((n, TOK_SEQ // 2, 128), jnp.bfloat16),
            jax.ShapeDtypeStruct((n * BPD // 2, 1, 128), jnp.float32),
        ),
        in_specs=[VMEM, SMEM],
        out_specs=(VMEM, VMEM),
        scratch_shapes=[
            pltpu.VMEM((n, TOK_SEQ, 128), jnp.bfloat16),
            pltpu.VMEM((8 * BLOCK, 128), jnp.bfloat16),
            pltpu.VMEM((8 * BLOCK, 128), jnp.bfloat16),
        ],
        compiler_params=pltpu.CompilerParams(vmem_limit_bytes=48 << 20),
        name="attend_heads",
    )(kvq, picks)


def attend_back_kernel(
    n, kvq_ref, picks_ref, lse_ref, grad_ref, out_ref, vk_ref, keys, values, sum_k, sum_v
):
    place = lax.axis_index("seq")
    head, mine = owned(place, n)

    @pl.when(mine)
    def _():
        turn_pairs(n, kvq_ref, vk_ref)

        def clear(s, _):
            sum_k[s] = jnp.zeros((TOK_SEQ, 128), jnp.float32)
            sum_v[s] = jnp.zeros((TOK_SEQ, 128), jnp.float32)
            return 0

        lax.fori_loop(0, n, clear, 0)

        def body(i, _):
            lists = key_list(i, n, picks_ref)
            fill_pair(lists, kvq_ref, vk_ref, keys, values)
            s, r = pair_place(i)
            query = two_blocks(kvq_ref[s, pl.ds(TOK_SEQ + r, BLOCK), :])
            grad = two_blocks(grad_ref[s, pl.ds(r, BLOCK), :])
            probs = jnp.exp(pair_scores(i, n, keys[...], query) - lse_ref[i])
            d_probs = outer_cols(values[...], grad)
            rows = jnp.sum(probs * d_probs, axis=0, keepdims=True)
            d_scores = (probs * (d_probs - rows)).astype(jnp.bfloat16)
            d_values = matmul(probs.astype(jnp.bfloat16), grad)
            d_keys = matmul(d_scores, query)
            full = inner_rows(d_scores, keys[...]) * HD ** (-0.5)
            left = low_lanes((BLOCK, 128))
            out_ref[s, pl.ds(TOK_SEQ + r, BLOCK), :] = jnp.where(
                left, full[:BLOCK], full[BLOCK:]
            ).astype(jnp.bfloat16)
            for j in range(8):
                part = slice(j * BLOCK, (j + 1) * BLOCK)
                for t in range(2):
                    sb, rb = lists[t][j]
                    lanes = slice(t * HD, (t + 1) * HD)
                    sum_k[sb, pl.ds(rb, BLOCK), lanes] += d_keys[part, lanes]
                    sum_v[sb, pl.ds(rb, BLOCK), lanes] += d_values[part, lanes]
            return 0

        lax.fori_loop(0, n * BPD // 2, body, 0)

        def close(s, _):
            left = low_lanes((TOK_SEQ, 128))
            k, v = sum_k[s], sum_v[s]
            both = jnp.where(left, k + swap_halves(k), v + swap_halves(v))
            out_ref[s, 0:TOK_SEQ, :] = both.astype(jnp.bfloat16)
            return 0

        lax.fori_loop(0, n, close, 0)


def attend_heads_back(kvq, picks, lse, grad):
    n = lax.axis_size("seq")
    return pl.pallas_call(
        functools.partial(attend_back_kernel, n),
        out_shape=jax.ShapeDtypeStruct((n, MSG, 128), jnp.bfloat16),
        in_specs=[VMEM, SMEM, VMEM, VMEM],
        out_specs=VMEM,
        scratch_shapes=[
            pltpu.VMEM((n, TOK_SEQ, 128), jnp.bfloat16),
            pltpu.VMEM((8 * BLOCK, 128), jnp.bfloat16),
            pltpu.VMEM((8 * BLOCK, 128), jnp.bfloat16),
            pltpu.VMEM((n, TOK_SEQ, 128), jnp.float32),
            pltpu.VMEM((n, TOK_SEQ, 128), jnp.float32),
        ],
        compiler_params=pltpu.CompilerParams(vmem_limit_bytes=56 << 20),
        name="attend_heads_back",
    )(kvq, picks, lse, grad)


def pack_heads(rows):
    parts = rows.reshape(BPD // 2, 2, BLOCK, H, HD).transpose(3, 0, 2, 1, 4)
    return parts.reshape(H, TOK_SEQ // 2, 128)


def unpack_heads(parts):
    parts = parts.reshape(H, BPD // 2, BLOCK, 2, HD).transpose(1, 3, 2, 0, 4)
    return parts.reshape(TOK_SEQ, D)


def unpack_keys(parts):
    parts = parts.reshape(H, TOK_SEQ, 2, HD).transpose(2, 1, 0, 3)
    return parts.reshape(2, TOK_SEQ, D)


def layer_forward(tokens, picks, weights):
    qkv, out_w, expand, contract, biases, gains, ffn_bias = weights
    rows = tokens.reshape(SEQ_GRP * TOK_SEQ, D)
    kvq, picks = project_and_send(rows, qkv, biases, picks)
    attended, lse = attend_heads(kvq, picks)
    mixed = unpack_heads(exchange(from_owners_kernel, H, attended, 3, "return_heads"))
    hidden1 = rows.astype(jnp.float32) + matmul(mixed, out_w) + biases[2]
    normed_out1, normed1, inverse1 = normalize(hidden1, gains[0], biases[3])
    lowered = normed_out1.astype(jnp.bfloat16)
    up = matmul(lowered, expand) + ffn_bias
    active = gelu_tanh(up).astype(jnp.bfloat16)
    hidden2 = normed_out1 + matmul(active, contract) + biases[4]
    result, normed2, inverse2 = normalize(hidden2, gains[1], biases[5])
    saved = (
        kvq,
        picks,
        lse,
        mixed,
        normed1,
        inverse1,
        lowered,
        up,
        active,
        normed2,
        inverse2,
    )
    return (result, saved)


def layer_backward(tokens, cotangent, weights, saved, planes):
    qkv, out_w, expand, contract, biases, gains, ffn_bias = weights
    (
        kvq,
        picks,
        lse,
        mixed,
        normed1,
        inverse1,
        lowered,
        up,
        active,
        normed2,
        inverse2,
    ) = saved
    rows = tokens.reshape(SEQ_GRP * TOK_SEQ, D)
    grad = cotangent.reshape(SEQ_GRP * TOK_SEQ, D).astype(jnp.float32)
    d_gain2 = jnp.sum(grad * normed2, axis=0)
    d_shift2 = jnp.sum(grad, axis=0)
    d_sum2 = normalize_back(grad, normed2, inverse2, gains[1])
    d_down = d_sum2.astype(jnp.bfloat16)
    d_bias2 = jnp.sum(d_down.astype(jnp.float32), axis=0)
    d_contract = inner_rows(active, d_down)
    d_active = outer_cols(d_down, contract)
    gelu_value, gelu_pull = jax.vjp(gelu_tanh, up)
    d_up = gelu_pull(d_active)[0].astype(jnp.bfloat16)
    d_ffn_bias = jnp.sum(d_up.astype(jnp.float32), axis=0)
    d_expand = inner_rows(lowered, d_up)
    d_norm1 = d_sum2 + outer_cols(d_up, expand)
    d_gain1 = jnp.sum(d_norm1 * normed1, axis=0)
    d_shift1 = jnp.sum(d_norm1, axis=0)
    d_sum1 = normalize_back(d_norm1, normed1, inverse1, gains[0])
    d_attn = d_sum1.astype(jnp.bfloat16)
    d_bias_out = jnp.sum(d_attn.astype(jnp.float32), axis=0)
    d_out_w = inner_rows(mixed, d_attn)
    d_mixed = outer_cols(d_attn, out_w).astype(jnp.bfloat16)
    d_heads = exchange(
        to_owners_kernel, lax.axis_size("seq"), pack_heads(d_mixed), 4, "send_head_grads"
    )
    d_heads = exchange(
        from_owners_kernel, H, attend_heads_back(kvq, picks, lse, d_heads), 5, "return_head_grads"
    )
    d_query = unpack_heads(d_heads[:, TOK_SEQ:])
    d_pair = unpack_keys(d_heads[:, :TOK_SEQ])
    d_proj = jnp.concatenate([d_query[None], d_pair], axis=0)
    d_qkv = jnp.einsum("rd,erf->edf", rows, d_proj, preferred_element_type=jnp.float32).reshape(3 * D, D)
    d_tokens = d_sum1 + jnp.einsum("erf,edf->rd", d_proj, qkv, preferred_element_type=jnp.float32)
    d_bias_q = jnp.sum(d_query.astype(jnp.float32), axis=0)
    d_bias_v = jnp.sum(d_pair[1].astype(jnp.float32), axis=0)
    d_biases = jnp.stack([d_bias_q, d_bias_v, d_bias_out, d_shift1, d_bias2, d_shift2]).reshape(
        6 * D
    )
    d_gains = jnp.stack([d_gain1, d_gain2]).reshape(2 * D)
    shares = scatter_grads(
        (d_qkv, d_out_w, d_expand, d_contract, d_biases, d_gains, d_ffn_bias), planes
    )
    return (d_tokens, shares)


def on_device(
    tokens,
    qkv_weight,
    out_weight,
    expand_weight,
    contract_weight,
    bias_vectors,
    gain_vectors,
    ffn_bias,
    random_blocks,
    cotangent,
):
    weights = gather_weights(
        qkv_weight, out_weight, expand_weight, contract_weight, bias_vectors, gain_vectors, ffn_bias
    )
    result, saved = layer_forward(tokens, random_blocks, weights)
    planes = kernel_planes((qkv_weight, out_weight, expand_weight, contract_weight))
    d_tokens, shares = layer_backward(tokens, cotangent, weights, saved, planes)
    return (
        result.reshape(SEQ_GRP, TOK_SEQ, D),
        d_tokens.reshape(SEQ_GRP, TOK_SEQ, D),
        shares[0],
        shares[1],
        shares[2],
        shares[3],
        shares[4],
        shares[5],
        shares[6],
    )


def solution(mesh):
    return jax.shard_map(
        on_device,
        mesh=mesh,
        in_specs=(
            P("dp", "seq", None),
            P(("dp", "seq")),
            P(("dp", "seq")),
            P(("dp", "seq")),
            P(("dp", "seq")),
            P(("dp", "seq")),
            P(("dp", "seq")),
            P(("dp", "seq")),
            P("dp", None, "seq", None),
            P("dp", "seq", None),
        ),
        out_specs=(
            P("dp", "seq", None),
            P("dp", "seq", None),
            P(("dp", "seq")),
            P(("dp", "seq")),
            P(("dp", "seq")),
            P(("dp", "seq")),
            P(("dp", "seq")),
            P(("dp", "seq")),
            P(("dp", "seq")),
        ),
        check_vma=False,
    )
```

```python
import functools

import jax
import jax.numpy as jnp
from jax import lax
from jax.experimental import pallas as pl
from jax.experimental.pallas import tpu as pltpu
from jax.sharding import PartitionSpec as P

MESH = pl.DeviceIdType.MESH

D = 768
FF = 3072
H = 12
HD = 64
BLOCK = 64
TOK_SEQ = 256
SEQ_GRP = 1
BPD = 4


norm_eps = 1e-12
masked_score = -1e30


def matmul(left, right):
    return jnp.dot(left, right, preferred_element_type=jnp.float32)


def inner_rows(left, right):
    return lax.dot_general(
        left, right, (((0,), (0,)), ((), ())), preferred_element_type=jnp.float32
    )


def outer_cols(left, right):
    return lax.dot_general(
        left, right, (((1,), (1,)), ((), ())), preferred_element_type=jnp.float32
    )


def normalize(value, gain, shift):
    mean = jnp.mean(value, axis=-1, keepdims=True)
    centred = value - mean
    inverse = lax.rsqrt(jnp.mean(centred * centred, axis=-1, keepdims=True) + norm_eps)
    normed = centred * inverse
    return (normed * gain + shift, normed, inverse)


def normalize_back(grad, normed, inverse, gain):
    scaled = grad * gain
    centred = scaled - jnp.mean(scaled, axis=-1, keepdims=True)
    return inverse * (centred - normed * jnp.mean(scaled * normed, axis=-1, keepdims=True))


def place(nz):
    y = lax.axis_index("dp")
    s = lax.axis_index("seq")
    return {"y": y, "z": s // 4, "x": (s // 2) % 2, "c": s % 2}

def device(p):
    return (p["y"], p["z"] * 4 + p["x"] * 2 + p["c"])

def chip(p, nz):
    return (p["y"] * nz + p["z"]) * 2 + p["x"]

def index(p, nz):
    return chip(p, nz) * 2 + p["c"]

def nearest(m, n, j):
    if n == 2:
        return m if j == 0 else 1 - m
    out = 0
    for i in range(n):
        rank = sorted(range(n), key=lambda s: (abs(s - i), s))
        out = jnp.where(m == i, rank[j], out)
    return out

ORDERS = (("z", "x", "y"), ("z", "y", "x"), ("x", "y", "z"))

def gather_kernel(nz, *refs):
    k = len(ORDERS)
    xs, gs = refs[:k], refs[k:2 * k]
    own_sem, send_sem, recv_sem, csend, crecv = refs[2 * k:]
    me = place(nz)
    size = {"y": 2, "z": nz, "x": 2}
    sib = dict(me, c=1 - me["c"])
    bar = pltpu.get_barrier_semaphore()
    for d in ("x", "y", "c"):
        pl.semaphore_signal(bar, inc=1, device_id=device(dict(me, **{d: 1 - me[d]})), device_id_type=MESH)
    @pl.when(me["z"] > 0)
    def _():
        pl.semaphore_signal(bar, inc=1, device_id=device(dict(me, z=me["z"] - 1)), device_id_type=MESH)
    @pl.when(me["z"] < nz - 1)
    def _():
        pl.semaphore_signal(bar, inc=1, device_id=device(dict(me, z=me["z"] + 1)), device_id_type=MESH)
    inside = jnp.where(me["z"] > 0, 1, 0) + jnp.where(me["z"] < nz - 1, 1, 0)
    pl.semaphore_wait(bar, 3 + inside)

    pending = []
    def remote(item, src_ref, slot, sem_slot, way, to, cond=None):
        cp = pltpu.make_async_remote_copy(src_ref=src_ref, dst_ref=gs[item].at[slot], send_sem=send_sem.at[item, sem_slot, way],
            recv_sem=recv_sem.at[item, sem_slot], device_id=device(to), device_id_type=MESH)
        if cond is None:
            cp.start()
        else:
            pl.when(cond)(cp.start)
        pending.append((cp, cond))

    work = []
    for item in range(k):
        order = ORDERS[item]
        n0, n1, n2 = (size[d] for d in order)
        for i2 in range(n2):
            for i1 in range(n1):
                for i0 in range(n0):
                    work.append((i0 + i1 + i2, item, i0, i1, i2))
    work.sort(key=lambda w: w[0])
    local = []
    for depth, item, i0, i1, i2 in work:
        order = ORDERS[item]
        src = dict(me)
        for d, i in zip(order, (i0, i1, i2)):
            src[d] = nearest(me[d], size[d], i)
        c = chip(src, nz)
        slot = c * 2 + me["c"]
        own = depth == 0
        ref = xs[item] if own else gs[item].at[slot]
        if not own:
            pltpu.make_async_remote_copy(src_ref=ref, dst_ref=ref, send_sem=send_sem.at[item, c, 0], recv_sem=recv_sem.at[item, c],
                device_id=device(sib), device_id_type=MESH).wait_recv()
        stage = 2 if i2 else (1 if i1 else 0)
        for t in range(stage, 3):
            d = order[t]
            onward = t == stage and not own
            if d == "z":
                if nz > 1:
                    up = me["z"] < nz - 1
                    dn = me["z"] > 0
                    if onward:
                        up = jnp.logical_and(up, src["z"] <= me["z"])
                        dn = jnp.logical_and(dn, src["z"] >= me["z"])
                    remote(item, ref, slot, c, 0, dict(me, z=jnp.minimum(me["z"] + 1, nz - 1)), up)
                    remote(item, ref, slot, c, 1, dict(me, z=jnp.maximum(me["z"] - 1, 0)), dn)
            elif not (onward and (i0, i1, i2)[t]):
                remote(item, ref, slot, c, 2 if d == "x" else 3, dict(me, **{d: 1 - me[d]}))
        cp = pltpu.make_async_remote_copy(src_ref=ref, dst_ref=gs[item].at[slot], send_sem=csend.at[item, c],
            recv_sem=crecv.at[item, c], device_id=device(sib), device_id_type=MESH)
        cp.start()
        pending.append((cp, None))
        if own:
            lc = pltpu.make_async_copy(xs[item], gs[item].at[slot], own_sem.at[item])
            lc.start()
            local.append(lc)
    for lc in local:
        lc.wait()
    for item in range(k):
        def body(c, _):
            ref = gs[item].at[c * 2 + 1 - me["c"]]
            pltpu.make_async_remote_copy(src_ref=ref, dst_ref=ref, send_sem=csend.at[item, c], recv_sem=crecv.at[item, c],
                device_id=device(sib), device_id_type=MESH).wait_recv()
            return 0
        lax.fori_loop(0, 4 * nz, body, 0)
    for cp, cond in pending:
        if cond is None:
            cp.wait_send()
        else:
            pl.when(cond)(cp.wait_send)

def gather_all(xs, nz):
    n = 8 * nz
    k = len(xs)
    chips = 4 * nz
    return pl.pallas_call(
        functools.partial(gather_kernel, nz),
        out_shape=[jax.ShapeDtypeStruct((n,) + x.shape, x.dtype) for x in xs],
        in_specs=[pl.BlockSpec(memory_space=pl.ANY)] * k,
        out_specs=[pl.BlockSpec(memory_space=pl.ANY)] * k,
        scratch_shapes=[pltpu.SemaphoreType.DMA((k,)), pltpu.SemaphoreType.DMA((k, chips, 4)), pltpu.SemaphoreType.DMA((k, chips)),
            pltpu.SemaphoreType.DMA((k, chips)), pltpu.SemaphoreType.DMA((k, chips))],
        compiler_params=pltpu.CompilerParams(collective_id=0, has_side_effects=True),
        name="gather_weights",
    )(*xs)


CHAIN_FIRST = (False, False, False, True, False)
LINKS = (("x", "y"), ("x", "y"), ("y", "x"), ("x", "y"), ("x", "y"))

def combine(dst, srcs):
    rows, cols = dst.shape
    step = min(cols, max(128, (24 * 1024 // rows) // 128 * 128))
    while cols % step:
        step -= 128
    def part(sl):
        total = srcs[0][:, sl].astype(jnp.float32)
        for s in srcs[1:]:
            total = total + s[:, sl].astype(jnp.float32)
        dst[:, sl] = total.astype(dst.dtype)
    if cols == step:
        part(slice(None))
    else:
        def body(i, _):
            part(pl.ds(pl.multiple_of(i * step, 128), step))
            return 0
        lax.fori_loop(0, cols // step, body, 0)

def scatter_kernel(nz, k, *refs):
    xs, outs = refs[:k], refs[k:2 * k]
    scr = refs[2 * k:]
    acc, rc, ra, rb, below, above = (scr[i * k:(i + 1) * k] for i in range(6))
    csend, crecv, send_sem, recv_sem = scr[6 * k:]
    me = place(nz)
    mz = me["z"]
    sib = dict(me, c=1 - me["c"])
    bar = pltpu.get_barrier_semaphore()
    for d in ("x", "y", "c"):
        pl.semaphore_signal(bar, inc=1, device_id=device(dict(me, **{d: 1 - me[d]})), device_id_type=MESH)
    @pl.when(mz > 0)
    def _():
        pl.semaphore_signal(bar, inc=1, device_id=device(dict(me, z=mz - 1)), device_id_type=MESH)
    @pl.when(mz < nz - 1)
    def _():
        pl.semaphore_signal(bar, inc=1, device_id=device(dict(me, z=mz + 1)), device_id_type=MESH)
    pl.semaphore_wait(bar, 3 + jnp.where(mz > 0, 1, 0) + jnp.where(mz < nz - 1, 1, 0))

    pending = []
    up_to = dict(me, z=jnp.minimum(mz + 1, nz - 1))
    dn_to = dict(me, z=jnp.maximum(mz - 1, 0))

    def copy(item, src, dst, ss, rs, to):
        return pltpu.make_async_remote_copy(src_ref=src, dst_ref=dst, send_sem=ss, recv_sem=rs, device_id=device(to), device_id_type=MESH)

    def start(cp, cond=None):
        if cond is None:
            cp.start()
        else:
            pl.when(cond)(cp.start)
        pending.append((cp, cond))

    def arrived(item, ref, sem):
        copy(item, ref, ref, send_sem.at[item, 0], sem, sib).wait_recv()

    def piece(z, x, y):
        return (y * nz + z) * 2 + x

    def coords(a, b, item):
        la, lb = LINKS[item]
        return {la: a, lb: b}

    def wanted(item):
        la, lb = LINKS[item]
        out = []
        zs = [0, nz - 1, 1, nz - 2][:nz] if nz == 4 else list(range(nz))
        if CHAIN_FIRST[item]:
            for z in zs:
                for fa in (1, 0):
                    for fb in (1, 0):
                        out.append((z, fa, fb))
        else:
            for fb in (1, 0):
                for fa in (1, 0):
                    for z in zs:
                        out.append((z, fa, fb))
        return out

    def flip(d, f):
        return 1 - me[d] if f else me[d]

    order_items = (1, 2, 3, 4, 0)
    lists = {i: wanted(i) for i in range(k)}
    for n in range(4 * nz):
        for item in order_items:
            z, fa, fb = lists[item][n]
            la, lb = LINKS[item]
            p = piece(z, **{la: flip(la, fa), lb: flip(lb, fb)})
            start(copy(item, xs[item].at[p * 2 + 1 - me["c"]], rc[item].at[p], csend.at[item, p], crecv.at[item, p], sib))

    steps = []
    def tail(item):
        la, lb = LINKS[item]
        def own(p):
            arrived(item, rc[item].at[p], crecv.at[item, p])
            return [xs[item].at[p * 2 + me["c"]], rc[item].at[p]]
        zs = [nz - 1, 0, nz - 2, 1] if nz == 4 else list(reversed(range(nz)))
        if not CHAIN_FIRST[item]:
            def stage_b(z, fa):
                def run():
                    a = flip(la, fa)
                    p = piece(z, **{la: a, lb: 1 - me[lb]})
                    combine(acc[item].at[p], own(p))
                    s = z * 2 + a
                    start(copy(item, acc[item].at[p], rb[item].at[s], send_sem.at[item, s], recv_sem.at[item, s], dict(me, **{lb: 1 - me[lb]})))
                return run
            def stage_a(z):
                def run():
                    a = 1 - me[la]
                    p = piece(z, **{la: a, lb: me[lb]})
                    s = z * 2 + a
                    srcs = own(p)
                    arrived(item, rb[item].at[s], recv_sem.at[item, s])
                    combine(acc[item].at[p], srcs + [rb[item].at[s]])
                    s2 = 2 * nz + z
                    start(copy(item, acc[item].at[p], ra[item].at[z], send_sem.at[item, s2], recv_sem.at[item, s2], dict(me, **{la: 1 - me[la]})))
                return run
            def base(z):
                p = piece(z, **{la: me[la], lb: me[lb]})
                s = z * 2 + me[la]
                srcs = own(p)
                arrived(item, rb[item].at[s], recv_sem.at[item, s])
                arrived(item, ra[item].at[z], recv_sem.at[item, 2 * nz + z])
                return p, srcs + [rb[item].at[s], ra[item].at[z]]
            def chain(z):
                def run():
                    p, srcs = base(z)
                    sb, sa = 3 * nz + z, 4 * nz + z
                    @pl.when(jnp.logical_and(mz == 0, z > 0))
                    def _():
                        combine(acc[item].at[p], srcs)
                    @pl.when(jnp.logical_and(mz > 0, mz < z))
                    def _():
                        arrived(item, below[item].at[z], recv_sem.at[item, sb])
                        combine(acc[item].at[p], srcs + [below[item].at[z]])
                    if z > 0:
                        start(copy(item, acc[item].at[p], below[item].at[z], send_sem.at[item, sb], recv_sem.at[item, sb], up_to), mz < z)
                    @pl.when(jnp.logical_and(mz == nz - 1, z < nz - 1))
                    def _():
                        combine(acc[item].at[p], srcs)
                    @pl.when(jnp.logical_and(mz < nz - 1, mz > z))
                    def _():
                        arrived(item, above[item].at[z], recv_sem.at[item, sa])
                        combine(acc[item].at[p], srcs + [above[item].at[z]])
                    if z < nz - 1:
                        start(copy(item, acc[item].at[p], above[item].at[z], send_sem.at[item, sa], recv_sem.at[item, sa], dn_to), mz > z)
                return run
            def last():
                for z in range(nz):
                    @pl.when(mz == z)
                    def _():
                        p, srcs = piece(z, **{la: me[la], lb: me[lb]}), None
                        s = z * 2 + me[la]
                        srcs = [xs[item].at[p * 2 + me["c"]], rc[item].at[p], rb[item].at[s], ra[item].at[z]]
                        if z > 0:
                            arrived(item, below[item].at[z], recv_sem.at[item, 3 * nz + z])
                            srcs.append(below[item].at[z])
                        if z < nz - 1:
                            arrived(item, above[item].at[z], recv_sem.at[item, 4 * nz + z])
                            srcs.append(above[item].at[z])
                        combine(outs[item], srcs)
            out = []
            for n, z in enumerate(zs):
                out.append((1 + n, stage_b(z, 1)))
            for n, z in enumerate(zs):
                out.append((5 + n, stage_b(z, 0)))
                out.append((5.5 + n, stage_a(z)))
            for n, z in enumerate(zs):
                out.append((9.5 + n, chain(z)))
            out.append((20, last))
            return out
        def chain(z, fa, fb):
            def run():
                a, b = flip(la, fa), flip(lb, fb)
                p = piece(z, **{la: a, lb: b})
                q = a * 2 + b
                srcs = own(p)
                sb, sa = z * 4 + q, 4 * nz + z * 4 + q
                bref, aref = below[item].at[z * 4 + q], above[item].at[z * 4 + q]
                if z > 0:
                    @pl.when(mz == 0)
                    def _():
                        combine(acc[item].at[p], srcs)
                    @pl.when(jnp.logical_and(mz > 0, mz < z))
                    def _():
                        arrived(item, bref, recv_sem.at[item, sb])
                        combine(acc[item].at[p], srcs + [bref])
                    start(copy(item, acc[item].at[p], bref, send_sem.at[item, sb], recv_sem.at[item, sb], up_to), mz < z)
                if z < nz - 1:
                    @pl.when(mz == nz - 1)
                    def _():
                        combine(acc[item].at[p], srcs)
                    @pl.when(jnp.logical_and(mz < nz - 1, mz > z))
                    def _():
                        arrived(item, aref, recv_sem.at[item, sa])
                        combine(acc[item].at[p], srcs + [aref])
                    start(copy(item, acc[item].at[p], aref, send_sem.at[item, sa], recv_sem.at[item, sa], dn_to), mz > z)
            return run
        def settle(fa, fb):
            a, b = flip(la, fa), flip(lb, fb)
            q = a * 2 + b
            for z in range(nz):
                @pl.when(mz == z)
                def _():
                    p = piece(z, **{la: a, lb: b})
                    srcs = [xs[item].at[p * 2 + me["c"]], rc[item].at[p]]
                    if z > 0:
                        arrived(item, below[item].at[z * 4 + q], recv_sem.at[item, z * 4 + q])
                        srcs.append(below[item].at[z * 4 + q])
                    if z < nz - 1:
                        arrived(item, above[item].at[z * 4 + q], recv_sem.at[item, 4 * nz + z * 4 + q])
                        srcs.append(above[item].at[z * 4 + q])
                    combine(acc[item].at[p], srcs)
            return piece(mz, **{la: a, lb: b})
        s0 = 8 * nz
        def to_b(fa):
            def run():
                p = settle(fa, 1)
                start(copy(item, acc[item].at[p], rb[item].at[fa], send_sem.at[item, s0 + fa], recv_sem.at[item, s0 + fa], dict(me, **{lb: 1 - me[lb]})))
            return run
        def to_a():
            p = settle(1, 0)
            arrived(item, rb[item].at[1], recv_sem.at[item, s0 + 1])
            combine(ra[item].at[0], [acc[item].at[p], rb[item].at[1]])
            start(copy(item, ra[item].at[0], ra[item].at[1], send_sem.at[item, s0 + 2], recv_sem.at[item, s0 + 2], dict(me, **{la: 1 - me[la]})))
        def last():
            p = settle(0, 0)
            arrived(item, rb[item].at[0], recv_sem.at[item, s0])
            arrived(item, ra[item].at[1], recv_sem.at[item, s0 + 2])
            combine(outs[item], [acc[item].at[p], rb[item].at[0], ra[item].at[1]])
        out = []
        for n, z in enumerate(zs):
            for m, (fa, fb) in enumerate(((1, 1), (0, 1), (1, 0), (0, 0))):
                out.append((1 + n * 3 + m * 0.5, chain(z, fa, fb)))
        out.append((12.6, to_b(1)))
        out.append((12.7, to_b(0)))
        out.append((14, to_a))
        out.append((21, last))
        return out

    for n, item in enumerate(order_items):
        steps += [(w + 0.01 * n, f) for w, f in tail(item)]
    for _, f in sorted(steps, key=lambda s: s[0]):
        f()
    for cp, cond in pending:
        if cond is None:
            cp.wait_send()
        else:
            pl.when(cond)(cp.wait_send)

def scatter_all(xs, nz):
    k = len(xs)
    chips = 4 * nz
    slab = [x.shape[1:] for x in xs]
    dt = [x.dtype for x in xs]
    def buf(counts):
        return [pltpu.VMEM((n,) + s, d) for n, s, d in zip(counts, slab, dt)]
    scr = buf([chips] * k) + buf([chips] * k)
    scr += buf([2 if CHAIN_FIRST[i] else nz for i in range(k)])
    scr += buf([2 if CHAIN_FIRST[i] else 2 * nz for i in range(k)])
    scr += buf([4 * nz if CHAIN_FIRST[i] else nz for i in range(k)]) * 2
    sems = 8 * nz + 3
    scr += [pltpu.SemaphoreType.DMA((k, chips)), pltpu.SemaphoreType.DMA((k, chips)), pltpu.SemaphoreType.DMA((k, sems)), pltpu.SemaphoreType.DMA((k, sems))]
    return pl.pallas_call(
        functools.partial(scatter_kernel, nz, k),
        out_shape=[jax.ShapeDtypeStruct(s, jnp.float32) for s in slab],
        in_specs=[pl.BlockSpec(memory_space=pltpu.VMEM)] * k,
        out_specs=[pl.BlockSpec(memory_space=pltpu.VMEM)] * k,
        scratch_shapes=scr,
        compiler_params=pltpu.CompilerParams(collective_id=1, has_side_effects=True, vmem_limit_bytes=60 << 20),
        name="scatter_grads",
    )(*xs)


def kernel_planes(arrays):
    seq = lax.axis_size("seq")
    if lax.axis_size("dp") != 2 or seq % 4 or seq > 16:
        return 0
    rows = [a.size % c for a, c in zip(arrays, (D, D, FF, D))]
    return 0 if any(rows) else seq // 4


def gather_weights(
    qkv_weight, out_weight, expand_weight, contract_weight, bias_vectors, gain_vectors, ffn_bias
):
    vectors = jnp.concatenate([bias_vectors, gain_vectors, ffn_bias])
    planes = kernel_planes((qkv_weight, out_weight, expand_weight, contract_weight))
    if planes:
        shards = 8 * planes
        depth = expand_weight.size // FF
        tail = jnp.pad(vectors, (0, depth * 128 - vectors.size)).reshape(depth, 128)
        first = jnp.concatenate(
            [expand_weight.reshape(depth, FF), out_weight.reshape(depth, D), tail], axis=1
        )
        first, contract, qkv = gather_all(
            (first, contract_weight.reshape(-1, D), qkv_weight.reshape(-1, D)), planes
        )
        first = first.reshape(D, FF + D + 128)
        vectors = first[:, FF + D :].reshape(shards, depth * 128)
        contract = contract.reshape(FF, D)
        qkv = qkv.reshape(3, D, D)
    else:
        gather = functools.partial(lax.all_gather, axis_name=("dp", "seq"), axis=0, tiled=True)
        qkv = gather(qkv_weight).reshape(3, D, D)
        first = jnp.concatenate(
            [gather(expand_weight).reshape(D, FF), gather(out_weight).reshape(D, D)], axis=1
        )
        contract = gather(contract_weight).reshape(FF, D)
        vectors = gather(vectors[None])
    a, b, c = bias_vectors.size, gain_vectors.size, ffn_bias.size
    vectors = vectors.astype(jnp.float32)
    rows = [vectors[:, :a].reshape(6, D), vectors[:, a : a + b].reshape(2, D)]
    return (
        qkv,
        first,
        contract,
        jnp.concatenate(rows),
        vectors[:, a + b : a + b + c].reshape(1, FF),
    )


def scatter_grads(grads, planes):
    d_qkv, d_out, d_expand, d_contract, d_biases, d_gains, d_ffn_bias = grads
    shards = lax.axis_size("dp") * lax.axis_size("seq")
    vectors = jnp.concatenate(
        [v.reshape(shards, -1) for v in (d_biases, d_gains, d_ffn_bias)], axis=1
    )
    if planes:
        low = [g.astype(jnp.bfloat16) for g in (d_expand, d_contract, d_qkv, d_out)]
        width = vectors.shape[1]
        padded = jnp.pad(vectors, ((0, 0), (0, -width % 1024)))
        parts = [padded.reshape(shards, -1, 128)]
        parts += [g.reshape(shards, -1, g.shape[-1]) for g in low]
        vectors, d_expand, d_contract, d_qkv, d_out = scatter_all(parts, planes)
        vectors = vectors.reshape(-1)[:width]
    else:
        d_expand, d_contract, d_qkv, d_out = [
            lax.psum_scatter(g.reshape(-1).astype(jnp.float32), ("dp", "seq"), scatter_dimension=0, tiled=True)
            for g in (d_expand, d_contract, d_qkv, d_out)
        ]
        vectors = lax.psum_scatter(vectors, ("dp", "seq"), scatter_dimension=0, tiled=True)[0]
    a, b = d_biases.size // shards, d_gains.size // shards
    return (
        d_qkv.reshape(-1),
        d_out.reshape(-1),
        d_expand.reshape(-1),
        d_contract.reshape(-1),
        vectors[:a],
        vectors[a : a + b],
        vectors[a + b :],
    )


def owner(head, n):
    return head * n // H


def owned(place, n):
    head = (place * H + n - 1) // n
    return jnp.minimum(head, H - 1), jnp.logical_and(head < H, owner(head, n) == place)


def greet_senders(n, place, mine, to_owners):
    row = lax.axis_index("dp")
    bar = pltpu.get_barrier_semaphore()

    def signal(to):
        @pl.when(to != place)
        def _():
            pl.semaphore_signal(bar, inc=1, device_id=(row, to), device_id_type=MESH)

    if to_owners:

        @pl.when(mine)
        def _():
            lax.fori_loop(0, n, lambda s, _: (signal(s), 0)[1], 0)

        pl.semaphore_wait(bar, H - jnp.where(mine, 1, 0))
    else:
        lax.fori_loop(0, H, lambda h, _: (signal(owner(h, n)), 0)[1], 0)

        @pl.when(mine)
        def _():
            pl.semaphore_wait(bar, n - 1)


def send_to_owners(n, place, head, mine, pairs, sems, meanwhile=None):
    row = lax.axis_index("dp")
    send_sem, recv_sem, own_sem = sems
    first = head + 1

    def walk(act):
        def body(k, _):
            h = (first + k) % H
            to = owner(h, n)
            for i, (src, dst) in enumerate(pairs):

                @pl.when(to != place)
                def _():
                    act(
                        pltpu.make_async_remote_copy(
                            src_ref=src.at[h],
                            dst_ref=dst.at[place],
                            send_sem=send_sem.at[i, h],
                            recv_sem=recv_sem.at[i, place],
                            device_id=(row, to),
                            device_id_type=MESH,
                        )
                    )

            return 0

        lax.fori_loop(0, H, body, 0)

    walk(lambda cp: cp.start())
    if meanwhile is not None:
        meanwhile()

    @pl.when(mine)
    def _():
        for i, (src, dst) in enumerate(pairs):
            cp = pltpu.make_async_copy(src.at[head], dst.at[place], own_sem.at[i])
            cp.start()
            cp.wait()

        def body(k, _):
            s = (place + 1 + k) % n
            for i, (src, dst) in enumerate(pairs):
                pltpu.make_async_remote_copy(
                    src_ref=src.at[0],
                    dst_ref=dst.at[s],
                    send_sem=send_sem.at[i, 0],
                    recv_sem=recv_sem.at[i, s],
                    device_id=(row, place),
                    device_id_type=MESH,
                ).wait_recv()
            return 0

        lax.fori_loop(0, n - 1, body, 0)

    walk(lambda cp: cp.wait_send())


def send_from_owners(n, place, head, mine, src, dst, sems):
    row = lax.axis_index("dp")
    send_sem, recv_sem, own_sem = sems

    def walk(act):
        def body(k, _):
            to = (place + 1 + k) % n
            act(
                pltpu.make_async_remote_copy(
                    src_ref=src.at[to],
                    dst_ref=dst.at[head],
                    send_sem=send_sem.at[0, to],
                    recv_sem=recv_sem.at[0, head],
                    device_id=(row, to),
                    device_id_type=MESH,
                )
            )
            return 0

        lax.fori_loop(0, n - 1, body, 0)

    @pl.when(mine)
    def _():
        walk(lambda cp: cp.start())
        cp = pltpu.make_async_copy(src.at[place], dst.at[head], own_sem.at[0])
        cp.start()
        cp.wait()

    def body(k, _):
        h = (head + k) % H

        @pl.when(owner(h, n) != place)
        def _():
            pltpu.make_async_remote_copy(
                src_ref=src.at[0],
                dst_ref=dst.at[h],
                send_sem=send_sem.at[0, 0],
                recv_sem=recv_sem.at[0, h],
                device_id=(row, place),
                device_id_type=MESH,
            ).wait_recv()

        return 0

    lax.fori_loop(0, H, body, 0)

    @pl.when(mine)
    def _():
        walk(lambda cp: cp.wait_send())


def swap_halves(tile):
    return pltpu.roll(tile, HD, tile.ndim - 1)


def low_lanes(shape):
    return lax.broadcasted_iota(jnp.int32, shape, len(shape) - 1) < HD


def project_kernel(n, rows_ref, w_ref, bias_ref, picks_ref, out_ref, out_picks_ref, box, *sems):
    place = lax.axis_index("seq")
    head, mine = owned(place, n)
    greet_senders(n, place, mine, True)
    rows = rows_ref[...]
    left = low_lanes((TOK_SEQ, 128))
    left_q = low_lanes((BLOCK, 128))
    wide = 256
    for g in range(D // wide):
        cols = slice(g * wide, (g + 1) * wide)
        q = (matmul(rows, w_ref[0, :, cols]) + bias_ref[0:1, cols]) * HD ** (-0.5)
        k = matmul(rows, w_ref[1, :, cols])
        v = matmul(rows, w_ref[2, :, cols]) + bias_ref[1:2, cols]
        for p in range(wide // 128):
            h = (g * wide + p * 128) // HD
            lanes = slice(p * 128, (p + 1) * 128)
            kp, vp, qp = k[:, lanes], v[:, lanes], q[:, lanes]
            box[h, 0:TOK_SEQ, :] = jnp.where(left, kp, swap_halves(vp)).astype(jnp.bfloat16)
            box[h + 1, 0:TOK_SEQ, :] = jnp.where(left, swap_halves(kp), vp).astype(jnp.bfloat16)
            turned = swap_halves(qp)
            for t in range(BPD // 2):
                a = slice(2 * t * BLOCK, (2 * t + 1) * BLOCK)
                b = slice((2 * t + 1) * BLOCK, (2 * t + 2) * BLOCK)
                to = slice(TOK_SEQ + t * BLOCK, TOK_SEQ + (t + 1) * BLOCK)
                box[h, to, :] = jnp.where(left_q, qp[a], turned[b]).astype(jnp.bfloat16)
                box[h + 1, to, :] = jnp.where(left_q, turned[a], qp[b]).astype(jnp.bfloat16)
    send_to_owners(
        n, place, head, mine, ((box, out_ref), (picks_ref, out_picks_ref)), sems
    )


def exchange_sems(n, pairs=1):
    return [
        pltpu.SemaphoreType.DMA((pairs, max(n, H))),
        pltpu.SemaphoreType.DMA((pairs, max(n, H))),
        pltpu.SemaphoreType.DMA((pairs,)),
    ]


ANY = pl.BlockSpec(memory_space=pl.ANY)
VMEM = pl.BlockSpec(memory_space=pltpu.VMEM)
SMEM = pl.BlockSpec(memory_space=pltpu.SMEM)
MSG = TOK_SEQ + TOK_SEQ // 2


def project_and_send(rows, qkv, biases, picks):
    n = lax.axis_size("seq")
    picks = jnp.pad(picks.reshape(H, 1, BPD * 3), ((0, 0), (0, 7), (0, 128 - BPD * 3)))
    return pl.pallas_call(
        functools.partial(project_kernel, n),
        out_shape=(
            jax.ShapeDtypeStruct((n, MSG, 128), jnp.bfloat16),
            jax.ShapeDtypeStruct((n, 8, 128), jnp.int32),
        ),
        in_specs=[VMEM, VMEM, VMEM, ANY],
        out_specs=(ANY, ANY),
        scratch_shapes=[pltpu.VMEM((H, MSG, 128), jnp.bfloat16)] + exchange_sems(n, 2),
        compiler_params=pltpu.CompilerParams(
            collective_id=2, has_side_effects=True, vmem_limit_bytes=48 << 20
        ),
        name="project_and_send",
    )(rows, qkv, biases, picks)


def from_owners_kernel(n, src, dst, *sems):
    place = lax.axis_index("seq")
    head, mine = owned(place, n)
    greet_senders(n, place, mine, False)
    send_from_owners(n, place, head, mine, src, dst, sems)


def exchange(kernel, slots, messages, ident, name):
    n = lax.axis_size("seq")
    return pl.pallas_call(
        functools.partial(kernel, n),
        out_shape=jax.ShapeDtypeStruct((slots,) + messages.shape[1:], messages.dtype),
        in_specs=[ANY],
        out_specs=ANY,
        scratch_shapes=exchange_sems(n),
        compiler_params=pltpu.CompilerParams(collective_id=ident, has_side_effects=True),
        name=name,
    )(messages)


def key_list(i, n, picks_ref):
    last = n * BPD - 1

    def of(b):
        s, r = b // BPD, b % BPD
        picked = [picks_ref[s, 0, r * 3 + j] for j in range(3)]
        return [jnp.maximum(b - 1, 0), b, jnp.minimum(b + 1, last), 0, last] + picked

    return [
        [(b // BPD, pl.multiple_of(b % BPD * BLOCK, BLOCK)) for b in of(2 * i + t)]
        for t in range(2)
    ]


def fill_pair(lists, kv_ref, vk_ref, keys, values):
    for j in range(8):
        (sa, ra), (sb, rb) = lists[0][j], lists[1][j]
        to = slice(j * BLOCK, (j + 1) * BLOCK)
        keys[to, 0:HD] = kv_ref[sa, pl.ds(ra, BLOCK), 0:HD]
        keys[to, HD:128] = vk_ref[sb, pl.ds(rb, BLOCK), HD:128]
        values[to, 0:HD] = vk_ref[sa, pl.ds(ra, BLOCK), 0:HD]
        values[to, HD:128] = kv_ref[sb, pl.ds(rb, BLOCK), HD:128]


def two_blocks(tile):
    left = low_lanes(tile.shape)
    zero = jnp.zeros_like(tile)
    return jnp.concatenate([jnp.where(left, tile, zero), jnp.where(left, zero, tile)], axis=0)


def pair_scores(i, n, keys, query):
    scores = outer_cols(keys, query)
    left = low_lanes((BLOCK, 128))
    right = jnp.logical_not(left)
    end = n * BPD // 2 - 1
    hide_first = jnp.logical_and(left, i == 0)
    hide_last = jnp.logical_and(right, i == end)
    return jnp.concatenate(
        [
            jnp.where(hide_first, masked_score, scores[0:BLOCK]),
            scores[BLOCK : 2 * BLOCK],
            jnp.where(hide_last, masked_score, scores[2 * BLOCK : 3 * BLOCK]),
            scores[3 * BLOCK :],
        ],
        axis=0,
    )


def pair_place(i):
    return i // (BPD // 2), pl.multiple_of(i % (BPD // 2) * BLOCK, BLOCK)


def turn_pairs(n, kv_ref, vk_ref):
    def body(s, _):
        tile = kv_ref[s, 0:TOK_SEQ, :].astype(jnp.float32)
        vk_ref[s] = swap_halves(tile).astype(jnp.bfloat16)
        return 0

    lax.fori_loop(0, n, body, 0)


def attend_kernel(n, kvq_ref, picks_ref, out_ref, lse_ref, vk_ref, keys, values):
    place = lax.axis_index("seq")
    head, mine = owned(place, n)

    @pl.when(mine)
    def _():
        turn_pairs(n, kvq_ref, vk_ref)

        def body(i, _):
            fill_pair(key_list(i, n, picks_ref), kvq_ref, vk_ref, keys, values)
            s, r = pair_place(i)
            query = two_blocks(kvq_ref[s, pl.ds(TOK_SEQ + r, BLOCK), :])
            scores = pair_scores(i, n, keys[...], query)
            top = jnp.max(scores, axis=0, keepdims=True)
            weights = jnp.exp(scores - top)
            total = jnp.sum(weights, axis=0, keepdims=True)
            probs = (weights * (1.0 / total)).astype(jnp.bfloat16)
            full = inner_rows(probs, values[...])
            left = low_lanes((BLOCK, 128))
            out_ref[s, pl.ds(r, BLOCK), :] = jnp.where(left, full[:BLOCK], full[BLOCK:]).astype(
                jnp.bfloat16
            )
            lse_ref[i] = top + jnp.log(total)
            return 0

        lax.fori_loop(0, n * BPD // 2, body, 0)


def attend_heads(kvq, picks):
    n = lax.axis_size("seq")
    return pl.pallas_call(
        functools.partial(attend_kernel, n),
        out_shape=(
            jax.ShapeDtypeStruct((n, TOK_SEQ // 2, 128), jnp.bfloat16),
            jax.ShapeDtypeStruct((n * BPD // 2, 1, 128), jnp.float32),
        ),
        in_specs=[VMEM, SMEM],
        out_specs=(VMEM, VMEM),
        scratch_shapes=[
            pltpu.VMEM((n, TOK_SEQ, 128), jnp.bfloat16),
            pltpu.VMEM((8 * BLOCK, 128), jnp.bfloat16),
            pltpu.VMEM((8 * BLOCK, 128), jnp.bfloat16),
        ],
        compiler_params=pltpu.CompilerParams(vmem_limit_bytes=48 << 20),
        name="attend_heads",
    )(kvq, picks)


def attend_back_kernel(
    n, kvq_ref, picks_ref, lse_ref, grad_ref, out_ref, vk_ref, keys, values, sum_k, sum_v
):
    place = lax.axis_index("seq")
    head, mine = owned(place, n)

    @pl.when(mine)
    def _():
        turn_pairs(n, kvq_ref, vk_ref)

        def clear(s, _):
            sum_k[s] = jnp.zeros((TOK_SEQ, 128), jnp.float32)
            sum_v[s] = jnp.zeros((TOK_SEQ, 128), jnp.float32)
            return 0

        lax.fori_loop(0, n, clear, 0)

        def body(i, _):
            lists = key_list(i, n, picks_ref)
            fill_pair(lists, kvq_ref, vk_ref, keys, values)
            s, r = pair_place(i)
            query = two_blocks(kvq_ref[s, pl.ds(TOK_SEQ + r, BLOCK), :])
            grad = two_blocks(grad_ref[s, pl.ds(r, BLOCK), :])
            probs = jnp.exp(pair_scores(i, n, keys[...], query) - lse_ref[i])
            d_probs = outer_cols(values[...], grad)
            rows = jnp.sum(probs * d_probs, axis=0, keepdims=True)
            d_scores = (probs * (d_probs - rows)).astype(jnp.bfloat16)
            d_values = matmul(probs.astype(jnp.bfloat16), grad)
            d_keys = matmul(d_scores, query)
            full = inner_rows(d_scores, keys[...]) * HD ** (-0.5)
            left = low_lanes((BLOCK, 128))
            out_ref[s, pl.ds(TOK_SEQ + r, BLOCK), :] = jnp.where(
                left, full[:BLOCK], full[BLOCK:]
            ).astype(jnp.bfloat16)
            for j in range(8):
                part = slice(j * BLOCK, (j + 1) * BLOCK)
                for t in range(2):
                    sb, rb = lists[t][j]
                    lanes = slice(t * HD, (t + 1) * HD)
                    sum_k[sb, pl.ds(rb, BLOCK), lanes] += d_keys[part, lanes]
                    sum_v[sb, pl.ds(rb, BLOCK), lanes] += d_values[part, lanes]
            return 0

        lax.fori_loop(0, n * BPD // 2, body, 0)

        def close(s, _):
            left = low_lanes((TOK_SEQ, 128))
            k, v = sum_k[s], sum_v[s]
            both = jnp.where(left, k + swap_halves(k), v + swap_halves(v))
            out_ref[s, 0:TOK_SEQ, :] = both.astype(jnp.bfloat16)
            return 0

        lax.fori_loop(0, n, close, 0)


def attend_heads_back(kvq, picks, lse, grad):
    n = lax.axis_size("seq")
    return pl.pallas_call(
        functools.partial(attend_back_kernel, n),
        out_shape=jax.ShapeDtypeStruct((n, MSG, 128), jnp.bfloat16),
        in_specs=[VMEM, SMEM, VMEM, VMEM],
        out_specs=VMEM,
        scratch_shapes=[
            pltpu.VMEM((n, TOK_SEQ, 128), jnp.bfloat16),
            pltpu.VMEM((8 * BLOCK, 128), jnp.bfloat16),
            pltpu.VMEM((8 * BLOCK, 128), jnp.bfloat16),
            pltpu.VMEM((n, TOK_SEQ, 128), jnp.float32),
            pltpu.VMEM((n, TOK_SEQ, 128), jnp.float32),
        ],
        compiler_params=pltpu.CompilerParams(vmem_limit_bytes=56 << 20),
        name="attend_heads_back",
    )(kvq, picks, lse, grad)


UNITS = 32
WIDE = 768


def greet_row(n, place, mine):
    row = lax.axis_index("dp")
    bar = pltpu.get_barrier_semaphore()

    def body(s, _):
        there = owned(s, n)[1]

        @pl.when(jnp.logical_and(s != place, jnp.logical_or(mine, there)))
        def _():
            pl.semaphore_signal(bar, inc=1, device_id=(row, s), device_id_type=MESH)

        return 0

    lax.fori_loop(0, n, body, 0)
    pl.semaphore_wait(bar, jnp.where(mine, n - 1, H))


def unpack_pair(tiles, odd, shape):
    left = low_lanes(shape)
    a, b = tiles.astype(jnp.float32), odd.astype(jnp.float32)
    return (jnp.where(left, a, swap_halves(b)), jnp.where(left, swap_halves(a), b))


def mid_kernel(n, *refs):
    (
        attended,
        rows_ref,
        cot_ref,
        first_hbm,
        second_hbm,
        vec_ref,
        ffn_ref,
        result_ref,
        d_sum1_ref,
        d_heads,
        dw1_hbm,
        dw2_hbm,
        dwo_hbm,
        small_ref,
        d_ffn_ref,
        inbox,
        box,
        w1_ref,
        wo_ref,
        w2_ref,
        slope_ref,
        active_ref,
        dw1_ref,
        dw2_ref,
        dwo_ref,
        mixed_ref,
        load_sem,
        store_sem,
    ) = refs[:28]
    sems_in, sems_out = refs[28:31], refs[31:34]
    place = lax.axis_index("seq")
    head, mine = owned(place, n)
    loads = [
        pltpu.make_async_copy(first_hbm.at[:, FF : FF + D], wo_ref, load_sem.at[0]),
        pltpu.make_async_copy(first_hbm.at[:, 0:FF], w1_ref, load_sem.at[1]),
        pltpu.make_async_copy(second_hbm, w2_ref, load_sem.at[2]),
    ]
    for cp in loads:
        cp.start()
    greet_row(n, place, mine)
    send_from_owners(n, place, head, mine, attended, inbox, sems_in)

    for h in range(0, H, 2):
        for t in range(BPD // 2):
            part = slice(t * BLOCK, (t + 1) * BLOCK)
            a, b = unpack_pair(inbox[h, part, :], inbox[h + 1, part, :], (BLOCK, 128))
            lanes = slice(h * HD, (h + 2) * HD)
            mixed_ref[2 * t * BLOCK : (2 * t + 1) * BLOCK, lanes] = a.astype(jnp.bfloat16)
            mixed_ref[(2 * t + 1) * BLOCK : (2 * t + 2) * BLOCK, lanes] = b.astype(jnp.bfloat16)
    loads[0].wait()
    hidden1 = rows_ref[...].astype(jnp.float32) + matmul(mixed_ref[...], wo_ref[...]) + vec_ref[2:3]
    normed_out1, normed1, inverse1 = normalize(hidden1, vec_ref[6:7], vec_ref[3:4])
    lowered = normed_out1.astype(jnp.bfloat16)
    loads[1].wait()
    loads[2].wait()

    def up_step(c, hidden):
        cols = pl.ds(pl.multiple_of(c * WIDE, WIDE), WIDE)
        up = matmul(lowered, w1_ref[:, cols]) + ffn_ref[:, cols]
        square = up * up
        inner = (2 / jnp.pi) ** 0.5 * (up + 0.044715 * up * square)
        curve = jnp.tanh(inner)
        active = (0.5 * up * (1 + curve)).astype(jnp.bfloat16)
        slope_ref[:, cols] = 0.5 * (1 + curve) + 0.5 * up * (1 - curve * curve) * (
            (2 / jnp.pi) ** 0.5 * (1 + 3 * 0.044715 * square)
        )
        active_ref[:, cols] = active
        return hidden + matmul(active, w2_ref[cols, :])

    hidden2 = lax.fori_loop(0, FF // WIDE, up_step, normed_out1 + vec_ref[4:5])
    result, normed2, inverse2 = normalize(hidden2, vec_ref[7:8], vec_ref[5:6])
    result_ref[...] = result
    grad = cot_ref[...].astype(jnp.float32)
    d_sum2 = normalize_back(grad, normed2, inverse2, vec_ref[7:8])
    d_down = d_sum2.astype(jnp.bfloat16)

    def add_rows(value):
        return jnp.sum(value, axis=0, keepdims=True)

    small_ref[2:3] = add_rows(d_down.astype(jnp.float32))
    small_ref[3:4] = add_rows(grad)
    small_ref[5:6] = add_rows(grad * normed2)

    def stores(c):
        cols = pl.ds(pl.multiple_of(c * WIDE, WIDE), WIDE)
        slabs = pl.ds(c * (UNITS * WIDE // FF), UNITS * WIDE // FF)
        return (
            pltpu.make_async_copy(dw1_ref.at[:, :, cols], dw1_hbm.at[:, :, cols], store_sem.at[0, c]),
            pltpu.make_async_copy(dw2_ref.at[slabs], dw2_hbm.at[slabs], store_sem.at[1, c]),
        )

    def back_step(c, d_norm1):
        cols = pl.ds(pl.multiple_of(c * WIDE, WIDE), WIDE)
        slabs = pl.ds(c * (UNITS * WIDE // FF), UNITS * WIDE // FF)
        d_active = outer_cols(d_down, w2_ref[cols, :])
        d_up = (d_active * slope_ref[:, cols]).astype(jnp.bfloat16)
        d_ffn_ref[:, cols] = add_rows(d_up.astype(jnp.float32))
        dw2 = inner_rows(active_ref[:, cols], d_down)
        dw2_ref[slabs] = dw2.reshape(UNITS * WIDE // FF, FF // UNITS, D).astype(jnp.bfloat16)
        dw1 = inner_rows(lowered, d_up)
        dw1_ref[:, :, cols] = dw1.reshape(UNITS, D // UNITS, WIDE).astype(jnp.bfloat16)
        for cp in stores(c):
            cp.start()
        return d_norm1 + outer_cols(d_up, w1_ref[:, cols])

    d_norm1 = lax.fori_loop(0, FF // WIDE, back_step, d_sum2)
    small_ref[1:2] = add_rows(d_norm1)
    small_ref[4:5] = add_rows(d_norm1 * normed1)
    d_sum1 = normalize_back(d_norm1, normed1, inverse1, vec_ref[6:7])
    d_sum1_ref[...] = d_sum1
    d_attn = d_sum1.astype(jnp.bfloat16)
    small_ref[0:1] = add_rows(d_attn.astype(jnp.float32))
    d_mixed = outer_cols(d_attn, wo_ref[...])
    for h in range(0, H, 2):
        for t in range(BPD // 2):
            part = slice(t * BLOCK, (t + 1) * BLOCK)
            lanes = slice(h * HD, (h + 2) * HD)
            a, b = unpack_pair(
                d_mixed[2 * t * BLOCK : (2 * t + 1) * BLOCK, lanes],
                d_mixed[(2 * t + 1) * BLOCK : (2 * t + 2) * BLOCK, lanes],
                (BLOCK, 128),
            )
            box[h, part, :] = a.astype(jnp.bfloat16)
            box[h + 1, part, :] = b.astype(jnp.bfloat16)

    def late():
        dwo_ref[...] = (
            inner_rows(mixed_ref[...], d_attn)
            .reshape(UNITS, D // UNITS, D)
            .astype(jnp.bfloat16)
        )
        cp = pltpu.make_async_copy(dwo_ref, dwo_hbm, load_sem.at[0])
        cp.start()
        cp.wait()

    send_to_owners(n, place, head, mine, ((box, d_heads),), sems_out, late)

    def drain(c, _):
        for cp in stores(c):
            cp.wait()
        return 0

    lax.fori_loop(0, FF // WIDE, drain, 0)


def middle(attended, rows, cotangent, first, second, vectors, ffn_bias):
    n = lax.axis_size("seq")
    low, full = jnp.bfloat16, jnp.float32
    part = (TOK_SEQ // 2, 128)
    units = [(UNITS, D // UNITS, FF), (UNITS, FF // UNITS, D), (UNITS, D // UNITS, D)]
    shapes = [((TOK_SEQ, D), full), ((TOK_SEQ, D), full), ((n,) + part, low)]
    shapes += [(u, low) for u in units] + [((8, D), full), ((1, FF), full)]
    return pl.pallas_call(
        functools.partial(mid_kernel, n),
        out_shape=[jax.ShapeDtypeStruct(s, d) for s, d in shapes],
        in_specs=[ANY, VMEM, VMEM, ANY, ANY, VMEM, VMEM],
        out_specs=[VMEM, VMEM, ANY, ANY, ANY, ANY, VMEM, VMEM],
        scratch_shapes=[
            pltpu.VMEM((H,) + part, low),
            pltpu.VMEM((H,) + part, low),
            pltpu.VMEM((D, FF), low),
            pltpu.VMEM((D, D), low),
            pltpu.VMEM((FF, D), low),
            pltpu.VMEM((TOK_SEQ, FF), full),
            pltpu.VMEM((TOK_SEQ, FF), low),
            *[pltpu.VMEM(u, low) for u in units],
            pltpu.VMEM((TOK_SEQ, D), low),
            pltpu.SemaphoreType.DMA((3,)),
            pltpu.SemaphoreType.DMA((2, FF // WIDE)),
            *exchange_sems(n),
            *exchange_sems(n),
        ],
        compiler_params=pltpu.CompilerParams(
            collective_id=3, has_side_effects=True, vmem_limit_bytes=58 << 20
        ),
        name="middle",
    )(attended, rows, cotangent, first, second, vectors, ffn_bias)


def unpack_heads(parts):
    parts = parts.reshape(H, BPD // 2, BLOCK, 2, HD).transpose(1, 3, 2, 0, 4)
    return parts.reshape(TOK_SEQ, D)


def unpack_keys(parts):
    parts = parts.reshape(H, TOK_SEQ, 2, HD).transpose(2, 1, 0, 3)
    return parts.reshape(2, TOK_SEQ, D)


def on_device(
    tokens,
    qkv_weight,
    out_weight,
    expand_weight,
    contract_weight,
    bias_vectors,
    gain_vectors,
    ffn_bias,
    random_blocks,
    cotangent,
):
    qkv, first, second, vectors, ffn = gather_weights(
        qkv_weight, out_weight, expand_weight, contract_weight, bias_vectors, gain_vectors, ffn_bias
    )
    planes = kernel_planes((qkv_weight, out_weight, expand_weight, contract_weight))
    rows = tokens.reshape(TOK_SEQ, D)
    kvq, picks = project_and_send(rows, qkv, vectors, random_blocks)
    attended, lse = attend_heads(kvq, picks)
    result, d_sum1, d_heads, d_expand, d_contract, d_out, small, d_ffn = middle(
        attended, rows, cotangent.reshape(TOK_SEQ, D), first, second, vectors, ffn
    )
    d_heads = exchange(
        from_owners_kernel, H, attend_heads_back(kvq, picks, lse, d_heads), 5, "return_head_grads"
    )
    d_query = unpack_heads(d_heads[:, TOK_SEQ:])
    d_pair = unpack_keys(d_heads[:, :TOK_SEQ])
    d_proj = jnp.concatenate([d_query[None], d_pair], axis=0)
    d_qkv = jnp.einsum("rd,erf->edf", rows, d_proj, preferred_element_type=jnp.float32)
    d_tokens = d_sum1 + jnp.einsum("erf,edf->rd", d_proj, qkv, preferred_element_type=jnp.float32)
    d_bias_q = jnp.sum(d_query.astype(jnp.float32), axis=0)
    d_bias_v = jnp.sum(d_pair[1].astype(jnp.float32), axis=0)
    d_biases = jnp.concatenate([jnp.stack([d_bias_q, d_bias_v]), small[0:4]])
    shares = scatter_grads(
        (d_qkv.reshape(3 * D, D), d_out, d_expand, d_contract, d_biases, small[4:6], d_ffn),
        planes,
    )
    return (result[None], d_tokens[None]) + shares


def solution(mesh):
    return jax.shard_map(
        on_device,
        mesh=mesh,
        in_specs=(
            P("dp", "seq", None),
            P(("dp", "seq")),
            P(("dp", "seq")),
            P(("dp", "seq")),
            P(("dp", "seq")),
            P(("dp", "seq")),
            P(("dp", "seq")),
            P(("dp", "seq")),
            P("dp", None, "seq", None),
            P("dp", "seq", None),
        ),
        out_specs=(
            P("dp", "seq", None),
            P("dp", "seq", None),
            P(("dp", "seq")),
            P(("dp", "seq")),
            P(("dp", "seq")),
            P(("dp", "seq")),
            P(("dp", "seq")),
            P(("dp", "seq")),
            P(("dp", "seq")),
        ),
        check_vma=False,
    )
```

```python
import functools

import jax
import jax.numpy as jnp
from jax import lax
from jax.experimental import pallas as pl
from jax.experimental.pallas import tpu as pltpu
from jax.sharding import PartitionSpec as P

MESH = pl.DeviceIdType.MESH

D = 768
FF = 3072
H = 12
HD = 64
BLOCK = 64
TOK_SEQ = 256
SEQ_GRP = 1
BPD = 4


norm_eps = 1e-12
masked_score = -1e30


def matmul(left, right):
    return jnp.dot(left, right, preferred_element_type=jnp.float32)


def inner_rows(left, right):
    return lax.dot_general(
        left, right, (((0,), (0,)), ((), ())), preferred_element_type=jnp.float32
    )


def outer_cols(left, right):
    return lax.dot_general(
        left, right, (((1,), (1,)), ((), ())), preferred_element_type=jnp.float32
    )


def normalize(value, gain, shift):
    mean = jnp.mean(value, axis=-1, keepdims=True)
    centred = value - mean
    inverse = lax.rsqrt(jnp.mean(centred * centred, axis=-1, keepdims=True) + norm_eps)
    normed = centred * inverse
    return (normed * gain + shift, normed, inverse)


def normalize_back(grad, normed, inverse, gain):
    scaled = grad * gain
    centred = scaled - jnp.mean(scaled, axis=-1, keepdims=True)
    return inverse * (centred - normed * jnp.mean(scaled * normed, axis=-1, keepdims=True))


def place(nz):
    y = lax.axis_index("dp")
    s = lax.axis_index("seq")
    return {"y": y, "z": s // 4, "x": (s // 2) % 2, "c": s % 2}

def device(p):
    return (p["y"], p["z"] * 4 + p["x"] * 2 + p["c"])

def chip(p, nz):
    return (p["y"] * nz + p["z"]) * 2 + p["x"]

def index(p, nz):
    return chip(p, nz) * 2 + p["c"]

def nearest(m, n, j):
    if n == 2:
        return m if j == 0 else 1 - m
    out = 0
    for i in range(n):
        rank = sorted(range(n), key=lambda s: (abs(s - i), s))
        out = jnp.where(m == i, rank[j], out)
    return out

ORDERS = (("z", "x", "y"), ("z", "y", "x"), ("x", "y", "z"))

def gather_kernel(nz, *refs):
    k = len(ORDERS)
    xs, gs = refs[:k], refs[k:2 * k]
    own_sem, send_sem, recv_sem, csend, crecv = refs[2 * k:]
    me = place(nz)
    size = {"y": 2, "z": nz, "x": 2}
    sib = dict(me, c=1 - me["c"])
    bar = pltpu.get_barrier_semaphore()
    for d in ("x", "y", "c"):
        pl.semaphore_signal(bar, inc=1, device_id=device(dict(me, **{d: 1 - me[d]})), device_id_type=MESH)
    @pl.when(me["z"] > 0)
    def _():
        pl.semaphore_signal(bar, inc=1, device_id=device(dict(me, z=me["z"] - 1)), device_id_type=MESH)
    @pl.when(me["z"] < nz - 1)
    def _():
        pl.semaphore_signal(bar, inc=1, device_id=device(dict(me, z=me["z"] + 1)), device_id_type=MESH)
    inside = jnp.where(me["z"] > 0, 1, 0) + jnp.where(me["z"] < nz - 1, 1, 0)
    pl.semaphore_wait(bar, 3 + inside)

    pending = []
    def remote(item, src_ref, slot, sem_slot, way, to, cond=None):
        cp = pltpu.make_async_remote_copy(src_ref=src_ref, dst_ref=gs[item].at[slot], send_sem=send_sem.at[item, sem_slot, way],
            recv_sem=recv_sem.at[item, sem_slot], device_id=device(to), device_id_type=MESH)
        if cond is None:
            cp.start()
        else:
            pl.when(cond)(cp.start)
        pending.append((cp, cond))

    work = []
    for item in range(k):
        order = ORDERS[item]
        n0, n1, n2 = (size[d] for d in order)
        for i2 in range(n2):
            for i1 in range(n1):
                for i0 in range(n0):
                    work.append((i0 + i1 + i2, item, i0, i1, i2))
    work.sort(key=lambda w: w[0])
    local = []
    for depth, item, i0, i1, i2 in work:
        order = ORDERS[item]
        src = dict(me)
        for d, i in zip(order, (i0, i1, i2)):
            src[d] = nearest(me[d], size[d], i)
        c = chip(src, nz)
        slot = c * 2 + me["c"]
        own = depth == 0
        ref = xs[item] if own else gs[item].at[slot]
        if not own:
            pltpu.make_async_remote_copy(src_ref=ref, dst_ref=ref, send_sem=send_sem.at[item, c, 0], recv_sem=recv_sem.at[item, c],
                device_id=device(sib), device_id_type=MESH).wait_recv()
        stage = 2 if i2 else (1 if i1 else 0)
        for t in range(stage, 3):
            d = order[t]
            onward = t == stage and not own
            if d == "z":
                if nz > 1:
                    up = me["z"] < nz - 1
                    dn = me["z"] > 0
                    if onward:
                        up = jnp.logical_and(up, src["z"] <= me["z"])
                        dn = jnp.logical_and(dn, src["z"] >= me["z"])
                    remote(item, ref, slot, c, 0, dict(me, z=jnp.minimum(me["z"] + 1, nz - 1)), up)
                    remote(item, ref, slot, c, 1, dict(me, z=jnp.maximum(me["z"] - 1, 0)), dn)
            elif not (onward and (i0, i1, i2)[t]):
                remote(item, ref, slot, c, 2 if d == "x" else 3, dict(me, **{d: 1 - me[d]}))
        cp = pltpu.make_async_remote_copy(src_ref=ref, dst_ref=gs[item].at[slot], send_sem=csend.at[item, c],
            recv_sem=crecv.at[item, c], device_id=device(sib), device_id_type=MESH)
        cp.start()
        pending.append((cp, None))
        if own:
            lc = pltpu.make_async_copy(xs[item], gs[item].at[slot], own_sem.at[item])
            lc.start()
            local.append(lc)
    for lc in local:
        lc.wait()
    for item in range(k):
        def body(c, _):
            ref = gs[item].at[c * 2 + 1 - me["c"]]
            pltpu.make_async_remote_copy(src_ref=ref, dst_ref=ref, send_sem=csend.at[item, c], recv_sem=crecv.at[item, c],
                device_id=device(sib), device_id_type=MESH).wait_recv()
            return 0
        lax.fori_loop(0, 4 * nz, body, 0)
    for cp, cond in pending:
        if cond is None:
            cp.wait_send()
        else:
            pl.when(cond)(cp.wait_send)

def gather_all(xs, nz):
    n = 8 * nz
    k = len(xs)
    chips = 4 * nz
    return pl.pallas_call(
        functools.partial(gather_kernel, nz),
        out_shape=[jax.ShapeDtypeStruct((n,) + x.shape, x.dtype) for x in xs],
        in_specs=[pl.BlockSpec(memory_space=pl.ANY)] * k,
        out_specs=[pl.BlockSpec(memory_space=pl.ANY)] * k,
        scratch_shapes=[pltpu.SemaphoreType.DMA((k,)), pltpu.SemaphoreType.DMA((k, chips, 4)), pltpu.SemaphoreType.DMA((k, chips)),
            pltpu.SemaphoreType.DMA((k, chips)), pltpu.SemaphoreType.DMA((k, chips))],
        compiler_params=pltpu.CompilerParams(collective_id=0, has_side_effects=True),
        name="gather_weights",
    )(*xs)


def combine(dst, srcs):
    rows, cols = dst.shape
    step = min(cols, max(128, (24 * 1024 // rows) // 128 * 128))
    while cols % step:
        step -= 128
    def part(sl):
        total = srcs[0][:, sl].astype(jnp.float32)
        for s in srcs[1:]:
            total = total + s[:, sl].astype(jnp.float32)
        dst[:, sl] = total.astype(dst.dtype)
    if cols == step:
        part(slice(None))
    else:
        def body(i, _):
            part(pl.ds(pl.multiple_of(i * step, 128), step))
            return 0
        lax.fori_loop(0, cols // step, body, 0)

def kernel_planes(arrays):
    seq = lax.axis_size("seq")
    if lax.axis_size("dp") != 2 or seq % 4:
        return 0
    if seq // 4 not in (2, 4) or 2 * seq != UNITS:
        return 0
    return seq // 4


def gather_weights(
    qkv_weight, out_weight, expand_weight, contract_weight, bias_vectors, gain_vectors, ffn_bias
):
    vectors = jnp.concatenate([bias_vectors, gain_vectors, ffn_bias])
    planes = kernel_planes((qkv_weight, out_weight, expand_weight, contract_weight))
    if planes:
        shards = 8 * planes
        depth = expand_weight.size // FF
        tail = jnp.pad(vectors, (0, depth * 128 - vectors.size)).reshape(depth, 128)
        first = jnp.concatenate(
            [expand_weight.reshape(depth, FF), out_weight.reshape(depth, D), tail], axis=1
        )
        first, contract, qkv = gather_all(
            (first, contract_weight.reshape(-1, D), qkv_weight.reshape(-1, D)), planes
        )
        first = first.reshape(D, FF + D + 128)
        vectors = first[:, FF + D :].reshape(shards, depth * 128)
        contract = contract.reshape(FF, D)
        qkv = qkv.reshape(3, D, D)
    else:
        gather = functools.partial(lax.all_gather, axis_name=("dp", "seq"), axis=0, tiled=True)
        qkv = gather(qkv_weight).reshape(3, D, D)
        first = jnp.concatenate(
            [gather(expand_weight).reshape(D, FF), gather(out_weight).reshape(D, D)], axis=1
        )
        contract = gather(contract_weight).reshape(FF, D)
        vectors = gather(vectors[None])
    a, b, c = bias_vectors.size, gain_vectors.size, ffn_bias.size
    vectors = vectors.astype(jnp.float32)
    rows = [vectors[:, :a].reshape(6, D), vectors[:, a : a + b].reshape(2, D)]
    return (
        qkv,
        first,
        contract,
        jnp.concatenate(rows),
        vectors[:, a + b : a + b + c].reshape(1, FF),
    )


def owner(head, n):
    return head * n // H


def owned(place, n):
    head = (place * H + n - 1) // n
    return jnp.minimum(head, H - 1), jnp.logical_and(head < H, owner(head, n) == place)


def greet_senders(n, place, mine, to_owners):
    row = lax.axis_index("dp")
    bar = pltpu.get_barrier_semaphore()

    def signal(to):
        @pl.when(to != place)
        def _():
            pl.semaphore_signal(bar, inc=1, device_id=(row, to), device_id_type=MESH)

    if to_owners:

        @pl.when(mine)
        def _():
            lax.fori_loop(0, n, lambda s, _: (signal(s), 0)[1], 0)

        pl.semaphore_wait(bar, H - jnp.where(mine, 1, 0))
    else:
        lax.fori_loop(0, H, lambda h, _: (signal(owner(h, n)), 0)[1], 0)

        @pl.when(mine)
        def _():
            pl.semaphore_wait(bar, n - 1)


def send_to_owners(n, place, head, mine, pairs, sems, meanwhile=None):
    row = lax.axis_index("dp")
    send_sem, recv_sem, own_sem = sems
    first = head + 1

    def walk(act):
        def body(k, _):
            h = (first + k) % H
            to = owner(h, n)
            for i, (src, dst) in enumerate(pairs):

                @pl.when(to != place)
                def _():
                    act(
                        pltpu.make_async_remote_copy(
                            src_ref=src.at[h],
                            dst_ref=dst.at[place],
                            send_sem=send_sem.at[i, h],
                            recv_sem=recv_sem.at[i, place],
                            device_id=(row, to),
                            device_id_type=MESH,
                        )
                    )

            return 0

        lax.fori_loop(0, H, body, 0)

    walk(lambda cp: cp.start())
    if meanwhile is not None:
        meanwhile()

    @pl.when(mine)
    def _():
        for i, (src, dst) in enumerate(pairs):
            cp = pltpu.make_async_copy(src.at[head], dst.at[place], own_sem.at[i])
            cp.start()
            cp.wait()

        def body(k, _):
            s = (place + 1 + k) % n
            for i, (src, dst) in enumerate(pairs):
                pltpu.make_async_remote_copy(
                    src_ref=src.at[0],
                    dst_ref=dst.at[s],
                    send_sem=send_sem.at[i, 0],
                    recv_sem=recv_sem.at[i, s],
                    device_id=(row, place),
                    device_id_type=MESH,
                ).wait_recv()
            return 0

        lax.fori_loop(0, n - 1, body, 0)

    walk(lambda cp: cp.wait_send())


def walk_from_owners(n, place, head, src, dst, sems, act):
    row = lax.axis_index("dp")

    def body(k, _):
        to = (place + 1 + k) % n
        act(
            pltpu.make_async_remote_copy(
                src_ref=src.at[to],
                dst_ref=dst.at[head],
                send_sem=sems[0].at[0, to],
                recv_sem=sems[1].at[0, head],
                device_id=(row, to),
                device_id_type=MESH,
            )
        )
        return 0

    lax.fori_loop(0, n - 1, body, 0)


def start_from_owners(n, place, head, mine, src, dst, sems):
    @pl.when(mine)
    def _():
        walk_from_owners(n, place, head, src, dst, sems, lambda cp: cp.start())
        cp = pltpu.make_async_copy(src.at[place], dst.at[head], sems[2].at[0])
        cp.start()
        cp.wait()


def wait_from_owners(n, place, head, src, dst, sems):
    def body(k, _):
        h = (head + k) % H

        @pl.when(owner(h, n) != place)
        def _():
            pltpu.make_async_remote_copy(
                src_ref=src.at[0],
                dst_ref=dst.at[h],
                send_sem=sems[0].at[0, 0],
                recv_sem=sems[1].at[0, h],
                device_id=(lax.axis_index("dp"), place),
                device_id_type=MESH,
            ).wait_recv()

        return 0

    lax.fori_loop(0, H, body, 0)


def finish_from_owners(n, place, head, mine, src, dst, sems):
    @pl.when(mine)
    def _():
        walk_from_owners(n, place, head, src, dst, sems, lambda cp: cp.wait_send())


def send_from_owners(n, place, head, mine, src, dst, sems):
    start_from_owners(n, place, head, mine, src, dst, sems)
    wait_from_owners(n, place, head, src, dst, sems)
    finish_from_owners(n, place, head, mine, src, dst, sems)


def swap_halves(tile):
    return pltpu.roll(tile, HD, tile.ndim - 1)


def low_lanes(shape):
    return lax.broadcasted_iota(jnp.int32, shape, len(shape) - 1) < HD


def project_kernel(n, rows_ref, w_ref, bias_ref, picks_ref, out_ref, out_picks_ref, box, *sems):
    place = lax.axis_index("seq")
    head, mine = owned(place, n)
    greet_senders(n, place, mine, True)
    rows = rows_ref[...]
    left = low_lanes((TOK_SEQ, 128))
    left_q = low_lanes((BLOCK, 128))
    wide = 256
    for g in range(D // wide):
        cols = slice(g * wide, (g + 1) * wide)
        q = (matmul(rows, w_ref[0, :, cols]) + bias_ref[0:1, cols]) * HD ** (-0.5)
        k = matmul(rows, w_ref[1, :, cols])
        v = matmul(rows, w_ref[2, :, cols]) + bias_ref[1:2, cols]
        for p in range(wide // 128):
            h = (g * wide + p * 128) // HD
            lanes = slice(p * 128, (p + 1) * 128)
            kp, vp, qp = k[:, lanes], v[:, lanes], q[:, lanes]
            box[h, 0:TOK_SEQ, :] = jnp.where(left, kp, swap_halves(vp)).astype(jnp.bfloat16)
            box[h + 1, 0:TOK_SEQ, :] = jnp.where(left, swap_halves(kp), vp).astype(jnp.bfloat16)
            turned = swap_halves(qp)
            for t in range(BPD // 2):
                a = slice(2 * t * BLOCK, (2 * t + 1) * BLOCK)
                b = slice((2 * t + 1) * BLOCK, (2 * t + 2) * BLOCK)
                to = slice(TOK_SEQ + t * BLOCK, TOK_SEQ + (t + 1) * BLOCK)
                box[h, to, :] = jnp.where(left_q, qp[a], turned[b]).astype(jnp.bfloat16)
                box[h + 1, to, :] = jnp.where(left_q, turned[a], qp[b]).astype(jnp.bfloat16)
    send_to_owners(
        n, place, head, mine, ((box, out_ref), (picks_ref, out_picks_ref)), sems
    )


def exchange_sems(n, pairs=1):
    return [
        pltpu.SemaphoreType.DMA((pairs, max(n, H))),
        pltpu.SemaphoreType.DMA((pairs, max(n, H))),
        pltpu.SemaphoreType.DMA((pairs,)),
    ]


ANY = pl.BlockSpec(memory_space=pl.ANY)
VMEM = pl.BlockSpec(memory_space=pltpu.VMEM)
SMEM = pl.BlockSpec(memory_space=pltpu.SMEM)
MSG = TOK_SEQ + TOK_SEQ // 2


def project_and_send(rows, qkv, biases, picks):
    n = lax.axis_size("seq")
    picks = jnp.pad(picks.reshape(H, 1, BPD * 3), ((0, 0), (0, 7), (0, 128 - BPD * 3)))
    return pl.pallas_call(
        functools.partial(project_kernel, n),
        out_shape=(
            jax.ShapeDtypeStruct((n, MSG, 128), jnp.bfloat16),
            jax.ShapeDtypeStruct((n, 8, 128), jnp.int32),
        ),
        in_specs=[VMEM, VMEM, VMEM, ANY],
        out_specs=(ANY, ANY),
        scratch_shapes=[pltpu.VMEM((H, MSG, 128), jnp.bfloat16)] + exchange_sems(n, 2),
        compiler_params=pltpu.CompilerParams(
            collective_id=2, has_side_effects=True, vmem_limit_bytes=48 << 20
        ),
        name="project_and_send",
    )(rows, qkv, biases, picks)


def from_owners_kernel(n, src, dst, *sems):
    place = lax.axis_index("seq")
    head, mine = owned(place, n)
    greet_senders(n, place, mine, False)
    send_from_owners(n, place, head, mine, src, dst, sems)


def exchange(kernel, slots, messages, ident, name):
    n = lax.axis_size("seq")
    return pl.pallas_call(
        functools.partial(kernel, n),
        out_shape=jax.ShapeDtypeStruct((slots,) + messages.shape[1:], messages.dtype),
        in_specs=[ANY],
        out_specs=ANY,
        scratch_shapes=exchange_sems(n),
        compiler_params=pltpu.CompilerParams(collective_id=ident, has_side_effects=True),
        name=name,
    )(messages)


def key_list(i, n, picks_ref):
    last = n * BPD - 1

    def of(b):
        s, r = b // BPD, b % BPD
        picked = [picks_ref[s, 0, r * 3 + j] for j in range(3)]
        return [jnp.maximum(b - 1, 0), b, jnp.minimum(b + 1, last), 0, last] + picked

    return [
        [(b // BPD, pl.multiple_of(b % BPD * BLOCK, BLOCK)) for b in of(2 * i + t)]
        for t in range(2)
    ]


def fill_pair(lists, kv_ref, vk_ref, keys, values):
    for j in range(8):
        (sa, ra), (sb, rb) = lists[0][j], lists[1][j]
        to = slice(j * BLOCK, (j + 1) * BLOCK)
        keys[to, 0:HD] = kv_ref[sa, pl.ds(ra, BLOCK), 0:HD]
        keys[to, HD:128] = vk_ref[sb, pl.ds(rb, BLOCK), HD:128]
        values[to, 0:HD] = vk_ref[sa, pl.ds(ra, BLOCK), 0:HD]
        values[to, HD:128] = kv_ref[sb, pl.ds(rb, BLOCK), HD:128]


def two_blocks(tile):
    left = low_lanes(tile.shape)
    zero = jnp.zeros_like(tile)
    return jnp.concatenate([jnp.where(left, tile, zero), jnp.where(left, zero, tile)], axis=0)


def pair_scores(i, n, keys, query):
    scores = outer_cols(keys, query)
    left = low_lanes((BLOCK, 128))
    right = jnp.logical_not(left)
    end = n * BPD // 2 - 1
    hide_first = jnp.logical_and(left, i == 0)
    hide_last = jnp.logical_and(right, i == end)
    return jnp.concatenate(
        [
            jnp.where(hide_first, masked_score, scores[0:BLOCK]),
            scores[BLOCK : 2 * BLOCK],
            jnp.where(hide_last, masked_score, scores[2 * BLOCK : 3 * BLOCK]),
            scores[3 * BLOCK :],
        ],
        axis=0,
    )


def pair_place(i):
    return i // (BPD // 2), pl.multiple_of(i % (BPD // 2) * BLOCK, BLOCK)


def turn_pairs(n, kv_ref, vk_ref):
    def body(s, _):
        tile = kv_ref[s, 0:TOK_SEQ, :].astype(jnp.float32)
        vk_ref[s] = swap_halves(tile).astype(jnp.bfloat16)
        return 0

    lax.fori_loop(0, n, body, 0)


def attend_kernel(n, kvq_ref, picks_ref, out_ref, lse_ref, vk_ref, keys, values):
    place = lax.axis_index("seq")
    head, mine = owned(place, n)

    @pl.when(mine)
    def _():
        turn_pairs(n, kvq_ref, vk_ref)

        def body(i, _):
            fill_pair(key_list(i, n, picks_ref), kvq_ref, vk_ref, keys, values)
            s, r = pair_place(i)
            query = two_blocks(kvq_ref[s, pl.ds(TOK_SEQ + r, BLOCK), :])
            scores = pair_scores(i, n, keys[...], query)
            top = jnp.max(scores, axis=0, keepdims=True)
            weights = jnp.exp(scores - top)
            total = jnp.sum(weights, axis=0, keepdims=True)
            probs = (weights * (1.0 / total)).astype(jnp.bfloat16)
            full = inner_rows(probs, values[...])
            left = low_lanes((BLOCK, 128))
            out_ref[s, pl.ds(r, BLOCK), :] = jnp.where(left, full[:BLOCK], full[BLOCK:]).astype(
                jnp.bfloat16
            )
            lse_ref[i] = top + jnp.log(total)
            return 0

        lax.fori_loop(0, n * BPD // 2, body, 0)


def attend_heads(kvq, picks):
    n = lax.axis_size("seq")
    return pl.pallas_call(
        functools.partial(attend_kernel, n),
        out_shape=(
            jax.ShapeDtypeStruct((n, TOK_SEQ // 2, 128), jnp.bfloat16),
            jax.ShapeDtypeStruct((n * BPD // 2, 1, 128), jnp.float32),
        ),
        in_specs=[VMEM, SMEM],
        out_specs=(VMEM, VMEM),
        scratch_shapes=[
            pltpu.VMEM((n, TOK_SEQ, 128), jnp.bfloat16),
            pltpu.VMEM((8 * BLOCK, 128), jnp.bfloat16),
            pltpu.VMEM((8 * BLOCK, 128), jnp.bfloat16),
        ],
        compiler_params=pltpu.CompilerParams(vmem_limit_bytes=48 << 20),
        name="attend_heads",
    )(kvq, picks)


def attend_back_kernel(
    n, kvq_ref, picks_ref, lse_ref, grad_ref, out_ref, vk_ref, keys, values, sum_k, sum_v
):
    place = lax.axis_index("seq")
    head, mine = owned(place, n)

    @pl.when(mine)
    def _():
        turn_pairs(n, kvq_ref, vk_ref)

        def clear(s, _):
            sum_k[s] = jnp.zeros((TOK_SEQ, 128), jnp.float32)
            sum_v[s] = jnp.zeros((TOK_SEQ, 128), jnp.float32)
            return 0

        lax.fori_loop(0, n, clear, 0)

        def body(i, _):
            lists = key_list(i, n, picks_ref)
            fill_pair(lists, kvq_ref, vk_ref, keys, values)
            s, r = pair_place(i)
            query = two_blocks(kvq_ref[s, pl.ds(TOK_SEQ + r, BLOCK), :])
            grad = two_blocks(grad_ref[s, pl.ds(r, BLOCK), :])
            probs = jnp.exp(pair_scores(i, n, keys[...], query) - lse_ref[i])
            d_probs = outer_cols(values[...], grad)
            rows = jnp.sum(probs * d_probs, axis=0, keepdims=True)
            d_scores = (probs * (d_probs - rows)).astype(jnp.bfloat16)
            d_values = matmul(probs.astype(jnp.bfloat16), grad)
            d_keys = matmul(d_scores, query)
            full = inner_rows(d_scores, keys[...]) * HD ** (-0.5)
            left = low_lanes((BLOCK, 128))
            out_ref[s, pl.ds(TOK_SEQ + r, BLOCK), :] = jnp.where(
                left, full[:BLOCK], full[BLOCK:]
            ).astype(jnp.bfloat16)
            for j in range(8):
                part = slice(j * BLOCK, (j + 1) * BLOCK)
                for t in range(2):
                    sb, rb = lists[t][j]
                    lanes = slice(t * HD, (t + 1) * HD)
                    sum_k[sb, pl.ds(rb, BLOCK), lanes] += d_keys[part, lanes]
                    sum_v[sb, pl.ds(rb, BLOCK), lanes] += d_values[part, lanes]
            return 0

        lax.fori_loop(0, n * BPD // 2, body, 0)

        def close(s, _):
            left = low_lanes((TOK_SEQ, 128))
            k, v = sum_k[s], sum_v[s]
            both = jnp.where(left, k + swap_halves(k), v + swap_halves(v))
            out_ref[s, 0:TOK_SEQ, :] = both.astype(jnp.bfloat16)
            return 0

        lax.fori_loop(0, n, close, 0)


def attend_heads_back(kvq, picks, lse, grad):
    n = lax.axis_size("seq")
    return pl.pallas_call(
        functools.partial(attend_back_kernel, n),
        out_shape=jax.ShapeDtypeStruct((n, MSG, 128), jnp.bfloat16),
        in_specs=[VMEM, SMEM, VMEM, VMEM],
        out_specs=VMEM,
        scratch_shapes=[
            pltpu.VMEM((n, TOK_SEQ, 128), jnp.bfloat16),
            pltpu.VMEM((8 * BLOCK, 128), jnp.bfloat16),
            pltpu.VMEM((8 * BLOCK, 128), jnp.bfloat16),
            pltpu.VMEM((n, TOK_SEQ, 128), jnp.float32),
            pltpu.VMEM((n, TOK_SEQ, 128), jnp.float32),
        ],
        compiler_params=pltpu.CompilerParams(vmem_limit_bytes=56 << 20),
        name="attend_heads_back",
    )(kvq, picks, lse, grad)


UNITS = 32
WIDE = 768


def greet_row(n, place, mine):
    row = lax.axis_index("dp")
    bar = pltpu.get_barrier_semaphore()

    def body(s, _):
        there = owned(s, n)[1]

        @pl.when(jnp.logical_and(s != place, jnp.logical_or(mine, there)))
        def _():
            pl.semaphore_signal(bar, inc=1, device_id=(row, s), device_id_type=MESH)

        return 0

    lax.fori_loop(0, n, body, 0)
    pl.semaphore_wait(bar, jnp.where(mine, n - 1, H))


def unpack_pair(tiles, odd, shape):
    left = low_lanes(shape)
    a, b = tiles.astype(jnp.float32), odd.astype(jnp.float32)
    return (jnp.where(left, a, swap_halves(b)), jnp.where(left, swap_halves(a), b))


def mid_kernel(n, *refs):
    (
        attended,
        rows_ref,
        cot_ref,
        first_hbm,
        second_hbm,
        vec_ref,
        ffn_ref,
        result_ref,
        d_sum1_ref,
        d_heads,
        dw1_hbm,
        dw2_hbm,
        dwo_hbm,
        small_ref,
        d_ffn_ref,
        inbox,
        box,
        w1_ref,
        wo_ref,
        w2_ref,
        slope_ref,
        active_ref,
        dw1_ref,
        dw2_ref,
        dwo_ref,
        mixed_ref,
        load_sem,
        store_sem,
    ) = refs[:28]
    sems_in, sems_out = refs[28:31], refs[31:34]
    place = lax.axis_index("seq")
    head, mine = owned(place, n)
    loads = [
        pltpu.make_async_copy(first_hbm.at[:, FF : FF + D], wo_ref, load_sem.at[0]),
        pltpu.make_async_copy(first_hbm.at[:, 0:FF], w1_ref, load_sem.at[1]),
        pltpu.make_async_copy(second_hbm, w2_ref, load_sem.at[2]),
    ]
    for cp in loads:
        cp.start()
    greet_row(n, place, mine)
    send_from_owners(n, place, head, mine, attended, inbox, sems_in)

    for h in range(0, H, 2):
        for t in range(BPD // 2):
            part = slice(t * BLOCK, (t + 1) * BLOCK)
            a, b = unpack_pair(inbox[h, part, :], inbox[h + 1, part, :], (BLOCK, 128))
            lanes = slice(h * HD, (h + 2) * HD)
            mixed_ref[2 * t * BLOCK : (2 * t + 1) * BLOCK, lanes] = a.astype(jnp.bfloat16)
            mixed_ref[(2 * t + 1) * BLOCK : (2 * t + 2) * BLOCK, lanes] = b.astype(jnp.bfloat16)
    loads[0].wait()
    hidden1 = rows_ref[...].astype(jnp.float32) + matmul(mixed_ref[...], wo_ref[...]) + vec_ref[2:3]
    normed_out1, normed1, inverse1 = normalize(hidden1, vec_ref[6:7], vec_ref[3:4])
    lowered = normed_out1.astype(jnp.bfloat16)
    loads[1].wait()
    loads[2].wait()

    def up_step(c, hidden):
        cols = pl.ds(pl.multiple_of(c * WIDE, WIDE), WIDE)
        up = matmul(lowered, w1_ref[:, cols]) + ffn_ref[:, cols]
        square = up * up
        inner = (2 / jnp.pi) ** 0.5 * (up + 0.044715 * up * square)
        curve = jnp.tanh(inner)
        active = (0.5 * up * (1 + curve)).astype(jnp.bfloat16)
        slope_ref[:, cols] = 0.5 * (1 + curve) + 0.5 * up * (1 - curve * curve) * (
            (2 / jnp.pi) ** 0.5 * (1 + 3 * 0.044715 * square)
        )
        active_ref[:, cols] = active
        return hidden + matmul(active, w2_ref[cols, :])

    hidden2 = lax.fori_loop(0, FF // WIDE, up_step, normed_out1 + vec_ref[4:5])
    result, normed2, inverse2 = normalize(hidden2, vec_ref[7:8], vec_ref[5:6])
    result_ref[...] = result
    grad = cot_ref[...].astype(jnp.float32)
    d_sum2 = normalize_back(grad, normed2, inverse2, vec_ref[7:8])
    d_down = d_sum2.astype(jnp.bfloat16)

    def add_rows(value):
        return jnp.sum(value, axis=0, keepdims=True)

    small_ref[2:3] = add_rows(d_down.astype(jnp.float32))
    small_ref[3:4] = add_rows(grad)
    small_ref[5:6] = add_rows(grad * normed2)

    def stores(c):
        cols = pl.ds(pl.multiple_of(c * WIDE, WIDE), WIDE)
        slabs = pl.ds(c * (UNITS * WIDE // FF), UNITS * WIDE // FF)
        return (
            pltpu.make_async_copy(dw1_ref.at[:, :, cols], dw1_hbm.at[:, :, cols], store_sem.at[0, c]),
            pltpu.make_async_copy(dw2_ref.at[slabs], dw2_hbm.at[slabs], store_sem.at[1, c]),
        )

    def back_step(c, d_norm1):
        cols = pl.ds(pl.multiple_of(c * WIDE, WIDE), WIDE)
        slabs = pl.ds(c * (UNITS * WIDE // FF), UNITS * WIDE // FF)
        d_active = outer_cols(d_down, w2_ref[cols, :])
        d_up = (d_active * slope_ref[:, cols]).astype(jnp.bfloat16)
        d_ffn_ref[:, cols] = add_rows(d_up.astype(jnp.float32))
        dw2 = inner_rows(active_ref[:, cols], d_down)
        dw2_ref[slabs] = dw2.reshape(UNITS * WIDE // FF, FF // UNITS, D).astype(jnp.bfloat16)
        dw1 = inner_rows(lowered, d_up)
        dw1_ref[:, :, cols] = dw1.reshape(UNITS, D // UNITS, WIDE).astype(jnp.bfloat16)
        for cp in stores(c):
            cp.start()
        return d_norm1 + outer_cols(d_up, w1_ref[:, cols])

    d_norm1 = lax.fori_loop(0, FF // WIDE, back_step, d_sum2)
    small_ref[1:2] = add_rows(d_norm1)
    small_ref[4:5] = add_rows(d_norm1 * normed1)
    d_sum1 = normalize_back(d_norm1, normed1, inverse1, vec_ref[6:7])
    d_sum1_ref[...] = d_sum1
    d_attn = d_sum1.astype(jnp.bfloat16)
    small_ref[0:1] = add_rows(d_attn.astype(jnp.float32))
    d_mixed = outer_cols(d_attn, wo_ref[...])
    for h in range(0, H, 2):
        for t in range(BPD // 2):
            part = slice(t * BLOCK, (t + 1) * BLOCK)
            lanes = slice(h * HD, (h + 2) * HD)
            a, b = unpack_pair(
                d_mixed[2 * t * BLOCK : (2 * t + 1) * BLOCK, lanes],
                d_mixed[(2 * t + 1) * BLOCK : (2 * t + 2) * BLOCK, lanes],
                (BLOCK, 128),
            )
            box[h, part, :] = a.astype(jnp.bfloat16)
            box[h + 1, part, :] = b.astype(jnp.bfloat16)

    def late():
        dwo_ref[...] = (
            inner_rows(mixed_ref[...], d_attn)
            .reshape(UNITS, D // UNITS, D)
            .astype(jnp.bfloat16)
        )
        cp = pltpu.make_async_copy(dwo_ref, dwo_hbm, load_sem.at[0])
        cp.start()
        cp.wait()

    send_to_owners(n, place, head, mine, ((box, d_heads),), sems_out, late)

    def drain(c, _):
        for cp in stores(c):
            cp.wait()
        return 0

    lax.fori_loop(0, FF // WIDE, drain, 0)


def middle(attended, rows, cotangent, first, second, vectors, ffn_bias):
    n = lax.axis_size("seq")
    low, full = jnp.bfloat16, jnp.float32
    part = (TOK_SEQ // 2, 128)
    units = [(UNITS, D // UNITS, FF), (UNITS, FF // UNITS, D), (UNITS, D // UNITS, D)]
    shapes = [((TOK_SEQ, D), full), ((TOK_SEQ, D), full), ((n,) + part, low)]
    shapes += [(u, low) for u in units] + [((8, D), full), ((1, FF), full)]
    return pl.pallas_call(
        functools.partial(mid_kernel, n),
        out_shape=[jax.ShapeDtypeStruct(s, d) for s, d in shapes],
        in_specs=[ANY, VMEM, VMEM, ANY, ANY, VMEM, VMEM],
        out_specs=[VMEM, VMEM, ANY, ANY, ANY, ANY, VMEM, VMEM],
        scratch_shapes=[
            pltpu.VMEM((H,) + part, low),
            pltpu.VMEM((H,) + part, low),
            pltpu.VMEM((D, FF), low),
            pltpu.VMEM((D, D), low),
            pltpu.VMEM((FF, D), low),
            pltpu.VMEM((TOK_SEQ, FF), full),
            pltpu.VMEM((TOK_SEQ, FF), low),
            *[pltpu.VMEM(u, low) for u in units],
            pltpu.VMEM((TOK_SEQ, D), low),
            pltpu.SemaphoreType.DMA((3,)),
            pltpu.SemaphoreType.DMA((2, FF // WIDE)),
            *exchange_sems(n),
            *exchange_sems(n),
        ],
        compiler_params=pltpu.CompilerParams(
            collective_id=3, has_side_effects=True, vmem_limit_bytes=58 << 20
        ),
        name="middle",
    )(attended, rows, cotangent, first, second, vectors, ffn_bias)


def add_flat(out_ref, base, srcs):
    rows, cols = srcs[0].shape
    for k in range(cols // 128):
        lanes = slice(k * 128, (k + 1) * 128)
        total = srcs[0][:, lanes].astype(jnp.float32)
        for s in srcs[1:]:
            total = total + s[:, lanes].astype(jnp.float32)
        out_ref[pl.ds(base + k, rows, stride=cols // 128), :] = total


class Reduction:
    def __init__(self, nz, me, links, z_first, own, give, emit, bufs, sems, pending):
        self.nz, self.me, self.links, self.z_first = nz, me, links, z_first
        self.own, self.give, self.emit = own, give, emit
        self.rc, self.ra, self.rb, self.below, self.above = bufs
        self.csend, self.crecv, self.send, self.recv = sems
        self.pending = pending

    @staticmethod
    def buffers(nz, slab, z_first):
        chips = 4 * nz
        counts = (chips, 2, 2, chips, chips) if z_first else (chips, nz, 2 * nz, nz, nz)
        return [pltpu.VMEM((c,) + slab, jnp.bfloat16) for c in counts]

    @staticmethod
    def semaphores(nz, z_first):
        count = 8 * nz + 3 if z_first else 5 * nz
        return [pltpu.SemaphoreType.DMA((c,)) for c in (4 * nz, 4 * nz, count, count)]

    def start(self, src, dst, slot, to, cond=None):
        cp = pltpu.make_async_remote_copy(
            src_ref=src,
            dst_ref=dst,
            send_sem=self.send.at[slot],
            recv_sem=self.recv.at[slot],
            device_id=device(to),
            device_id_type=MESH,
        )
        if cond is None:
            cp.start()
        else:
            pl.when(cond)(cp.start)
        self.pending.append((cp, cond))

    def arrived(self, ref, sem):
        pltpu.make_async_remote_copy(
            src_ref=ref,
            dst_ref=ref,
            send_sem=self.send.at[0],
            recv_sem=sem,
            device_id=device(dict(self.me, c=1 - self.me["c"])),
            device_id_type=MESH,
        ).wait_recv()

    def flip(self, which, f):
        d = self.links[which]
        return 1 - self.me[d] if f else self.me[d]

    def piece(self, z, a, b):
        c = {self.links[0]: a, self.links[1]: b}
        return (c["y"] * self.nz + z) * 2 + c["x"]

    def across(self, which):
        d = self.links[which]
        return dict(self.me, **{d: 1 - self.me[d]})

    def hand_over(self):
        nz = self.nz
        zs = sorted(range(nz), key=lambda z: -abs(2 * z - nz + 1))
        if self.z_first:
            order = [(z, fa, fb) for z in zs for fa, fb in ((1, 1), (0, 1), (1, 0), (0, 0))]
        else:
            order = [(z, fa, fb) for fb in (1, 0) for fa in (1, 0) for z in zs]

        def one(z, fa, fb):
            def run():
                p = self.piece(z, self.flip(0, fa), self.flip(1, fb))
                cp = pltpu.make_async_remote_copy(
                    src_ref=self.give(p),
                    dst_ref=self.rc.at[p],
                    send_sem=self.csend.at[p],
                    recv_sem=self.crecv.at[p],
                    device_id=device(dict(self.me, c=1 - self.me["c"])),
                    device_id_type=MESH,
                )
                cp.start()
                self.pending.append((cp, None))

            return run

        return [one(*o) for o in order]

    def mine(self, p):
        self.arrived(self.rc.at[p], self.crecv.at[p])
        return [self.own(p), self.rc.at[p]]

    def relay(self, z, p, srcs, bref, aref, sb, sa):
        nz, mz, acc = self.nz, self.me["z"], self.rc.at[p]
        if z > 0:

            @pl.when(mz == 0)
            def _():
                combine(acc, srcs)

            @pl.when(jnp.logical_and(mz > 0, mz < z))
            def _():
                self.arrived(bref, self.recv.at[sb])
                combine(acc, srcs + [bref])

            self.start(acc, bref, sb, dict(self.me, z=jnp.minimum(mz + 1, nz - 1)), mz < z)
        if z < nz - 1:

            @pl.when(mz == nz - 1)
            def _():
                combine(acc, srcs)

            @pl.when(jnp.logical_and(mz < nz - 1, mz > z))
            def _():
                self.arrived(aref, self.recv.at[sa])
                combine(acc, srcs + [aref])

            self.start(acc, aref, sa, dict(self.me, z=jnp.maximum(mz - 1, 0)), mz > z)

    def ends(self, z, bref, aref, sb, sa):
        out = []
        if z > 0:
            self.arrived(bref, self.recv.at[sb])
            out.append(bref)
        if z < self.nz - 1:
            self.arrived(aref, self.recv.at[sa])
            out.append(aref)
        return out

    def steps(self):
        return self.steps_z_first() if self.z_first else self.steps_z_last()

    def steps_z_last(self):
        nz, me = self.nz, self.me
        zs = sorted(range(nz), key=lambda z: -abs(2 * z - nz + 1))

        def along_b(z, fa):
            def run():
                a = self.flip(0, fa)
                p = self.piece(z, a, self.flip(1, 1))
                combine(self.rc.at[p], self.mine(p))
                s = z * 2 + a
                self.start(self.rc.at[p], self.rb.at[s], s, self.across(1))

            return run

        def along_a(z):
            def run():
                a = self.flip(0, 1)
                p = self.piece(z, a, self.flip(1, 0))
                s = z * 2 + a
                srcs = self.mine(p)
                self.arrived(self.rb.at[s], self.recv.at[s])
                combine(self.rc.at[p], srcs + [self.rb.at[s]])
                self.start(self.rc.at[p], self.ra.at[z], 2 * nz + z, self.across(0))

            return run

        def chain(z):
            def run():
                p = self.piece(z, self.flip(0, 0), self.flip(1, 0))
                s = z * 2 + self.flip(0, 0)
                srcs = self.mine(p)
                self.arrived(self.rb.at[s], self.recv.at[s])
                self.arrived(self.ra.at[z], self.recv.at[2 * nz + z])
                srcs += [self.rb.at[s], self.ra.at[z]]
                bref, aref = self.below.at[z], self.above.at[z]
                self.relay(z, p, srcs, bref, aref, 3 * nz + z, 4 * nz + z)

            return run

        def last():
            for z in range(nz):

                @pl.when(me["z"] == z)
                def _():
                    p = self.piece(z, self.flip(0, 0), self.flip(1, 0))
                    s = z * 2 + self.flip(0, 0)
                    srcs = [self.own(p), self.rc.at[p], self.rb.at[s], self.ra.at[z]]
                    bref, aref = self.below.at[z], self.above.at[z]
                    self.emit(srcs + self.ends(z, bref, aref, 3 * nz + z, 4 * nz + z))

        out = [(1 + i, along_b(z, 1)) for i, z in enumerate(zs)]
        out += [(5 + i, along_b(z, 0)) for i, z in enumerate(zs)]
        out += [(5.5 + i, along_a(z)) for i, z in enumerate(zs)]
        out += [(9.5 + i, chain(z)) for i, z in enumerate(zs)]
        return out + [(20, last)]

    def steps_z_first(self):
        nz, me = self.nz, self.me
        zs = sorted(range(nz), key=lambda z: -abs(2 * z - nz + 1))
        s0 = 8 * nz

        def slots(z, fa, fb):
            q = self.flip(0, fa) * 2 + self.flip(1, fb)
            return self.below.at[z * 4 + q], self.above.at[z * 4 + q], z * 4 + q, 4 * nz + z * 4 + q

        def chain(z, fa, fb):
            def run():
                p = self.piece(z, self.flip(0, fa), self.flip(1, fb))
                self.relay(z, p, self.mine(p), *slots(z, fa, fb))

            return run

        def settle(fa, fb):
            for z in range(nz):

                @pl.when(me["z"] == z)
                def _():
                    p = self.piece(z, self.flip(0, fa), self.flip(1, fb))
                    srcs = [self.own(p), self.rc.at[p]] + self.ends(z, *slots(z, fa, fb))
                    combine(self.rc.at[p], srcs)

            return self.rc.at[self.piece(me["z"], self.flip(0, fa), self.flip(1, fb))]

        def along_b(fa):
            def run():
                self.start(settle(fa, 1), self.rb.at[fa], s0 + fa, self.across(1))

            return run

        def along_a():
            ref = settle(1, 0)
            self.arrived(self.rb.at[1], self.recv.at[s0 + 1])
            combine(self.ra.at[0], [ref, self.rb.at[1]])
            self.start(self.ra.at[0], self.ra.at[1], s0 + 2, self.across(0))

        def last():
            ref = settle(0, 0)
            self.arrived(self.rb.at[0], self.recv.at[s0])
            self.arrived(self.ra.at[1], self.recv.at[s0 + 2])
            self.emit([ref, self.rb.at[0], self.ra.at[1]])

        out = []
        for i, z in enumerate(zs):
            for m, (fa, fb) in enumerate(((1, 1), (0, 1), (1, 0), (0, 0))):
                out.append((1 + i * 2.5 + m * 0.5, chain(z, fa, fb)))
        return out + [(11.1, along_b(1)), (11.2, along_b(0)), (12.5, along_a), (21, last)]


FFN_KINDS = (
    ("expand", 0, D // UNITS, ("x", "y"), False),
    ("contract", FF // UNITS // 3, FF // UNITS, ("y", "x"), False),
    ("contract", 0, FF // UNITS // 3, ("x", "y"), False),
    ("out", 0, D // UNITS, ("x", "y"), False),
)
QKV_KINDS = (
    (0, ("x", "y"), False),
    (1, ("y", "x"), False),
    (2, ("x", "y"), True),
)
QKV_UNITS = 3 * UNITS
UNIT = D // UNITS


def finish_kernel(n, nz, *refs):
    heads, rows_ref, w_hbm, d_sum1_ref, dw1, dw2, dwo, small_ref, ffn_ref = refs[:9]
    d_tokens_ref, qkv_out, out_out, expand_out, contract_out, vec_out = refs[9:15]
    inbox, proj, w_ref, own1, own2, owno, ownq, value, land = refs[15:24]
    load_sem, vsend, vrecv = refs[24:27]
    sems_in = refs[27:30]
    rest = list(refs[30:])
    place_row = lax.axis_index("seq")
    head, mine = owned(place_row, n)
    me = place(nz)

    loads = [
        pltpu.make_async_copy(src, dst, load_sem.at[i])
        for i, (src, dst) in enumerate(((dw1, own1), (dw2, own2), (dwo, owno), (w_hbm, w_ref)))
    ]
    for cp in loads:
        cp.start()
    bar = pltpu.get_barrier_semaphore()

    def greet(k, _):
        to = (place_row + 1 + k) % n
        pl.semaphore_signal(bar, inc=1, device_id=(me["y"], to), device_id_type=MESH)
        return 0

    lax.fori_loop(0, n - 1, greet, 0)
    pl.semaphore_signal(bar, inc=1, device_id=(1 - me["y"], place_row), device_id_type=MESH)
    pl.semaphore_wait(bar, n)

    start_from_owners(n, place_row, head, mine, heads, inbox, sems_in)
    pending = []
    core = me["c"]

    def take(count):
        out = rest[:count]
        del rest[:count]
        return out

    sources = {"expand": (dw1, own1), "contract": (dw2, own2), "out": (dwo, owno)}
    targets = {"expand": expand_out, "contract": contract_out, "out": out_out}

    def ffn_item(kind, lo, hi, links, z_first):
        far, near = sources[kind]
        whole = lo == 0 and hi == far.shape[1]

        def at(ref, t):
            return ref.at[t] if whole else ref.at[t, lo:hi]

        cols = far.shape[2] // 128
        return Reduction(
            nz,
            me,
            links,
            z_first,
            lambda p: at(near, p * 2 + core),
            lambda p: at(far, p * 2 + 1 - core),
            lambda srcs: add_flat(targets[kind], lo * cols, srcs),
            take(5),
            take(4),
            pending,
        )

    def qkv_item(j, links, z_first):
        return Reduction(
            nz,
            me,
            links,
            z_first,
            lambda p: ownq.at[(p * 2 + core) * 3 + j],
            lambda p: ownq.at[(p * 2 + 1 - core) * 3 + j],
            lambda srcs: add_flat(qkv_out, j * UNIT * (D // 128), srcs),
            take(5),
            take(4),
            pending,
        )

    ffn = [ffn_item(*k) for k in FFN_KINDS]
    qkv = [qkv_item(*k) for k in QKV_KINDS]

    def hand_all(items):
        for group in zip(*[i.hand_over() for i in items]):
            for f in group:
                f()

    def ordered(items):
        steps = [(w + 0.01 * i, f) for i, item in enumerate(items) for w, f in item.steps()]
        return sorted(steps, key=lambda s: s[0])

    hand_all(ffn)
    for cp in loads[:3]:
        cp.wait()
    ffn_steps = ordered(ffn)
    for w, f in ffn_steps:
        if w < 20:
            f()

    wait_from_owners(n, place_row, head, heads, inbox, sems_in)
    loads[3].wait()
    half = TOK_SEQ // 2
    for h in range(0, H, 2):
        lanes = slice(h * HD, (h + 2) * HD)
        k, v = unpack_pair(inbox[h, 0:TOK_SEQ, :], inbox[h + 1, 0:TOK_SEQ, :], (TOK_SEQ, 128))
        proj[1, :, lanes] = k.astype(jnp.bfloat16)
        proj[2, :, lanes] = v.astype(jnp.bfloat16)
        for t in range(BPD // 2):
            part = slice(TOK_SEQ + t * BLOCK, TOK_SEQ + (t + 1) * BLOCK)
            a, b = unpack_pair(inbox[h, part, :], inbox[h + 1, part, :], (BLOCK, 128))
            proj[0, 2 * t * BLOCK : (2 * t + 1) * BLOCK, lanes] = a.astype(jnp.bfloat16)
            proj[0, (2 * t + 1) * BLOCK : (2 * t + 2) * BLOCK, lanes] = b.astype(jnp.bfloat16)

    def weight_grad(e, _):
        grad = inner_rows(rows_ref[...], proj[e])
        ownq[pl.ds(e * UNITS, UNITS)] = grad.reshape(UNITS, UNIT, D).astype(jnp.bfloat16)
        return 0

    lax.fori_loop(0, 3, weight_grad, 0)
    hand_all(qkv)

    def add_rows(x):
        return jnp.sum(x.astype(jnp.float32), axis=0, keepdims=True)

    value[0, 0:1] = add_rows(proj[0])
    value[0, 1:2] = add_rows(proj[2])
    value[0, 2:8] = small_ref[0:6]
    for c in range(FF // D):
        value[0, 8 + c : 9 + c] = ffn_ref[:, c * D : (c + 1) * D]
    partners = [dict(me, c=1 - core), dict(me, x=1 - me["x"]), dict(me, y=1 - me["y"])]
    step = 1
    while step < nz:
        partners.append(dict(me, z=me["z"] + step - 2 * step * ((me["z"] // step) % 2)))
        step *= 2

    def vector_copy(i):
        return pltpu.make_async_remote_copy(
            src_ref=value.at[i],
            dst_ref=land.at[i],
            send_sem=vsend.at[i],
            recv_sem=vrecv.at[i],
            device_id=device(partners[i]),
            device_id_type=MESH,
        )

    vector_copy(0).start()
    for w, f in ffn_steps:
        if w >= 20:
            f()
    d_tokens = d_sum1_ref[...]
    for e in range(3):
        d_tokens = d_tokens + outer_cols(proj[e], w_ref[e])
    d_tokens_ref[...] = d_tokens
    stage = 0
    for w, f in ordered(qkv):
        f()
        if w > 3 + 2 * stage and stage < len(partners):
            vector_copy(stage).wait_recv()
            total = value[stage] + land[stage]
            stage += 1
            if stage < len(partners):
                value[stage] = total
                vector_copy(stage).start()
            else:
                vec_out[...] = total
    for i in range(len(partners)):
        vector_copy(i).wait_send()
    finish_from_owners(n, place_row, head, mine, heads, inbox, sems_in)
    for cp, cond in pending:
        if cond is None:
            cp.wait_send()
        else:
            pl.when(cond)(cp.wait_send)


def finish(heads, rows, qkv, d_sum1, d_expand, d_contract, d_out, small, d_ffn, nz):
    n = lax.axis_size("seq")
    low, full = jnp.bfloat16, jnp.float32
    flat = [(3 * UNIT * D // 128, 128), (UNIT * D // 128, 128)]
    flat += [(UNIT * FF // 128, 128)] * 2
    stages = 3 + (nz - 1).bit_length()
    extra = []
    for kind, lo, hi, links, z_first in FFN_KINDS:
        width = FF if kind == "expand" else D
        extra += Reduction.buffers(nz, (hi - lo, width), z_first)
        extra += Reduction.semaphores(nz, z_first)
    for j, links, z_first in QKV_KINDS:
        extra += Reduction.buffers(nz, (UNIT, D), z_first)
        extra += Reduction.semaphores(nz, z_first)
    return pl.pallas_call(
        functools.partial(finish_kernel, n, nz),
        out_shape=[jax.ShapeDtypeStruct(s, full) for s in [(TOK_SEQ, D)] + flat + [(16, D)]],
        in_specs=[ANY, VMEM, ANY, VMEM, ANY, ANY, ANY, VMEM, VMEM],
        out_specs=[VMEM] * 6,
        scratch_shapes=[
            pltpu.VMEM((H, MSG, 128), low),
            pltpu.VMEM((3, TOK_SEQ, D), low),
            pltpu.VMEM((3, D, D), low),
            pltpu.VMEM(d_expand.shape, low),
            pltpu.VMEM(d_contract.shape, low),
            pltpu.VMEM(d_out.shape, low),
            pltpu.VMEM((QKV_UNITS, UNIT, D), low),
            pltpu.VMEM((stages, 16, D), full),
            pltpu.VMEM((stages, 16, D), full),
            pltpu.SemaphoreType.DMA((4,)),
            pltpu.SemaphoreType.DMA((stages,)),
            pltpu.SemaphoreType.DMA((stages,)),
            *exchange_sems(n),
            *extra,
        ],
        compiler_params=pltpu.CompilerParams(
            collective_id=5, has_side_effects=True, vmem_limit_bytes=60 << 20
        ),
        name="finish",
    )(heads, rows, qkv, d_sum1, d_expand, d_contract, d_out, small, d_ffn)


def unpack_heads(parts):
    parts = parts.reshape(H, BPD // 2, BLOCK, 2, HD).transpose(1, 3, 2, 0, 4)
    return parts.reshape(TOK_SEQ, D)


def unpack_keys(parts):
    parts = parts.reshape(H, TOK_SEQ, 2, HD).transpose(2, 1, 0, 3)
    return parts.reshape(2, TOK_SEQ, D)


def on_device(
    tokens,
    qkv_weight,
    out_weight,
    expand_weight,
    contract_weight,
    bias_vectors,
    gain_vectors,
    ffn_bias,
    random_blocks,
    cotangent,
):
    qkv, first, second, vectors, ffn = gather_weights(
        qkv_weight, out_weight, expand_weight, contract_weight, bias_vectors, gain_vectors, ffn_bias
    )
    planes = kernel_planes((qkv_weight, out_weight, expand_weight, contract_weight))
    rows = tokens.reshape(TOK_SEQ, D)
    kvq, picks = project_and_send(rows, qkv, vectors, random_blocks)
    attended, lse = attend_heads(kvq, picks)
    result, d_sum1, d_heads, d_expand, d_contract, d_out, small, d_ffn = middle(
        attended, rows, cotangent.reshape(TOK_SEQ, D), first, second, vectors, ffn
    )
    d_heads = attend_heads_back(kvq, picks, lse, d_heads)
    shards = lax.axis_size("dp") * lax.axis_size("seq")
    if planes:
        d_tokens, d_qkv, d_out, d_expand, d_contract, totals = finish(
            d_heads, rows, qkv, d_sum1, d_expand, d_contract, d_out, small, d_ffn, planes
        )
        me = lax.axis_index("dp") * lax.axis_size("seq") + lax.axis_index("seq")
        vectors = (totals[0:6], totals[6:8], totals[8 : 8 + FF // D])
        vectors = [
            lax.dynamic_slice(v.reshape(-1), (me * (v.size // shards),), (v.size // shards,))
            for v in vectors
        ]
    else:
        d_heads = exchange(from_owners_kernel, H, d_heads, 4, "return_head_grads")
        d_query = unpack_heads(d_heads[:, TOK_SEQ:])
        d_pair = unpack_keys(d_heads[:, :TOK_SEQ])
        d_proj = jnp.concatenate([d_query[None], d_pair], axis=0)
        d_qkv = jnp.einsum("rd,erf->edf", rows, d_proj, preferred_element_type=jnp.float32)
        d_tokens = d_sum1 + jnp.einsum(
            "erf,edf->rd", d_proj, qkv, preferred_element_type=jnp.float32
        )
        d_bias_q = jnp.sum(d_query.astype(jnp.float32), axis=0)
        d_bias_v = jnp.sum(d_pair[1].astype(jnp.float32), axis=0)
        d_biases = jnp.concatenate([jnp.stack([d_bias_q, d_bias_v]), small[0:4]])
        *vectors, d_qkv, d_out, d_expand, d_contract = [
            lax.psum_scatter(
                g.astype(jnp.float32).reshape(-1),
                ("dp", "seq"),
                scatter_dimension=0,
                tiled=True,
            )
            for g in (d_biases, small[4:6], d_ffn, d_qkv, d_out, d_expand, d_contract)
        ]
    grads = [g.reshape(-1) for g in (d_qkv, d_out, d_expand, d_contract)]
    return (result[None], d_tokens[None], *grads, *vectors)


def solution(mesh):
    return jax.shard_map(
        on_device,
        mesh=mesh,
        in_specs=(
            P("dp", "seq", None),
            P(("dp", "seq")),
            P(("dp", "seq")),
            P(("dp", "seq")),
            P(("dp", "seq")),
            P(("dp", "seq")),
            P(("dp", "seq")),
            P(("dp", "seq")),
            P("dp", None, "seq", None),
            P("dp", "seq", None),
        ),
        out_specs=(
            P("dp", "seq", None),
            P("dp", "seq", None),
            P(("dp", "seq")),
            P(("dp", "seq")),
            P(("dp", "seq")),
            P(("dp", "seq")),
            P(("dp", "seq")),
            P(("dp", "seq")),
            P(("dp", "seq")),
        ),
        check_vma=False,
    )
```

```python
import functools

import jax
import jax.numpy as jnp
from jax import lax
from jax.experimental import pallas as pl
from jax.experimental.pallas import tpu as pltpu
from jax.sharding import PartitionSpec as P

MESH = pl.DeviceIdType.MESH

D = 768
FF = 3072
H = 12
HD = 64
BLOCK = 64
TOK_SEQ = 256
SEQ_GRP = 1
BPD = 4


norm_eps = 1e-12
masked_score = -1e30


def matmul(left, right):
    return jnp.dot(left, right, preferred_element_type=jnp.float32)


def inner_rows(left, right):
    return lax.dot_general(
        left, right, (((0,), (0,)), ((), ())), preferred_element_type=jnp.float32
    )


def outer_cols(left, right):
    return lax.dot_general(
        left, right, (((1,), (1,)), ((), ())), preferred_element_type=jnp.float32
    )


def normalize(value, gain, shift):
    mean = jnp.mean(value, axis=-1, keepdims=True)
    centred = value - mean
    inverse = lax.rsqrt(jnp.mean(centred * centred, axis=-1, keepdims=True) + norm_eps)
    normed = centred * inverse
    return (normed * gain + shift, normed, inverse)


def normalize_back(grad, normed, inverse, gain):
    scaled = grad * gain
    centred = scaled - jnp.mean(scaled, axis=-1, keepdims=True)
    return inverse * (centred - normed * jnp.mean(scaled * normed, axis=-1, keepdims=True))


def place(nz):
    y = lax.axis_index("dp")
    s = lax.axis_index("seq")
    return {"y": y, "z": s // 4, "x": (s // 2) % 2, "c": s % 2}

def device(p):
    return (p["y"], p["z"] * 4 + p["x"] * 2 + p["c"])

def chip(p, nz):
    return (p["y"] * nz + p["z"]) * 2 + p["x"]

def index(p, nz):
    return chip(p, nz) * 2 + p["c"]

def nearest(m, n, j):
    if n == 2:
        return m if j == 0 else 1 - m
    out = 0
    for i in range(n):
        rank = sorted(range(n), key=lambda s: (abs(s - i), s))
        out = jnp.where(m == i, rank[j], out)
    return out

def combine(dst, srcs):
    rows, cols = dst.shape
    step = min(cols, max(128, (24 * 1024 // rows) // 128 * 128))
    while cols % step:
        step -= 128
    def part(sl):
        total = srcs[0][:, sl].astype(jnp.float32)
        for s in srcs[1:]:
            total = total + s[:, sl].astype(jnp.float32)
        dst[:, sl] = total.astype(dst.dtype)
    if cols == step:
        part(slice(None))
    else:
        def body(i, _):
            part(pl.ds(pl.multiple_of(i * step, 128), step))
            return 0
        lax.fori_loop(0, cols // step, body, 0)

def owner(head, n):
    return head * n // H


def owned(place, n):
    head = (place * H + n - 1) // n
    return jnp.minimum(head, H - 1), jnp.logical_and(head < H, owner(head, n) == place)


def greet_senders(n, place, mine, to_owners):
    row = lax.axis_index("dp")
    bar = pltpu.get_barrier_semaphore()

    def signal(to):
        @pl.when(to != place)
        def _():
            pl.semaphore_signal(bar, inc=1, device_id=(row, to), device_id_type=MESH)

    if to_owners:

        @pl.when(mine)
        def _():
            lax.fori_loop(0, n, lambda s, _: (signal(s), 0)[1], 0)

        pl.semaphore_wait(bar, H - jnp.where(mine, 1, 0))
    else:
        lax.fori_loop(0, H, lambda h, _: (signal(owner(h, n)), 0)[1], 0)

        @pl.when(mine)
        def _():
            pl.semaphore_wait(bar, n - 1)


def walk_to_owners(n, place, head, pairs, sems, act):
    row = lax.axis_index("dp")

    def body(k, _):
        h = (head + 1 + k) % H
        to = owner(h, n)
        for i, (src, dst) in enumerate(pairs):

            @pl.when(to != place)
            def _():
                act(
                    pltpu.make_async_remote_copy(
                        src_ref=src.at[h],
                        dst_ref=dst(place),
                        send_sem=sems[0].at[i, h],
                        recv_sem=sems[1].at[i, place],
                        device_id=(row, to),
                        device_id_type=MESH,
                    )
                )

        return 0

    lax.fori_loop(0, H, body, 0)


def finish_to_owners(n, place, head, pairs, sems):
    walk_to_owners(n, place, head, pairs, sems, lambda cp: cp.wait_send())


def send_to_owners(n, place, head, mine, pairs, sems, meanwhile, wait_sends=True):
    walk_to_owners(n, place, head, pairs, sems, lambda cp: cp.start())
    meanwhile()

    @pl.when(mine)
    def _():
        for i, (src, dst) in enumerate(pairs):
            cp = pltpu.make_async_copy(src.at[head], dst(place), sems[2].at[i])
            cp.start()
            cp.wait()

        def body(k, _):
            s = (place + 1 + k) % n
            for i, (src, dst) in enumerate(pairs):
                pltpu.make_async_remote_copy(
                    src_ref=src.at[0],
                    dst_ref=dst(s),
                    send_sem=sems[0].at[i, 0],
                    recv_sem=sems[1].at[i, s],
                    device_id=(lax.axis_index("dp"), place),
                    device_id_type=MESH,
                ).wait_recv()
            return 0

        lax.fori_loop(0, n - 1, body, 0)

    if wait_sends:
        finish_to_owners(n, place, head, pairs, sems)


def walk_from_owners(n, place, head, src, dst, sems, act):
    row = lax.axis_index("dp")

    def body(k, _):
        to = (place + 1 + k) % n
        act(
            pltpu.make_async_remote_copy(
                src_ref=src.at[to],
                dst_ref=dst.at[head],
                send_sem=sems[0].at[0, to],
                recv_sem=sems[1].at[0, head],
                device_id=(row, to),
                device_id_type=MESH,
            )
        )
        return 0

    lax.fori_loop(0, n - 1, body, 0)


def start_from_owners(n, place, head, mine, src, dst, sems):
    @pl.when(mine)
    def _():
        walk_from_owners(n, place, head, src, dst, sems, lambda cp: cp.start())
        cp = pltpu.make_async_copy(src.at[place], dst.at[head], sems[2].at[0])
        cp.start()
        cp.wait()


def wait_from_owners(n, place, head, src, dst, sems):
    def body(k, _):
        h = (head + k) % H

        @pl.when(owner(h, n) != place)
        def _():
            pltpu.make_async_remote_copy(
                src_ref=src.at[0],
                dst_ref=dst.at[h],
                send_sem=sems[0].at[0, 0],
                recv_sem=sems[1].at[0, h],
                device_id=(lax.axis_index("dp"), place),
                device_id_type=MESH,
            ).wait_recv()

        return 0

    lax.fori_loop(0, H, body, 0)


def finish_from_owners(n, place, head, mine, src, dst, sems):
    @pl.when(mine)
    def _():
        walk_from_owners(n, place, head, src, dst, sems, lambda cp: cp.wait_send())


def send_from_owners(n, place, head, mine, src, dst, sems):
    start_from_owners(n, place, head, mine, src, dst, sems)
    wait_from_owners(n, place, head, src, dst, sems)
    finish_from_owners(n, place, head, mine, src, dst, sems)


def swap_halves(tile):
    return pltpu.roll(tile, HD, tile.ndim - 1)


def low_lanes(shape):
    return lax.broadcasted_iota(jnp.int32, shape, len(shape) - 1) < HD


def exchange_sems(n, pairs=1):
    return [
        pltpu.SemaphoreType.DMA((pairs, max(n, H))),
        pltpu.SemaphoreType.DMA((pairs, max(n, H))),
        pltpu.SemaphoreType.DMA((pairs,)),
    ]


ANY = pl.BlockSpec(memory_space=pl.ANY)
VMEM = pl.BlockSpec(memory_space=pltpu.VMEM)
SMEM = pl.BlockSpec(memory_space=pltpu.SMEM)
MSG = TOK_SEQ + TOK_SEQ // 2


def from_owners_kernel(n, src, dst, *sems):
    place = lax.axis_index("seq")
    head, mine = owned(place, n)
    greet_senders(n, place, mine, False)
    send_from_owners(n, place, head, mine, src, dst, sems)


def exchange(kernel, slots, messages, ident, name):
    n = lax.axis_size("seq")
    return pl.pallas_call(
        functools.partial(kernel, n),
        out_shape=jax.ShapeDtypeStruct((slots,) + messages.shape[1:], messages.dtype),
        in_specs=[ANY],
        out_specs=ANY,
        scratch_shapes=exchange_sems(n),
        compiler_params=pltpu.CompilerParams(collective_id=ident, has_side_effects=True),
        name=name,
    )(messages)


def key_list(i, n, picks_ref):
    last = n * BPD - 1

    def of(b):
        s, r = b // BPD, b % BPD
        picked = [picks_ref[s, 0, r * 3 + j] for j in range(3)]
        return [jnp.maximum(b - 1, 0), b, jnp.minimum(b + 1, last), 0, last] + picked

    return [of(2 * i), of(2 * i + 1)]


def fill_pair(lists, kv_ref, vk_ref, keys, values):
    for j in range(8):
        a, b = lists[0][j], lists[1][j]
        to = slice(j * BLOCK, (j + 1) * BLOCK)
        keys[to, 0:HD] = kv_ref[a][:, 0:HD]
        keys[to, HD:128] = vk_ref[b][:, HD:128]
        values[to, 0:HD] = vk_ref[a][:, 0:HD]
        values[to, HD:128] = kv_ref[b][:, HD:128]


def two_blocks(tile):
    left = low_lanes(tile.shape)
    zero = jnp.zeros_like(tile)
    return jnp.concatenate([jnp.where(left, tile, zero), jnp.where(left, zero, tile)], axis=0)


def pair_scores(i, n, keys, query):
    scores = outer_cols(keys, query)
    left = low_lanes((BLOCK, 128))
    right = jnp.logical_not(left)
    end = n * BPD // 2 - 1
    hide_first = jnp.logical_and(left, i == 0)
    hide_last = jnp.logical_and(right, i == end)
    return jnp.concatenate(
        [
            jnp.where(hide_first, masked_score, scores[0:BLOCK]),
            scores[BLOCK : 2 * BLOCK],
            jnp.where(hide_last, masked_score, scores[2 * BLOCK : 3 * BLOCK]),
            scores[3 * BLOCK :],
        ],
        axis=0,
    )


def turn_pairs(n, kv_ref, vk_ref):
    def body(b, _):
        for t in range(BPD):
            tile = kv_ref[b * BPD + t].astype(jnp.float32)
            vk_ref[b * BPD + t] = swap_halves(tile).astype(jnp.bfloat16)
        return 0

    lax.fori_loop(0, n, body, 0)


def attend_back_kernel(
    n, kv_ref, q_ref, picks_ref, lse_ref, grad_ref, out_ref, vk_ref, keys, values, sum_k, sum_v
):
    place = lax.axis_index("seq")
    head, mine = owned(place, n)

    @pl.when(mine)
    def _():
        turn_pairs(n, kv_ref, vk_ref)

        def clear(s, _):
            for t in range(BPD):
                sum_k[s * BPD + t] = jnp.zeros((BLOCK, 128), jnp.float32)
                sum_v[s * BPD + t] = jnp.zeros((BLOCK, 128), jnp.float32)
            return 0

        lax.fori_loop(0, n, clear, 0)
        left = low_lanes((BLOCK, 128))

        def body(s, _):
            lists = [key_list(s * (BPD // 2) + t, n, picks_ref) for t in range(BPD // 2)]
            for t in range(BPD // 2):
                fill_pair(lists[t], kv_ref, vk_ref, keys.at[t], values.at[t])
            parts = []
            for t in range(BPD // 2):
                i = s * (BPD // 2) + t
                part = slice(t * BLOCK, (t + 1) * BLOCK)
                query = two_blocks(q_ref[s, part, :])
                grad = two_blocks(grad_ref[s, part, :])
                probs = jnp.exp(pair_scores(i, n, keys[t], query) - lse_ref[i])
                d_probs = outer_cols(values[t], grad)
                rows = jnp.sum(probs * d_probs, axis=0, keepdims=True)
                d_scores = (probs * (d_probs - rows)).astype(jnp.bfloat16)
                d_values = matmul(probs.astype(jnp.bfloat16), grad)
                d_keys = matmul(d_scores, query)
                full = inner_rows(d_scores, keys[t]) * HD ** (-0.5)
                to = slice(TOK_SEQ + t * BLOCK, TOK_SEQ + (t + 1) * BLOCK)
                out_ref[s, to, :] = jnp.where(left, full[:BLOCK], full[BLOCK:]).astype(jnp.bfloat16)
                parts.append((d_keys, d_values))
            for t in range(BPD // 2):
                for j in range(8):
                    part = slice(j * BLOCK, (j + 1) * BLOCK)
                    for u in range(2):
                        b = lists[t][u][j]
                        lanes = slice(u * HD, (u + 1) * HD)
                        sum_k[b, :, lanes] += parts[t][0][part, lanes]
                        sum_v[b, :, lanes] += parts[t][1][part, lanes]
            return 0

        lax.fori_loop(0, n, body, 0)

        def close(s, _):
            for t in range(BPD):
                k, v = sum_k[s * BPD + t], sum_v[s * BPD + t]
                both = jnp.where(left, k + swap_halves(k), v + swap_halves(v))
                out_ref[s, t * BLOCK : (t + 1) * BLOCK, :] = both.astype(jnp.bfloat16)
            return 0

        lax.fori_loop(0, n, close, 0)


def attend_heads_back(kv, queries, picks, lse, grad):
    n = lax.axis_size("seq")
    return pl.pallas_call(
        functools.partial(attend_back_kernel, n),
        out_shape=jax.ShapeDtypeStruct((n, MSG, 128), jnp.bfloat16),
        in_specs=[VMEM, VMEM, SMEM, VMEM, VMEM],
        out_specs=VMEM,
        scratch_shapes=[
            pltpu.VMEM((n * BPD, BLOCK, 128), jnp.bfloat16),
            pltpu.VMEM((BPD // 2, 8 * BLOCK, 128), jnp.bfloat16),
            pltpu.VMEM((BPD // 2, 8 * BLOCK, 128), jnp.bfloat16),
            pltpu.VMEM((n * BPD, BLOCK, 128), jnp.float32),
            pltpu.VMEM((n * BPD, BLOCK, 128), jnp.float32),
        ],
        compiler_params=pltpu.CompilerParams(vmem_limit_bytes=56 << 20),
        name="attend_heads_back",
    )(kv, queries, picks, lse, grad)


UNITS = 32
WIDE = 768


def greet_row(n, place, mine):
    row = lax.axis_index("dp")
    bar = pltpu.get_barrier_semaphore()

    def body(s, _):
        there = owned(s, n)[1]

        @pl.when(jnp.logical_and(s != place, jnp.logical_or(mine, there)))
        def _():
            pl.semaphore_signal(bar, inc=1, device_id=(row, s), device_id_type=MESH)

        return 0

    lax.fori_loop(0, n, body, 0)
    pl.semaphore_wait(bar, jnp.where(mine, n - 1, H))


def unpack_pair(tiles, odd, shape):
    left = low_lanes(shape)
    a, b = tiles.astype(jnp.float32), odd.astype(jnp.float32)
    return (jnp.where(left, a, swap_halves(b)), jnp.where(left, swap_halves(a), b))


def add_flat(out_ref, base, srcs):
    rows, cols = srcs[0].shape
    for k in range(cols // 128):
        lanes = slice(k * 128, (k + 1) * 128)
        total = srcs[0][:, lanes].astype(jnp.float32)
        for s in srcs[1:]:
            total = total + s[:, lanes].astype(jnp.float32)
        out_ref[pl.ds(base + k, rows, stride=cols // 128), :] = total


class Reduction:
    def __init__(self, nz, me, links, z_first, own, give, emit, bufs, sems, pending):
        self.nz, self.me, self.links, self.z_first = nz, me, links, z_first
        self.own, self.give, self.emit = own, give, emit
        self.rc, self.ra, self.rb, self.below, self.above = bufs
        self.csend, self.crecv, self.send, self.recv = sems
        self.pending = pending

    @staticmethod
    def buffers(nz, slab, z_first):
        chips = 4 * nz
        counts = (chips, 2, 2, chips, chips) if z_first else (chips, nz, 2 * nz, nz, nz)
        return [pltpu.VMEM((c,) + slab, jnp.bfloat16) for c in counts]

    @staticmethod
    def semaphores(nz, z_first):
        count = 8 * nz + 3 if z_first else 5 * nz
        return [pltpu.SemaphoreType.DMA((c,)) for c in (4 * nz, 4 * nz, count, count)]

    def start(self, src, dst, slot, to, cond=None):
        cp = pltpu.make_async_remote_copy(
            src_ref=src,
            dst_ref=dst,
            send_sem=self.send.at[slot],
            recv_sem=self.recv.at[slot],
            device_id=device(to),
            device_id_type=MESH,
        )
        if cond is None:
            cp.start()
        else:
            pl.when(cond)(cp.start)
        self.pending.append((cp, cond))

    def arrived(self, ref, sem):
        pltpu.make_async_remote_copy(
            src_ref=ref,
            dst_ref=ref,
            send_sem=self.send.at[0],
            recv_sem=sem,
            device_id=device(dict(self.me, c=1 - self.me["c"])),
            device_id_type=MESH,
        ).wait_recv()

    def flip(self, which, f):
        d = self.links[which]
        return 1 - self.me[d] if f else self.me[d]

    def piece(self, z, a, b):
        c = {self.links[0]: a, self.links[1]: b}
        return (c["y"] * self.nz + z) * 2 + c["x"]

    def across(self, which):
        d = self.links[which]
        return dict(self.me, **{d: 1 - self.me[d]})

    def hand_over(self):
        nz = self.nz
        zs = sorted(range(nz), key=lambda z: -abs(2 * z - nz + 1))
        if self.z_first:
            order = [(z, fa, fb) for z in zs for fa, fb in ((1, 1), (0, 1), (1, 0), (0, 0))]
        else:
            order = [(z, fa, fb) for fb in (1, 0) for fa in (1, 0) for z in zs]

        def one(z, fa, fb):
            def run():
                p = self.piece(z, self.flip(0, fa), self.flip(1, fb))
                cp = pltpu.make_async_remote_copy(
                    src_ref=self.give(p),
                    dst_ref=self.rc.at[p],
                    send_sem=self.csend.at[p],
                    recv_sem=self.crecv.at[p],
                    device_id=device(dict(self.me, c=1 - self.me["c"])),
                    device_id_type=MESH,
                )
                cp.start()
                self.pending.append((cp, None))

            return run

        return [one(*o) for o in order]

    def mine(self, p):
        self.arrived(self.rc.at[p], self.crecv.at[p])
        return [self.own(p), self.rc.at[p]]

    def relay(self, z, p, srcs, bref, aref, sb, sa):
        nz, mz, acc = self.nz, self.me["z"], self.rc.at[p]
        if z > 0:

            @pl.when(mz == 0)
            def _():
                combine(acc, srcs)

            @pl.when(jnp.logical_and(mz > 0, mz < z))
            def _():
                self.arrived(bref, self.recv.at[sb])
                combine(acc, srcs + [bref])

            self.start(acc, bref, sb, dict(self.me, z=jnp.minimum(mz + 1, nz - 1)), mz < z)
        if z < nz - 1:

            @pl.when(mz == nz - 1)
            def _():
                combine(acc, srcs)

            @pl.when(jnp.logical_and(mz < nz - 1, mz > z))
            def _():
                self.arrived(aref, self.recv.at[sa])
                combine(acc, srcs + [aref])

            self.start(acc, aref, sa, dict(self.me, z=jnp.maximum(mz - 1, 0)), mz > z)

    def ends(self, z, bref, aref, sb, sa):
        out = []
        if z > 0:
            self.arrived(bref, self.recv.at[sb])
            out.append(bref)
        if z < self.nz - 1:
            self.arrived(aref, self.recv.at[sa])
            out.append(aref)
        return out

    def steps(self):
        return self.steps_z_first() if self.z_first else self.steps_z_last()

    def steps_z_last(self):
        nz, me = self.nz, self.me
        zs = sorted(range(nz), key=lambda z: -abs(2 * z - nz + 1))

        def along_b(z, fa):
            def run():
                a = self.flip(0, fa)
                p = self.piece(z, a, self.flip(1, 1))
                combine(self.rc.at[p], self.mine(p))
                s = z * 2 + a
                self.start(self.rc.at[p], self.rb.at[s], s, self.across(1))

            return run

        def along_a(z):
            def run():
                a = self.flip(0, 1)
                p = self.piece(z, a, self.flip(1, 0))
                s = z * 2 + a
                srcs = self.mine(p)
                self.arrived(self.rb.at[s], self.recv.at[s])
                combine(self.rc.at[p], srcs + [self.rb.at[s]])
                self.start(self.rc.at[p], self.ra.at[z], 2 * nz + z, self.across(0))

            return run

        def chain(z):
            def run():
                p = self.piece(z, self.flip(0, 0), self.flip(1, 0))
                s = z * 2 + self.flip(0, 0)
                srcs = self.mine(p)
                self.arrived(self.rb.at[s], self.recv.at[s])
                self.arrived(self.ra.at[z], self.recv.at[2 * nz + z])
                srcs += [self.rb.at[s], self.ra.at[z]]
                bref, aref = self.below.at[z], self.above.at[z]
                self.relay(z, p, srcs, bref, aref, 3 * nz + z, 4 * nz + z)

            return run

        def last():
            for z in range(nz):

                @pl.when(me["z"] == z)
                def _():
                    p = self.piece(z, self.flip(0, 0), self.flip(1, 0))
                    s = z * 2 + self.flip(0, 0)
                    srcs = [self.own(p), self.rc.at[p], self.rb.at[s], self.ra.at[z]]
                    bref, aref = self.below.at[z], self.above.at[z]
                    self.emit(srcs + self.ends(z, bref, aref, 3 * nz + z, 4 * nz + z))

        out = [(1 + i, along_b(z, 1)) for i, z in enumerate(zs)]
        out += [(5 + i, along_b(z, 0)) for i, z in enumerate(zs)]
        out += [(5.5 + i, along_a(z)) for i, z in enumerate(zs)]
        out += [(9.5 + i, chain(z)) for i, z in enumerate(zs)]
        return out + [(20, last)]

    def steps_z_first(self):
        nz, me = self.nz, self.me
        zs = sorted(range(nz), key=lambda z: -abs(2 * z - nz + 1))
        s0 = 8 * nz

        def slots(z, fa, fb):
            q = self.flip(0, fa) * 2 + self.flip(1, fb)
            return self.below.at[z * 4 + q], self.above.at[z * 4 + q], z * 4 + q, 4 * nz + z * 4 + q

        def chain(z, fa, fb):
            def run():
                p = self.piece(z, self.flip(0, fa), self.flip(1, fb))
                self.relay(z, p, self.mine(p), *slots(z, fa, fb))

            return run

        def settle(fa, fb):
            for z in range(nz):

                @pl.when(me["z"] == z)
                def _():
                    p = self.piece(z, self.flip(0, fa), self.flip(1, fb))
                    srcs = [self.own(p), self.rc.at[p]] + self.ends(z, *slots(z, fa, fb))
                    combine(self.rc.at[p], srcs)

            return self.rc.at[self.piece(me["z"], self.flip(0, fa), self.flip(1, fb))]

        def along_b(fa):
            def run():
                self.start(settle(fa, 1), self.rb.at[fa], s0 + fa, self.across(1))

            return run

        def along_a():
            ref = settle(1, 0)
            self.arrived(self.rb.at[1], self.recv.at[s0 + 1])
            combine(self.ra.at[0], [ref, self.rb.at[1]])
            self.start(self.ra.at[0], self.ra.at[1], s0 + 2, self.across(0))

        def last():
            ref = settle(0, 0)
            self.arrived(self.rb.at[0], self.recv.at[s0])
            self.arrived(self.ra.at[1], self.recv.at[s0 + 2])
            self.emit([ref, self.rb.at[0], self.ra.at[1]])

        out = []
        for i, z in enumerate(zs):
            for m, (fa, fb) in enumerate(((1, 1), (0, 1), (1, 0), (0, 0))):
                out.append((1 + i * 2.5 + m * 0.5, chain(z, fa, fb)))
        return out + [(11.1, along_b(1)), (11.2, along_b(0)), (12.5, along_a), (21, last)]


class Spread:
    def __init__(self, nz, me, order, at, sems, pending):
        self.nz, self.me, self.order, self.at = nz, me, order, at
        self.send, self.recv, self.csend, self.crecv = sems
        self.pending = pending

    @staticmethod
    def semaphores(nz):
        chips = 4 * nz
        return [pltpu.SemaphoreType.DMA((chips, 4))] + [pltpu.SemaphoreType.DMA((chips,))] * 3

    def copy(self, slot, send, recv, to):
        ref = self.at(slot)
        return pltpu.make_async_remote_copy(
            src_ref=ref,
            dst_ref=ref,
            send_sem=send,
            recv_sem=recv,
            device_id=device(to),
            device_id_type=MESH,
        )

    def start(self, cp, cond=None):
        if cond is None:
            cp.start()
        else:
            pl.when(cond)(cp.start)
        self.pending.append((cp, cond))

    def one(self, steps):
        nz, me = self.nz, self.me
        size = {"y": 2, "z": nz, "x": 2}
        own = not any(steps)

        def run():
            src = dict(me)
            for d, i in zip(self.order, steps):
                src[d] = nearest(me[d], size[d], i)
            c = chip(src, nz)
            slot = c * 2 + me["c"]
            if not own:
                self.copy(slot, self.send.at[c, 0], self.recv.at[c], me).wait_recv()
            stage = 2 if steps[2] else (1 if steps[1] else 0)
            for t in range(stage, 3):
                d = self.order[t]
                onward = t == stage and not own
                if d == "z":
                    up, down = me["z"] < nz - 1, me["z"] > 0
                    if onward:
                        up = jnp.logical_and(up, src["z"] <= me["z"])
                        down = jnp.logical_and(down, src["z"] >= me["z"])
                    above = dict(me, z=jnp.minimum(me["z"] + 1, nz - 1))
                    below = dict(me, z=jnp.maximum(me["z"] - 1, 0))
                    self.start(self.copy(slot, self.send.at[c, 0], self.recv.at[c], above), up)
                    self.start(self.copy(slot, self.send.at[c, 1], self.recv.at[c], below), down)
                elif not (onward and steps[t]):
                    way = 2 if d == "x" else 3
                    to = dict(me, **{d: 1 - me[d]})
                    self.start(self.copy(slot, self.send.at[c, way], self.recv.at[c], to))
            sibling = dict(me, c=1 - me["c"])
            self.start(self.copy(slot, self.csend.at[c], self.crecv.at[c], sibling))

        return run

    def steps(self):
        size = {"y": 2, "z": self.nz, "x": 2}
        n0, n1, n2 = (size[d] for d in self.order)
        return [
            (i0 + i1 + i2, self.one((i0, i1, i2)))
            for i2 in range(n2)
            for i1 in range(n1)
            for i0 in range(n0)
        ]

    def finish(self):
        def body(c, _):
            slot = c * 2 + 1 - self.me["c"]
            self.copy(slot, self.csend.at[c], self.crecv.at[c], self.me).wait_recv()
            return 0

        lax.fori_loop(0, 4 * self.nz, body, 0)


def run_in_order(items, low, high):
    steps = [(w, i, f) for i, item in enumerate(items) for w, f in item.steps()]
    for w, _, f in sorted(steps, key=lambda s: s[:2]):
        if low <= w < high:
            f()


def exchange_partners(me, nz):
    partners = [dict(me, **{d: 1 - me[d]}) for d in ("c", "x", "y")]
    step = 1
    while step < nz:
        partners.append(dict(me, z=me["z"] + step - 2 * step * ((me["z"] // step) % 2)))
        step *= 2
    return partners


def vector_copy(i, value, land, sems, partners):
    return pltpu.make_async_remote_copy(
        src_ref=value.at[i],
        dst_ref=land.at[i],
        send_sem=sems[0].at[i],
        recv_sem=sems[1].at[i],
        device_id=device(partners[i]),
        device_id_type=MESH,
    )


def greet_row_and_y(n, me, place_row):
    bar = pltpu.get_barrier_semaphore()

    def greet(k, _):
        to = (place_row + 1 + k) % n
        pl.semaphore_signal(bar, inc=1, device_id=(me["y"], to), device_id_type=MESH)
        return 0

    lax.fori_loop(0, n - 1, greet, 0)
    pl.semaphore_signal(bar, inc=1, device_id=(1 - me["y"], place_row), device_id_type=MESH)
    return lambda: pl.semaphore_wait(bar, n)


UNIT = D // UNITS
THIRD = FF // UNITS // 3
QKV_ORDERS = (("z", "x", "y"), ("z", "y", "x"), ("x", "y", "z"))
REST = (
    ("second", THIRD, FF // UNITS, ("z", "y", "x")),
    ("first", 0, UNIT, ("z", "x", "y")),
    ("second", 0, THIRD, ("z", "x", "y")),
)


def from_flat(flat, cols, rows):
    step = cols // 128
    return [flat[pl.ds(k, rows, stride=step), :] for k in range(step)]


def as_matrix(units):
    count, rows, cols = units.shape
    return units.astype(jnp.float32).reshape(count * rows, cols).astype(jnp.bfloat16)


def kernel_planes():
    seq = lax.axis_size("seq")
    if lax.axis_size("dp") != 2 or 2 * seq != UNITS or seq % 4:
        return 0
    return seq // 4


def front_kernel(n, nz, *refs):
    rows_ref, cot_ref, picks_ref, vec_in, qkv_in, first_in, out_in, second_in = refs[:8]
    (
        result_ref,
        d_sum1_ref,
        kv_hbm,
        q_hbm,
        picks_hbm,
        lse_ref,
        d_heads,
        dw1_hbm,
        dw2_hbm,
        dwo_hbm,
        small_ref,
        d_ffn_ref,
        w_hbm,
    ) = refs[8:21]
    (
        w_ref,
        first_ref,
        second_ref,
        flat,
        value,
        land,
        box_kv,
        box_q,
        kv_ref,
        q_ref,
        vk_ref,
        picks_smem,
        keys,
        values,
        attended,
        inbox,
        grad_box,
        slope_ref,
        active_ref,
        dw1_ref,
        dw2_ref,
        dwo_ref,
        mixed_ref,
        load_sem,
        store_sem,
        keep_sem,
        vsend,
        vrecv,
    ) = refs[21:49]
    sems_qkv, sems_in, sems_out = refs[49:52], refs[52:55], refs[55:58]
    rest = list(refs[58:])
    place_row = lax.axis_index("seq")
    head, mine = owned(place_row, n)
    pending = []

    if nz:
        me = place(nz)
        slot = index(me, nz)
        hold = greet_row_and_y(n, me, place_row)
        stages = 3 + (nz - 1).bit_length()

        def take():
            out = rest[:4]
            del rest[:4]
            return out

        def widen(src):
            count = src.shape[0]
            flat[0:count] = src[...].astype(jnp.float32)

        widen(qkv_in)
        for j in range(3):
            step = D // 128
            for k in range(step):
                col = flat[pl.ds(j * UNIT * step + k, UNIT, stride=step), :]
                w_ref[slot * 3 + j, :, k * 128 : (k + 1) * 128] = col.astype(jnp.bfloat16)
        value[0] = vec_in[...]
        hold()
        qkv_items = [
            Spread(nz, me, order, lambda s, j=j: w_ref.at[s * 3 + j], take(), pending)
            for j, order in enumerate(QKV_ORDERS)
        ]
        buffers = {"first": first_ref, "second": second_ref}

        def part(kind, lo, hi):
            ref = buffers[kind]
            if hi - lo == ref.shape[1]:
                return lambda s: ref.at[s]
            return lambda s: ref.at[s, lo:hi]

        rest_items = [
            Spread(nz, me, order, part(kind, lo, hi), take(), pending)
            for kind, lo, hi, order in REST
        ]
        partners = exchange_partners(me, nz)
        vsems = (vsend, vrecv)
        vector_copy(0, value, land, vsems, partners).start()
        run_in_order(qkv_items, 0, 1)
        for src, dst, at, cols, count in (
            (first_in, first_ref, 0, FF, UNIT),
            (out_in, first_ref, FF, D, UNIT),
            (second_in, second_ref, 0, D, FF // UNITS),
        ):
            widen(src)
            for k, col in enumerate(from_flat(flat, cols, count)):
                dst[slot, :, at + k * 128 : at + (k + 1) * 128] = col.astype(jnp.bfloat16)

        def vector_stage(i):
            vector_copy(i, value, land, vsems, partners).wait_recv()
            value[i + 1] = value[i] + land[i]
            if i + 1 < stages:
                vector_copy(i + 1, value, land, vsems, partners).start()

        for depth in range(1, nz + 2):
            vector_stage(min(depth - 1, stages)) if depth <= stages else None
            run_in_order(qkv_items, depth, depth + 1)
            if depth == 2:
                run_in_order(rest_items, 0, 1)
        for i in range(nz + 1, stages):
            vector_stage(i)
        for item in qkv_items:
            item.finish()
        vec = value.at[stages]
    else:
        greet_row(n, place_row, mine)
        loads = [
            pltpu.make_async_copy(src, dst, load_sem.at[i])
            for i, (src, dst) in enumerate(
                ((qkv_in, w_ref), (first_in, first_ref), (second_in, second_ref))
            )
        ]
        for cp in loads:
            cp.start()
        for cp in loads:
            cp.wait()
        vec = vec_in

    def rest_steps(low, high):
        if nz:
            run_in_order(rest_items, low, high)

    rows = rows_ref[...]
    left = low_lanes((TOK_SEQ, 128))
    left_q = low_lanes((BLOCK, 128))
    wide = 256
    for g in range(D // wide):
        cols = slice(g * wide, (g + 1) * wide)

        def project(e):
            return matmul(rows, as_matrix(w_ref[e * UNITS : (e + 1) * UNITS, :, cols]))

        q = (project(0) + vec[0:1, cols]) * HD ** (-0.5)
        k = project(1)
        v = project(2) + vec[1:2, cols]
        for p in range(wide // 128):
            h = (g * wide + p * 128) // HD
            lanes = slice(p * 128, (p + 1) * 128)
            kp, vp, qp = k[:, lanes], v[:, lanes], q[:, lanes]
            even, odd = jnp.where(left, kp, swap_halves(vp)), jnp.where(left, swap_halves(kp), vp)
            for t in range(BPD):
                part = slice(t * BLOCK, (t + 1) * BLOCK)
                box_kv[h, t] = even[part].astype(jnp.bfloat16)
                box_kv[h + 1, t] = odd[part].astype(jnp.bfloat16)
            turned = swap_halves(qp)
            for t in range(BPD // 2):
                a = slice(2 * t * BLOCK, (2 * t + 1) * BLOCK)
                b = slice((2 * t + 1) * BLOCK, (2 * t + 2) * BLOCK)
                to = slice(t * BLOCK, (t + 1) * BLOCK)
                box_q[h, to, :] = jnp.where(left_q, qp[a], turned[b]).astype(jnp.bfloat16)
                box_q[h + 1, to, :] = jnp.where(left_q, turned[a], qp[b]).astype(jnp.bfloat16)
    parcels = (
        (box_kv, lambda s: kv_ref.at[pl.ds(s * BPD, BPD)]),
        (box_q, lambda s: q_ref.at[s]),
        (picks_ref, lambda s: picks_hbm.at[s]),
    )
    send_to_owners(
        n,
        place_row,
        head,
        mine,
        parcels,
        sems_qkv,
        lambda: rest_steps(1, 3),
        wait_sends=False,
    )

    keep = (
        pltpu.make_async_copy(kv_ref, kv_hbm, keep_sem.at[0]),
        pltpu.make_async_copy(q_ref, q_hbm, keep_sem.at[3]),
    )
    keep_w = pltpu.make_async_copy(w_ref, w_hbm, keep_sem.at[2])
    keep_w.start()
    groups = 4

    @pl.when(mine)
    def _():
        for copy in keep:
            copy.start()
        cp = pltpu.make_async_copy(picks_hbm, picks_smem, keep_sem.at[1])
        cp.start()
        cp.wait()
        turn_pairs(n, kv_ref, vk_ref)

    def attend_some(k, _):
        s = (place_row + 1 + k) % n
        for t in range(BPD // 2):
            i = s * (BPD // 2) + t
            fill_pair(key_list(i, n, picks_smem), kv_ref, vk_ref, keys.at[t], values.at[t])
        for t in range(BPD // 2):
            i = s * (BPD // 2) + t
            part = slice(t * BLOCK, (t + 1) * BLOCK)
            query = two_blocks(q_ref[s, part, :])
            scores = pair_scores(i, n, keys[t], query)
            top = jnp.max(scores, axis=0, keepdims=True)
            weights = jnp.exp(scores - top)
            total = jnp.sum(weights, axis=0, keepdims=True)
            probs = (weights * (1.0 / total)).astype(jnp.bfloat16)
            full = inner_rows(probs, values[t])
            attended[s, part, :] = jnp.where(left_q, full[:BLOCK], full[BLOCK:]).astype(
                jnp.bfloat16
            )
            lse_ref[i] = top + jnp.log(total)

        @pl.when(s != place_row)
        def _():
            pltpu.make_async_remote_copy(
                src_ref=attended.at[s],
                dst_ref=inbox.at[head],
                send_sem=sems_in[0].at[0, s],
                recv_sem=sems_in[1].at[0, head],
                device_id=(lax.axis_index("dp"), s),
                device_id_type=MESH,
            ).start()

        return 0

    for g in range(groups):

        @pl.when(mine)
        def _():
            lax.fori_loop(g * (n // groups), (g + 1) * (n // groups), attend_some, 0)

        rest_steps(3 + g, 4 + g if g < groups - 1 else 99)

    @pl.when(mine)
    def _():
        cp = pltpu.make_async_copy(attended.at[place_row], inbox.at[head], sems_in[2].at[0])
        cp.start()
        cp.wait()

    if nz:
        for item in rest_items:
            item.finish()
    wait_from_owners(n, place_row, head, attended, inbox, sems_in)

    for h in range(0, H, 2):
        for t in range(BPD // 2):
            part = slice(t * BLOCK, (t + 1) * BLOCK)
            a, b = unpack_pair(inbox[h, part, :], inbox[h + 1, part, :], (BLOCK, 128))
            lanes = slice(h * HD, (h + 2) * HD)
            mixed_ref[2 * t * BLOCK : (2 * t + 1) * BLOCK, lanes] = a.astype(jnp.bfloat16)
            mixed_ref[(2 * t + 1) * BLOCK : (2 * t + 2) * BLOCK, lanes] = b.astype(jnp.bfloat16)
    out_w = as_matrix(first_ref[:, :, FF : FF + D])
    hidden1 = rows_ref[...].astype(jnp.float32) + matmul(mixed_ref[...], out_w) + vec[2:3]
    normed_out1, normed1, inverse1 = normalize(hidden1, vec[6:7], vec[3:4])
    lowered = normed_out1.astype(jnp.bfloat16)
    per = UNITS * WIDE // FF

    def second_rows(c):
        return second_ref[pl.ds(c * per, per)].reshape(WIDE, D)

    def up_step(c, hidden):
        cols = pl.ds(pl.multiple_of(c * WIDE, WIDE), WIDE)
        up = matmul(lowered, as_matrix(first_ref[:, :, cols])) + vec[pl.ds(8 + c, 1)]
        square = up * up
        inner = (2 / jnp.pi) ** 0.5 * (up + 0.044715 * up * square)
        curve = jnp.tanh(inner)
        active = (0.5 * up * (1 + curve)).astype(jnp.bfloat16)
        slope_ref[:, cols] = 0.5 * (1 + curve) + 0.5 * up * (1 - curve * curve) * (
            (2 / jnp.pi) ** 0.5 * (1 + 3 * 0.044715 * square)
        )
        active_ref[:, cols] = active
        return hidden + matmul(active, second_rows(c))

    hidden2 = lax.fori_loop(0, FF // WIDE, up_step, normed_out1 + vec[4:5])
    result, normed2, inverse2 = normalize(hidden2, vec[7:8], vec[5:6])
    result_ref[...] = result
    grad = cot_ref[...].astype(jnp.float32)
    d_sum2 = normalize_back(grad, normed2, inverse2, vec[7:8])
    d_down = d_sum2.astype(jnp.bfloat16)

    def add_rows(x):
        return jnp.sum(x, axis=0, keepdims=True)

    small_ref[2:3] = add_rows(d_down.astype(jnp.float32))
    small_ref[3:4] = add_rows(grad)
    small_ref[5:6] = add_rows(grad * normed2)

    def stores(c):
        cols = pl.ds(pl.multiple_of(c * WIDE, WIDE), WIDE)
        slabs = pl.ds(c * per, per)
        return (
            pltpu.make_async_copy(dw1_ref.at[:, :, cols], dw1_hbm.at[:, :, cols], store_sem.at[0, c]),
            pltpu.make_async_copy(dw2_ref.at[slabs], dw2_hbm.at[slabs], store_sem.at[1, c]),
        )

    def back_step(c, d_norm1):
        cols = pl.ds(pl.multiple_of(c * WIDE, WIDE), WIDE)
        d_active = outer_cols(d_down, second_rows(c))
        d_up = (d_active * slope_ref[:, cols]).astype(jnp.bfloat16)
        d_ffn_ref[:, cols] = add_rows(d_up.astype(jnp.float32))
        dw2 = inner_rows(active_ref[:, cols], d_down)
        dw2_ref[pl.ds(c * per, per)] = dw2.reshape(per, FF // UNITS, D).astype(jnp.bfloat16)
        dw1 = inner_rows(lowered, d_up)
        dw1_ref[:, :, cols] = dw1.reshape(UNITS, UNIT, WIDE).astype(jnp.bfloat16)
        for cp in stores(c):
            cp.start()
        return d_norm1 + outer_cols(d_up, as_matrix(first_ref[:, :, cols]))

    d_norm1 = lax.fori_loop(0, FF // WIDE, back_step, d_sum2)
    small_ref[1:2] = add_rows(d_norm1)
    small_ref[4:5] = add_rows(d_norm1 * normed1)
    d_sum1 = normalize_back(d_norm1, normed1, inverse1, vec[6:7])
    d_sum1_ref[...] = d_sum1
    d_attn = d_sum1.astype(jnp.bfloat16)
    small_ref[0:1] = add_rows(d_attn.astype(jnp.float32))
    d_mixed = outer_cols(d_attn, as_matrix(first_ref[:, :, FF : FF + D]))
    for h in range(0, H, 2):
        for t in range(BPD // 2):
            part = slice(t * BLOCK, (t + 1) * BLOCK)
            lanes = slice(h * HD, (h + 2) * HD)
            a, b = unpack_pair(
                d_mixed[2 * t * BLOCK : (2 * t + 1) * BLOCK, lanes],
                d_mixed[(2 * t + 1) * BLOCK : (2 * t + 2) * BLOCK, lanes],
                (BLOCK, 128),
            )
            grad_box[h, part, :] = a.astype(jnp.bfloat16)
            grad_box[h + 1, part, :] = b.astype(jnp.bfloat16)

    store_out = pltpu.make_async_copy(dwo_ref, dwo_hbm, load_sem.at[0])

    def late():
        dwo = inner_rows(mixed_ref[...], d_attn).reshape(UNITS, UNIT, D)
        dwo_ref[...] = dwo.astype(jnp.bfloat16)
        store_out.start()

    send_to_owners(n, place_row, head, mine, ((grad_box, lambda s: d_heads.at[s]),), sems_out, late)
    store_out.wait()

    def drain(c, _):
        for cp in stores(c):
            cp.wait()
        return 0

    lax.fori_loop(0, FF // WIDE, drain, 0)

    @pl.when(mine)
    def _():
        for copy in keep:
            copy.wait()

    keep_w.wait()
    finish_from_owners(n, place_row, head, mine, attended, inbox, sems_in)
    finish_to_owners(n, place_row, head, parcels, sems_qkv)
    if nz:
        for i in range(stages):
            vector_copy(i, value, land, vsems, partners).wait_send()
    for cp, cond in pending:
        if cond is None:
            cp.wait_send()
        else:
            pl.when(cond)(cp.wait_send)


def front(rows, cotangent, picks, vec, qkv, first, out, second, nz):
    n = lax.axis_size("seq")
    low, full = jnp.bfloat16, jnp.float32
    picks = jnp.pad(picks.reshape(H, 1, BPD * 3), ((0, 0), (0, 7), (0, 128 - BPD * 3)))
    part = (TOK_SEQ // 2, 128)
    pairs = n * BPD // 2
    units = [(UNITS, UNIT, FF), (UNITS, FF // UNITS, D), (UNITS, UNIT, D)]
    shapes = [((TOK_SEQ, D), full), ((TOK_SEQ, D), full)]
    shapes += [((n * BPD, BLOCK, 128), low), ((n,) + part, low)]
    shapes += [((n, 8, 128), jnp.int32), ((pairs, 1, 128), full), ((n,) + part, low)]
    shapes += [(u, low) for u in units] + [((8, D), full), ((1, FF), full)]
    shapes += [((3 * UNITS, UNIT, D), low)]
    stages = 3 + (max(nz, 1) - 1).bit_length()
    where = VMEM if nz else ANY
    extra = []
    for _ in range(6 if nz else 0):
        extra += Spread.semaphores(nz)
    return pl.pallas_call(
        functools.partial(front_kernel, n, nz),
        out_shape=[jax.ShapeDtypeStruct(s, d) for s, d in shapes],
        in_specs=[VMEM, VMEM, ANY, VMEM, where, where, where, where],
        out_specs=[VMEM, VMEM, ANY, ANY, ANY, VMEM, ANY, ANY, ANY, ANY, VMEM, VMEM, ANY],
        scratch_shapes=[
            pltpu.VMEM((3 * UNITS, UNIT, D), low),
            pltpu.VMEM((UNITS, UNIT, FF + D), low),
            pltpu.VMEM((UNITS, FF // UNITS, D), low),
            pltpu.VMEM((UNIT * FF // 128, 128), full),
            pltpu.VMEM((stages + 1, 16, D), full),
            pltpu.VMEM((stages, 16, D), full),
            pltpu.VMEM((H, BPD, BLOCK, 128), low),
            pltpu.VMEM((H,) + part, low),
            pltpu.VMEM((n * BPD, BLOCK, 128), low),
            pltpu.VMEM((n,) + part, low),
            pltpu.VMEM((n * BPD, BLOCK, 128), low),
            pltpu.SMEM((n, 8, 128), jnp.int32),
            pltpu.VMEM((BPD // 2, 8 * BLOCK, 128), low),
            pltpu.VMEM((BPD // 2, 8 * BLOCK, 128), low),
            pltpu.VMEM((n,) + part, low),
            pltpu.VMEM((H,) + part, low),
            pltpu.VMEM((H,) + part, low),
            pltpu.VMEM((TOK_SEQ, FF), full),
            pltpu.VMEM((TOK_SEQ, FF), low),
            *[pltpu.VMEM(u, low) for u in units],
            pltpu.VMEM((TOK_SEQ, D), low),
            pltpu.SemaphoreType.DMA((3,)),
            pltpu.SemaphoreType.DMA((2, FF // WIDE)),
            pltpu.SemaphoreType.DMA((4,)),
            pltpu.SemaphoreType.DMA((stages,)),
            pltpu.SemaphoreType.DMA((stages,)),
            *exchange_sems(n, 3),
            *exchange_sems(n),
            *exchange_sems(n),
            *extra,
        ],
        compiler_params=pltpu.CompilerParams(
            collective_id=0, has_side_effects=True, vmem_limit_bytes=60 << 20
        ),
        name="front",
    )(rows, cotangent, picks, vec, qkv, first, out, second)


FFN_KINDS = (
    ("expand", 0, D // UNITS, ("x", "y"), False),
    ("contract", FF // UNITS // 3, FF // UNITS, ("y", "x"), False),
    ("contract", 0, FF // UNITS // 3, ("x", "y"), False),
    ("out", 0, D // UNITS, ("x", "y"), False),
)
QKV_KINDS = (
    (0, ("x", "y"), False),
    (1, ("y", "x"), False),
    (2, ("x", "y"), True),
)
QKV_UNITS = 3 * UNITS


def finish_kernel(n, nz, *refs):
    heads, rows_ref, w_hbm, d_sum1_ref, dw1, dw2, dwo, small_ref, ffn_ref = refs[:9]
    d_tokens_ref, qkv_out, out_out, expand_out, contract_out, vec_out = refs[9:15]
    inbox, proj, w_ref, own1, own2, owno, ownq, value, land = refs[15:24]
    load_sem, vsend, vrecv = refs[24:27]
    sems_in = refs[27:30]
    rest = list(refs[30:])
    place_row = lax.axis_index("seq")
    head, mine = owned(place_row, n)
    me = place(nz)

    loads = [
        pltpu.make_async_copy(src, dst, load_sem.at[i])
        for i, (src, dst) in enumerate(((dw1, own1), (dw2, own2), (dwo, owno), (w_hbm, w_ref)))
    ]
    for cp in loads:
        cp.start()
    bar = pltpu.get_barrier_semaphore()

    def greet(k, _):
        to = (place_row + 1 + k) % n
        pl.semaphore_signal(bar, inc=1, device_id=(me["y"], to), device_id_type=MESH)
        return 0

    lax.fori_loop(0, n - 1, greet, 0)
    pl.semaphore_signal(bar, inc=1, device_id=(1 - me["y"], place_row), device_id_type=MESH)
    pl.semaphore_wait(bar, n)

    start_from_owners(n, place_row, head, mine, heads, inbox, sems_in)
    pending = []
    core = me["c"]

    def take(count):
        out = rest[:count]
        del rest[:count]
        return out

    sources = {"expand": (dw1, own1), "contract": (dw2, own2), "out": (dwo, owno)}
    targets = {"expand": expand_out, "contract": contract_out, "out": out_out}

    def ffn_item(kind, lo, hi, links, z_first):
        far, near = sources[kind]
        whole = lo == 0 and hi == far.shape[1]

        def at(ref, t):
            return ref.at[t] if whole else ref.at[t, lo:hi]

        cols = far.shape[2] // 128
        return Reduction(
            nz,
            me,
            links,
            z_first,
            lambda p: at(near, p * 2 + core),
            lambda p: at(far, p * 2 + 1 - core),
            lambda srcs: add_flat(targets[kind], lo * cols, srcs),
            take(5),
            take(4),
            pending,
        )

    def qkv_item(j, links, z_first):
        return Reduction(
            nz,
            me,
            links,
            z_first,
            lambda p: ownq.at[(p * 2 + core) * 3 + j],
            lambda p: ownq.at[(p * 2 + 1 - core) * 3 + j],
            lambda srcs: add_flat(qkv_out, j * UNIT * (D // 128), srcs),
            take(5),
            take(4),
            pending,
        )

    ffn = [ffn_item(*k) for k in FFN_KINDS]
    qkv = [qkv_item(*k) for k in QKV_KINDS]

    def hand_all(items):
        for group in zip(*[i.hand_over() for i in items]):
            for f in group:
                f()

    def ordered(items):
        steps = [(w + 0.01 * i, f) for i, item in enumerate(items) for w, f in item.steps()]
        return sorted(steps, key=lambda s: s[0])

    hand_all(ffn)
    for cp in loads[:3]:
        cp.wait()
    ffn_steps = ordered(ffn)
    for w, f in ffn_steps:
        if w < 20:
            f()

    wait_from_owners(n, place_row, head, heads, inbox, sems_in)
    loads[3].wait()
    half = TOK_SEQ // 2
    for h in range(0, H, 2):
        lanes = slice(h * HD, (h + 2) * HD)
        k, v = unpack_pair(inbox[h, 0:TOK_SEQ, :], inbox[h + 1, 0:TOK_SEQ, :], (TOK_SEQ, 128))
        proj[1, :, lanes] = k.astype(jnp.bfloat16)
        proj[2, :, lanes] = v.astype(jnp.bfloat16)
        for t in range(BPD // 2):
            part = slice(TOK_SEQ + t * BLOCK, TOK_SEQ + (t + 1) * BLOCK)
            a, b = unpack_pair(inbox[h, part, :], inbox[h + 1, part, :], (BLOCK, 128))
            proj[0, 2 * t * BLOCK : (2 * t + 1) * BLOCK, lanes] = a.astype(jnp.bfloat16)
            proj[0, (2 * t + 1) * BLOCK : (2 * t + 2) * BLOCK, lanes] = b.astype(jnp.bfloat16)

    def weight_grad(e, _):
        grad = inner_rows(rows_ref[...], proj[e])
        ownq[pl.ds(e * UNITS, UNITS)] = grad.reshape(UNITS, UNIT, D).astype(jnp.bfloat16)
        return 0

    lax.fori_loop(0, 3, weight_grad, 0)
    hand_all(qkv)

    def add_rows(x):
        return jnp.sum(x.astype(jnp.float32), axis=0, keepdims=True)

    value[0, 0:1] = add_rows(proj[0])
    value[0, 1:2] = add_rows(proj[2])
    value[0, 2:8] = small_ref[0:6]
    for c in range(FF // D):
        value[0, 8 + c : 9 + c] = ffn_ref[:, c * D : (c + 1) * D]
    partners = [dict(me, c=1 - core), dict(me, x=1 - me["x"]), dict(me, y=1 - me["y"])]
    step = 1
    while step < nz:
        partners.append(dict(me, z=me["z"] + step - 2 * step * ((me["z"] // step) % 2)))
        step *= 2

    def vector_copy(i):
        return pltpu.make_async_remote_copy(
            src_ref=value.at[i],
            dst_ref=land.at[i],
            send_sem=vsend.at[i],
            recv_sem=vrecv.at[i],
            device_id=device(partners[i]),
            device_id_type=MESH,
        )

    vector_copy(0).start()
    for w, f in ffn_steps:
        if w >= 20:
            f()
    d_tokens = d_sum1_ref[...]
    for e in range(3):
        d_tokens = d_tokens + outer_cols(proj[e], as_matrix(w_ref[e * UNITS : (e + 1) * UNITS]))
    d_tokens_ref[...] = d_tokens
    stage = 0
    for w, f in ordered(qkv):
        f()
        if w > 3 + 2 * stage and stage < len(partners):
            vector_copy(stage).wait_recv()
            total = value[stage] + land[stage]
            stage += 1
            if stage < len(partners):
                value[stage] = total
                vector_copy(stage).start()
            else:
                vec_out[...] = total
    for i in range(len(partners)):
        vector_copy(i).wait_send()
    finish_from_owners(n, place_row, head, mine, heads, inbox, sems_in)
    for cp, cond in pending:
        if cond is None:
            cp.wait_send()
        else:
            pl.when(cond)(cp.wait_send)


def finish(heads, rows, qkv, d_sum1, d_expand, d_contract, d_out, small, d_ffn, nz):
    n = lax.axis_size("seq")
    low, full = jnp.bfloat16, jnp.float32
    flat = [(3 * UNIT * D // 128, 128), (UNIT * D // 128, 128)]
    flat += [(UNIT * FF // 128, 128)] * 2
    stages = 3 + (nz - 1).bit_length()
    extra = []
    for kind, lo, hi, links, z_first in FFN_KINDS:
        width = FF if kind == "expand" else D
        extra += Reduction.buffers(nz, (hi - lo, width), z_first)
        extra += Reduction.semaphores(nz, z_first)
    for j, links, z_first in QKV_KINDS:
        extra += Reduction.buffers(nz, (UNIT, D), z_first)
        extra += Reduction.semaphores(nz, z_first)
    return pl.pallas_call(
        functools.partial(finish_kernel, n, nz),
        out_shape=[jax.ShapeDtypeStruct(s, full) for s in [(TOK_SEQ, D)] + flat + [(16, D)]],
        in_specs=[ANY, VMEM, ANY, VMEM, ANY, ANY, ANY, VMEM, VMEM],
        out_specs=[VMEM] * 6,
        scratch_shapes=[
            pltpu.VMEM((H, MSG, 128), low),
            pltpu.VMEM((3, TOK_SEQ, D), low),
            pltpu.VMEM((QKV_UNITS, UNIT, D), low),
            pltpu.VMEM(d_expand.shape, low),
            pltpu.VMEM(d_contract.shape, low),
            pltpu.VMEM(d_out.shape, low),
            pltpu.VMEM((QKV_UNITS, UNIT, D), low),
            pltpu.VMEM((stages, 16, D), full),
            pltpu.VMEM((stages, 16, D), full),
            pltpu.SemaphoreType.DMA((4,)),
            pltpu.SemaphoreType.DMA((stages,)),
            pltpu.SemaphoreType.DMA((stages,)),
            *exchange_sems(n),
            *extra,
        ],
        compiler_params=pltpu.CompilerParams(
            collective_id=5, has_side_effects=True, vmem_limit_bytes=60 << 20
        ),
        name="finish",
    )(heads, rows, qkv, d_sum1, d_expand, d_contract, d_out, small, d_ffn)


def unpack_heads(parts):
    parts = parts.reshape(H, BPD // 2, BLOCK, 2, HD).transpose(1, 3, 2, 0, 4)
    return parts.reshape(TOK_SEQ, D)


def unpack_keys(parts):
    parts = parts.reshape(H, TOK_SEQ, 2, HD).transpose(2, 1, 0, 3)
    return parts.reshape(2, TOK_SEQ, D)


def on_device(
    tokens,
    qkv_weight,
    out_weight,
    expand_weight,
    contract_weight,
    bias_vectors,
    gain_vectors,
    ffn_bias,
    random_blocks,
    cotangent,
):
    shards = lax.axis_size("dp") * lax.axis_size("seq")
    me = lax.axis_index("dp") * lax.axis_size("seq") + lax.axis_index("seq")
    planes = kernel_planes()
    rows = tokens.reshape(TOK_SEQ, D)
    weights = (qkv_weight, expand_weight, out_weight, contract_weight)
    vectors = (bias_vectors, gain_vectors, ffn_bias)
    if planes:
        placed = [
            lax.dynamic_update_slice(
                jnp.zeros((v.size * shards,), jnp.float32), v.astype(jnp.float32), (me * v.size,)
            )
            for v in vectors
        ]
        qkv, first, out, second = [w.reshape(-1, 128) for w in weights]
    else:
        gather = functools.partial(lax.all_gather, axis_name=("dp", "seq"), axis=0, tiled=True)
        placed = [gather(v).astype(jnp.float32) for v in vectors]
        qkv, first, out, second = [gather(w) for w in weights]
        qkv = qkv.reshape(3 * UNITS, UNIT, D)
        first, out = first.reshape(UNITS, UNIT, FF), out.reshape(UNITS, UNIT, D)
        first = jnp.concatenate([first, out], axis=2)
        second = second.reshape(UNITS, FF // UNITS, D)
    vec = jnp.pad(jnp.concatenate(placed).reshape(-1, D), ((0, 4), (0, 0)))
    (
        result,
        d_sum1,
        kv,
        queries,
        picks,
        lse,
        d_heads,
        d_expand,
        d_contract,
        d_out,
        small,
        d_ffn,
        w_all,
    ) = front(
        rows, cotangent.reshape(TOK_SEQ, D), random_blocks, vec, qkv, first, out, second, planes
    )
    d_heads = attend_heads_back(kv, queries, picks, lse, d_heads)
    if planes:
        d_tokens, d_qkv, d_out, d_expand, d_contract, totals = finish(
            d_heads, rows, w_all, d_sum1, d_expand, d_contract, d_out, small, d_ffn, planes
        )
        vectors = (totals[0:6], totals[6:8], totals[8 : 8 + FF // D])
        vectors = [
            lax.dynamic_slice(v.reshape(-1), (me * (v.size // shards),), (v.size // shards,))
            for v in vectors
        ]
    else:
        d_heads = exchange(from_owners_kernel, H, d_heads, 4, "return_head_grads")
        d_query = unpack_heads(d_heads[:, TOK_SEQ:])
        d_pair = unpack_keys(d_heads[:, :TOK_SEQ])
        d_proj = jnp.concatenate([d_query[None], d_pair], axis=0)
        d_qkv = jnp.einsum("rd,erf->edf", rows, d_proj, preferred_element_type=jnp.float32)
        d_tokens = d_sum1 + jnp.einsum(
            "erf,edf->rd", d_proj, qkv.reshape(3, D, D), preferred_element_type=jnp.float32
        )
        d_bias_q = jnp.sum(d_query.astype(jnp.float32), axis=0)
        d_bias_v = jnp.sum(d_pair[1].astype(jnp.float32), axis=0)
        d_biases = jnp.concatenate([jnp.stack([d_bias_q, d_bias_v]), small[0:4]])
        *vectors, d_qkv, d_out, d_expand, d_contract = [
            lax.psum_scatter(
                g.astype(jnp.float32).reshape(-1),
                ("dp", "seq"),
                scatter_dimension=0,
                tiled=True,
            )
            for g in (d_biases, small[4:6], d_ffn, d_qkv, d_out, d_expand, d_contract)
        ]
    grads = [g.reshape(-1) for g in (d_qkv, d_out, d_expand, d_contract)]
    return (result[None], d_tokens[None], *grads, *vectors)


def solution(mesh):
    return jax.shard_map(
        on_device,
        mesh=mesh,
        in_specs=(
            P("dp", "seq", None),
            P(("dp", "seq")),
            P(("dp", "seq")),
            P(("dp", "seq")),
            P(("dp", "seq")),
            P(("dp", "seq")),
            P(("dp", "seq")),
            P(("dp", "seq")),
            P("dp", None, "seq", None),
            P("dp", "seq", None),
        ),
        out_specs=(
            P("dp", "seq", None),
            P("dp", "seq", None),
            P(("dp", "seq")),
            P(("dp", "seq")),
            P(("dp", "seq")),
            P(("dp", "seq")),
            P(("dp", "seq")),
            P(("dp", "seq")),
            P(("dp", "seq")),
        ),
        check_vma=False,
    )
```

```python
import functools

import jax
import jax.numpy as jnp
from jax import lax
from jax.experimental import pallas as pl
from jax.experimental.pallas import tpu as pltpu
from jax.sharding import PartitionSpec as P

MESH = pl.DeviceIdType.MESH

D = 768
FF = 3072
H = 12
HD = 64
BLOCK = 64
TOK_SEQ = 256
SEQ_GRP = 1
BPD = 4


norm_eps = 1e-12
masked_score = -1e30


def matmul(left, right):
    return jnp.dot(left, right, preferred_element_type=jnp.float32)


def inner_rows(left, right):
    return lax.dot_general(
        left, right, (((0,), (0,)), ((), ())), preferred_element_type=jnp.float32
    )


def outer_cols(left, right):
    return lax.dot_general(
        left, right, (((1,), (1,)), ((), ())), preferred_element_type=jnp.float32
    )


def normalize(value, gain, shift):
    mean = jnp.mean(value, axis=-1, keepdims=True)
    centred = value - mean
    inverse = lax.rsqrt(jnp.mean(centred * centred, axis=-1, keepdims=True) + norm_eps)
    normed = centred * inverse
    return (normed * gain + shift, normed, inverse)


def normalize_back(grad, normed, inverse, gain):
    scaled = grad * gain
    centred = scaled - jnp.mean(scaled, axis=-1, keepdims=True)
    return inverse * (centred - normed * jnp.mean(scaled * normed, axis=-1, keepdims=True))


def place(nz):
    y = lax.axis_index("dp")
    s = lax.axis_index("seq")
    return {"y": y, "z": s // 4, "x": (s // 2) % 2, "c": s % 2}

def device(p):
    return (p["y"], p["z"] * 4 + p["x"] * 2 + p["c"])

def chip(p, nz):
    return (p["y"] * nz + p["z"]) * 2 + p["x"]

def index(p, nz):
    return chip(p, nz) * 2 + p["c"]

def nearest(m, n, j):
    if n == 2:
        return m if j == 0 else 1 - m
    out = 0
    for i in range(n):
        rank = sorted(range(n), key=lambda s: (abs(s - i), s))
        out = jnp.where(m == i, rank[j], out)
    return out

def combine(dst, srcs):
    rows, cols = dst.shape
    step = min(cols, max(128, (24 * 1024 // rows) // 128 * 128))
    while cols % step:
        step -= 128
    def part(sl):
        total = srcs[0][:, sl].astype(jnp.float32)
        for s in srcs[1:]:
            total = total + s[:, sl].astype(jnp.float32)
        dst[:, sl] = total.astype(dst.dtype)
    if cols == step:
        part(slice(None))
    else:
        def body(i, _):
            part(pl.ds(pl.multiple_of(i * step, 128), step))
            return 0
        lax.fori_loop(0, cols // step, body, 0)

def owner(head, n):
    return head * n // H


def owned(place, n):
    head = (place * H + n - 1) // n
    return jnp.minimum(head, H - 1), jnp.logical_and(head < H, owner(head, n) == place)


def walk_to_owners(n, place, head, pairs, sems, act):
    row = lax.axis_index("dp")

    def body(k, _):
        h = (head + 1 + k) % H
        to = owner(h, n)
        for i, (src, dst) in enumerate(pairs):

            @pl.when(to != place)
            def _():
                act(
                    pltpu.make_async_remote_copy(
                        src_ref=src.at[h],
                        dst_ref=dst(place),
                        send_sem=sems[0].at[i, h],
                        recv_sem=sems[1].at[i, place],
                        device_id=(row, to),
                        device_id_type=MESH,
                    )
                )

        return 0

    lax.fori_loop(0, H, body, 0)


def finish_to_owners(n, place, head, pairs, sems):
    walk_to_owners(n, place, head, pairs, sems, lambda cp: cp.wait_send())


def send_to_owners(n, place, head, mine, pairs, sems, meanwhile, wait_sends=True):
    walk_to_owners(n, place, head, pairs, sems, lambda cp: cp.start())
    meanwhile()

    @pl.when(mine)
    def _():
        for i, (src, dst) in enumerate(pairs):
            cp = pltpu.make_async_copy(src.at[head], dst(place), sems[2].at[i])
            cp.start()
            cp.wait()

        def body(k, _):
            s = (place + 1 + k) % n
            for i, (src, dst) in enumerate(pairs):
                pltpu.make_async_remote_copy(
                    src_ref=src.at[0],
                    dst_ref=dst(s),
                    send_sem=sems[0].at[i, 0],
                    recv_sem=sems[1].at[i, s],
                    device_id=(lax.axis_index("dp"), place),
                    device_id_type=MESH,
                ).wait_recv()
            return 0

        lax.fori_loop(0, n - 1, body, 0)

    if wait_sends:
        finish_to_owners(n, place, head, pairs, sems)


def walk_from_owners(n, place, head, src, dst, sems, act):
    row = lax.axis_index("dp")

    def body(k, _):
        to = (place + 1 + k) % n
        act(
            pltpu.make_async_remote_copy(
                src_ref=src.at[to],
                dst_ref=dst.at[head],
                send_sem=sems[0].at[0, to],
                recv_sem=sems[1].at[0, head],
                device_id=(row, to),
                device_id_type=MESH,
            )
        )
        return 0

    lax.fori_loop(0, n - 1, body, 0)


def start_from_owners(n, place, head, mine, src, dst, sems):
    @pl.when(mine)
    def _():
        walk_from_owners(n, place, head, src, dst, sems, lambda cp: cp.start())
        cp = pltpu.make_async_copy(src.at[place], dst.at[head], sems[2].at[0])
        cp.start()
        cp.wait()


def wait_from_owners(n, place, head, src, dst, sems):
    def body(k, _):
        h = (head + k) % H

        @pl.when(owner(h, n) != place)
        def _():
            pltpu.make_async_remote_copy(
                src_ref=src.at[0],
                dst_ref=dst.at[h],
                send_sem=sems[0].at[0, 0],
                recv_sem=sems[1].at[0, h],
                device_id=(lax.axis_index("dp"), place),
                device_id_type=MESH,
            ).wait_recv()

        return 0

    lax.fori_loop(0, H, body, 0)


def finish_from_owners(n, place, head, mine, src, dst, sems):
    @pl.when(mine)
    def _():
        walk_from_owners(n, place, head, src, dst, sems, lambda cp: cp.wait_send())


def swap_halves(tile):
    return pltpu.roll(tile, HD, tile.ndim - 1)


def low_lanes(shape):
    return lax.broadcasted_iota(jnp.int32, shape, len(shape) - 1) < HD


def exchange_sems(n, pairs=1):
    return [
        pltpu.SemaphoreType.DMA((pairs, max(n, H))),
        pltpu.SemaphoreType.DMA((pairs, max(n, H))),
        pltpu.SemaphoreType.DMA((pairs,)),
    ]


ANY = pl.BlockSpec(memory_space=pl.ANY)
VMEM = pl.BlockSpec(memory_space=pltpu.VMEM)
SMEM = pl.BlockSpec(memory_space=pltpu.SMEM)
MSG = TOK_SEQ + TOK_SEQ // 2


def key_list(i, n, picks_ref):
    last = n * BPD - 1

    def of(b):
        s, r = b // BPD, b % BPD
        picked = [picks_ref[s, 0, r * 3 + j] for j in range(3)]
        return [jnp.maximum(b - 1, 0), b, jnp.minimum(b + 1, last), 0, last] + picked

    return [of(2 * i), of(2 * i + 1)]


def fill_pair(lists, kv_ref, vk_ref, keys, values):
    for j in range(8):
        a, b = lists[0][j], lists[1][j]
        to = slice(j * BLOCK, (j + 1) * BLOCK)
        keys[to, 0:HD] = kv_ref[a][:, 0:HD]
        keys[to, HD:128] = vk_ref[b][:, HD:128]
        values[to, 0:HD] = vk_ref[a][:, 0:HD]
        values[to, HD:128] = kv_ref[b][:, HD:128]


def two_blocks(tile):
    left = low_lanes(tile.shape)
    zero = jnp.zeros_like(tile)
    return jnp.concatenate([jnp.where(left, tile, zero), jnp.where(left, zero, tile)], axis=0)


def pair_scores(i, n, keys, query):
    scores = outer_cols(keys, query)
    left = low_lanes((BLOCK, 128))
    right = jnp.logical_not(left)
    end = n * BPD // 2 - 1
    hide_first = jnp.logical_and(left, i == 0)
    hide_last = jnp.logical_and(right, i == end)
    return jnp.concatenate(
        [
            jnp.where(hide_first, masked_score, scores[0:BLOCK]),
            scores[BLOCK : 2 * BLOCK],
            jnp.where(hide_last, masked_score, scores[2 * BLOCK : 3 * BLOCK]),
            scores[3 * BLOCK :],
        ],
        axis=0,
    )


def turn_pairs(n, kv_ref, vk_ref):
    def body(b, _):
        for t in range(BPD):
            tile = kv_ref[b * BPD + t].astype(jnp.float32)
            vk_ref[b * BPD + t] = swap_halves(tile).astype(jnp.bfloat16)
        return 0

    lax.fori_loop(0, n, body, 0)


def chain_table(n, place, picks_vmem, picks_smem, links_ref):
    none = PICKS * n
    lane = lax.broadcasted_iota(jnp.int32, (n, 128), 1)
    turn = (lax.broadcasted_iota(jnp.int32, (n, 128), 0) + 2 * n - place - 1) % n
    order = jnp.where(lane < PICKS, turn * PICKS + lane, -1)
    picks = picks_vmem[:, 0, :]
    blocks = lax.broadcasted_iota(jnp.int32, (8, 128), 1)

    def body(k, tables):
        before, final = tables
        s = (place + 1 + k) % n
        for j in range(PICKS):
            pick, e = picks_smem[s, 0, j], k * PICKS + j
            before = jnp.where(jnp.logical_and(picks == pick, order > e), e, before)
            final = jnp.where(blocks == pick, e, final)
        return before, final

    start = (jnp.full((n, 128), none, jnp.int32), jnp.full((8, 128), none, jnp.int32))
    before, final = lax.fori_loop(0, n, body, start)
    links_ref[0:n] = before
    links_ref[n : n + 8] = final


PICKS = 3 * BPD
UNITS = 32
WIDE = 768


def greet_row(n, place, mine):
    row = lax.axis_index("dp")
    bar = pltpu.get_barrier_semaphore()

    def body(s, _):
        there = owned(s, n)[1]

        @pl.when(jnp.logical_and(s != place, jnp.logical_or(mine, there)))
        def _():
            pl.semaphore_signal(bar, inc=1, device_id=(row, s), device_id_type=MESH)

        return 0

    lax.fori_loop(0, n, body, 0)
    pl.semaphore_wait(bar, jnp.where(mine, n - 1, H))


def unpack_pair(tiles, odd, shape):
    left = low_lanes(shape)
    a, b = tiles.astype(jnp.float32), odd.astype(jnp.float32)
    return (jnp.where(left, a, swap_halves(b)), jnp.where(left, swap_halves(a), b))


def add_flat(out_ref, base, srcs, width=None):
    rows, cols = srcs[0].shape
    width = width or cols
    for k in range(cols // 128):
        lanes = slice(k * 128, (k + 1) * 128)
        total = srcs[0][:, lanes].astype(jnp.float32)
        for s in srcs[1:]:
            total = total + s[:, lanes].astype(jnp.float32)
        out_ref[pl.ds(base + k, rows, stride=width // 128), :] = total


class Reduction:
    def __init__(self, nz, me, links, direct, own, give, emit, bufs, sems, pending):
        self.nz, self.me, self.links, self.direct = nz, me, links, direct
        self.own, self.give, self.emit = own, give, emit
        self.rc, self.ra, self.rb, self.below, self.above = bufs
        self.csend, self.crecv, self.send, self.recv = sems
        self.pending = pending

    @staticmethod
    def buffers(nz, slab):
        counts = (4 * nz, nz, 2 * nz, nz, nz)
        return [pltpu.VMEM((c,) + slab, jnp.bfloat16) for c in counts]

    @staticmethod
    def semaphores(nz):
        return [pltpu.SemaphoreType.DMA((c * nz,)) for c in (4, 4, 5, 5)]

    def start(self, src, dst, slot, to, cond=None, there=None):
        cp = pltpu.make_async_remote_copy(
            src_ref=src,
            dst_ref=dst,
            send_sem=self.send.at[slot],
            recv_sem=self.recv.at[slot if there is None else there],
            device_id=device(to),
            device_id_type=MESH,
        )
        if cond is None:
            cp.start()
        else:
            pl.when(cond)(cp.start)
        self.pending.append((cp, cond))

    def arrived(self, ref, sem):
        pltpu.make_async_remote_copy(
            src_ref=ref,
            dst_ref=ref,
            send_sem=self.send.at[0],
            recv_sem=sem,
            device_id=device(dict(self.me, c=1 - self.me["c"])),
            device_id_type=MESH,
        ).wait_recv()

    def flip(self, which, f):
        d = self.links[which]
        return 1 - self.me[d] if f else self.me[d]

    def piece(self, z, a, b):
        c = {self.links[0]: a, self.links[1]: b}
        return (c["y"] * self.nz + z) * 2 + c["x"]

    def across(self, which):
        d = self.links[which]
        return dict(self.me, **{d: 1 - self.me[d]})

    def hand_over(self):
        nz = self.nz
        zs = sorted(range(nz), key=lambda z: -abs(2 * z - nz + 1))
        order = [(z, fa, fb) for fb in (1, 0) for fa in (1, 0) for z in zs]

        def one(z, fa, fb):
            def run():
                p = self.piece(z, self.flip(0, fa), self.flip(1, fb))
                cp = pltpu.make_async_remote_copy(
                    src_ref=self.give(p),
                    dst_ref=self.rc.at[p],
                    send_sem=self.csend.at[p],
                    recv_sem=self.crecv.at[p],
                    device_id=device(dict(self.me, c=1 - self.me["c"])),
                    device_id_type=MESH,
                )
                cp.start()
                self.pending.append((cp, None))

            return run

        return [one(*o) for o in order]

    def mine(self, p):
        self.arrived(self.rc.at[p], self.crecv.at[p])
        return [self.own(p), self.rc.at[p]]

    def relay(self, z, p, srcs, bref, aref, sb, sa):
        nz, mz, acc = self.nz, self.me["z"], self.rc.at[p]
        if z > 0:

            @pl.when(mz == 0)
            def _():
                combine(acc, srcs)

            @pl.when(jnp.logical_and(mz > 0, mz < z))
            def _():
                self.arrived(bref, self.recv.at[sb])
                combine(acc, srcs + [bref])

            self.start(acc, bref, sb, dict(self.me, z=jnp.minimum(mz + 1, nz - 1)), mz < z)
        if z < nz - 1:

            @pl.when(mz == nz - 1)
            def _():
                combine(acc, srcs)

            @pl.when(jnp.logical_and(mz < nz - 1, mz > z))
            def _():
                self.arrived(aref, self.recv.at[sa])
                combine(acc, srcs + [aref])

            self.start(acc, aref, sa, dict(self.me, z=jnp.maximum(mz - 1, 0)), mz > z)

    def ends(self, z, bref, aref, sb, sa):
        out = []
        if z > 0:
            self.arrived(bref, self.recv.at[sb])
            out.append(bref)
        if z < self.nz - 1:
            self.arrived(aref, self.recv.at[sa])
            out.append(aref)
        return out

    def steps(self):
        nz, me = self.nz, self.me
        zs = sorted(range(nz), key=lambda z: -abs(2 * z - nz + 1))

        def along_b(z, fa):
            def run():
                a = self.flip(0, fa)
                p = self.piece(z, a, self.flip(1, 1))
                combine(self.rc.at[p], self.mine(p))
                s = z * 2 + a
                self.start(self.rc.at[p], self.rb.at[s], s, self.across(1))

            return run

        def along_a(z):
            def run():
                a = self.flip(0, 1)
                p = self.piece(z, a, self.flip(1, 0))
                s = z * 2 + a
                srcs = self.mine(p)
                self.arrived(self.rb.at[s], self.recv.at[s])
                combine(self.rc.at[p], srcs + [self.rb.at[s]])
                self.start(self.rc.at[p], self.ra.at[z], 2 * nz + z, self.across(0))

            return run

        def chain(z):
            def run():
                p = self.piece(z, self.flip(0, 0), self.flip(1, 0))
                s = z * 2 + self.flip(0, 0)
                srcs = self.mine(p)
                self.arrived(self.rb.at[s], self.recv.at[s])
                self.arrived(self.ra.at[z], self.recv.at[2 * nz + z])
                srcs += [self.rb.at[s], self.ra.at[z]]
                if self.direct:
                    mz = me["z"]

                    @pl.when(mz != z)
                    def _():
                        combine(self.rc.at[p], srcs)

                    to = dict(me, z=z)
                    self.start(
                        self.rc.at[p], self.below.at[mz], 3 * nz + z, to, mz != z, 3 * nz + mz
                    )
                    return
                bref, aref = self.below.at[z], self.above.at[z]
                self.relay(z, p, srcs, bref, aref, 3 * nz + z, 4 * nz + z)

            return run

        def last():
            for z in range(nz):

                @pl.when(me["z"] == z)
                def _():
                    p = self.piece(z, self.flip(0, 0), self.flip(1, 0))
                    s = z * 2 + self.flip(0, 0)
                    srcs = [self.own(p), self.rc.at[p], self.rb.at[s], self.ra.at[z]]
                    if self.direct:
                        for other in range(nz):
                            if other != z:
                                ref = self.below.at[other]
                                self.arrived(ref, self.recv.at[3 * nz + other])
                                srcs.append(ref)
                        self.emit(srcs)
                        return
                    bref, aref = self.below.at[z], self.above.at[z]
                    self.emit(srcs + self.ends(z, bref, aref, 3 * nz + z, 4 * nz + z))

        out = [(1 + i, along_b(z, 1)) for i, z in enumerate(zs)]
        out += [(5 + i, along_b(z, 0)) for i, z in enumerate(zs)]
        out += [(5.5 + i, along_a(z)) for i, z in enumerate(zs)]
        out += [(9.5 + i, chain(z)) for i, z in enumerate(zs)]
        return out + [(20, last)]


class Spread:
    def __init__(self, nz, me, order, at, sems, pending):
        self.nz, self.me, self.order, self.at = nz, me, order, at
        self.send, self.recv, self.csend, self.crecv = sems
        self.pending = pending

    @staticmethod
    def semaphores(nz):
        chips = 4 * nz
        return [pltpu.SemaphoreType.DMA((chips, 4))] + [pltpu.SemaphoreType.DMA((chips,))] * 3

    def copy(self, slot, send, recv, to):
        ref = self.at(slot)
        return pltpu.make_async_remote_copy(
            src_ref=ref,
            dst_ref=ref,
            send_sem=send,
            recv_sem=recv,
            device_id=device(to),
            device_id_type=MESH,
        )

    def start(self, cp, cond=None):
        if cond is None:
            cp.start()
        else:
            pl.when(cond)(cp.start)
        self.pending.append((cp, cond))

    def one(self, steps):
        nz, me = self.nz, self.me
        size = {"y": 2, "z": nz, "x": 2}
        own = not any(steps)

        def run():
            src = dict(me)
            for d, i in zip(self.order, steps):
                src[d] = nearest(me[d], size[d], i)
            c = chip(src, nz)
            slot = c * 2 + me["c"]
            if not own:
                self.copy(slot, self.send.at[c, 0], self.recv.at[c], me).wait_recv()
            stage = 2 if steps[2] else (1 if steps[1] else 0)
            for t in range(stage, 3):
                d = self.order[t]
                onward = t == stage and not own
                if d == "z":
                    up, down = me["z"] < nz - 1, me["z"] > 0
                    if onward:
                        up = jnp.logical_and(up, src["z"] <= me["z"])
                        down = jnp.logical_and(down, src["z"] >= me["z"])
                    above = dict(me, z=jnp.minimum(me["z"] + 1, nz - 1))
                    below = dict(me, z=jnp.maximum(me["z"] - 1, 0))
                    self.start(self.copy(slot, self.send.at[c, 0], self.recv.at[c], above), up)
                    self.start(self.copy(slot, self.send.at[c, 1], self.recv.at[c], below), down)
                elif not (onward and steps[t]):
                    way = 2 if d == "x" else 3
                    to = dict(me, **{d: 1 - me[d]})
                    self.start(self.copy(slot, self.send.at[c, way], self.recv.at[c], to))
            sibling = dict(me, c=1 - me["c"])
            self.start(self.copy(slot, self.csend.at[c], self.crecv.at[c], sibling))

        return run

    def steps(self):
        size = {"y": 2, "z": self.nz, "x": 2}
        n0, n1, n2 = (size[d] for d in self.order)
        return [
            (i0 + i1 + i2, self.one((i0, i1, i2)))
            for i2 in range(n2)
            for i1 in range(n1)
            for i0 in range(n0)
        ]

    def finish(self):
        def body(c, _):
            slot = c * 2 + 1 - self.me["c"]
            self.copy(slot, self.csend.at[c], self.crecv.at[c], self.me).wait_recv()
            return 0

        lax.fori_loop(0, 4 * self.nz, body, 0)


def run_in_order(items, low, high):
    steps = [(w, i, f) for i, item in enumerate(items) for w, f in item.steps()]
    for w, _, f in sorted(steps, key=lambda s: s[:2]):
        if low <= w < high:
            f()


def exchange_partners(me, nz):
    partners = [dict(me, **{d: 1 - me[d]}) for d in ("c", "x", "y")]
    step = 1
    while step < nz:
        partners.append(dict(me, z=me["z"] + step - 2 * step * ((me["z"] // step) % 2)))
        step *= 2
    return partners


def vector_copy(i, value, land, sems, partners):
    return pltpu.make_async_remote_copy(
        src_ref=value.at[i],
        dst_ref=land.at[i],
        send_sem=sems[0].at[i],
        recv_sem=sems[1].at[i],
        device_id=device(partners[i]),
        device_id_type=MESH,
    )


def greet_row_and_y(n, me, place_row):
    bar = pltpu.get_barrier_semaphore()

    def greet(k, _):
        to = (place_row + 1 + k) % n
        pl.semaphore_signal(bar, inc=1, device_id=(me["y"], to), device_id_type=MESH)
        return 0

    lax.fori_loop(0, n - 1, greet, 0)
    pl.semaphore_signal(bar, inc=1, device_id=(1 - me["y"], place_row), device_id_type=MESH)
    return lambda: pl.semaphore_wait(bar, n)


UNIT = D // UNITS
THIRD = FF // UNITS // 3
QKV_ORDERS = (("z", "x", "y"), ("z", "y", "x"), ("x", "y", "z"))
REST = (
    ("second", THIRD, FF // UNITS, ("z", "y", "x")),
    ("first", 0, UNIT, ("z", "x", "y")),
    ("second", 0, THIRD, ("z", "x", "y")),
)


def from_flat(flat, cols, rows):
    step = cols // 128
    return [flat[pl.ds(k, rows, stride=step), :] for k in range(step)]


def as_matrix(units):
    count, rows, cols = units.shape
    return units.astype(jnp.float32).reshape(count * rows, cols).astype(jnp.bfloat16)


def kernel_planes():
    seq = lax.axis_size("seq")
    if lax.axis_size("dp") != 2 or 2 * seq != UNITS or seq % 4:
        return 0
    return seq // 4


def front_kernel(n, nz, *refs):
    rows_ref, cot_ref, picks_ref, vec_in, qkv_in, first_in, out_in, second_in = refs[:8]
    (
        result_ref,
        d_sum1_ref,
        kv_hbm,
        q_hbm,
        picks_hbm,
        lse_ref,
        d_heads,
        dw1_hbm,
        dw2_hbm,
        dwo_hbm,
        small_ref,
        d_ffn_ref,
        w_hbm,
        links_hbm,
    ) = refs[8:22]
    (
        w_ref,
        first_ref,
        second_ref,
        flat,
        value,
        land,
        box_kv,
        box_q,
        kv_ref,
        q_ref,
        vk_ref,
        picks_smem,
        keys,
        values,
        attended,
        inbox,
        grad_box,
        slope_ref,
        active_ref,
        dw1_ref,
        dw2_ref,
        dwo_ref,
        mixed_ref,
        load_sem,
        store_sem,
        keep_sem,
        vsend,
        vrecv,
        links_ref,
        picks_vmem,
    ) = refs[22:52]
    sems_qkv, sems_in, sems_out = refs[52:55], refs[55:58], refs[58:61]
    rest = list(refs[61:])
    place_row = lax.axis_index("seq")
    head, mine = owned(place_row, n)
    pending = []

    if nz:
        me = place(nz)
        slot = index(me, nz)
        hold = greet_row_and_y(n, me, place_row)
        stages = 3 + (nz - 1).bit_length()

        def take():
            out = rest[:4]
            del rest[:4]
            return out

        def widen(src):
            count = src.shape[0]
            flat[0:count] = src[...].astype(jnp.float32)

        widen(qkv_in)
        for j in range(3):
            step = D // 128
            for k in range(step):
                col = flat[pl.ds(j * UNIT * step + k, UNIT, stride=step), :]
                w_ref[slot * 3 + j, :, k * 128 : (k + 1) * 128] = col.astype(jnp.bfloat16)
        value[0] = vec_in[...]
        hold()
        qkv_items = [
            Spread(nz, me, order, lambda s, j=j: w_ref.at[s * 3 + j], take(), pending)
            for j, order in enumerate(QKV_ORDERS)
        ]
        buffers = {"first": first_ref, "second": second_ref}

        def part(kind, lo, hi):
            ref = buffers[kind]
            if hi - lo == ref.shape[1]:
                return lambda s: ref.at[s]
            return lambda s: ref.at[s, lo:hi]

        rest_items = [
            Spread(nz, me, order, part(kind, lo, hi), take(), pending)
            for kind, lo, hi, order in REST
        ]
        partners = exchange_partners(me, nz)
        vsems = (vsend, vrecv)
        vector_copy(0, value, land, vsems, partners).start()
        run_in_order(qkv_items, 0, 1)
        for src, dst, at, cols, count in (
            (first_in, first_ref, 0, FF, UNIT),
            (out_in, first_ref, FF, D, UNIT),
            (second_in, second_ref, 0, D, FF // UNITS),
        ):
            widen(src)
            for k, col in enumerate(from_flat(flat, cols, count)):
                dst[slot, :, at + k * 128 : at + (k + 1) * 128] = col.astype(jnp.bfloat16)

        def vector_stage(i):
            vector_copy(i, value, land, vsems, partners).wait_recv()
            value[i + 1] = value[i] + land[i]
            if i + 1 < stages:
                vector_copy(i + 1, value, land, vsems, partners).start()

        for depth in range(1, nz + 2):
            vector_stage(min(depth - 1, stages)) if depth <= stages else None
            run_in_order(qkv_items, depth, depth + 1)
            if depth == 2:
                run_in_order(rest_items, 0, 1)
        for i in range(nz + 1, stages):
            vector_stage(i)
        for item in qkv_items:
            item.finish()
        vec = value.at[stages]
    else:
        greet_row(n, place_row, mine)
        loads = [
            pltpu.make_async_copy(src, dst, load_sem.at[i])
            for i, (src, dst) in enumerate(
                ((qkv_in, w_ref), (first_in, first_ref), (second_in, second_ref))
            )
        ]
        for cp in loads:
            cp.start()
        for cp in loads:
            cp.wait()
        vec = vec_in

    def rest_steps(low, high):
        if nz:
            run_in_order(rest_items, low, high)

    rows = rows_ref[...]
    left = low_lanes((TOK_SEQ, 128))
    left_q = low_lanes((BLOCK, 128))
    wide = 256
    for g in range(D // wide):
        cols = slice(g * wide, (g + 1) * wide)

        def project(e):
            return matmul(rows, as_matrix(w_ref[e * UNITS : (e + 1) * UNITS, :, cols]))

        q = (project(0) + vec[0:1, cols]) * HD ** (-0.5)
        k = project(1)
        v = project(2) + vec[1:2, cols]
        for p in range(wide // 128):
            h = (g * wide + p * 128) // HD
            lanes = slice(p * 128, (p + 1) * 128)
            kp, vp, qp = k[:, lanes], v[:, lanes], q[:, lanes]
            even, odd = jnp.where(left, kp, swap_halves(vp)), jnp.where(left, swap_halves(kp), vp)
            for t in range(BPD):
                part = slice(t * BLOCK, (t + 1) * BLOCK)
                box_kv[h, t] = even[part].astype(jnp.bfloat16)
                box_kv[h + 1, t] = odd[part].astype(jnp.bfloat16)
            turned = swap_halves(qp)
            for t in range(BPD // 2):
                a = slice(2 * t * BLOCK, (2 * t + 1) * BLOCK)
                b = slice((2 * t + 1) * BLOCK, (2 * t + 2) * BLOCK)
                to = slice(t * BLOCK, (t + 1) * BLOCK)
                box_q[h, to, :] = jnp.where(left_q, qp[a], turned[b]).astype(jnp.bfloat16)
                box_q[h + 1, to, :] = jnp.where(left_q, turned[a], qp[b]).astype(jnp.bfloat16)
    parcels = (
        (box_kv, lambda s: kv_ref.at[pl.ds(s * BPD, BPD)]),
        (box_q, lambda s: q_ref.at[s]),
        (picks_ref, lambda s: picks_hbm.at[s]),
    )
    send_to_owners(
        n,
        place_row,
        head,
        mine,
        parcels,
        sems_qkv,
        lambda: rest_steps(1, 3),
        wait_sends=False,
    )

    keep = (
        pltpu.make_async_copy(kv_ref, kv_hbm, keep_sem.at[0]),
        pltpu.make_async_copy(q_ref, q_hbm, keep_sem.at[3]),
    )
    keep_w = pltpu.make_async_copy(w_ref, w_hbm, keep_sem.at[2])
    keep_w.start()
    keep_links = pltpu.make_async_copy(links_ref, links_hbm, keep_sem.at[4])
    groups = 4

    @pl.when(mine)
    def _():
        for copy in keep:
            copy.start()
        copies = (
            pltpu.make_async_copy(picks_hbm, picks_smem, keep_sem.at[1]),
            pltpu.make_async_copy(picks_hbm, picks_vmem, keep_sem.at[5]),
        )
        for cp in copies:
            cp.start()
        for cp in copies:
            cp.wait()
        turn_pairs(n, kv_ref, vk_ref)
        chain_table(n, place_row, picks_vmem, picks_smem, links_ref)
        keep_links.start()

    def attend_some(k, _):
        s = (place_row + 1 + k) % n
        for t in range(BPD // 2):
            i = s * (BPD // 2) + t
            fill_pair(key_list(i, n, picks_smem), kv_ref, vk_ref, keys.at[t], values.at[t])
        for t in range(BPD // 2):
            i = s * (BPD // 2) + t
            part = slice(t * BLOCK, (t + 1) * BLOCK)
            query = two_blocks(q_ref[s, part, :])
            scores = pair_scores(i, n, keys[t], query)
            top = jnp.max(scores, axis=0, keepdims=True)
            weights = jnp.exp(scores - top)
            total = jnp.sum(weights, axis=0, keepdims=True)
            probs = (weights * (1.0 / total)).astype(jnp.bfloat16)
            full = inner_rows(probs, values[t])
            attended[s, part, :] = jnp.where(left_q, full[:BLOCK], full[BLOCK:]).astype(
                jnp.bfloat16
            )
            lse_ref[i] = top + jnp.log(total)

        @pl.when(s != place_row)
        def _():
            pltpu.make_async_remote_copy(
                src_ref=attended.at[s],
                dst_ref=inbox.at[head],
                send_sem=sems_in[0].at[0, s],
                recv_sem=sems_in[1].at[0, head],
                device_id=(lax.axis_index("dp"), s),
                device_id_type=MESH,
            ).start()

        return 0

    for g in range(groups):

        @pl.when(mine)
        def _():
            lax.fori_loop(g * (n // groups), (g + 1) * (n // groups), attend_some, 0)

        rest_steps(3 + g, 4 + g if g < groups - 1 else 99)

    @pl.when(mine)
    def _():
        cp = pltpu.make_async_copy(attended.at[place_row], inbox.at[head], sems_in[2].at[0])
        cp.start()
        cp.wait()

    if nz:
        for item in rest_items:
            item.finish()
    wait_from_owners(n, place_row, head, attended, inbox, sems_in)

    for h in range(0, H, 2):
        for t in range(BPD // 2):
            part = slice(t * BLOCK, (t + 1) * BLOCK)
            a, b = unpack_pair(inbox[h, part, :], inbox[h + 1, part, :], (BLOCK, 128))
            lanes = slice(h * HD, (h + 2) * HD)
            mixed_ref[2 * t * BLOCK : (2 * t + 1) * BLOCK, lanes] = a.astype(jnp.bfloat16)
            mixed_ref[(2 * t + 1) * BLOCK : (2 * t + 2) * BLOCK, lanes] = b.astype(jnp.bfloat16)
    out_w = as_matrix(first_ref[:, :, FF : FF + D])
    hidden1 = rows_ref[...].astype(jnp.float32) + matmul(mixed_ref[...], out_w) + vec[2:3]
    normed_out1, normed1, inverse1 = normalize(hidden1, vec[6:7], vec[3:4])
    lowered = normed_out1.astype(jnp.bfloat16)
    per = UNITS * WIDE // FF

    def second_rows(c):
        return second_ref[pl.ds(c * per, per)].reshape(WIDE, D)

    def up_step(c, hidden):
        cols = pl.ds(pl.multiple_of(c * WIDE, WIDE), WIDE)
        up = matmul(lowered, as_matrix(first_ref[:, :, cols])) + vec[pl.ds(8 + c, 1)]
        square = up * up
        inner = (2 / jnp.pi) ** 0.5 * (up + 0.044715 * up * square)
        curve = jnp.tanh(inner)
        active = (0.5 * up * (1 + curve)).astype(jnp.bfloat16)
        slope_ref[:, cols] = 0.5 * (1 + curve) + 0.5 * up * (1 - curve * curve) * (
            (2 / jnp.pi) ** 0.5 * (1 + 3 * 0.044715 * square)
        )
        active_ref[:, cols] = active
        return hidden + matmul(active, second_rows(c))

    hidden2 = lax.fori_loop(0, FF // WIDE, up_step, normed_out1 + vec[4:5])
    result, normed2, inverse2 = normalize(hidden2, vec[7:8], vec[5:6])
    result_ref[...] = result
    grad = cot_ref[...].astype(jnp.float32)
    d_sum2 = normalize_back(grad, normed2, inverse2, vec[7:8])
    d_down = d_sum2.astype(jnp.bfloat16)

    def add_rows(x):
        return jnp.sum(x, axis=0, keepdims=True)

    small_ref[2:3] = add_rows(d_down.astype(jnp.float32))
    small_ref[3:4] = add_rows(grad)
    small_ref[5:6] = add_rows(grad * normed2)

    def stores(c):
        cols = pl.ds(pl.multiple_of(c * WIDE, WIDE), WIDE)
        slabs = pl.ds(c * per, per)
        return (
            pltpu.make_async_copy(dw1_ref.at[:, :, cols], dw1_hbm.at[:, :, cols], store_sem.at[0, c]),
            pltpu.make_async_copy(dw2_ref.at[slabs], dw2_hbm.at[slabs], store_sem.at[1, c]),
        )

    def back_step(c, d_norm1):
        cols = pl.ds(pl.multiple_of(c * WIDE, WIDE), WIDE)
        d_active = outer_cols(d_down, second_rows(c))
        d_up = (d_active * slope_ref[:, cols]).astype(jnp.bfloat16)
        d_ffn_ref[:, cols] = add_rows(d_up.astype(jnp.float32))
        dw2 = inner_rows(active_ref[:, cols], d_down)
        dw2_ref[pl.ds(c * per, per)] = dw2.reshape(per, FF // UNITS, D).astype(jnp.bfloat16)
        dw1 = inner_rows(lowered, d_up)
        dw1_ref[:, :, cols] = dw1.reshape(UNITS, UNIT, WIDE).astype(jnp.bfloat16)
        for cp in stores(c):
            cp.start()
        return d_norm1 + outer_cols(d_up, as_matrix(first_ref[:, :, cols]))

    d_norm1 = lax.fori_loop(0, FF // WIDE, back_step, d_sum2)
    small_ref[1:2] = add_rows(d_norm1)
    small_ref[4:5] = add_rows(d_norm1 * normed1)
    d_sum1 = normalize_back(d_norm1, normed1, inverse1, vec[6:7])
    d_sum1_ref[...] = d_sum1
    d_attn = d_sum1.astype(jnp.bfloat16)
    small_ref[0:1] = add_rows(d_attn.astype(jnp.float32))
    d_mixed = outer_cols(d_attn, as_matrix(first_ref[:, :, FF : FF + D]))
    for h in range(0, H, 2):
        for t in range(BPD // 2):
            part = slice(t * BLOCK, (t + 1) * BLOCK)
            lanes = slice(h * HD, (h + 2) * HD)
            a, b = unpack_pair(
                d_mixed[2 * t * BLOCK : (2 * t + 1) * BLOCK, lanes],
                d_mixed[(2 * t + 1) * BLOCK : (2 * t + 2) * BLOCK, lanes],
                (BLOCK, 128),
            )
            grad_box[h, part, :] = a.astype(jnp.bfloat16)
            grad_box[h + 1, part, :] = b.astype(jnp.bfloat16)

    store_out = pltpu.make_async_copy(dwo_ref, dwo_hbm, load_sem.at[0])

    def late():
        dwo = inner_rows(mixed_ref[...], d_attn).reshape(UNITS, UNIT, D)
        dwo_ref[...] = dwo.astype(jnp.bfloat16)
        store_out.start()

    send_to_owners(n, place_row, head, mine, ((grad_box, lambda s: d_heads.at[s]),), sems_out, late)
    store_out.wait()

    def drain(c, _):
        for cp in stores(c):
            cp.wait()
        return 0

    lax.fori_loop(0, FF // WIDE, drain, 0)

    @pl.when(mine)
    def _():
        for copy in keep:
            copy.wait()
        keep_links.wait()

    keep_w.wait()
    finish_from_owners(n, place_row, head, mine, attended, inbox, sems_in)
    finish_to_owners(n, place_row, head, parcels, sems_qkv)
    if nz:
        for i in range(stages):
            vector_copy(i, value, land, vsems, partners).wait_send()
    for cp, cond in pending:
        if cond is None:
            cp.wait_send()
        else:
            pl.when(cond)(cp.wait_send)


def front(rows, cotangent, picks, vec, qkv, first, out, second, nz):
    n = lax.axis_size("seq")
    low, full = jnp.bfloat16, jnp.float32
    picks = jnp.pad(picks.reshape(H, 1, BPD * 3), ((0, 0), (0, 7), (0, 128 - BPD * 3)))
    part = (TOK_SEQ // 2, 128)
    pairs = n * BPD // 2
    units = [(UNITS, UNIT, FF), (UNITS, FF // UNITS, D), (UNITS, UNIT, D)]
    shapes = [((TOK_SEQ, D), full), ((TOK_SEQ, D), full)]
    shapes += [((n * BPD, BLOCK, 128), low), ((n,) + part, low)]
    shapes += [((n, 8, 128), jnp.int32), ((pairs, 1, 128), full), ((n,) + part, low)]
    shapes += [(u, low) for u in units] + [((8, D), full), ((1, FF), full)]
    shapes += [((3 * UNITS, UNIT, D), low), ((n + 8, 128), jnp.int32)]
    stages = 3 + (max(nz, 1) - 1).bit_length()
    where = VMEM if nz else ANY
    extra = []
    for _ in range(6 if nz else 0):
        extra += Spread.semaphores(nz)
    return pl.pallas_call(
        functools.partial(front_kernel, n, nz),
        out_shape=[jax.ShapeDtypeStruct(s, d) for s, d in shapes],
        in_specs=[VMEM, VMEM, ANY, VMEM, where, where, where, where],
        out_specs=[VMEM, VMEM, ANY, ANY, ANY, VMEM, ANY, ANY, ANY, ANY, VMEM, VMEM, ANY, ANY],
        scratch_shapes=[
            pltpu.VMEM((3 * UNITS, UNIT, D), low),
            pltpu.VMEM((UNITS, UNIT, FF + D), low),
            pltpu.VMEM((UNITS, FF // UNITS, D), low),
            pltpu.VMEM((UNIT * FF // 128, 128), full),
            pltpu.VMEM((stages + 1, 16, D), full),
            pltpu.VMEM((stages, 16, D), full),
            pltpu.VMEM((H, BPD, BLOCK, 128), low),
            pltpu.VMEM((H,) + part, low),
            pltpu.VMEM((n * BPD, BLOCK, 128), low),
            pltpu.VMEM((n,) + part, low),
            pltpu.VMEM((n * BPD, BLOCK, 128), low),
            pltpu.SMEM((n, 8, 128), jnp.int32),
            pltpu.VMEM((BPD // 2, 8 * BLOCK, 128), low),
            pltpu.VMEM((BPD // 2, 8 * BLOCK, 128), low),
            pltpu.VMEM((n,) + part, low),
            pltpu.VMEM((H,) + part, low),
            pltpu.VMEM((H,) + part, low),
            pltpu.VMEM((TOK_SEQ, FF), full),
            pltpu.VMEM((TOK_SEQ, FF), low),
            *[pltpu.VMEM(u, low) for u in units],
            pltpu.VMEM((TOK_SEQ, D), low),
            pltpu.SemaphoreType.DMA((3,)),
            pltpu.SemaphoreType.DMA((2, FF // WIDE)),
            pltpu.SemaphoreType.DMA((6,)),
            pltpu.SemaphoreType.DMA((stages,)),
            pltpu.SemaphoreType.DMA((stages,)),
            pltpu.VMEM((n + 8, 128), jnp.int32),
            pltpu.VMEM((n, 8, 128), jnp.int32),
            *exchange_sems(n, 3),
            *exchange_sems(n),
            *exchange_sems(n),
            *extra,
        ],
        compiler_params=pltpu.CompilerParams(
            collective_id=0, has_side_effects=True, vmem_limit_bytes=60 << 20
        ),
        name="front",
    )(rows, cotangent, picks, vec, qkv, first, out, second)


FFN_KINDS = (
    ("expand", 0, UNIT, ("x", "y")),
    ("contract", THIRD, FF // UNITS, ("y", "x")),
    ("contract", 0, THIRD, ("x", "y")),
    ("out", 0, UNIT, ("x", "y")),
)
QKV_KINDS = (
    (0, 0, D, ("x", "y")),
    (1, 0, D, ("y", "x")),
    (2, 0, D // 2, ("x", "y")),
    (2, D // 2, D, ("y", "x")),
)
QKV_UNITS = 3 * UNITS


def send_one(sems, src, dst, head, to):
    return pltpu.make_async_remote_copy(
        src_ref=src.at[to],
        dst_ref=dst.at[head],
        send_sem=sems[0].at[0, to],
        recv_sem=sems[1].at[0, head],
        device_id=(lax.axis_index("dp"), to),
        device_id_type=MESH,
    )


def back_kernel(n, nz, *refs):
    kv_ref, q_ref, picks_ref, links_ref, lse_ref, grad_ref = refs[:6]
    rows_ref, w_hbm, d_sum1_ref, small_ref, ffn_ref, dw1, dw2, dwo = refs[6:14]
    d_tokens_ref, vec_out = refs[14:16]
    outs = refs[16 : 20 if nz else 17]
    rest = list(refs[20 if nz else 17 :])
    vk_ref, keys, values, acc, out_q, out_kv, inbox_q, inbox_kv, proj, w_ref, ownq = rest[:11]
    value, land, load_sem, vsend, vrecv = rest[11:16]
    sems_q, sems_kv = rest[16:19], rest[19:22]
    own1, own2, owno = rest[22:25] if nz else (None, None, None)
    rest = rest[25:]
    place_row = lax.axis_index("seq")
    head, mine = owned(place_row, n)
    blocks, none = n * BPD, n * BPD + n * PICKS
    pending = []

    load_w = pltpu.make_async_copy(w_hbm, w_ref, load_sem.at[0])
    load_w.start()
    if nz:
        me = place(nz)
        core = me["c"]
        loads = [
            pltpu.make_async_copy(src, dst, load_sem.at[1 + i])
            for i, (src, dst) in enumerate(((dw1, own1), (dw2, own2), (dwo, owno)))
        ]
        for cp in loads:
            cp.start()
        hold = greet_row_and_y(n, me, place_row)
    else:
        greet_row(n, place_row, mine)

    @pl.when(mine)
    def _():
        turn_pairs(n, kv_ref, vk_ref)

        def clear(b, _):
            acc[b] = jnp.zeros((BLOCK, 128), jnp.float32)
            return 0

        lax.fori_loop(0, blocks, clear, 0)
        clear(none, 0)

    def take(count):
        out = rest[:count]
        del rest[:count]
        return out

    def ffn_item(kind, lo, hi, links):
        far, near = {"expand": (dw1, own1), "contract": (dw2, own2), "out": (dwo, owno)}[kind]
        target = outs[("out", "expand", "contract").index(kind) + 1]
        whole = hi - lo == far.shape[1]

        def at(ref, t):
            return ref.at[t] if whole else ref.at[t, lo:hi]

        return Reduction(
            nz,
            me,
            links,
            False,
            lambda p: at(near, p * 2 + core),
            lambda p: at(far, p * 2 + 1 - core),
            lambda srcs: add_flat(target, lo * (far.shape[2] // 128), srcs),
            take(5),
            take(4),
            pending,
        )

    def qkv_item(j, lo, hi, links):
        def at(t):
            ref = ownq.at[t * 3 + j]
            return ref if hi - lo == D else ref.at[:, lo:hi]

        return Reduction(
            nz,
            me,
            links,
            True,
            lambda p: at(p * 2 + core),
            lambda p: at(p * 2 + 1 - core),
            lambda srcs: add_flat(outs[0], (j * UNIT * D + lo) // 128, srcs, D),
            take(5),
            take(4),
            pending,
        )

    def hand_all(items):
        for group in zip(*[i.hand_over() for i in items]):
            for f in group:
                f()

    def ordered(items):
        steps = [(w + 0.01 * i, f) for i, item in enumerate(items) for w, f in item.steps()]
        return sorted(steps, key=lambda s: s[0])

    ffn_steps = []
    if nz:
        ffn = [ffn_item(*k) for k in FFN_KINDS]
        qkv = [qkv_item(*k) for k in QKV_KINDS]
        ffn_steps = ordered(ffn)
        hold()
        hand_all(ffn)
        for cp in loads:
            cp.wait()

    def ffn_run(low, high, whole_only=False):
        for w, f in ffn_steps:
            if low <= w < high and not (whole_only and w % 1 >= 0.5):
                f()

    left = low_lanes((BLOCK, 128))
    both = range(BPD // 2)

    def attend_some(k, _):
        s = (place_row + 1 + k) % n
        lists = [key_list(s * (BPD // 2) + t, n, picks_ref) for t in both]
        for t in both:
            fill_pair(lists[t], kv_ref, vk_ref, keys.at[t], values.at[t])
        parts = []
        for t in both:
            i = s * (BPD // 2) + t
            part = slice(t * BLOCK, (t + 1) * BLOCK)
            query = two_blocks(q_ref[s, part, :])
            grad = two_blocks(grad_ref[s, part, :])
            probs = jnp.exp(pair_scores(i, n, keys[t], query) - lse_ref[i])
            d_probs = outer_cols(values[t], grad)
            rows = jnp.sum(probs * d_probs, axis=0, keepdims=True)
            d_scores = (probs * (d_probs - rows)).astype(jnp.bfloat16)
            d_values = matmul(probs.astype(jnp.bfloat16), grad)
            d_keys = matmul(d_scores, query)
            full = inner_rows(d_scores, keys[t]) * HD ** (-0.5)
            out_q[s, part, :] = jnp.where(left, full[:BLOCK], full[BLOCK:]).astype(jnp.bfloat16)
            parts.append((d_keys, d_values))

        @pl.when(s != place_row)
        def _():
            send_one(sems_q, out_q, inbox_q, head, s).start()

        for t in both:
            tiles = []
            for j in range(8):
                part = slice(j * BLOCK, (j + 1) * BLOCK)
                dk, dv = parts[t][0][part], parts[t][1][part]
                a = jnp.where(left, dk, swap_halves(dv))
                b = jnp.where(left, swap_halves(dk), dv)
                tiles.append((a, b))
            a = (s * (BPD // 2) + t) * 2
            acc[jnp.maximum(a - 1, 0)] += tiles[0][0]
            acc[a] += tiles[1][0] + tiles[0][1]
            acc[a + 1] += tiles[2][0] + tiles[1][1]
            acc[jnp.minimum(a + 2, blocks - 1)] += tiles[2][1]
            acc[0] += tiles[3][0] + tiles[3][1]
            acc[blocks - 1] += tiles[4][0] + tiles[4][1]
            for u in range(2):
                for j in range(3):
                    e = (2 * t + u) * 3 + j
                    acc[blocks + k * PICKS + e] = tiles[5 + j][u] + acc[blocks + links_ref[s, e]]
        return 0

    groups = 4
    for g in range(groups):

        @pl.when(mine)
        def _():
            lax.fori_loop(g * (n // groups), (g + 1) * (n // groups), attend_some, 0)

        if g < 2:
            ffn_run(4 * g + 1, 4 * g + 5, True)

    @pl.when(mine)
    def _():
        def close(k, _):
            s = (place_row + 1 + k) % n
            for t in range(BPD):
                b = s * BPD + t
                total = acc[b] + acc[blocks + links_ref[n, b]]
                out_kv[s, t * BLOCK : (t + 1) * BLOCK, :] = total.astype(jnp.bfloat16)

            @pl.when(s != place_row)
            def _():
                send_one(sems_kv, out_kv, inbox_kv, head, s).start()

            return 0

        lax.fori_loop(0, n, close, 0)
        copies = (
            pltpu.make_async_copy(out_q.at[place_row], inbox_q.at[head], sems_q[2].at[0]),
            pltpu.make_async_copy(out_kv.at[place_row], inbox_kv.at[head], sems_kv[2].at[0]),
        )
        for cp in copies:
            cp.start()
        for cp in copies:
            cp.wait()

    for w, f in ffn_steps:
        if 5 < w < 20 and (w % 1 >= 0.5 or w > 9):
            f()

    wait_from_owners(n, place_row, head, out_q, inbox_q, sems_q)
    wait_from_owners(n, place_row, head, out_kv, inbox_kv, sems_kv)
    for h in range(0, H, 2):
        lanes = slice(h * HD, (h + 2) * HD)
        k, v = unpack_pair(inbox_kv[h], inbox_kv[h + 1], (TOK_SEQ, 128))
        proj[1, :, lanes] = k.astype(jnp.bfloat16)
        proj[2, :, lanes] = v.astype(jnp.bfloat16)
        for t in both:
            part = slice(t * BLOCK, (t + 1) * BLOCK)
            a, b = unpack_pair(inbox_q[h, part, :], inbox_q[h + 1, part, :], (BLOCK, 128))
            proj[0, 2 * t * BLOCK : (2 * t + 1) * BLOCK, lanes] = a.astype(jnp.bfloat16)
            proj[0, (2 * t + 1) * BLOCK : (2 * t + 2) * BLOCK, lanes] = b.astype(jnp.bfloat16)

    def weight_grad(e, _):
        grad = inner_rows(rows_ref[...], proj[e])
        ownq[pl.ds(e * UNITS, UNITS)] = grad.reshape(UNITS, UNIT, D).astype(jnp.bfloat16)
        return 0

    lax.fori_loop(0, 3, weight_grad, 0)
    if nz:
        hand_all(qkv)

    def add_rows(x):
        return jnp.sum(x.astype(jnp.float32), axis=0, keepdims=True)

    value[0, 0:1] = add_rows(proj[0])
    value[0, 1:2] = add_rows(proj[2])
    value[0, 2:8] = small_ref[0:6]
    for c in range(FF // D):
        value[0, 8 + c : 9 + c] = ffn_ref[:, c * D : (c + 1) * D]
    partners = exchange_partners(me, nz) if nz else []
    vsems = (vsend, vrecv)
    if nz:
        vector_copy(0, value, land, vsems, partners).start()
        ffn_run(20, 99)
    load_w.wait()
    d_tokens = d_sum1_ref[...]
    for e in range(3):
        d_tokens = d_tokens + outer_cols(proj[e], as_matrix(w_ref[e * UNITS : (e + 1) * UNITS]))
    d_tokens_ref[...] = d_tokens
    stage = 0
    for w, f in ordered(qkv) if nz else ():
        f()
        if w > 3 + 2 * stage and stage < len(partners):
            vector_copy(stage, value, land, vsems, partners).wait_recv()
            total = value[stage] + land[stage]
            stage += 1
            if stage < len(partners):
                value[stage] = total
                vector_copy(stage, value, land, vsems, partners).start()
            else:
                vec_out[...] = total
    if not nz:
        vec_out[...] = value[0]
        outs[0][...] = ownq[...]
    for i in range(len(partners)):
        vector_copy(i, value, land, vsems, partners).wait_send()
    finish_from_owners(n, place_row, head, mine, out_q, inbox_q, sems_q)
    finish_from_owners(n, place_row, head, mine, out_kv, inbox_kv, sems_kv)
    for cp, cond in pending:
        if cond is None:
            cp.wait_send()
        else:
            pl.when(cond)(cp.wait_send)


def back(heads, local, weight_grads, nz):
    n = lax.axis_size("seq")
    low, full = jnp.bfloat16, jnp.float32
    rows, w_all, d_sum1, small, d_ffn = local
    outs = [((TOK_SEQ, D), full), ((16, D), full)]
    if nz:
        outs += [((3 * UNIT * D // 128, 128), full), ((UNIT * D // 128, 128), full)]
        outs += [((UNIT * FF // 128, 128), full)] * 2
    else:
        outs += [((QKV_UNITS, UNIT, D), low)]
    stages = 3 + (max(nz, 1) - 1).bit_length()
    part = (TOK_SEQ // 2, 128)
    extra = [pltpu.VMEM(g.shape, low) for g in weight_grads] if nz else []
    slabs = [(hi - lo, FF if kind == "expand" else D) for kind, lo, hi, _ in FFN_KINDS]
    slabs += [(UNIT, hi - lo) for _, lo, hi, _ in QKV_KINDS]
    for slab in slabs if nz else ():
        extra += Reduction.buffers(nz, slab)
        extra += Reduction.semaphores(nz)
    return pl.pallas_call(
        functools.partial(back_kernel, n, nz),
        out_shape=[jax.ShapeDtypeStruct(s, d) for s, d in outs],
        in_specs=[VMEM, VMEM, SMEM, SMEM, VMEM, VMEM]
        + [VMEM, ANY, VMEM, VMEM, VMEM, ANY, ANY, ANY],
        out_specs=[VMEM] * len(outs),
        scratch_shapes=[
            pltpu.VMEM((n * BPD, BLOCK, 128), low),
            pltpu.VMEM((BPD // 2, 8 * BLOCK, 128), low),
            pltpu.VMEM((BPD // 2, 8 * BLOCK, 128), low),
            pltpu.VMEM((n * (BPD + PICKS) + 1, BLOCK, 128), full),
            pltpu.VMEM((n,) + part, low),
            pltpu.VMEM((n, TOK_SEQ, 128), low),
            pltpu.VMEM((H,) + part, low),
            pltpu.VMEM((H, TOK_SEQ, 128), low),
            pltpu.VMEM((3, TOK_SEQ, D), low),
            pltpu.VMEM((QKV_UNITS, UNIT, D), low),
            pltpu.VMEM((QKV_UNITS, UNIT, D), low),
            pltpu.VMEM((stages, 16, D), full),
            pltpu.VMEM((stages, 16, D), full),
            pltpu.SemaphoreType.DMA((4,)),
            pltpu.SemaphoreType.DMA((stages,)),
            pltpu.SemaphoreType.DMA((stages,)),
            *exchange_sems(n),
            *exchange_sems(n),
            *extra,
        ],
        compiler_params=pltpu.CompilerParams(
            collective_id=5, has_side_effects=True, vmem_limit_bytes=61 << 20
        ),
        name="back",
    )(*heads, *local, *weight_grads)


def on_device(
    tokens,
    qkv_weight,
    out_weight,
    expand_weight,
    contract_weight,
    bias_vectors,
    gain_vectors,
    ffn_bias,
    random_blocks,
    cotangent,
):
    shards = lax.axis_size("dp") * lax.axis_size("seq")
    me = lax.axis_index("dp") * lax.axis_size("seq") + lax.axis_index("seq")
    planes = kernel_planes()
    rows = tokens.reshape(TOK_SEQ, D)
    weights = (qkv_weight, expand_weight, out_weight, contract_weight)
    vectors = (bias_vectors, gain_vectors, ffn_bias)
    if planes:
        placed = [
            lax.dynamic_update_slice(
                jnp.zeros((v.size * shards,), jnp.float32), v.astype(jnp.float32), (me * v.size,)
            )
            for v in vectors
        ]
        qkv, first, out, second = [w.reshape(-1, 128) for w in weights]
    else:
        gather = functools.partial(lax.all_gather, axis_name=("dp", "seq"), axis=0, tiled=True)
        placed = [gather(v).astype(jnp.float32) for v in vectors]
        qkv, first, out, second = [gather(w) for w in weights]
        qkv = qkv.reshape(3 * UNITS, UNIT, D)
        first, out = first.reshape(UNITS, UNIT, FF), out.reshape(UNITS, UNIT, D)
        first = jnp.concatenate([first, out], axis=2)
        second = second.reshape(UNITS, FF // UNITS, D)
    vec = jnp.pad(jnp.concatenate(placed).reshape(-1, D), ((0, 4), (0, 0)))
    (
        result,
        d_sum1,
        kv,
        queries,
        picks,
        lse,
        d_heads,
        d_expand,
        d_contract,
        d_out,
        small,
        d_ffn,
        w_all,
        links,
    ) = front(
        rows, cotangent.reshape(TOK_SEQ, D), random_blocks, vec, qkv, first, out, second, planes
    )
    d_tokens, totals, *grads = back(
        (kv, queries, picks, links, lse, d_heads),
        (rows, w_all, d_sum1, small, d_ffn),
        (d_expand, d_contract, d_out),
        planes,
    )
    totals = (totals[0:6], totals[6:8], totals[8 : 8 + FF // D])
    if planes:
        vectors = [
            lax.dynamic_slice(v.reshape(-1), (me * (v.size // shards),), (v.size // shards,))
            for v in totals
        ]
    else:
        grads = [grads[0], d_out, d_expand, d_contract]
        *vectors, d_qkv, d_out, d_expand, d_contract = [
            lax.psum_scatter(
                g.astype(jnp.float32).reshape(-1),
                ("dp", "seq"),
                scatter_dimension=0,
                tiled=True,
            )
            for g in (*totals, *grads)
        ]
        grads = (d_qkv, d_out, d_expand, d_contract)
    return (result[None], d_tokens[None], *[g.reshape(-1) for g in grads], *vectors)


def solution(mesh):
    return jax.shard_map(
        on_device,
        mesh=mesh,
        in_specs=(
            P("dp", "seq", None),
            P(("dp", "seq")),
            P(("dp", "seq")),
            P(("dp", "seq")),
            P(("dp", "seq")),
            P(("dp", "seq")),
            P(("dp", "seq")),
            P(("dp", "seq")),
            P("dp", None, "seq", None),
            P("dp", "seq", None),
        ),
        out_specs=(
            P("dp", "seq", None),
            P("dp", "seq", None),
            P(("dp", "seq")),
            P(("dp", "seq")),
            P(("dp", "seq")),
            P(("dp", "seq")),
            P(("dp", "seq")),
            P(("dp", "seq")),
            P(("dp", "seq")),
        ),
        check_vma=False,
    )
```

```python
import functools

import jax
import jax.numpy as jnp
from jax import lax
from jax.experimental import pallas as pl
from jax.experimental.pallas import tpu as pltpu
from jax.sharding import PartitionSpec as P

MESH = pl.DeviceIdType.MESH

D = 768
FF = 3072
H = 12
HD = 64
BLOCK = 64
TOK_SEQ = 256
SEQ_GRP = 1
BPD = 4


norm_eps = 1e-12
masked_score = -1e30


def matmul(left, right):
    return jnp.dot(left, right, preferred_element_type=jnp.float32)


def inner_rows(left, right):
    return lax.dot_general(
        left, right, (((0,), (0,)), ((), ())), preferred_element_type=jnp.float32
    )


def outer_cols(left, right):
    return lax.dot_general(
        left, right, (((1,), (1,)), ((), ())), preferred_element_type=jnp.float32
    )


def normalize(value, gain, shift):
    mean = jnp.mean(value, axis=-1, keepdims=True)
    centred = value - mean
    inverse = lax.rsqrt(jnp.mean(centred * centred, axis=-1, keepdims=True) + norm_eps)
    normed = centred * inverse
    return (normed * gain + shift, normed, inverse)


def normalize_back(grad, normed, inverse, gain):
    scaled = grad * gain
    centred = scaled - jnp.mean(scaled, axis=-1, keepdims=True)
    return inverse * (centred - normed * jnp.mean(scaled * normed, axis=-1, keepdims=True))


def place(nz):
    y = lax.axis_index("dp")
    s = lax.axis_index("seq")
    return {"y": y, "z": s // 4, "x": (s // 2) % 2, "c": s % 2}

def device(p):
    return (p["y"], p["z"] * 4 + p["x"] * 2 + p["c"])

def chip(p, nz):
    return (p["y"] * nz + p["z"]) * 2 + p["x"]

def index(p, nz):
    return chip(p, nz) * 2 + p["c"]

def nearest(m, n, j):
    if n == 2:
        return m if j == 0 else 1 - m
    out = 0
    for i in range(n):
        rank = sorted(range(n), key=lambda s: (abs(s - i), s))
        out = jnp.where(m == i, rank[j], out)
    return out

def combine(dst, srcs):
    rows, cols = dst.shape
    step = min(cols, max(128, (24 * 1024 // rows) // 128 * 128))
    while cols % step:
        step -= 128
    def part(sl):
        total = srcs[0][:, sl].astype(jnp.float32)
        for s in srcs[1:]:
            total = total + s[:, sl].astype(jnp.float32)
        dst[:, sl] = total.astype(dst.dtype)
    if cols == step:
        part(slice(None))
    else:
        def body(i, _):
            part(pl.ds(pl.multiple_of(i * step, 128), step))
            return 0
        lax.fori_loop(0, cols // step, body, 0)

def owner(head, n):
    return head * n // H


def owned(place, n):
    head = (place * H + n - 1) // n
    return jnp.minimum(head, H - 1), jnp.logical_and(head < H, owner(head, n) == place)


def post(place, h, pairs, sems, act, n):
    to = owner(h, n)
    for i, (src, dst) in enumerate(pairs):

        @pl.when(to != place)
        def _():
            act(
                pltpu.make_async_remote_copy(
                    src_ref=src.at[h],
                    dst_ref=dst(place),
                    send_sem=sems[0].at[i, h],
                    recv_sem=sems[1].at[i, place],
                    device_id=(lax.axis_index("dp"), to),
                    device_id_type=MESH,
                )
            )


def walk_to_owners(n, place, head, pairs, sems, act):
    def body(k, _):
        post(place, (head + 1 + k) % H, pairs, sems, act, n)
        return 0

    lax.fori_loop(0, H, body, 0)


def finish_to_owners(n, place, head, pairs, sems):
    walk_to_owners(n, place, head, pairs, sems, lambda cp: cp.wait_send())


def wait_to_owner(n, place, head, mine, pairs, sems):
    @pl.when(mine)
    def _():
        for i, (src, dst) in enumerate(pairs):
            cp = pltpu.make_async_copy(src.at[head], dst(place), sems[2].at[i])
            cp.start()
            cp.wait()

        def body(k, _):
            s = (place + 1 + k) % n
            for i, (src, dst) in enumerate(pairs):
                pltpu.make_async_remote_copy(
                    src_ref=src.at[0],
                    dst_ref=dst(s),
                    send_sem=sems[0].at[i, 0],
                    recv_sem=sems[1].at[i, s],
                    device_id=(lax.axis_index("dp"), place),
                    device_id_type=MESH,
                ).wait_recv()
            return 0

        lax.fori_loop(0, n - 1, body, 0)


def send_to_owners(n, place, head, mine, pairs, sems, meanwhile):
    walk_to_owners(n, place, head, pairs, sems, lambda cp: cp.start())
    meanwhile()
    wait_to_owner(n, place, head, mine, pairs, sems)
    finish_to_owners(n, place, head, pairs, sems)


def walk_from_owners(n, place, head, src, dst, sems, act):
    row = lax.axis_index("dp")

    def body(k, _):
        to = (place + 1 + k) % n
        act(
            pltpu.make_async_remote_copy(
                src_ref=src.at[to],
                dst_ref=dst.at[head],
                send_sem=sems[0].at[0, to],
                recv_sem=sems[1].at[0, head],
                device_id=(row, to),
                device_id_type=MESH,
            )
        )
        return 0

    lax.fori_loop(0, n - 1, body, 0)


def start_from_owners(n, place, head, mine, src, dst, sems):
    @pl.when(mine)
    def _():
        walk_from_owners(n, place, head, src, dst, sems, lambda cp: cp.start())
        cp = pltpu.make_async_copy(src.at[place], dst.at[head], sems[2].at[0])
        cp.start()
        cp.wait()


def wait_head(n, place, h, src, dst, sems):
    @pl.when(owner(h, n) != place)
    def _():
        pltpu.make_async_remote_copy(
            src_ref=src.at[0],
            dst_ref=dst.at[h],
            send_sem=sems[0].at[0, 0],
            recv_sem=sems[1].at[0, h],
            device_id=(lax.axis_index("dp"), place),
            device_id_type=MESH,
        ).wait_recv()


def wait_from_owners(n, place, head, src, dst, sems):
    def body(k, _):
        wait_head(n, place, (head + k) % H, src, dst, sems)
        return 0

    lax.fori_loop(0, H, body, 0)


def finish_from_owners(n, place, head, mine, src, dst, sems):
    @pl.when(mine)
    def _():
        walk_from_owners(n, place, head, src, dst, sems, lambda cp: cp.wait_send())


def swap_halves(tile):
    return pltpu.roll(tile, HD, tile.ndim - 1)


def low_lanes(shape):
    return lax.broadcasted_iota(jnp.int32, shape, len(shape) - 1) < HD


def exchange_sems(n, pairs=1):
    return [
        pltpu.SemaphoreType.DMA((pairs, max(n, H))),
        pltpu.SemaphoreType.DMA((pairs, max(n, H))),
        pltpu.SemaphoreType.DMA((pairs,)),
    ]


ANY = pl.BlockSpec(memory_space=pl.ANY)
VMEM = pl.BlockSpec(memory_space=pltpu.VMEM)
SMEM = pl.BlockSpec(memory_space=pltpu.SMEM)
MSG = TOK_SEQ + TOK_SEQ // 2


def key_list(i, n, picks_ref):
    last = n * BPD - 1

    def of(b):
        s, r = b // BPD, b % BPD
        picked = [picks_ref[s, 0, r * 3 + j] for j in range(3)]
        return [jnp.maximum(b - 1, 0), b, jnp.minimum(b + 1, last), 0, last] + picked

    return [of(2 * i), of(2 * i + 1)]


def fill_pair(lists, kv_ref, vk_ref, keys, values):
    for j in range(8):
        a, b = lists[0][j], lists[1][j]
        to = slice(j * BLOCK, (j + 1) * BLOCK)
        keys[to, 0:HD] = kv_ref[a][:, 0:HD]
        keys[to, HD:128] = vk_ref[b][:, HD:128]
        values[to, 0:HD] = vk_ref[a][:, 0:HD]
        values[to, HD:128] = kv_ref[b][:, HD:128]


def two_blocks(tile):
    left = low_lanes(tile.shape)
    zero = jnp.zeros_like(tile)
    return jnp.concatenate([jnp.where(left, tile, zero), jnp.where(left, zero, tile)], axis=0)


def pair_scores(i, n, keys, query):
    scores = outer_cols(keys, query)
    left = low_lanes((BLOCK, 128))
    right = jnp.logical_not(left)
    end = n * BPD // 2 - 1
    hide_first = jnp.logical_and(left, i == 0)
    hide_last = jnp.logical_and(right, i == end)
    return jnp.concatenate(
        [
            jnp.where(hide_first, masked_score, scores[0:BLOCK]),
            scores[BLOCK : 2 * BLOCK],
            jnp.where(hide_last, masked_score, scores[2 * BLOCK : 3 * BLOCK]),
            scores[3 * BLOCK :],
        ],
        axis=0,
    )


def turn_pairs(n, kv_ref, vk_ref):
    def body(b, _):
        for t in range(BPD):
            tile = kv_ref[b * BPD + t].astype(jnp.float32)
            vk_ref[b * BPD + t] = swap_halves(tile).astype(jnp.bfloat16)
        return 0

    lax.fori_loop(0, n, body, 0)


def chain_table(n, place, picks_vmem, picks_smem, links_ref):
    none = PICKS * n
    lane = lax.broadcasted_iota(jnp.int32, (n, 128), 1)
    turn = (lax.broadcasted_iota(jnp.int32, (n, 128), 0) + 2 * n - place - 1) % n
    order = jnp.where(lane < PICKS, turn * PICKS + lane, -1)
    picks = picks_vmem[:, 0, :]
    blocks = lax.broadcasted_iota(jnp.int32, (8, 128), 1)

    def body(k, tables):
        before, final = tables
        s = (place + 1 + k) % n
        for j in range(PICKS):
            pick, e = picks_smem[s, 0, j], k * PICKS + j
            before = jnp.where(jnp.logical_and(picks == pick, order > e), e, before)
            final = jnp.where(blocks == pick, e, final)
        return before, final

    start = (jnp.full((n, 128), none, jnp.int32), jnp.full((8, 128), none, jnp.int32))
    before, final = lax.fori_loop(0, n, body, start)
    links_ref[0:n] = before
    links_ref[n : n + 8] = final


PICKS = 3 * BPD
UNITS = 32
WIDE = 768


def greet_row(n, place, mine):
    row = lax.axis_index("dp")
    bar = pltpu.get_barrier_semaphore()

    def body(s, _):
        there = owned(s, n)[1]

        @pl.when(jnp.logical_and(s != place, jnp.logical_or(mine, there)))
        def _():
            pl.semaphore_signal(bar, inc=1, device_id=(row, s), device_id_type=MESH)

        return 0

    lax.fori_loop(0, n, body, 0)
    pl.semaphore_wait(bar, jnp.where(mine, n - 1, H))


def unpack_pair(tiles, odd, shape):
    left = low_lanes(shape)
    a, b = tiles.astype(jnp.float32), odd.astype(jnp.float32)
    return (jnp.where(left, a, swap_halves(b)), jnp.where(left, swap_halves(a), b))


def add_flat(out_ref, base, srcs, width=None):
    rows, cols = srcs[0].shape
    width = width or cols
    for k in range(cols // 128):
        lanes = slice(k * 128, (k + 1) * 128)
        total = srcs[0][:, lanes].astype(jnp.float32)
        for s in srcs[1:]:
            total = total + s[:, lanes].astype(jnp.float32)
        out_ref[pl.ds(base + k, rows, stride=width // 128), :] = total


class Reduction:
    def __init__(self, nz, me, links, direct, own, give, emit, bufs, sems, pending):
        self.nz, self.me, self.links, self.direct = nz, me, links, direct
        self.own, self.give, self.emit = own, give, emit
        self.rc, self.ra, self.rb, self.below, self.above = bufs
        self.csend, self.crecv, self.send, self.recv = sems
        self.pending = pending

    @staticmethod
    def buffers(nz, slab):
        counts = (4 * nz, nz, 2 * nz, nz, nz)
        return [pltpu.VMEM((c,) + slab, jnp.bfloat16) for c in counts]

    @staticmethod
    def semaphores(nz):
        return [pltpu.SemaphoreType.DMA((c * nz,)) for c in (4, 4, 5, 5)]

    def start(self, src, dst, slot, to, cond=None, there=None):
        cp = pltpu.make_async_remote_copy(
            src_ref=src,
            dst_ref=dst,
            send_sem=self.send.at[slot],
            recv_sem=self.recv.at[slot if there is None else there],
            device_id=device(to),
            device_id_type=MESH,
        )
        if cond is None:
            cp.start()
        else:
            pl.when(cond)(cp.start)
        self.pending.append((cp, cond))

    def arrived(self, ref, sem):
        pltpu.make_async_remote_copy(
            src_ref=ref,
            dst_ref=ref,
            send_sem=self.send.at[0],
            recv_sem=sem,
            device_id=device(dict(self.me, c=1 - self.me["c"])),
            device_id_type=MESH,
        ).wait_recv()

    def flip(self, which, f):
        d = self.links[which]
        return 1 - self.me[d] if f else self.me[d]

    def piece(self, z, a, b):
        c = {self.links[0]: a, self.links[1]: b}
        return (c["y"] * self.nz + z) * 2 + c["x"]

    def across(self, which):
        d = self.links[which]
        return dict(self.me, **{d: 1 - self.me[d]})

    def hand_over(self):
        nz = self.nz
        zs = sorted(range(nz), key=lambda z: -abs(2 * z - nz + 1))
        order = [(z, fa, fb) for fb in (1, 0) for fa in (1, 0) for z in zs]

        def one(z, fa, fb):
            def run():
                p = self.piece(z, self.flip(0, fa), self.flip(1, fb))
                cp = pltpu.make_async_remote_copy(
                    src_ref=self.give(p),
                    dst_ref=self.rc.at[p],
                    send_sem=self.csend.at[p],
                    recv_sem=self.crecv.at[p],
                    device_id=device(dict(self.me, c=1 - self.me["c"])),
                    device_id_type=MESH,
                )
                cp.start()
                self.pending.append((cp, None))

            return run

        return [one(*o) for o in order]

    def mine(self, p):
        self.arrived(self.rc.at[p], self.crecv.at[p])
        return [self.own(p), self.rc.at[p]]

    def relay(self, z, p, srcs, bref, aref, sb, sa):
        nz, mz, acc = self.nz, self.me["z"], self.rc.at[p]
        if z > 0:

            @pl.when(mz == 0)
            def _():
                combine(acc, srcs)

            @pl.when(jnp.logical_and(mz > 0, mz < z))
            def _():
                self.arrived(bref, self.recv.at[sb])
                combine(acc, srcs + [bref])

            self.start(acc, bref, sb, dict(self.me, z=jnp.minimum(mz + 1, nz - 1)), mz < z)
        if z < nz - 1:

            @pl.when(mz == nz - 1)
            def _():
                combine(acc, srcs)

            @pl.when(jnp.logical_and(mz < nz - 1, mz > z))
            def _():
                self.arrived(aref, self.recv.at[sa])
                combine(acc, srcs + [aref])

            self.start(acc, aref, sa, dict(self.me, z=jnp.maximum(mz - 1, 0)), mz > z)

    def ends(self, z, bref, aref, sb, sa):
        out = []
        if z > 0:
            self.arrived(bref, self.recv.at[sb])
            out.append(bref)
        if z < self.nz - 1:
            self.arrived(aref, self.recv.at[sa])
            out.append(aref)
        return out

    def steps(self):
        nz, me = self.nz, self.me
        zs = sorted(range(nz), key=lambda z: -abs(2 * z - nz + 1))

        def along_b(z, fa):
            def run():
                a = self.flip(0, fa)
                p = self.piece(z, a, self.flip(1, 1))
                combine(self.rc.at[p], self.mine(p))
                s = z * 2 + a
                self.start(self.rc.at[p], self.rb.at[s], s, self.across(1))

            return run

        def along_a(z):
            def run():
                a = self.flip(0, 1)
                p = self.piece(z, a, self.flip(1, 0))
                s = z * 2 + a
                srcs = self.mine(p)
                self.arrived(self.rb.at[s], self.recv.at[s])
                combine(self.rc.at[p], srcs + [self.rb.at[s]])
                self.start(self.rc.at[p], self.ra.at[z], 2 * nz + z, self.across(0))

            return run

        def chain(z):
            def run():
                p = self.piece(z, self.flip(0, 0), self.flip(1, 0))
                s = z * 2 + self.flip(0, 0)
                srcs = self.mine(p)
                self.arrived(self.rb.at[s], self.recv.at[s])
                self.arrived(self.ra.at[z], self.recv.at[2 * nz + z])
                srcs += [self.rb.at[s], self.ra.at[z]]
                if self.direct:
                    mz = me["z"]

                    @pl.when(mz != z)
                    def _():
                        combine(self.rc.at[p], srcs)

                    to = dict(me, z=z)
                    self.start(
                        self.rc.at[p], self.below.at[mz], 3 * nz + z, to, mz != z, 3 * nz + mz
                    )
                    return
                bref, aref = self.below.at[z], self.above.at[z]
                self.relay(z, p, srcs, bref, aref, 3 * nz + z, 4 * nz + z)

            return run

        def last():
            for z in range(nz):

                @pl.when(me["z"] == z)
                def _():
                    p = self.piece(z, self.flip(0, 0), self.flip(1, 0))
                    s = z * 2 + self.flip(0, 0)
                    srcs = [self.own(p), self.rc.at[p], self.rb.at[s], self.ra.at[z]]
                    if self.direct:
                        for other in range(nz):
                            if other != z:
                                ref = self.below.at[other]
                                self.arrived(ref, self.recv.at[3 * nz + other])
                                srcs.append(ref)
                        self.emit(srcs)
                        return
                    bref, aref = self.below.at[z], self.above.at[z]
                    self.emit(srcs + self.ends(z, bref, aref, 3 * nz + z, 4 * nz + z))

        out = [(1 + i, along_b(z, 1)) for i, z in enumerate(zs)]
        out += [(5 + i, along_b(z, 0)) for i, z in enumerate(zs)]
        out += [(5.5 + i, along_a(z)) for i, z in enumerate(zs)]
        out += [(9.5 + i, chain(z)) for i, z in enumerate(zs)]
        return out + [(20, last)]


class Spread:
    def __init__(self, nz, me, order, at, sems, pending):
        self.nz, self.me, self.order, self.at = nz, me, order, at
        self.send, self.recv, self.csend, self.crecv = sems
        self.pending = pending

    @staticmethod
    def semaphores(nz):
        chips = 4 * nz
        return [pltpu.SemaphoreType.DMA((chips, 4))] + [pltpu.SemaphoreType.DMA((chips,))] * 3

    def copy(self, slot, send, recv, to):
        ref = self.at(slot)
        return pltpu.make_async_remote_copy(
            src_ref=ref,
            dst_ref=ref,
            send_sem=send,
            recv_sem=recv,
            device_id=device(to),
            device_id_type=MESH,
        )

    def start(self, cp, cond=None):
        if cond is None:
            cp.start()
        else:
            pl.when(cond)(cp.start)
        self.pending.append((cp, cond))

    def one(self, steps):
        nz, me = self.nz, self.me
        size = {"y": 2, "z": nz, "x": 2}
        own = not any(steps)

        def run():
            src = dict(me)
            for d, i in zip(self.order, steps):
                src[d] = nearest(me[d], size[d], i)
            c = chip(src, nz)
            slot = c * 2 + me["c"]
            if not own:
                self.copy(slot, self.send.at[c, 0], self.recv.at[c], me).wait_recv()
            stage = 2 if steps[2] else (1 if steps[1] else 0)
            for t in range(stage, 3):
                d = self.order[t]
                onward = t == stage and not own
                if d == "z":
                    up, down = me["z"] < nz - 1, me["z"] > 0
                    if onward:
                        up = jnp.logical_and(up, src["z"] <= me["z"])
                        down = jnp.logical_and(down, src["z"] >= me["z"])
                    above = dict(me, z=jnp.minimum(me["z"] + 1, nz - 1))
                    below = dict(me, z=jnp.maximum(me["z"] - 1, 0))
                    self.start(self.copy(slot, self.send.at[c, 0], self.recv.at[c], above), up)
                    self.start(self.copy(slot, self.send.at[c, 1], self.recv.at[c], below), down)
                elif not (onward and steps[t]):
                    way = 2 if d == "x" else 3
                    to = dict(me, **{d: 1 - me[d]})
                    self.start(self.copy(slot, self.send.at[c, way], self.recv.at[c], to))
            sibling = dict(me, c=1 - me["c"])
            self.start(self.copy(slot, self.csend.at[c], self.crecv.at[c], sibling))

        return run

    def steps(self):
        size = {"y": 2, "z": self.nz, "x": 2}
        n0, n1, n2 = (size[d] for d in self.order)
        return [
            (i0 + i1 + i2, self.one((i0, i1, i2)))
            for i2 in range(n2)
            for i1 in range(n1)
            for i0 in range(n0)
        ]

    def finish(self):
        def body(c, _):
            slot = c * 2 + 1 - self.me["c"]
            self.copy(slot, self.csend.at[c], self.crecv.at[c], self.me).wait_recv()
            return 0

        lax.fori_loop(0, 4 * self.nz, body, 0)


def run_in_order(items, low, high):
    steps = [(w, i, f) for i, item in enumerate(items) for w, f in item.steps()]
    for w, _, f in sorted(steps, key=lambda s: s[:2]):
        if low <= w < high:
            f()


def exchange_partners(me, nz):
    partners = [dict(me, **{d: 1 - me[d]}) for d in ("c", "x", "y")]
    step = 1
    while step < nz:
        partners.append(dict(me, z=me["z"] + step - 2 * step * ((me["z"] // step) % 2)))
        step *= 2
    return partners


def vector_copy(i, value, land, sems, partners):
    return pltpu.make_async_remote_copy(
        src_ref=value.at[i],
        dst_ref=land.at[i],
        send_sem=sems[0].at[i],
        recv_sem=sems[1].at[i],
        device_id=device(partners[i]),
        device_id_type=MESH,
    )


def greet_row_and_y(n, me, place_row):
    bar = pltpu.get_barrier_semaphore()

    def greet(k, _):
        to = (place_row + 1 + k) % n
        pl.semaphore_signal(bar, inc=1, device_id=(me["y"], to), device_id_type=MESH)
        return 0

    lax.fori_loop(0, n - 1, greet, 0)
    pl.semaphore_signal(bar, inc=1, device_id=(1 - me["y"], place_row), device_id_type=MESH)
    return lambda: pl.semaphore_wait(bar, n)


UNIT = D // UNITS
THIRD = FF // UNITS // 3
QKV_ORDERS = (("z", "x", "y"), ("z", "y", "x"), ("x", "y", "z"))
REST = (
    ("second", THIRD, FF // UNITS, ("z", "y", "x")),
    ("first", 0, UNIT, ("z", "x", "y")),
    ("second", 0, THIRD, ("z", "x", "y")),
)


EARLY = {1: (0, 1), 4: (1, 2), 5: (2, 3)}
LATE = ((3, 4), (4, 5), (5, 99), (99, 99), (99, 99))


def from_flat(flat, cols, rows):
    step = cols // 128
    return [flat[pl.ds(k, rows, stride=step), :] for k in range(step)]


def as_matrix(units):
    count, rows, cols = units.shape
    return units.astype(jnp.float32).reshape(count * rows, cols).astype(jnp.bfloat16)


def kernel_planes():
    seq = lax.axis_size("seq")
    if lax.axis_size("dp") != 2 or 2 * seq != UNITS or seq % 4:
        return 0
    return seq // 4


def place_vectors(me, shards, pieces, line, value):
    packed = pieces[...]
    at, row = 0, 0
    value[0] = jnp.zeros_like(value[0])
    for size in VECTORS:
        width = size // shards
        start = me * width
        inside = lax.broadcasted_iota(jnp.int32, packed.shape, 1)
        inside = jnp.logical_and(inside >= at, inside < at + width)
        moved = jnp.where(inside, packed, 0.0)
        line[...] = jnp.zeros_like(line)
        base = pl.multiple_of(start // 128 * 128, 128)
        line[:, pl.ds(base, 384)] = pltpu.roll(moved, (start % 128 - at) % 384, 1)
        for r in range(size // D):
            value[0, row + r : row + r + 1] = line[:, r * D : (r + 1) * D]
        row += size // D
        at += width


def front_kernel(n, nz, *refs):
    rows_ref, cot_ref, picks_ref, vec_in, qkv_in, first_in, out_in, second_in = refs[:8]
    (
        result_ref,
        d_sum1_ref,
        kv_hbm,
        q_hbm,
        picks_hbm,
        lse_ref,
        d_heads,
        dw1_hbm,
        dw2_hbm,
        dwo_hbm,
        small_ref,
        d_ffn_ref,
        w_hbm,
        links_hbm,
    ) = refs[8:22]
    (
        w_ref,
        first_ref,
        second_ref,
        flat,
        value,
        land,
        box_kv,
        box_q,
        kv_ref,
        q_ref,
        vk_ref,
        picks_smem,
        keys,
        values,
        attended,
        inbox,
        grad_box,
        slope_ref,
        active_ref,
        dw1_ref,
        dw2_ref,
        dwo_ref,
        mixed_ref,
        load_sem,
        store_sem,
        keep_sem,
        vsend,
        vrecv,
        links_ref,
        picks_vmem,
        line,
    ) = refs[22:53]
    sems_qkv, sems_in, sems_out = refs[53:56], refs[56:59], refs[59:62]
    rest = list(refs[62:])
    place_row = lax.axis_index("seq")
    head, mine = owned(place_row, n)
    pending = []

    if nz:
        me = place(nz)
        slot = index(me, nz)
        hold = greet_row_and_y(n, me, place_row)
        stages = 3 + (nz - 1).bit_length()

        def take():
            out = rest[:4]
            del rest[:4]
            return out

        def widen(src):
            count = src.shape[0]
            flat[0:count] = src[...].astype(jnp.float32)

        widen(qkv_in)
        for j in range(3):
            step = D // 128
            for k in range(step):
                col = flat[pl.ds(j * UNIT * step + k, UNIT, stride=step), :]
                w_ref[slot * 3 + j, :, k * 128 : (k + 1) * 128] = col.astype(jnp.bfloat16)
        place_vectors(slot, 8 * nz, vec_in, line, value)
        hold()
        qkv_items = [
            Spread(nz, me, order, lambda s, j=j: w_ref.at[s * 3 + j], take(), pending)
            for j, order in enumerate(QKV_ORDERS)
        ]
        buffers = {"first": first_ref, "second": second_ref}

        def part(kind, lo, hi):
            ref = buffers[kind]
            if hi - lo == ref.shape[1]:
                return lambda s: ref.at[s]
            return lambda s: ref.at[s, lo:hi]

        rest_items = [
            Spread(nz, me, order, part(kind, lo, hi), take(), pending)
            for kind, lo, hi, order in REST
        ]
        partners = exchange_partners(me, nz)
        vsems = (vsend, vrecv)
        vector_copy(0, value, land, vsems, partners).start()
        run_in_order(qkv_items, 0, 1)
        for src, dst, at, cols, count in (
            (first_in, first_ref, 0, FF, UNIT),
            (out_in, first_ref, FF, D, UNIT),
            (second_in, second_ref, 0, D, FF // UNITS),
        ):
            widen(src)
            for k, col in enumerate(from_flat(flat, cols, count)):
                dst[slot, :, at + k * 128 : at + (k + 1) * 128] = col.astype(jnp.bfloat16)

        def vector_stage(i):
            vector_copy(i, value, land, vsems, partners).wait_recv()
            value[i + 1] = value[i] + land[i]
            if i + 1 < stages:
                vector_copy(i + 1, value, land, vsems, partners).start()

        for depth in range(1, nz + 2):
            vector_stage(min(depth - 1, stages)) if depth <= stages else None
            run_in_order(qkv_items, depth, depth + 1)
            if depth in EARLY:
                run_in_order(rest_items, *EARLY[depth])
        for i in range(nz + 1, stages):
            vector_stage(i)
        for item in qkv_items:
            item.finish()
        vec = value.at[stages]
    else:
        greet_row(n, place_row, mine)
        loads = [
            pltpu.make_async_copy(src, dst, load_sem.at[i])
            for i, (src, dst) in enumerate(
                ((qkv_in, w_ref), (first_in, first_ref), (second_in, second_ref))
            )
        ]
        for cp in loads:
            cp.start()
        for cp in loads:
            cp.wait()
        vec = vec_in

    def rest_steps(low, high):
        if nz:
            run_in_order(rest_items, low, high)

    rows = rows_ref[...]
    left = low_lanes((TOK_SEQ, 128))
    left_q = low_lanes((BLOCK, 128))
    wide = 256
    parcels = (
        (box_kv, lambda s: kv_ref.at[pl.ds(s * BPD, BPD)]),
        (box_q, lambda s: q_ref.at[s]),
        (picks_ref, lambda s: picks_hbm.at[s]),
    )

    def project_some(step, _):
        g = (place_row + step) % (D // wide)
        cols = pl.ds(pl.multiple_of(g * wide, wide), wide)

        def project(e):
            return matmul(rows, as_matrix(w_ref[e * UNITS : (e + 1) * UNITS, :, cols]))

        q = (project(0) + vec[0:1, cols]) * HD ** (-0.5)
        k = project(1)
        v = project(2) + vec[1:2, cols]
        for p in range(wide // 128):
            h = g * (wide // HD) + p * 2
            lanes = slice(p * 128, (p + 1) * 128)
            kp, vp, qp = k[:, lanes], v[:, lanes], q[:, lanes]
            even, odd = jnp.where(left, kp, swap_halves(vp)), jnp.where(left, swap_halves(kp), vp)
            for t in range(BPD):
                part = slice(t * BLOCK, (t + 1) * BLOCK)
                box_kv[h, t] = even[part].astype(jnp.bfloat16)
                box_kv[h + 1, t] = odd[part].astype(jnp.bfloat16)
            turned = swap_halves(qp)
            for t in range(BPD // 2):
                a = slice(2 * t * BLOCK, (2 * t + 1) * BLOCK)
                b = slice((2 * t + 1) * BLOCK, (2 * t + 2) * BLOCK)
                to = slice(t * BLOCK, (t + 1) * BLOCK)
                box_q[h, to, :] = jnp.where(left_q, qp[a], turned[b]).astype(jnp.bfloat16)
                box_q[h + 1, to, :] = jnp.where(left_q, turned[a], qp[b]).astype(jnp.bfloat16)
            for u in range(2):
                post(place_row, h + u, parcels, sems_qkv, lambda cp: cp.start(), n)
        return 0

    lax.fori_loop(0, D // wide, project_some, 0)
    rest_steps(*LATE[0])
    wait_to_owner(n, place_row, head, mine, parcels, sems_qkv)

    keep = (
        pltpu.make_async_copy(kv_ref, kv_hbm, keep_sem.at[0]),
        pltpu.make_async_copy(q_ref, q_hbm, keep_sem.at[3]),
    )
    keep_w = pltpu.make_async_copy(w_ref, w_hbm, keep_sem.at[2])
    keep_w.start()
    keep_links = pltpu.make_async_copy(links_ref, links_hbm, keep_sem.at[4])
    groups = 4

    @pl.when(mine)
    def _():
        for copy in keep:
            copy.start()
        copies = (
            pltpu.make_async_copy(picks_hbm, picks_smem, keep_sem.at[1]),
            pltpu.make_async_copy(picks_hbm, picks_vmem, keep_sem.at[5]),
        )
        for cp in copies:
            cp.start()
        for cp in copies:
            cp.wait()
        turn_pairs(n, kv_ref, vk_ref)
        chain_table(n, place_row, picks_vmem, picks_smem, links_ref)
        keep_links.start()

    def attend_some(k, _):
        s = (place_row + 1 + k) % n
        for t in range(BPD // 2):
            i = s * (BPD // 2) + t
            fill_pair(key_list(i, n, picks_smem), kv_ref, vk_ref, keys.at[t], values.at[t])
        for t in range(BPD // 2):
            i = s * (BPD // 2) + t
            part = slice(t * BLOCK, (t + 1) * BLOCK)
            query = two_blocks(q_ref[s, part, :])
            scores = pair_scores(i, n, keys[t], query)
            top = jnp.max(scores, axis=0, keepdims=True)
            weights = jnp.exp(scores - top)
            total = jnp.sum(weights, axis=0, keepdims=True)
            probs = (weights * (1.0 / total)).astype(jnp.bfloat16)
            full = inner_rows(probs, values[t])
            attended[s, part, :] = jnp.where(left_q, full[:BLOCK], full[BLOCK:]).astype(
                jnp.bfloat16
            )
            lse_ref[i] = top + jnp.log(total)

        @pl.when(s != place_row)
        def _():
            pltpu.make_async_remote_copy(
                src_ref=attended.at[s],
                dst_ref=inbox.at[head],
                send_sem=sems_in[0].at[0, s],
                recv_sem=sems_in[1].at[0, head],
                device_id=(lax.axis_index("dp"), s),
                device_id_type=MESH,
            ).start()

        return 0

    for g in range(groups):

        @pl.when(mine)
        def _():
            lax.fori_loop(g * (n // groups), (g + 1) * (n // groups), attend_some, 0)

        rest_steps(*LATE[1 + g])

    @pl.when(mine)
    def _():
        cp = pltpu.make_async_copy(attended.at[place_row], inbox.at[head], sems_in[2].at[0])
        cp.start()
        cp.wait()

    if nz:
        for item in rest_items:
            item.finish()
    wait_from_owners(n, place_row, head, attended, inbox, sems_in)

    for h in range(0, H, 2):
        for t in range(BPD // 2):
            part = slice(t * BLOCK, (t + 1) * BLOCK)
            a, b = unpack_pair(inbox[h, part, :], inbox[h + 1, part, :], (BLOCK, 128))
            lanes = slice(h * HD, (h + 2) * HD)
            mixed_ref[2 * t * BLOCK : (2 * t + 1) * BLOCK, lanes] = a.astype(jnp.bfloat16)
            mixed_ref[(2 * t + 1) * BLOCK : (2 * t + 2) * BLOCK, lanes] = b.astype(jnp.bfloat16)
    out_w = as_matrix(first_ref[:, :, FF : FF + D])
    hidden1 = rows_ref[...].astype(jnp.float32) + matmul(mixed_ref[...], out_w) + vec[2:3]
    normed_out1, normed1, inverse1 = normalize(hidden1, vec[6:7], vec[3:4])
    lowered = normed_out1.astype(jnp.bfloat16)
    per = UNITS * WIDE // FF

    def second_rows(c):
        return second_ref[pl.ds(c * per, per)].reshape(WIDE, D)

    def up_step(c, hidden):
        cols = pl.ds(pl.multiple_of(c * WIDE, WIDE), WIDE)
        up = matmul(lowered, as_matrix(first_ref[:, :, cols])) + vec[pl.ds(8 + c, 1)]
        square = up * up
        inner = (2 / jnp.pi) ** 0.5 * (up + 0.044715 * up * square)
        curve = jnp.tanh(inner)
        active = (0.5 * up * (1 + curve)).astype(jnp.bfloat16)
        slope_ref[:, cols] = 0.5 * (1 + curve) + 0.5 * up * (1 - curve * curve) * (
            (2 / jnp.pi) ** 0.5 * (1 + 3 * 0.044715 * square)
        )
        active_ref[:, cols] = active
        return hidden + matmul(active, second_rows(c))

    hidden2 = lax.fori_loop(0, FF // WIDE, up_step, normed_out1 + vec[4:5])
    result, normed2, inverse2 = normalize(hidden2, vec[7:8], vec[5:6])
    result_ref[...] = result
    grad = cot_ref[...].astype(jnp.float32)
    d_sum2 = normalize_back(grad, normed2, inverse2, vec[7:8])
    d_down = d_sum2.astype(jnp.bfloat16)

    def add_rows(x):
        return jnp.sum(x, axis=0, keepdims=True)

    small_ref[2:3] = add_rows(d_down.astype(jnp.float32))
    small_ref[3:4] = add_rows(grad)
    small_ref[5:6] = add_rows(grad * normed2)

    def stores(c):
        cols = pl.ds(pl.multiple_of(c * WIDE, WIDE), WIDE)
        slabs = pl.ds(c * per, per)
        return (
            pltpu.make_async_copy(dw1_ref.at[:, :, cols], dw1_hbm.at[:, :, cols], store_sem.at[0, c]),
            pltpu.make_async_copy(dw2_ref.at[slabs], dw2_hbm.at[slabs], store_sem.at[1, c]),
        )

    def back_step(c, d_norm1):
        cols = pl.ds(pl.multiple_of(c * WIDE, WIDE), WIDE)
        d_active = outer_cols(d_down, second_rows(c))
        d_up = (d_active * slope_ref[:, cols]).astype(jnp.bfloat16)
        d_ffn_ref[:, cols] = add_rows(d_up.astype(jnp.float32))
        dw2 = inner_rows(active_ref[:, cols], d_down)
        dw2_ref[pl.ds(c * per, per)] = dw2.reshape(per, FF // UNITS, D).astype(jnp.bfloat16)
        dw1 = inner_rows(lowered, d_up)
        dw1_ref[:, :, cols] = dw1.reshape(UNITS, UNIT, WIDE).astype(jnp.bfloat16)
        for cp in stores(c):
            cp.start()
        return d_norm1 + outer_cols(d_up, as_matrix(first_ref[:, :, cols]))

    d_norm1 = lax.fori_loop(0, FF // WIDE, back_step, d_sum2)
    small_ref[1:2] = add_rows(d_norm1)
    small_ref[4:5] = add_rows(d_norm1 * normed1)
    d_sum1 = normalize_back(d_norm1, normed1, inverse1, vec[6:7])
    d_sum1_ref[...] = d_sum1
    d_attn = d_sum1.astype(jnp.bfloat16)
    small_ref[0:1] = add_rows(d_attn.astype(jnp.float32))
    d_mixed = outer_cols(d_attn, as_matrix(first_ref[:, :, FF : FF + D]))
    for h in range(0, H, 2):
        for t in range(BPD // 2):
            part = slice(t * BLOCK, (t + 1) * BLOCK)
            lanes = slice(h * HD, (h + 2) * HD)
            a, b = unpack_pair(
                d_mixed[2 * t * BLOCK : (2 * t + 1) * BLOCK, lanes],
                d_mixed[(2 * t + 1) * BLOCK : (2 * t + 2) * BLOCK, lanes],
                (BLOCK, 128),
            )
            grad_box[h, part, :] = a.astype(jnp.bfloat16)
            grad_box[h + 1, part, :] = b.astype(jnp.bfloat16)

    store_out = pltpu.make_async_copy(dwo_ref, dwo_hbm, load_sem.at[0])

    def late():
        dwo = inner_rows(mixed_ref[...], d_attn).reshape(UNITS, UNIT, D)
        dwo_ref[...] = dwo.astype(jnp.bfloat16)
        store_out.start()

    send_to_owners(n, place_row, head, mine, ((grad_box, lambda s: d_heads.at[s]),), sems_out, late)
    store_out.wait()

    def drain(c, _):
        for cp in stores(c):
            cp.wait()
        return 0

    lax.fori_loop(0, FF // WIDE, drain, 0)

    @pl.when(mine)
    def _():
        for copy in keep:
            copy.wait()
        keep_links.wait()

    keep_w.wait()
    finish_from_owners(n, place_row, head, mine, attended, inbox, sems_in)
    finish_to_owners(n, place_row, head, parcels, sems_qkv)
    if nz:
        for i in range(stages):
            vector_copy(i, value, land, vsems, partners).wait_send()
    for cp, cond in pending:
        if cond is None:
            cp.wait_send()
        else:
            pl.when(cond)(cp.wait_send)


def front(rows, cotangent, picks, vec, qkv, first, out, second, nz):
    n = lax.axis_size("seq")
    low, full = jnp.bfloat16, jnp.float32
    picks = jnp.pad(picks.reshape(H, 1, BPD * 3), ((0, 0), (0, 7), (0, 128 - BPD * 3)))
    part = (TOK_SEQ // 2, 128)
    pairs = n * BPD // 2
    units = [(UNITS, UNIT, FF), (UNITS, FF // UNITS, D), (UNITS, UNIT, D)]
    shapes = [((TOK_SEQ, D), full), ((TOK_SEQ, D), full)]
    shapes += [((n * BPD, BLOCK, 128), low), ((n,) + part, low)]
    shapes += [((n, 8, 128), jnp.int32), ((pairs, 1, 128), full), ((n,) + part, low)]
    shapes += [(u, low) for u in units] + [((8, D), full), ((1, FF), full)]
    shapes += [((3 * UNITS, UNIT, D), low), ((n + 8, 128), jnp.int32)]
    stages = 3 + (max(nz, 1) - 1).bit_length()
    where = VMEM if nz else ANY
    extra = []
    for _ in range(6 if nz else 0):
        extra += Spread.semaphores(nz)
    return pl.pallas_call(
        functools.partial(front_kernel, n, nz),
        out_shape=[jax.ShapeDtypeStruct(s, d) for s, d in shapes],
        in_specs=[VMEM, VMEM, ANY, VMEM, where, where, where, where],
        out_specs=[VMEM, VMEM, ANY, ANY, ANY, VMEM, ANY, ANY, ANY, ANY, VMEM, VMEM, ANY, ANY],
        scratch_shapes=[
            pltpu.VMEM((3 * UNITS, UNIT, D), low),
            pltpu.VMEM((UNITS, UNIT, FF + D), low),
            pltpu.VMEM((UNITS, FF // UNITS, D), low),
            pltpu.VMEM((UNIT * FF // 128, 128), full),
            pltpu.VMEM((stages + 1, 16, D), full),
            pltpu.VMEM((stages, 16, D), full),
            pltpu.VMEM((H, BPD, BLOCK, 128), low),
            pltpu.VMEM((H,) + part, low),
            pltpu.VMEM((n * BPD, BLOCK, 128), low),
            pltpu.VMEM((n,) + part, low),
            pltpu.VMEM((n * BPD, BLOCK, 128), low),
            pltpu.SMEM((n, 8, 128), jnp.int32),
            pltpu.VMEM((BPD // 2, 8 * BLOCK, 128), low),
            pltpu.VMEM((BPD // 2, 8 * BLOCK, 128), low),
            pltpu.VMEM((n,) + part, low),
            pltpu.VMEM((H,) + part, low),
            pltpu.VMEM((H,) + part, low),
            pltpu.VMEM((TOK_SEQ, FF), full),
            pltpu.VMEM((TOK_SEQ, FF), low),
            *[pltpu.VMEM(u, low) for u in units],
            pltpu.VMEM((TOK_SEQ, D), low),
            pltpu.SemaphoreType.DMA((3,)),
            pltpu.SemaphoreType.DMA((2, FF // WIDE)),
            pltpu.SemaphoreType.DMA((6,)),
            pltpu.SemaphoreType.DMA((stages,)),
            pltpu.SemaphoreType.DMA((stages,)),
            pltpu.VMEM((n + 8, 128), jnp.int32),
            pltpu.VMEM((n, 8, 128), jnp.int32),
            pltpu.VMEM((1, max(VECTORS) + 384), full),
            *exchange_sems(n, 3),
            *exchange_sems(n),
            *exchange_sems(n),
            *extra,
        ],
        compiler_params=pltpu.CompilerParams(
            collective_id=0, has_side_effects=True, vmem_limit_bytes=60 << 20
        ),
        name="front",
    )(rows, cotangent, picks, vec, qkv, first, out, second)


FFN_KINDS = (
    ("expand", 0, UNIT, ("x", "y")),
    ("contract", THIRD, FF // UNITS, ("y", "x")),
    ("contract", 0, THIRD, ("x", "y")),
    ("out", 0, UNIT, ("x", "y")),
)
QKV_KINDS = (
    (0, 0, D, ("x", "y")),
    (1, 0, D, ("y", "x")),
    (2, 0, D // 2, ("x", "y")),
    (2, D // 2, D, ("y", "x")),
)
QKV_UNITS = 3 * UNITS


def send_one(sems, src, dst, head, to):
    return pltpu.make_async_remote_copy(
        src_ref=src.at[to],
        dst_ref=dst.at[head],
        send_sem=sems[0].at[0, to],
        recv_sem=sems[1].at[0, head],
        device_id=(lax.axis_index("dp"), to),
        device_id_type=MESH,
    )


def back_kernel(n, nz, *refs):
    kv_ref, q_ref, picks_ref, links_ref, lse_ref, grad_ref = refs[:6]
    rows_ref, w_hbm, d_sum1_ref, small_ref, ffn_ref, dw1, dw2, dwo = refs[6:14]
    d_tokens_ref, vec_out = refs[14:16]
    outs = refs[16 : 20 if nz else 17]
    rest = list(refs[20 if nz else 17 :])
    vk_ref, keys, values, acc, out_q, out_kv, inbox_q, inbox_kv, proj, w_ref, ownq = rest[:11]
    turned_rows, value, land, load_sem, vsend, vrecv = rest[11:17]
    sems_q, sems_kv = rest[17:20], rest[20:23]
    own1, own2, owno = rest[23:26] if nz else (None, None, None)
    rest = rest[26:]
    place_row = lax.axis_index("seq")
    head, mine = owned(place_row, n)
    blocks, none = n * BPD, n * BPD + n * PICKS
    pending = []

    load_w = pltpu.make_async_copy(w_hbm, w_ref, load_sem.at[0])
    load_w.start()
    if nz:
        me = place(nz)
        core = me["c"]
        loads = [
            pltpu.make_async_copy(src, dst, load_sem.at[1 + i])
            for i, (src, dst) in enumerate(((dw1, own1), (dw2, own2), (dwo, owno)))
        ]
        for cp in loads:
            cp.start()
        hold = greet_row_and_y(n, me, place_row)
    else:
        greet_row(n, place_row, mine)

    @pl.when(mine)
    def _():
        turn_pairs(n, kv_ref, vk_ref)

        def clear(b, _):
            acc[b] = jnp.zeros((BLOCK, 128), jnp.float32)
            return 0

        lax.fori_loop(0, blocks, clear, 0)
        clear(none, 0)

    def take(count):
        out = rest[:count]
        del rest[:count]
        return out

    def ffn_item(kind, lo, hi, links):
        far, near = {"expand": (dw1, own1), "contract": (dw2, own2), "out": (dwo, owno)}[kind]
        target = outs[("out", "expand", "contract").index(kind) + 1]
        whole = hi - lo == far.shape[1]

        def at(ref, t):
            return ref.at[t] if whole else ref.at[t, lo:hi]

        return Reduction(
            nz,
            me,
            links,
            False,
            lambda p: at(near, p * 2 + core),
            lambda p: at(far, p * 2 + 1 - core),
            lambda srcs: add_flat(target, lo * (far.shape[2] // 128), srcs),
            take(5),
            take(4),
            pending,
        )

    def qkv_item(j, lo, hi, links):
        def at(t):
            ref = ownq.at[t * 3 + j]
            return ref if hi - lo == D else ref.at[:, lo:hi]

        return Reduction(
            nz,
            me,
            links,
            True,
            lambda p: at(p * 2 + core),
            lambda p: at(p * 2 + 1 - core),
            lambda srcs: add_flat(outs[0], (j * UNIT * D + lo) // 128, srcs, D),
            take(5),
            take(4),
            pending,
        )

    def hand_all(items):
        for group in zip(*[i.hand_over() for i in items]):
            for f in group:
                f()

    def ordered(items):
        steps = [(w + 0.01 * i, f) for i, item in enumerate(items) for w, f in item.steps()]
        return sorted(steps, key=lambda s: s[0])

    turned_rows[...] = rows_ref[...].T
    ffn_steps = []
    if nz:
        ffn = [ffn_item(*k) for k in FFN_KINDS]
        qkv = [qkv_item(*k) for k in QKV_KINDS]
        ffn_steps = ordered(ffn)
        hold()
        hand_all(ffn)
        for cp in loads:
            cp.wait()

    def ffn_run(low, high, whole_only=False):
        for w, f in ffn_steps:
            if low <= w < high and not (whole_only and w % 1 >= 0.5):
                f()

    left = low_lanes((BLOCK, 128))
    both = range(BPD // 2)

    def attend_some(k, _):
        s = (place_row + 1 + k) % n
        lists = [key_list(s * (BPD // 2) + t, n, picks_ref) for t in both]
        for t in both:
            fill_pair(lists[t], kv_ref, vk_ref, keys.at[t], values.at[t])
        parts = []
        for t in both:
            i = s * (BPD // 2) + t
            part = slice(t * BLOCK, (t + 1) * BLOCK)
            query = two_blocks(q_ref[s, part, :])
            grad = two_blocks(grad_ref[s, part, :])
            probs = jnp.exp(pair_scores(i, n, keys[t], query) - lse_ref[i])
            d_probs = outer_cols(values[t], grad)
            rows = jnp.sum(probs * d_probs, axis=0, keepdims=True)
            d_scores = (probs * (d_probs - rows)).astype(jnp.bfloat16)
            d_values = matmul(probs.astype(jnp.bfloat16), grad)
            d_keys = matmul(d_scores, query)
            full = inner_rows(d_scores, keys[t]) * HD ** (-0.5)
            out_q[s, part, :] = jnp.where(left, full[:BLOCK], full[BLOCK:]).astype(jnp.bfloat16)
            parts.append((d_keys, d_values))

        @pl.when(s != place_row)
        def _():
            send_one(sems_q, out_q, inbox_q, head, s).start()

        for t in both:
            tiles = []
            for j in range(8):
                part = slice(j * BLOCK, (j + 1) * BLOCK)
                dk, dv = parts[t][0][part], parts[t][1][part]
                a = jnp.where(left, dk, swap_halves(dv))
                b = jnp.where(left, swap_halves(dk), dv)
                tiles.append((a, b))
            a = (s * (BPD // 2) + t) * 2
            acc[jnp.maximum(a - 1, 0)] += tiles[0][0]
            acc[a] += tiles[1][0] + tiles[0][1]
            acc[a + 1] += tiles[2][0] + tiles[1][1]
            acc[jnp.minimum(a + 2, blocks - 1)] += tiles[2][1]
            acc[0] += tiles[3][0] + tiles[3][1]
            acc[blocks - 1] += tiles[4][0] + tiles[4][1]
            for u in range(2):
                for j in range(3):
                    e = (2 * t + u) * 3 + j
                    acc[blocks + k * PICKS + e] = tiles[5 + j][u] + acc[blocks + links_ref[s, e]]
        return 0

    groups = 4
    for g in range(groups):

        @pl.when(mine)
        def _():
            lax.fori_loop(g * (n // groups), (g + 1) * (n // groups), attend_some, 0)

        if g < 2:
            ffn_run(4 * g + 1, 4 * g + 5, True)

    @pl.when(mine)
    def _():
        def close(k, _):
            s = (place_row + 1 + k) % n
            for t in range(BPD):
                b = s * BPD + t
                total = acc[b] + acc[blocks + links_ref[n, b]]
                out_kv[s, t * BLOCK : (t + 1) * BLOCK, :] = total.astype(jnp.bfloat16)

            @pl.when(s != place_row)
            def _():
                send_one(sems_kv, out_kv, inbox_kv, head, s).start()

            return 0

        lax.fori_loop(0, n, close, 0)
        copies = (
            pltpu.make_async_copy(out_q.at[place_row], inbox_q.at[head], sems_q[2].at[0]),
            pltpu.make_async_copy(out_kv.at[place_row], inbox_kv.at[head], sems_kv[2].at[0]),
        )
        for cp in copies:
            cp.start()
        for cp in copies:
            cp.wait()

    for w, f in ffn_steps:
        if w < 9 and w % 1 >= 0.5:
            f()

    def head_pair(k, _):
        p = (place_row + k) % (H // 2)
        for u in range(2):
            wait_head(n, place_row, 2 * p + u, out_q, inbox_q, sems_q)
            wait_head(n, place_row, 2 * p + u, out_kv, inbox_kv, sems_kv)
        lanes = pl.ds(pl.multiple_of(p * 128, 128), 128)
        keys_values = unpack_pair(inbox_kv[2 * p], inbox_kv[2 * p + 1], (TOK_SEQ, 128))
        queries = []
        for t in both:
            part = slice(t * BLOCK, (t + 1) * BLOCK)
            queries += unpack_pair(inbox_q[2 * p, part, :], inbox_q[2 * p + 1, part, :], (BLOCK, 128))
        grads = (jnp.concatenate(queries, axis=0), *keys_values)
        for e in range(3):
            proj[e, :, lanes] = grads[e].astype(jnp.bfloat16)
        joined = jnp.concatenate(grads, axis=1).astype(jnp.bfloat16)
        grad = matmul(turned_rows[...], joined).reshape(UNITS, UNIT, 3 * 128).astype(jnp.bfloat16)
        for e in range(3):
            ownq[pl.ds(e * UNITS, UNITS), :, lanes] = grad[:, :, e * 128 : (e + 1) * 128]
        return 0

    lax.fori_loop(0, H // 2, head_pair, 0)
    qkv_steps = []
    if nz:
        hand_all(qkv)
        qkv_steps = ordered(qkv)

    def qkv_run(low, high):
        for w, f in qkv_steps:
            if low <= w < high:
                f()

    def add_rows(x):
        return jnp.sum(x.astype(jnp.float32), axis=0, keepdims=True)

    value[0, 0:1] = add_rows(proj[0])
    value[0, 1:2] = add_rows(proj[2])
    value[0, 2:8] = small_ref[0:6]
    for c in range(FF // D):
        value[0, 8 + c : 9 + c] = ffn_ref[:, c * D : (c + 1) * D]
    partners = exchange_partners(me, nz) if nz else []
    vsems = (vsend, vrecv)
    if nz:
        vector_copy(0, value, land, vsems, partners).start()

    def vector_stage(i):
        if i < len(partners):
            vector_copy(i, value, land, vsems, partners).wait_recv()
            total = value[i] + land[i]
            if i + 1 < len(partners):
                value[i + 1] = total
                vector_copy(i + 1, value, land, vsems, partners).start()
            else:
                vec_out[...] = total

    qkv_run(1, 5)
    ffn_run(9, 20)
    vector_stage(0)
    qkv_run(5, 9)
    load_w.wait()
    d_tokens = d_sum1_ref[...]
    for e in range(3):
        d_tokens = d_tokens + outer_cols(proj[e], as_matrix(w_ref[e * UNITS : (e + 1) * UNITS]))
    d_tokens_ref[...] = d_tokens
    vector_stage(1)
    ffn_run(20, 99)
    vector_stage(2)
    qkv_run(9, 20)
    vector_stage(3)
    vector_stage(4)
    qkv_run(20, 99)
    if not nz:
        vec_out[...] = value[0]
        outs[0][...] = ownq[...]
    for i in range(len(partners)):
        vector_copy(i, value, land, vsems, partners).wait_send()
    finish_from_owners(n, place_row, head, mine, out_q, inbox_q, sems_q)
    finish_from_owners(n, place_row, head, mine, out_kv, inbox_kv, sems_kv)
    for cp, cond in pending:
        if cond is None:
            cp.wait_send()
        else:
            pl.when(cond)(cp.wait_send)


def back(heads, local, weight_grads, nz):
    n = lax.axis_size("seq")
    low, full = jnp.bfloat16, jnp.float32
    rows, w_all, d_sum1, small, d_ffn = local
    outs = [((TOK_SEQ, D), full), ((16, D), full)]
    if nz:
        outs += [((3 * UNIT * D // 128, 128), full), ((UNIT * D // 128, 128), full)]
        outs += [((UNIT * FF // 128, 128), full)] * 2
    else:
        outs += [((QKV_UNITS, UNIT, D), low)]
    stages = 3 + (max(nz, 1) - 1).bit_length()
    part = (TOK_SEQ // 2, 128)
    extra = [pltpu.VMEM(g.shape, low) for g in weight_grads] if nz else []
    slabs = [(hi - lo, FF if kind == "expand" else D) for kind, lo, hi, _ in FFN_KINDS]
    slabs += [(UNIT, hi - lo) for _, lo, hi, _ in QKV_KINDS]
    for slab in slabs if nz else ():
        extra += Reduction.buffers(nz, slab)
        extra += Reduction.semaphores(nz)
    return pl.pallas_call(
        functools.partial(back_kernel, n, nz),
        out_shape=[jax.ShapeDtypeStruct(s, d) for s, d in outs],
        in_specs=[VMEM, VMEM, SMEM, SMEM, VMEM, VMEM]
        + [VMEM, ANY, VMEM, VMEM, VMEM, ANY, ANY, ANY],
        out_specs=[VMEM] * len(outs),
        scratch_shapes=[
            pltpu.VMEM((n * BPD, BLOCK, 128), low),
            pltpu.VMEM((BPD // 2, 8 * BLOCK, 128), low),
            pltpu.VMEM((BPD // 2, 8 * BLOCK, 128), low),
            pltpu.VMEM((n * (BPD + PICKS) + 1, BLOCK, 128), full),
            pltpu.VMEM((n,) + part, low),
            pltpu.VMEM((n, TOK_SEQ, 128), low),
            pltpu.VMEM((H,) + part, low),
            pltpu.VMEM((H, TOK_SEQ, 128), low),
            pltpu.VMEM((3, TOK_SEQ, D), low),
            pltpu.VMEM((QKV_UNITS, UNIT, D), low),
            pltpu.VMEM((QKV_UNITS, UNIT, D), low),
            pltpu.VMEM((D, TOK_SEQ), low),
            pltpu.VMEM((stages, 16, D), full),
            pltpu.VMEM((stages, 16, D), full),
            pltpu.SemaphoreType.DMA((4,)),
            pltpu.SemaphoreType.DMA((stages,)),
            pltpu.SemaphoreType.DMA((stages,)),
            *exchange_sems(n),
            *exchange_sems(n),
            *extra,
        ],
        compiler_params=pltpu.CompilerParams(
            collective_id=5, has_side_effects=True, vmem_limit_bytes=61 << 20
        ),
        name="back",
    )(*heads, *local, *weight_grads)


VECTORS = (6 * D, 2 * D, FF)


def hand_out_kernel(shards, *refs):
    count = (len(refs) - 6) // 3
    arrays, totals, outs = refs[:count], refs[count], refs[count + 1 : 2 * count + 1]
    pieces = refs[2 * count + 1 : 2 * count + 4]
    held, (line, sem) = refs[2 * count + 4 : -2], refs[-2:]
    into = [pltpu.make_async_copy(*pair, sem.at[i]) for i, pair in enumerate(zip(arrays, held))]
    onto = [pltpu.make_async_copy(*pair, sem.at[i]) for i, pair in enumerate(zip(held, outs))]
    for cp in into:
        cp.start()
    for first, second in zip(into, onto):
        first.wait()
        second.start()
    me = lax.axis_index("dp") * lax.axis_size("seq") + lax.axis_index("seq")
    row = 0
    for size, out in zip(VECTORS, pieces):
        for r in range(size // D):
            line[:, r * D : (r + 1) * D] = totals[row + r : row + r + 1]
        row += size // D
        start = me * (size // shards)
        base = pl.multiple_of(start // 128 * 128, 128)
        some = line[:, pl.ds(base, 384)]
        out[...] = pltpu.roll(some, 384 - start % 128, 1)[:, 0 : size // shards]
    for cp in onto:
        cp.wait()


def hand_out(arrays, totals):
    shards = lax.axis_size("dp") * lax.axis_size("seq")
    shapes = [a.shape for a in arrays] + [(1, v // shards) for v in VECTORS]
    return pl.pallas_call(
        functools.partial(hand_out_kernel, shards),
        out_shape=[jax.ShapeDtypeStruct(s, jnp.float32) for s in shapes],
        in_specs=[ANY] * len(arrays) + [VMEM],
        out_specs=[ANY] * len(arrays) + [VMEM] * 3,
        scratch_shapes=[
            *[pltpu.VMEM(a.shape, jnp.float32) for a in arrays],
            pltpu.VMEM((1, max(VECTORS) + 384), jnp.float32),
            pltpu.SemaphoreType.DMA((len(arrays),)),
        ],
        name="hand_out",
    )(*arrays, totals)


def on_device(
    tokens,
    qkv_weight,
    out_weight,
    expand_weight,
    contract_weight,
    bias_vectors,
    gain_vectors,
    ffn_bias,
    random_blocks,
    cotangent,
):
    shards = lax.axis_size("dp") * lax.axis_size("seq")
    me = lax.axis_index("dp") * lax.axis_size("seq") + lax.axis_index("seq")
    planes = kernel_planes()
    rows = tokens.reshape(TOK_SEQ, D)
    weights = (qkv_weight, expand_weight, out_weight, contract_weight)
    vectors = (bias_vectors, gain_vectors, ffn_bias)
    if planes:
        vec = jnp.concatenate(vectors).astype(jnp.float32)
        vec = jnp.pad(vec, (0, -vec.size % 128)).reshape(1, -1)
        qkv, first, out, second = [w.reshape(-1, 128) for w in weights]
    else:
        gather = functools.partial(lax.all_gather, axis_name=("dp", "seq"), axis=0, tiled=True)
        placed = [gather(v).astype(jnp.float32) for v in vectors]
        qkv, first, out, second = [gather(w) for w in weights]
        qkv = qkv.reshape(3 * UNITS, UNIT, D)
        first, out = first.reshape(UNITS, UNIT, FF), out.reshape(UNITS, UNIT, D)
        first = jnp.concatenate([first, out], axis=2)
        second = second.reshape(UNITS, FF // UNITS, D)
        vec = jnp.pad(jnp.concatenate(placed).reshape(-1, D), ((0, 4), (0, 0)))
    (
        result,
        d_sum1,
        kv,
        queries,
        picks,
        lse,
        d_heads,
        d_expand,
        d_contract,
        d_out,
        small,
        d_ffn,
        w_all,
        links,
    ) = front(
        rows, cotangent.reshape(TOK_SEQ, D), random_blocks, vec, qkv, first, out, second, planes
    )
    d_tokens, totals, *grads = back(
        (kv, queries, picks, links, lse, d_heads),
        (rows, w_all, d_sum1, small, d_ffn),
        (d_expand, d_contract, d_out),
        planes,
    )
    if planes:
        result, d_tokens, *grads = hand_out((result, d_tokens, *grads), totals)
        grads, vectors = grads[:4], [v.reshape(-1) for v in grads[4:]]
    else:
        grads = [grads[0], d_out, d_expand, d_contract]
        *vectors, d_qkv, d_out, d_expand, d_contract = [
            lax.psum_scatter(
                g.astype(jnp.float32).reshape(-1),
                ("dp", "seq"),
                scatter_dimension=0,
                tiled=True,
            )
            for g in (totals[0:6], totals[6:8], totals[8 : 8 + FF // D], *grads)
        ]
        grads = (d_qkv, d_out, d_expand, d_contract)
    return (result[None], d_tokens[None], *[g.reshape(-1) for g in grads], *vectors)


def solution(mesh):
    return jax.shard_map(
        on_device,
        mesh=mesh,
        in_specs=(
            P("dp", "seq", None),
            P(("dp", "seq")),
            P(("dp", "seq")),
            P(("dp", "seq")),
            P(("dp", "seq")),
            P(("dp", "seq")),
            P(("dp", "seq")),
            P(("dp", "seq")),
            P("dp", None, "seq", None),
            P("dp", "seq", None),
        ),
        out_specs=(
            P("dp", "seq", None),
            P("dp", "seq", None),
            P(("dp", "seq")),
            P(("dp", "seq")),
            P(("dp", "seq")),
            P(("dp", "seq")),
            P(("dp", "seq")),
            P(("dp", "seq")),
            P(("dp", "seq")),
        ),
        check_vma=False,
    )
```

```python
import functools

import jax
import jax.numpy as jnp
from jax import lax
from jax.experimental import pallas as pl
from jax.experimental.pallas import tpu as pltpu
from jax.sharding import PartitionSpec as P

MESH = pl.DeviceIdType.MESH

D = 768
FF = 3072
H = 12
HD = 64
BLOCK = 64
TOK_SEQ = 256
SEQ_GRP = 1
BPD = 4


norm_eps = 1e-12
masked_score = -1e30


def matmul(left, right):
    return jnp.dot(left, right, preferred_element_type=jnp.float32)


def inner_rows(left, right):
    return lax.dot_general(
        left, right, (((0,), (0,)), ((), ())), preferred_element_type=jnp.float32
    )


def outer_cols(left, right):
    return lax.dot_general(
        left, right, (((1,), (1,)), ((), ())), preferred_element_type=jnp.float32
    )


def normalize(value, gain, shift):
    mean = jnp.mean(value, axis=-1, keepdims=True)
    centred = value - mean
    inverse = lax.rsqrt(jnp.mean(centred * centred, axis=-1, keepdims=True) + norm_eps)
    normed = centred * inverse
    return (normed * gain + shift, normed, inverse)


def normalize_back(grad, normed, inverse, gain):
    scaled = grad * gain
    centred = scaled - jnp.mean(scaled, axis=-1, keepdims=True)
    return inverse * (centred - normed * jnp.mean(scaled * normed, axis=-1, keepdims=True))


def place(nz):
    y = lax.axis_index("dp")
    s = lax.axis_index("seq")
    return {"y": y, "z": s // 4, "x": (s // 2) % 2, "c": s % 2}

def device(p):
    return (p["y"], p["z"] * 4 + p["x"] * 2 + p["c"])

def chip(p, nz):
    return (p["y"] * nz + p["z"]) * 2 + p["x"]

def index(p, nz):
    return chip(p, nz) * 2 + p["c"]

def nearest(m, n, j):
    if n == 2:
        return m if j == 0 else 1 - m
    out = 0
    for i in range(n):
        rank = sorted(range(n), key=lambda s: (abs(s - i), s))
        out = jnp.where(m == i, rank[j], out)
    return out

def combine(dst, srcs):
    rows, cols = dst.shape
    step = min(cols, max(128, (24 * 1024 // rows) // 128 * 128))
    while cols % step:
        step -= 128
    def part(sl):
        total = srcs[0][:, sl].astype(jnp.float32)
        for s in srcs[1:]:
            total = total + s[:, sl].astype(jnp.float32)
        dst[:, sl] = total.astype(dst.dtype)
    if cols == step:
        part(slice(None))
    else:
        def body(i, _):
            part(pl.ds(pl.multiple_of(i * step, 128), step))
            return 0
        lax.fori_loop(0, cols // step, body, 0)

def owner(head, n):
    return head * n // H


def owned(place, n):
    head = (place * H + n - 1) // n
    return jnp.minimum(head, H - 1), jnp.logical_and(head < H, owner(head, n) == place)


def post(place, h, pairs, sems, act, n):
    to = owner(h, n)
    for i, (src, dst) in enumerate(pairs):

        @pl.when(to != place)
        def _():
            act(
                pltpu.make_async_remote_copy(
                    src_ref=src.at[h],
                    dst_ref=dst(place),
                    send_sem=sems[0].at[i, h],
                    recv_sem=sems[1].at[i, place],
                    device_id=(lax.axis_index("dp"), to),
                    device_id_type=MESH,
                )
            )


def walk_to_owners(n, place, head, pairs, sems, act):
    def body(k, _):
        post(place, (head + 1 + k) % H, pairs, sems, act, n)
        return 0

    lax.fori_loop(0, H, body, 0)


def finish_to_owners(n, place, head, pairs, sems):
    walk_to_owners(n, place, head, pairs, sems, lambda cp: cp.wait_send())


def wait_to_owner(n, place, head, mine, pairs, sems):
    @pl.when(mine)
    def _():
        for i, (src, dst) in enumerate(pairs):
            cp = pltpu.make_async_copy(src.at[head], dst(place), sems[2].at[i])
            cp.start()
            cp.wait()

        def body(k, _):
            s = (place + 1 + k) % n
            for i, (src, dst) in enumerate(pairs):
                pltpu.make_async_remote_copy(
                    src_ref=src.at[0],
                    dst_ref=dst(s),
                    send_sem=sems[0].at[i, 0],
                    recv_sem=sems[1].at[i, s],
                    device_id=(lax.axis_index("dp"), place),
                    device_id_type=MESH,
                ).wait_recv()
            return 0

        lax.fori_loop(0, n - 1, body, 0)


def send_to_owners(n, place, head, mine, pairs, sems, meanwhile):
    walk_to_owners(n, place, head, pairs, sems, lambda cp: cp.start())
    meanwhile()
    wait_to_owner(n, place, head, mine, pairs, sems)
    finish_to_owners(n, place, head, pairs, sems)


def walk_from_owners(n, place, head, src, dst, sems, act):
    row = lax.axis_index("dp")

    def body(k, _):
        to = (place + 1 + k) % n
        act(
            pltpu.make_async_remote_copy(
                src_ref=src.at[to],
                dst_ref=dst.at[head],
                send_sem=sems[0].at[0, to],
                recv_sem=sems[1].at[0, head],
                device_id=(row, to),
                device_id_type=MESH,
            )
        )
        return 0

    lax.fori_loop(0, n - 1, body, 0)


def start_from_owners(n, place, head, mine, src, dst, sems):
    @pl.when(mine)
    def _():
        walk_from_owners(n, place, head, src, dst, sems, lambda cp: cp.start())
        cp = pltpu.make_async_copy(src.at[place], dst.at[head], sems[2].at[0])
        cp.start()
        cp.wait()


def wait_head(n, place, h, src, dst, sems):
    @pl.when(owner(h, n) != place)
    def _():
        pltpu.make_async_remote_copy(
            src_ref=src.at[0],
            dst_ref=dst.at[h],
            send_sem=sems[0].at[0, 0],
            recv_sem=sems[1].at[0, h],
            device_id=(lax.axis_index("dp"), place),
            device_id_type=MESH,
        ).wait_recv()


def wait_from_owners(n, place, head, src, dst, sems):
    def body(k, _):
        wait_head(n, place, (head + k) % H, src, dst, sems)
        return 0

    lax.fori_loop(0, H, body, 0)


def finish_from_owners(n, place, head, mine, src, dst, sems):
    @pl.when(mine)
    def _():
        walk_from_owners(n, place, head, src, dst, sems, lambda cp: cp.wait_send())


def swap_halves(tile):
    return pltpu.roll(tile, HD, tile.ndim - 1)


def low_lanes(shape):
    return lax.broadcasted_iota(jnp.int32, shape, len(shape) - 1) < HD


def exchange_sems(n, pairs=1):
    return [
        pltpu.SemaphoreType.DMA((pairs, max(n, H))),
        pltpu.SemaphoreType.DMA((pairs, max(n, H))),
        pltpu.SemaphoreType.DMA((pairs,)),
    ]


ANY = pl.BlockSpec(memory_space=pl.ANY)
VMEM = pl.BlockSpec(memory_space=pltpu.VMEM)
SMEM = pl.BlockSpec(memory_space=pltpu.SMEM)
MSG = TOK_SEQ + TOK_SEQ // 2


def key_list(i, n, picks_ref):
    last = n * BPD - 1

    def of(b):
        s, r = b // BPD, b % BPD
        picked = [picks_ref[s, 0, r * 3 + j] for j in range(3)]
        return [jnp.maximum(b - 1, 0), b, jnp.minimum(b + 1, last), 0, last] + picked

    return [of(2 * i), of(2 * i + 1)]


def fill_pair(lists, kv_ref, vk_ref, keys, values):
    for j in range(8):
        a, b = lists[0][j], lists[1][j]
        to = slice(j * BLOCK, (j + 1) * BLOCK)
        keys[to, 0:HD] = kv_ref[a][:, 0:HD]
        keys[to, HD:128] = vk_ref[b][:, HD:128]
        values[to, 0:HD] = vk_ref[a][:, 0:HD]
        values[to, HD:128] = kv_ref[b][:, HD:128]


def two_blocks(tile):
    left = low_lanes(tile.shape)
    zero = jnp.zeros_like(tile)
    return jnp.concatenate([jnp.where(left, tile, zero), jnp.where(left, zero, tile)], axis=0)


def pair_scores(i, n, keys, query):
    scores = outer_cols(keys, query)
    left = low_lanes((BLOCK, 128))
    right = jnp.logical_not(left)
    end = n * BPD // 2 - 1
    hide_first = jnp.logical_and(left, i == 0)
    hide_last = jnp.logical_and(right, i == end)
    return jnp.concatenate(
        [
            jnp.where(hide_first, masked_score, scores[0:BLOCK]),
            scores[BLOCK : 2 * BLOCK],
            jnp.where(hide_last, masked_score, scores[2 * BLOCK : 3 * BLOCK]),
            scores[3 * BLOCK :],
        ],
        axis=0,
    )


def turn_pairs(n, kv_ref, vk_ref):
    def body(b, _):
        for t in range(BPD):
            tile = kv_ref[b * BPD + t].astype(jnp.float32)
            vk_ref[b * BPD + t] = swap_halves(tile).astype(jnp.bfloat16)
        return 0

    lax.fori_loop(0, n, body, 0)


def chain_table(n, place, picks_vmem, picks_smem, links_ref):
    none = PICKS * n
    lane = lax.broadcasted_iota(jnp.int32, (n, 128), 1)
    turn = (lax.broadcasted_iota(jnp.int32, (n, 128), 0) + 2 * n - place - 1) % n
    order = jnp.where(lane < PICKS, turn * PICKS + lane, -1)
    picks = picks_vmem[:, 0, :]
    blocks = lax.broadcasted_iota(jnp.int32, (8, 128), 1)

    def body(k, tables):
        before, final = tables
        s = (place + 1 + k) % n
        for j in range(PICKS):
            pick, e = picks_smem[s, 0, j], k * PICKS + j
            before = jnp.where(jnp.logical_and(picks == pick, order > e), e, before)
            final = jnp.where(blocks == pick, e, final)
        return before, final

    start = (jnp.full((n, 128), none, jnp.int32), jnp.full((8, 128), none, jnp.int32))
    before, final = lax.fori_loop(0, n, body, start)
    links_ref[0:n] = before
    links_ref[n : n + 8] = final


PICKS = 3 * BPD
UNITS = 32
WIDE = 768


def greet_row(n, place, mine):
    row = lax.axis_index("dp")
    bar = pltpu.get_barrier_semaphore()

    def body(s, _):
        there = owned(s, n)[1]

        @pl.when(jnp.logical_and(s != place, jnp.logical_or(mine, there)))
        def _():
            pl.semaphore_signal(bar, inc=1, device_id=(row, s), device_id_type=MESH)

        return 0

    lax.fori_loop(0, n, body, 0)
    pl.semaphore_wait(bar, jnp.where(mine, n - 1, H))


def unpack_pair(tiles, odd, shape):
    left = low_lanes(shape)
    a, b = tiles.astype(jnp.float32), odd.astype(jnp.float32)
    return (jnp.where(left, a, swap_halves(b)), jnp.where(left, swap_halves(a), b))


def add_flat(out_ref, base, srcs, width=None):
    rows, cols = srcs[0].shape
    width = width or cols
    for k in range(cols // 128):
        lanes = slice(k * 128, (k + 1) * 128)
        total = srcs[0][:, lanes].astype(jnp.float32)
        for s in srcs[1:]:
            total = total + s[:, lanes].astype(jnp.float32)
        out_ref[pl.ds(base + k, rows, stride=width // 128), :] = total


class Reduction:
    def __init__(self, nz, me, links, direct, own, give, emit, bufs, sems, pending):
        self.nz, self.me, self.links, self.direct = nz, me, links, direct
        self.own, self.give, self.emit = own, give, emit
        self.rc, self.ra, self.rb, self.below, self.above = bufs
        self.csend, self.crecv, self.send, self.recv = sems
        self.pending = pending

    @staticmethod
    def buffers(nz, slab):
        counts = (4 * nz, nz, 2 * nz, nz, nz)
        return [pltpu.VMEM((c,) + slab, jnp.bfloat16) for c in counts]

    @staticmethod
    def semaphores(nz):
        return [pltpu.SemaphoreType.DMA((c * nz,)) for c in (4, 4, 5, 5)]

    def start(self, src, dst, slot, to, cond=None, there=None):
        cp = pltpu.make_async_remote_copy(
            src_ref=src,
            dst_ref=dst,
            send_sem=self.send.at[slot],
            recv_sem=self.recv.at[slot if there is None else there],
            device_id=device(to),
            device_id_type=MESH,
        )
        if cond is None:
            cp.start()
        else:
            pl.when(cond)(cp.start)
        self.pending.append((cp, cond))

    def arrived(self, ref, sem):
        pltpu.make_async_remote_copy(
            src_ref=ref,
            dst_ref=ref,
            send_sem=self.send.at[0],
            recv_sem=sem,
            device_id=device(dict(self.me, c=1 - self.me["c"])),
            device_id_type=MESH,
        ).wait_recv()

    def flip(self, which, f):
        d = self.links[which]
        return 1 - self.me[d] if f else self.me[d]

    def piece(self, z, a, b):
        c = {self.links[0]: a, self.links[1]: b}
        return (c["y"] * self.nz + z) * 2 + c["x"]

    def across(self, which):
        d = self.links[which]
        return dict(self.me, **{d: 1 - self.me[d]})

    def hand_over(self):
        nz = self.nz
        zs = sorted(range(nz), key=lambda z: -abs(2 * z - nz + 1))
        order = [(z, fa, fb) for fb in (1, 0) for fa in (1, 0) for z in zs]

        def one(z, fa, fb):
            def run():
                p = self.piece(z, self.flip(0, fa), self.flip(1, fb))
                cp = pltpu.make_async_remote_copy(
                    src_ref=self.give(p),
                    dst_ref=self.rc.at[p],
                    send_sem=self.csend.at[p],
                    recv_sem=self.crecv.at[p],
                    device_id=device(dict(self.me, c=1 - self.me["c"])),
                    device_id_type=MESH,
                )
                cp.start()
                self.pending.append((cp, None))

            return run

        return [one(*o) for o in order]

    def mine(self, p):
        self.arrived(self.rc.at[p], self.crecv.at[p])
        return [self.own(p), self.rc.at[p]]

    def relay(self, z, p, srcs, bref, aref, sb, sa):
        nz, mz, acc = self.nz, self.me["z"], self.rc.at[p]
        if z > 0:

            @pl.when(mz == 0)
            def _():
                combine(acc, srcs)

            @pl.when(jnp.logical_and(mz > 0, mz < z))
            def _():
                self.arrived(bref, self.recv.at[sb])
                combine(acc, srcs + [bref])

            self.start(acc, bref, sb, dict(self.me, z=jnp.minimum(mz + 1, nz - 1)), mz < z)
        if z < nz - 1:

            @pl.when(mz == nz - 1)
            def _():
                combine(acc, srcs)

            @pl.when(jnp.logical_and(mz < nz - 1, mz > z))
            def _():
                self.arrived(aref, self.recv.at[sa])
                combine(acc, srcs + [aref])

            self.start(acc, aref, sa, dict(self.me, z=jnp.maximum(mz - 1, 0)), mz > z)

    def ends(self, z, bref, aref, sb, sa):
        out = []
        if z > 0:
            self.arrived(bref, self.recv.at[sb])
            out.append(bref)
        if z < self.nz - 1:
            self.arrived(aref, self.recv.at[sa])
            out.append(aref)
        return out

    def steps(self):
        nz, me = self.nz, self.me
        zs = sorted(range(nz), key=lambda z: -abs(2 * z - nz + 1))

        def along_b(z, fa):
            def run():
                a = self.flip(0, fa)
                p = self.piece(z, a, self.flip(1, 1))
                combine(self.rc.at[p], self.mine(p))
                s = z * 2 + a
                self.start(self.rc.at[p], self.rb.at[s], s, self.across(1))

            return run

        def along_a(z):
            def run():
                a = self.flip(0, 1)
                p = self.piece(z, a, self.flip(1, 0))
                s = z * 2 + a
                srcs = self.mine(p)
                self.arrived(self.rb.at[s], self.recv.at[s])
                combine(self.rc.at[p], srcs + [self.rb.at[s]])
                self.start(self.rc.at[p], self.ra.at[z], 2 * nz + z, self.across(0))

            return run

        def chain(z):
            def run():
                p = self.piece(z, self.flip(0, 0), self.flip(1, 0))
                s = z * 2 + self.flip(0, 0)
                srcs = self.mine(p)
                self.arrived(self.rb.at[s], self.recv.at[s])
                self.arrived(self.ra.at[z], self.recv.at[2 * nz + z])
                srcs += [self.rb.at[s], self.ra.at[z]]
                if self.direct:
                    mz = me["z"]

                    @pl.when(mz != z)
                    def _():
                        combine(self.rc.at[p], srcs)

                    to = dict(me, z=z)
                    self.start(
                        self.rc.at[p], self.below.at[mz], 3 * nz + z, to, mz != z, 3 * nz + mz
                    )
                    return
                bref, aref = self.below.at[z], self.above.at[z]
                self.relay(z, p, srcs, bref, aref, 3 * nz + z, 4 * nz + z)

            return run

        def last():
            for z in range(nz):

                @pl.when(me["z"] == z)
                def _():
                    p = self.piece(z, self.flip(0, 0), self.flip(1, 0))
                    s = z * 2 + self.flip(0, 0)
                    srcs = [self.own(p), self.rc.at[p], self.rb.at[s], self.ra.at[z]]
                    if self.direct:
                        for other in range(nz):
                            if other != z:
                                ref = self.below.at[other]
                                self.arrived(ref, self.recv.at[3 * nz + other])
                                srcs.append(ref)
                        self.emit(srcs)
                        return
                    bref, aref = self.below.at[z], self.above.at[z]
                    self.emit(srcs + self.ends(z, bref, aref, 3 * nz + z, 4 * nz + z))

        out = [(1 + i, along_b(z, 1)) for i, z in enumerate(zs)]
        out += [(5 + i, along_b(z, 0)) for i, z in enumerate(zs)]
        out += [(5.5 + i, along_a(z)) for i, z in enumerate(zs)]
        out += [(9.5 + i, chain(z)) for i, z in enumerate(zs)]
        return out + [(20, last)]


class Spread:
    def __init__(self, nz, me, order, at, sems, pending):
        self.nz, self.me, self.order, self.at = nz, me, order, at
        self.send, self.recv, self.csend, self.crecv = sems
        self.pending = pending

    @staticmethod
    def semaphores(nz):
        chips = 4 * nz
        return [pltpu.SemaphoreType.DMA((chips, 4))] + [pltpu.SemaphoreType.DMA((chips,))] * 3

    def copy(self, slot, send, recv, to):
        ref = self.at(slot)
        return pltpu.make_async_remote_copy(
            src_ref=ref,
            dst_ref=ref,
            send_sem=send,
            recv_sem=recv,
            device_id=device(to),
            device_id_type=MESH,
        )

    def start(self, cp, cond=None):
        if cond is None:
            cp.start()
        else:
            pl.when(cond)(cp.start)
        self.pending.append((cp, cond))

    def one(self, steps):
        nz, me = self.nz, self.me
        size = {"y": 2, "z": nz, "x": 2}
        own = not any(steps)

        def run():
            src = dict(me)
            for d, i in zip(self.order, steps):
                src[d] = nearest(me[d], size[d], i)
            c = chip(src, nz)
            slot = c * 2 + me["c"]
            if not own:
                self.copy(slot, self.send.at[c, 0], self.recv.at[c], me).wait_recv()
            stage = 2 if steps[2] else (1 if steps[1] else 0)
            for t in range(stage, 3):
                d = self.order[t]
                onward = t == stage and not own
                if d == "z":
                    up, down = me["z"] < nz - 1, me["z"] > 0
                    if onward:
                        up = jnp.logical_and(up, src["z"] <= me["z"])
                        down = jnp.logical_and(down, src["z"] >= me["z"])
                    above = dict(me, z=jnp.minimum(me["z"] + 1, nz - 1))
                    below = dict(me, z=jnp.maximum(me["z"] - 1, 0))
                    self.start(self.copy(slot, self.send.at[c, 0], self.recv.at[c], above), up)
                    self.start(self.copy(slot, self.send.at[c, 1], self.recv.at[c], below), down)
                elif not (onward and steps[t]):
                    way = 2 if d == "x" else 3
                    to = dict(me, **{d: 1 - me[d]})
                    self.start(self.copy(slot, self.send.at[c, way], self.recv.at[c], to))
            sibling = dict(me, c=1 - me["c"])
            self.start(self.copy(slot, self.csend.at[c], self.crecv.at[c], sibling))

        return run

    def steps(self):
        size = {"y": 2, "z": self.nz, "x": 2}
        n0, n1, n2 = (size[d] for d in self.order)
        return [
            (i0 + i1 + i2, self.one((i0, i1, i2)))
            for i2 in range(n2)
            for i1 in range(n1)
            for i0 in range(n0)
        ]

    def finish(self):
        def body(c, _):
            slot = c * 2 + 1 - self.me["c"]
            self.copy(slot, self.csend.at[c], self.crecv.at[c], self.me).wait_recv()
            return 0

        lax.fori_loop(0, 4 * self.nz, body, 0)


def run_in_order(items, low, high):
    steps = [(w, i, f) for i, item in enumerate(items) for w, f in item.steps()]
    for w, _, f in sorted(steps, key=lambda s: s[:2]):
        if low <= w < high:
            f()


def exchange_partners(me, nz):
    partners = [dict(me, **{d: 1 - me[d]}) for d in ("c", "x", "y")]
    step = 1
    while step < nz:
        partners.append(dict(me, z=me["z"] + step - 2 * step * ((me["z"] // step) % 2)))
        step *= 2
    return partners


def vector_copy(i, value, land, sems, partners):
    return pltpu.make_async_remote_copy(
        src_ref=value.at[i],
        dst_ref=land.at[i],
        send_sem=sems[0].at[i],
        recv_sem=sems[1].at[i],
        device_id=device(partners[i]),
        device_id_type=MESH,
    )


def greet_row_and_y(n, me, place_row):
    bar = pltpu.get_barrier_semaphore()

    def greet(k, _):
        to = (place_row + 1 + k) % n
        pl.semaphore_signal(bar, inc=1, device_id=(me["y"], to), device_id_type=MESH)
        return 0

    lax.fori_loop(0, n - 1, greet, 0)
    pl.semaphore_signal(bar, inc=1, device_id=(1 - me["y"], place_row), device_id_type=MESH)
    return lambda: pl.semaphore_wait(bar, n)


UNIT = D // UNITS
THIRD = FF // UNITS // 3
QKV_ORDERS = (("z", "x", "y"), ("z", "y", "x"), ("x", "y", "z"))
REST = (
    ("second", THIRD, FF // UNITS, ("z", "y", "x")),
    ("first", 0, UNIT, ("z", "x", "y")),
    ("second", 0, THIRD, ("z", "x", "y")),
)


EARLY = {1: (0, 1), 4: (1, 2), 5: (2, 3)}
LATE = ((3, 4), (4, 5), (5, 99), (99, 99), (99, 99))


def from_flat(flat, cols, rows):
    step = cols // 128
    return [flat[pl.ds(k, rows, stride=step), :] for k in range(step)]


def as_matrix(units):
    count, rows, cols = units.shape
    return units.astype(jnp.float32).reshape(count * rows, cols).astype(jnp.bfloat16)


def kernel_planes():
    seq = lax.axis_size("seq")
    if lax.axis_size("dp") != 2 or 2 * seq != UNITS or seq % 4:
        return 0
    return seq // 4


def place_vectors(me, shards, pieces, line, value):
    packed = pieces[...]
    at, row = 0, 0
    value[0] = jnp.zeros_like(value[0])
    for size in VECTORS:
        width = size // shards
        start = me * width
        inside = lax.broadcasted_iota(jnp.int32, packed.shape, 1)
        inside = jnp.logical_and(inside >= at, inside < at + width)
        moved = jnp.where(inside, packed, 0.0)
        line[...] = jnp.zeros_like(line)
        base = pl.multiple_of(start // 128 * 128, 128)
        line[:, pl.ds(base, 384)] = pltpu.roll(moved, (start % 128 - at) % 384, 1)
        for r in range(size // D):
            value[0, row + r : row + r + 1] = line[:, r * D : (r + 1) * D]
        row += size // D
        at += width


def front_kernel(n, nz, *refs):
    rows_ref, cot_ref, picks_ref, vec_in, qkv_in, first_in, out_in, second_in = refs[:8]
    (
        result_ref,
        d_sum1_ref,
        kv_hbm,
        q_hbm,
        picks_hbm,
        lse_ref,
        d_heads,
        dw1_hbm,
        dw2_hbm,
        dwo_hbm,
        small_ref,
        d_ffn_ref,
        w_hbm,
        links_hbm,
    ) = refs[8:22]
    (
        w_ref,
        first_ref,
        second_ref,
        flat,
        value,
        land,
        box_kv,
        box_q,
        kv_ref,
        q_ref,
        vk_ref,
        picks_smem,
        keys,
        values,
        attended,
        inbox,
        grad_box,
        slope_ref,
        active_ref,
        dw1_ref,
        dw2_ref,
        dwo_ref,
        mixed_ref,
        load_sem,
        store_sem,
        keep_sem,
        vsend,
        vrecv,
        links_ref,
        picks_vmem,
        line,
        d_up_ref,
    ) = refs[22:54]
    sems_qkv, sems_in, sems_out = refs[54:57], refs[57:60], refs[60:63]
    rest = list(refs[63:])
    place_row = lax.axis_index("seq")
    head, mine = owned(place_row, n)
    pending = []

    if nz:
        me = place(nz)
        slot = index(me, nz)
        hold = greet_row_and_y(n, me, place_row)
        stages = 3 + (nz - 1).bit_length()

        def take():
            out = rest[:4]
            del rest[:4]
            return out

        def widen(src):
            count = src.shape[0]
            flat[0:count] = src[...].astype(jnp.float32)

        widen(qkv_in)
        for j in range(3):
            step = D // 128
            for k in range(step):
                col = flat[pl.ds(j * UNIT * step + k, UNIT, stride=step), :]
                w_ref[slot * 3 + j, :, k * 128 : (k + 1) * 128] = col.astype(jnp.bfloat16)
        place_vectors(slot, 8 * nz, vec_in, line, value)
        hold()
        qkv_items = [
            Spread(nz, me, order, lambda s, j=j: w_ref.at[s * 3 + j], take(), pending)
            for j, order in enumerate(QKV_ORDERS)
        ]
        buffers = {"first": first_ref, "second": second_ref}

        def part(kind, lo, hi):
            ref = buffers[kind]
            if hi - lo == ref.shape[1]:
                return lambda s: ref.at[s]
            return lambda s: ref.at[s, lo:hi]

        rest_items = [
            Spread(nz, me, order, part(kind, lo, hi), take(), pending)
            for kind, lo, hi, order in REST
        ]
        partners = exchange_partners(me, nz)
        vsems = (vsend, vrecv)
        vector_copy(0, value, land, vsems, partners).start()
        run_in_order(qkv_items, 0, 1)
        for src, dst, at, cols, count in (
            (first_in, first_ref, 0, FF, UNIT),
            (out_in, first_ref, FF, D, UNIT),
            (second_in, second_ref, 0, D, FF // UNITS),
        ):
            widen(src)
            for k, col in enumerate(from_flat(flat, cols, count)):
                dst[slot, :, at + k * 128 : at + (k + 1) * 128] = col.astype(jnp.bfloat16)

        def vector_stage(i):
            vector_copy(i, value, land, vsems, partners).wait_recv()
            value[i + 1] = value[i] + land[i]
            if i + 1 < stages:
                vector_copy(i + 1, value, land, vsems, partners).start()

        for depth in range(1, nz + 2):
            vector_stage(min(depth - 1, stages)) if depth <= stages else None
            run_in_order(qkv_items, depth, depth + 1)
            if depth in EARLY:
                run_in_order(rest_items, *EARLY[depth])
        for i in range(nz + 1, stages):
            vector_stage(i)
        for item in qkv_items:
            item.finish()
        vec = value.at[stages]
    else:
        greet_row(n, place_row, mine)
        loads = [
            pltpu.make_async_copy(src, dst, load_sem.at[i])
            for i, (src, dst) in enumerate(
                ((qkv_in, w_ref), (first_in, first_ref), (second_in, second_ref))
            )
        ]
        for cp in loads:
            cp.start()
        for cp in loads:
            cp.wait()
        vec = vec_in

    def rest_steps(low, high):
        if nz:
            run_in_order(rest_items, low, high)

    rows = rows_ref[...]
    left = low_lanes((TOK_SEQ, 128))
    left_q = low_lanes((BLOCK, 128))
    wide = 256
    parcels = (
        (box_kv, lambda s: kv_ref.at[pl.ds(s * BPD, BPD)]),
        (box_q, lambda s: q_ref.at[s]),
        (picks_ref, lambda s: picks_hbm.at[s]),
    )

    def project_some(step, _):
        g = (place_row + step) % (D // wide)
        cols = pl.ds(pl.multiple_of(g * wide, wide), wide)

        def project(e):
            return matmul(rows, as_matrix(w_ref[e * UNITS : (e + 1) * UNITS, :, cols]))

        q = (project(0) + vec[0:1, cols]) * HD ** (-0.5)
        k = project(1)
        v = project(2) + vec[1:2, cols]
        for p in range(wide // 128):
            h = g * (wide // HD) + p * 2
            lanes = slice(p * 128, (p + 1) * 128)
            kp, vp, qp = k[:, lanes], v[:, lanes], q[:, lanes]
            even, odd = jnp.where(left, kp, swap_halves(vp)), jnp.where(left, swap_halves(kp), vp)
            for t in range(BPD):
                part = slice(t * BLOCK, (t + 1) * BLOCK)
                box_kv[h, t] = even[part].astype(jnp.bfloat16)
                box_kv[h + 1, t] = odd[part].astype(jnp.bfloat16)
            turned = swap_halves(qp)
            for t in range(BPD // 2):
                a = slice(2 * t * BLOCK, (2 * t + 1) * BLOCK)
                b = slice((2 * t + 1) * BLOCK, (2 * t + 2) * BLOCK)
                to = slice(t * BLOCK, (t + 1) * BLOCK)
                box_q[h, to, :] = jnp.where(left_q, qp[a], turned[b]).astype(jnp.bfloat16)
                box_q[h + 1, to, :] = jnp.where(left_q, turned[a], qp[b]).astype(jnp.bfloat16)
            for u in range(2):
                post(place_row, h + u, parcels, sems_qkv, lambda cp: cp.start(), n)
        return 0

    lax.fori_loop(0, D // wide, project_some, 0)
    rest_steps(*LATE[0])
    wait_to_owner(n, place_row, head, mine, parcels, sems_qkv)

    keep = (
        pltpu.make_async_copy(kv_ref, kv_hbm, keep_sem.at[0]),
        pltpu.make_async_copy(q_ref, q_hbm, keep_sem.at[3]),
    )
    keep_w = pltpu.make_async_copy(w_ref, w_hbm, keep_sem.at[2])
    keep_w.start()
    keep_links = pltpu.make_async_copy(links_ref, links_hbm, keep_sem.at[4])
    groups = 4

    @pl.when(mine)
    def _():
        for copy in keep:
            copy.start()
        copies = (
            pltpu.make_async_copy(picks_hbm, picks_smem, keep_sem.at[1]),
            pltpu.make_async_copy(picks_hbm, picks_vmem, keep_sem.at[5]),
        )
        for cp in copies:
            cp.start()
        for cp in copies:
            cp.wait()
        turn_pairs(n, kv_ref, vk_ref)
        chain_table(n, place_row, picks_vmem, picks_smem, links_ref)
        keep_links.start()

    def attend_some(k, _):
        s = (place_row + 1 + k) % n
        for t in range(BPD // 2):
            i = s * (BPD // 2) + t
            fill_pair(key_list(i, n, picks_smem), kv_ref, vk_ref, keys.at[t], values.at[t])
        for t in range(BPD // 2):
            i = s * (BPD // 2) + t
            part = slice(t * BLOCK, (t + 1) * BLOCK)
            query = two_blocks(q_ref[s, part, :])
            scores = pair_scores(i, n, keys[t], query)
            top = jnp.max(scores, axis=0, keepdims=True)
            weights = jnp.exp(scores - top)
            total = jnp.sum(weights, axis=0, keepdims=True)
            probs = (weights * (1.0 / total)).astype(jnp.bfloat16)
            full = inner_rows(probs, values[t])
            attended[s, part, :] = jnp.where(left_q, full[:BLOCK], full[BLOCK:]).astype(
                jnp.bfloat16
            )
            lse_ref[i] = top + jnp.log(total)

        @pl.when(s != place_row)
        def _():
            pltpu.make_async_remote_copy(
                src_ref=attended.at[s],
                dst_ref=inbox.at[head],
                send_sem=sems_in[0].at[0, s],
                recv_sem=sems_in[1].at[0, head],
                device_id=(lax.axis_index("dp"), s),
                device_id_type=MESH,
            ).start()

        return 0

    for g in range(groups):

        @pl.when(mine)
        def _():
            lax.fori_loop(g * (n // groups), (g + 1) * (n // groups), attend_some, 0)

        rest_steps(*LATE[1 + g])

    @pl.when(mine)
    def _():
        cp = pltpu.make_async_copy(attended.at[place_row], inbox.at[head], sems_in[2].at[0])
        cp.start()
        cp.wait()

    if nz:
        for item in rest_items:
            item.finish()
    wait_from_owners(n, place_row, head, attended, inbox, sems_in)

    for h in range(0, H, 2):
        for t in range(BPD // 2):
            part = slice(t * BLOCK, (t + 1) * BLOCK)
            a, b = unpack_pair(inbox[h, part, :], inbox[h + 1, part, :], (BLOCK, 128))
            lanes = slice(h * HD, (h + 2) * HD)
            mixed_ref[2 * t * BLOCK : (2 * t + 1) * BLOCK, lanes] = a.astype(jnp.bfloat16)
            mixed_ref[(2 * t + 1) * BLOCK : (2 * t + 2) * BLOCK, lanes] = b.astype(jnp.bfloat16)
    out_w = as_matrix(first_ref[:, :, FF : FF + D])
    hidden1 = rows_ref[...].astype(jnp.float32) + matmul(mixed_ref[...], out_w) + vec[2:3]
    normed_out1, normed1, inverse1 = normalize(hidden1, vec[6:7], vec[3:4])
    lowered = normed_out1.astype(jnp.bfloat16)
    per = UNITS * WIDE // FF

    def second_rows(c):
        return second_ref[pl.ds(c * per, per)].reshape(WIDE, D)

    def up_step(c, hidden):
        cols = pl.ds(pl.multiple_of(c * WIDE, WIDE), WIDE)
        up = matmul(lowered, as_matrix(first_ref[:, :, cols])) + vec[pl.ds(8 + c, 1)]
        square = up * up
        inner = (2 / jnp.pi) ** 0.5 * (up + 0.044715 * up * square)
        curve = jnp.tanh(inner)
        active = (0.5 * up * (1 + curve)).astype(jnp.bfloat16)
        slope_ref[:, cols] = 0.5 * (1 + curve) + 0.5 * up * (1 - curve * curve) * (
            (2 / jnp.pi) ** 0.5 * (1 + 3 * 0.044715 * square)
        )
        active_ref[:, cols] = active
        return hidden + matmul(active, second_rows(c))

    hidden2 = lax.fori_loop(0, FF // WIDE, up_step, normed_out1 + vec[4:5])
    result, normed2, inverse2 = normalize(hidden2, vec[7:8], vec[5:6])
    result_ref[...] = result
    grad = cot_ref[...].astype(jnp.float32)
    d_sum2 = normalize_back(grad, normed2, inverse2, vec[7:8])
    d_down = d_sum2.astype(jnp.bfloat16)

    def add_rows(x):
        return jnp.sum(x, axis=0, keepdims=True)

    small_ref[2:3] = add_rows(d_down.astype(jnp.float32))
    small_ref[3:4] = add_rows(grad)
    small_ref[5:6] = add_rows(grad * normed2)

    def stores(c):
        cols = pl.ds(pl.multiple_of(c * WIDE, WIDE), WIDE)
        slabs = pl.ds(c * per, per)
        return (
            pltpu.make_async_copy(dw1_ref.at[:, :, cols], dw1_hbm.at[:, :, cols], store_sem.at[0, c]),
            pltpu.make_async_copy(dw2_ref.at[slabs], dw2_hbm.at[slabs], store_sem.at[1, c]),
        )

    def back_step(c, d_norm1):
        cols = pl.ds(pl.multiple_of(c * WIDE, WIDE), WIDE)
        d_active = outer_cols(d_down, second_rows(c))
        d_up = (d_active * slope_ref[:, cols]).astype(jnp.bfloat16)
        d_ffn_ref[:, cols] = add_rows(d_up.astype(jnp.float32))
        d_up_ref[:, cols] = d_up
        return d_norm1 + outer_cols(d_up, as_matrix(first_ref[:, :, cols]))

    d_norm1 = lax.fori_loop(0, FF // WIDE, back_step, d_sum2)
    small_ref[1:2] = add_rows(d_norm1)
    small_ref[4:5] = add_rows(d_norm1 * normed1)
    d_sum1 = normalize_back(d_norm1, normed1, inverse1, vec[6:7])
    d_sum1_ref[...] = d_sum1
    d_attn = d_sum1.astype(jnp.bfloat16)
    small_ref[0:1] = add_rows(d_attn.astype(jnp.float32))
    d_mixed = outer_cols(d_attn, as_matrix(first_ref[:, :, FF : FF + D]))
    for h in range(0, H, 2):
        for t in range(BPD // 2):
            part = slice(t * BLOCK, (t + 1) * BLOCK)
            lanes = slice(h * HD, (h + 2) * HD)
            a, b = unpack_pair(
                d_mixed[2 * t * BLOCK : (2 * t + 1) * BLOCK, lanes],
                d_mixed[(2 * t + 1) * BLOCK : (2 * t + 2) * BLOCK, lanes],
                (BLOCK, 128),
            )
            grad_box[h, part, :] = a.astype(jnp.bfloat16)
            grad_box[h + 1, part, :] = b.astype(jnp.bfloat16)

    store_out = pltpu.make_async_copy(dwo_ref, dwo_hbm, load_sem.at[0])

    def weight_grads(c, _):
        cols = pl.ds(pl.multiple_of(c * WIDE, WIDE), WIDE)
        dw2 = inner_rows(active_ref[:, cols], d_down)
        dw2_ref[pl.ds(c * per, per)] = dw2.reshape(per, FF // UNITS, D).astype(jnp.bfloat16)
        dw1 = inner_rows(lowered, d_up_ref[:, cols])
        dw1_ref[:, :, cols] = dw1.reshape(UNITS, UNIT, WIDE).astype(jnp.bfloat16)
        for cp in stores(c):
            cp.start()
        return 0

    def late():
        lax.fori_loop(0, FF // WIDE, weight_grads, 0)
        dwo = inner_rows(mixed_ref[...], d_attn).reshape(UNITS, UNIT, D)
        dwo_ref[...] = dwo.astype(jnp.bfloat16)
        store_out.start()

    send_to_owners(n, place_row, head, mine, ((grad_box, lambda s: d_heads.at[s]),), sems_out, late)
    store_out.wait()

    def drain(c, _):
        for cp in stores(c):
            cp.wait()
        return 0

    lax.fori_loop(0, FF // WIDE, drain, 0)

    @pl.when(mine)
    def _():
        for copy in keep:
            copy.wait()
        keep_links.wait()

    keep_w.wait()
    finish_from_owners(n, place_row, head, mine, attended, inbox, sems_in)
    finish_to_owners(n, place_row, head, parcels, sems_qkv)
    if nz:
        for i in range(stages):
            vector_copy(i, value, land, vsems, partners).wait_send()
    for cp, cond in pending:
        if cond is None:
            cp.wait_send()
        else:
            pl.when(cond)(cp.wait_send)


def front(rows, cotangent, picks, vec, qkv, first, out, second, nz):
    n = lax.axis_size("seq")
    low, full = jnp.bfloat16, jnp.float32
    picks = jnp.pad(picks.reshape(H, 1, BPD * 3), ((0, 0), (0, 7), (0, 128 - BPD * 3)))
    part = (TOK_SEQ // 2, 128)
    pairs = n * BPD // 2
    units = [(UNITS, UNIT, FF), (UNITS, FF // UNITS, D), (UNITS, UNIT, D)]
    shapes = [((TOK_SEQ, D), full), ((TOK_SEQ, D), full)]
    shapes += [((n * BPD, BLOCK, 128), low), ((n,) + part, low)]
    shapes += [((n, 8, 128), jnp.int32), ((pairs, 1, 128), full), ((n,) + part, low)]
    shapes += [(u, low) for u in units] + [((8, D), full), ((1, FF), full)]
    shapes += [((3 * UNITS, UNIT, D), low), ((n + 8, 128), jnp.int32)]
    stages = 3 + (max(nz, 1) - 1).bit_length()
    where = VMEM if nz else ANY
    extra = []
    for _ in range(6 if nz else 0):
        extra += Spread.semaphores(nz)
    return pl.pallas_call(
        functools.partial(front_kernel, n, nz),
        out_shape=[jax.ShapeDtypeStruct(s, d) for s, d in shapes],
        in_specs=[VMEM, VMEM, ANY, VMEM, where, where, where, where],
        out_specs=[VMEM, VMEM, ANY, ANY, ANY, VMEM, ANY, ANY, ANY, ANY, VMEM, VMEM, ANY, ANY],
        scratch_shapes=[
            pltpu.VMEM((3 * UNITS, UNIT, D), low),
            pltpu.VMEM((UNITS, UNIT, FF + D), low),
            pltpu.VMEM((UNITS, FF // UNITS, D), low),
            pltpu.VMEM((UNIT * FF // 128, 128), full),
            pltpu.VMEM((stages + 1, 16, D), full),
            pltpu.VMEM((stages, 16, D), full),
            pltpu.VMEM((H, BPD, BLOCK, 128), low),
            pltpu.VMEM((H,) + part, low),
            pltpu.VMEM((n * BPD, BLOCK, 128), low),
            pltpu.VMEM((n,) + part, low),
            pltpu.VMEM((n * BPD, BLOCK, 128), low),
            pltpu.SMEM((n, 8, 128), jnp.int32),
            pltpu.VMEM((BPD // 2, 8 * BLOCK, 128), low),
            pltpu.VMEM((BPD // 2, 8 * BLOCK, 128), low),
            pltpu.VMEM((n,) + part, low),
            pltpu.VMEM((H,) + part, low),
            pltpu.VMEM((H,) + part, low),
            pltpu.VMEM((TOK_SEQ, FF), full),
            pltpu.VMEM((TOK_SEQ, FF), low),
            *[pltpu.VMEM(u, low) for u in units],
            pltpu.VMEM((TOK_SEQ, D), low),
            pltpu.SemaphoreType.DMA((3,)),
            pltpu.SemaphoreType.DMA((2, FF // WIDE)),
            pltpu.SemaphoreType.DMA((6,)),
            pltpu.SemaphoreType.DMA((stages,)),
            pltpu.SemaphoreType.DMA((stages,)),
            pltpu.VMEM((n + 8, 128), jnp.int32),
            pltpu.VMEM((n, 8, 128), jnp.int32),
            pltpu.VMEM((1, max(VECTORS) + 384), full),
            pltpu.VMEM((TOK_SEQ, FF), low),
            *exchange_sems(n, 3),
            *exchange_sems(n),
            *exchange_sems(n),
            *extra,
        ],
        compiler_params=pltpu.CompilerParams(
            collective_id=0, has_side_effects=True, vmem_limit_bytes=60 << 20
        ),
        name="front",
    )(rows, cotangent, picks, vec, qkv, first, out, second)


FFN_KINDS = (
    ("expand", 0, UNIT, ("x", "y")),
    ("contract", THIRD, FF // UNITS, ("y", "x")),
    ("contract", 0, THIRD, ("x", "y")),
    ("out", 0, UNIT, ("x", "y")),
)
QKV_KINDS = (
    (0, 0, D, ("x", "y")),
    (1, 0, D, ("y", "x")),
    (2, 0, D // 2, ("x", "y")),
    (2, D // 2, D, ("y", "x")),
)
QKV_UNITS = 3 * UNITS


FFN_WITH = ((1,), (2,), (3,), (4,))
FFN_AFTER = ((5, 5.5, 6, 6.5, 7, 7.5, 8, 8.5), (9.5, 10.5, 11.5, 12.5))


def send_one(sems, src, dst, head, to):
    return pltpu.make_async_remote_copy(
        src_ref=src.at[to],
        dst_ref=dst.at[head],
        send_sem=sems[0].at[0, to],
        recv_sem=sems[1].at[0, head],
        device_id=(lax.axis_index("dp"), to),
        device_id_type=MESH,
    )


def back_kernel(n, nz, *refs):
    kv_ref, q_ref, picks_ref, links_ref, lse_ref, grad_ref = refs[:6]
    rows_ref, w_hbm, d_sum1_ref, small_ref, ffn_ref, dw1, dw2, dwo = refs[6:14]
    d_tokens_ref, vec_out = refs[14:16]
    outs = refs[16 : 20 if nz else 17]
    rest = list(refs[20 if nz else 17 :])
    vk_ref, keys, values, acc, out_q, out_kv, inbox_q, inbox_kv, proj, w_ref, ownq = rest[:11]
    turned_rows, value, land, load_sem, vsend, vrecv = rest[11:17]
    sems_q, sems_kv = rest[17:20], rest[20:23]
    own1, own2, owno = rest[23:26] if nz else (None, None, None)
    rest = rest[26:]
    place_row = lax.axis_index("seq")
    head, mine = owned(place_row, n)
    blocks, none = n * BPD, n * BPD + n * PICKS
    pending = []

    load_w = pltpu.make_async_copy(w_hbm, w_ref, load_sem.at[0])
    load_w.start()
    if nz:
        me = place(nz)
        core = me["c"]
        loads = [
            pltpu.make_async_copy(src, dst, load_sem.at[1 + i])
            for i, (src, dst) in enumerate(((dw1, own1), (dw2, own2), (dwo, owno)))
        ]
        for cp in loads:
            cp.start()
        hold = greet_row_and_y(n, me, place_row)
    else:
        greet_row(n, place_row, mine)

    @pl.when(mine)
    def _():
        turn_pairs(n, kv_ref, vk_ref)

        def clear(b, _):
            acc[b] = jnp.zeros((BLOCK, 128), jnp.float32)
            return 0

        lax.fori_loop(0, blocks, clear, 0)
        clear(none, 0)

    def take(count):
        out = rest[:count]
        del rest[:count]
        return out

    def ffn_item(kind, lo, hi, links):
        far, near = {"expand": (dw1, own1), "contract": (dw2, own2), "out": (dwo, owno)}[kind]
        target = outs[("out", "expand", "contract").index(kind) + 1]
        whole = hi - lo == far.shape[1]

        def at(ref, t):
            return ref.at[t] if whole else ref.at[t, lo:hi]

        return Reduction(
            nz,
            me,
            links,
            False,
            lambda p: at(near, p * 2 + core),
            lambda p: at(far, p * 2 + 1 - core),
            lambda srcs: add_flat(target, lo * (far.shape[2] // 128), srcs),
            take(5),
            take(4),
            pending,
        )

    def qkv_item(j, lo, hi, links):
        def at(t):
            ref = ownq.at[t * 3 + j]
            return ref if hi - lo == D else ref.at[:, lo:hi]

        return Reduction(
            nz,
            me,
            links,
            True,
            lambda p: at(p * 2 + core),
            lambda p: at(p * 2 + 1 - core),
            lambda srcs: add_flat(outs[0], (j * UNIT * D + lo) // 128, srcs, D),
            take(5),
            take(4),
            pending,
        )

    def hand_all(items):
        for group in zip(*[i.hand_over() for i in items]):
            for f in group:
                f()

    def ordered(items):
        steps = [(w + 0.01 * i, f) for i, item in enumerate(items) for w, f in item.steps()]
        return sorted(steps, key=lambda s: s[0])

    turned_rows[...] = rows_ref[...].T
    ffn_steps = []
    if nz:
        ffn = [ffn_item(*k) for k in FFN_KINDS]
        qkv = [qkv_item(*k) for k in QKV_KINDS]
        ffn_steps = ordered(ffn)
        hold()
        hand_all(ffn)
        for cp in loads:
            cp.wait()

    def ffn_run(*wanted):
        for at in wanted:
            for w, f in ffn_steps:
                if abs(w - at) < 0.1:
                    f()

    left = low_lanes((BLOCK, 128))
    both = range(BPD // 2)

    def attend_some(k, _):
        s = (place_row + 1 + k) % n
        lists = [key_list(s * (BPD // 2) + t, n, picks_ref) for t in both]
        for t in both:
            fill_pair(lists[t], kv_ref, vk_ref, keys.at[t], values.at[t])
        parts = []
        for t in both:
            i = s * (BPD // 2) + t
            part = slice(t * BLOCK, (t + 1) * BLOCK)
            query = two_blocks(q_ref[s, part, :])
            grad = two_blocks(grad_ref[s, part, :])
            probs = jnp.exp(pair_scores(i, n, keys[t], query) - lse_ref[i])
            d_probs = outer_cols(values[t], grad)
            rows = jnp.sum(probs * d_probs, axis=0, keepdims=True)
            d_scores = (probs * (d_probs - rows)).astype(jnp.bfloat16)
            d_values = matmul(probs.astype(jnp.bfloat16), grad)
            d_keys = matmul(d_scores, query)
            full = inner_rows(d_scores, keys[t]) * HD ** (-0.5)
            out_q[s, part, :] = jnp.where(left, full[:BLOCK], full[BLOCK:]).astype(jnp.bfloat16)
            parts.append((d_keys, d_values))

        @pl.when(s != place_row)
        def _():
            send_one(sems_q, out_q, inbox_q, head, s).start()

        for t in both:
            tiles = []
            for j in range(8):
                part = slice(j * BLOCK, (j + 1) * BLOCK)
                dk, dv = parts[t][0][part], parts[t][1][part]
                a = jnp.where(left, dk, swap_halves(dv))
                b = jnp.where(left, swap_halves(dk), dv)
                tiles.append((a, b))
            a = (s * (BPD // 2) + t) * 2
            acc[jnp.maximum(a - 1, 0)] += tiles[0][0]
            acc[a] += tiles[1][0] + tiles[0][1]
            acc[a + 1] += tiles[2][0] + tiles[1][1]
            acc[jnp.minimum(a + 2, blocks - 1)] += tiles[2][1]
            acc[0] += tiles[3][0] + tiles[3][1]
            acc[blocks - 1] += tiles[4][0] + tiles[4][1]
            for u in range(2):
                for j in range(3):
                    e = (2 * t + u) * 3 + j
                    acc[blocks + k * PICKS + e] = tiles[5 + j][u] + acc[blocks + links_ref[s, e]]
        return 0

    groups = 4
    for g in range(groups):

        @pl.when(mine)
        def _():
            lax.fori_loop(g * (n // groups), (g + 1) * (n // groups), attend_some, 0)

        ffn_run(*FFN_WITH[g])

    @pl.when(mine)
    def _():
        def close(k, _):
            s = (place_row + 1 + k) % n
            for t in range(BPD):
                b = s * BPD + t
                total = acc[b] + acc[blocks + links_ref[n, b]]
                out_kv[s, t * BLOCK : (t + 1) * BLOCK, :] = total.astype(jnp.bfloat16)

            @pl.when(s != place_row)
            def _():
                send_one(sems_kv, out_kv, inbox_kv, head, s).start()

            return 0

        lax.fori_loop(0, n, close, 0)
        copies = (
            pltpu.make_async_copy(out_q.at[place_row], inbox_q.at[head], sems_q[2].at[0]),
            pltpu.make_async_copy(out_kv.at[place_row], inbox_kv.at[head], sems_kv[2].at[0]),
        )
        for cp in copies:
            cp.start()
        for cp in copies:
            cp.wait()

    ffn_run(*FFN_AFTER[0])

    def head_pair(k, _):
        p = (place_row + k) % (H // 2)
        for u in range(2):
            wait_head(n, place_row, 2 * p + u, out_q, inbox_q, sems_q)
            wait_head(n, place_row, 2 * p + u, out_kv, inbox_kv, sems_kv)
        lanes = pl.ds(pl.multiple_of(p * 128, 128), 128)
        keys_values = unpack_pair(inbox_kv[2 * p], inbox_kv[2 * p + 1], (TOK_SEQ, 128))
        queries = []
        for t in both:
            part = slice(t * BLOCK, (t + 1) * BLOCK)
            queries += unpack_pair(inbox_q[2 * p, part, :], inbox_q[2 * p + 1, part, :], (BLOCK, 128))
        grads = (jnp.concatenate(queries, axis=0), *keys_values)
        for e in range(3):
            proj[e, :, lanes] = grads[e].astype(jnp.bfloat16)
        joined = jnp.concatenate(grads, axis=1).astype(jnp.bfloat16)
        grad = matmul(turned_rows[...], joined).reshape(UNITS, UNIT, 3 * 128).astype(jnp.bfloat16)
        for e in range(3):
            ownq[pl.ds(e * UNITS, UNITS), :, lanes] = grad[:, :, e * 128 : (e + 1) * 128]
        return 0

    lax.fori_loop(0, H // 2, head_pair, 0)
    qkv_steps = []
    if nz:
        hand_all(qkv)
        qkv_steps = ordered(qkv)

    def qkv_run(low, high):
        for w, f in qkv_steps:
            if low <= w < high:
                f()

    def add_rows(x):
        return jnp.sum(x.astype(jnp.float32), axis=0, keepdims=True)

    value[0, 0:1] = add_rows(proj[0])
    value[0, 1:2] = add_rows(proj[2])
    value[0, 2:8] = small_ref[0:6]
    for c in range(FF // D):
        value[0, 8 + c : 9 + c] = ffn_ref[:, c * D : (c + 1) * D]
    partners = exchange_partners(me, nz) if nz else []
    vsems = (vsend, vrecv)
    if nz:
        vector_copy(0, value, land, vsems, partners).start()

    def vector_stage(i):
        if i < len(partners):
            vector_copy(i, value, land, vsems, partners).wait_recv()
            total = value[i] + land[i]
            if i + 1 < len(partners):
                value[i + 1] = total
                vector_copy(i + 1, value, land, vsems, partners).start()
            else:
                vec_out[...] = total

    qkv_run(1, 5)
    ffn_run(*FFN_AFTER[1])
    vector_stage(0)
    qkv_run(5, 9)
    load_w.wait()
    d_tokens = d_sum1_ref[...]
    for e in range(3):
        d_tokens = d_tokens + outer_cols(proj[e], as_matrix(w_ref[e * UNITS : (e + 1) * UNITS]))
    d_tokens_ref[...] = d_tokens
    vector_stage(1)
    ffn_run(20)
    vector_stage(2)
    qkv_run(9, 20)
    vector_stage(3)
    vector_stage(4)
    qkv_run(20, 99)
    if not nz:
        vec_out[...] = value[0]
        outs[0][...] = ownq[...]
    for i in range(len(partners)):
        vector_copy(i, value, land, vsems, partners).wait_send()
    finish_from_owners(n, place_row, head, mine, out_q, inbox_q, sems_q)
    finish_from_owners(n, place_row, head, mine, out_kv, inbox_kv, sems_kv)
    for cp, cond in pending:
        if cond is None:
            cp.wait_send()
        else:
            pl.when(cond)(cp.wait_send)


def back(heads, local, weight_grads, nz):
    n = lax.axis_size("seq")
    low, full = jnp.bfloat16, jnp.float32
    rows, w_all, d_sum1, small, d_ffn = local
    outs = [((TOK_SEQ, D), full), ((16, D), full)]
    if nz:
        outs += [((3 * UNIT * D // 128, 128), full), ((UNIT * D // 128, 128), full)]
        outs += [((UNIT * FF // 128, 128), full)] * 2
    else:
        outs += [((QKV_UNITS, UNIT, D), low)]
    stages = 3 + (max(nz, 1) - 1).bit_length()
    part = (TOK_SEQ // 2, 128)
    extra = [pltpu.VMEM(g.shape, low) for g in weight_grads] if nz else []
    slabs = [(hi - lo, FF if kind == "expand" else D) for kind, lo, hi, _ in FFN_KINDS]
    slabs += [(UNIT, hi - lo) for _, lo, hi, _ in QKV_KINDS]
    for slab in slabs if nz else ():
        extra += Reduction.buffers(nz, slab)
        extra += Reduction.semaphores(nz)
    return pl.pallas_call(
        functools.partial(back_kernel, n, nz),
        out_shape=[jax.ShapeDtypeStruct(s, d) for s, d in outs],
        in_specs=[VMEM, VMEM, SMEM, SMEM, VMEM, VMEM]
        + [VMEM, ANY, VMEM, VMEM, VMEM, ANY, ANY, ANY],
        out_specs=[VMEM] * len(outs),
        scratch_shapes=[
            pltpu.VMEM((n * BPD, BLOCK, 128), low),
            pltpu.VMEM((BPD // 2, 8 * BLOCK, 128), low),
            pltpu.VMEM((BPD // 2, 8 * BLOCK, 128), low),
            pltpu.VMEM((n * (BPD + PICKS) + 1, BLOCK, 128), full),
            pltpu.VMEM((n,) + part, low),
            pltpu.VMEM((n, TOK_SEQ, 128), low),
            pltpu.VMEM((H,) + part, low),
            pltpu.VMEM((H, TOK_SEQ, 128), low),
            pltpu.VMEM((3, TOK_SEQ, D), low),
            pltpu.VMEM((QKV_UNITS, UNIT, D), low),
            pltpu.VMEM((QKV_UNITS, UNIT, D), low),
            pltpu.VMEM((D, TOK_SEQ), low),
            pltpu.VMEM((stages, 16, D), full),
            pltpu.VMEM((stages, 16, D), full),
            pltpu.SemaphoreType.DMA((4,)),
            pltpu.SemaphoreType.DMA((stages,)),
            pltpu.SemaphoreType.DMA((stages,)),
            *exchange_sems(n),
            *exchange_sems(n),
            *extra,
        ],
        compiler_params=pltpu.CompilerParams(
            collective_id=5, has_side_effects=True, vmem_limit_bytes=61 << 20
        ),
        name="back",
    )(*heads, *local, *weight_grads)


VECTORS = (6 * D, 2 * D, FF)


def hand_out_kernel(shards, *refs):
    count = (len(refs) - 6) // 3
    arrays, totals, outs = refs[:count], refs[count], refs[count + 1 : 2 * count + 1]
    pieces = refs[2 * count + 1 : 2 * count + 4]
    held, (line, sem) = refs[2 * count + 4 : -2], refs[-2:]
    into = [pltpu.make_async_copy(*pair, sem.at[i]) for i, pair in enumerate(zip(arrays, held))]
    onto = [pltpu.make_async_copy(*pair, sem.at[i]) for i, pair in enumerate(zip(held, outs))]
    for cp in into:
        cp.start()
    for first, second in zip(into, onto):
        first.wait()
        second.start()
    me = lax.axis_index("dp") * lax.axis_size("seq") + lax.axis_index("seq")
    row = 0
    for size, out in zip(VECTORS, pieces):
        for r in range(size // D):
            line[:, r * D : (r + 1) * D] = totals[row + r : row + r + 1]
        row += size // D
        start = me * (size // shards)
        base = pl.multiple_of(start // 128 * 128, 128)
        some = line[:, pl.ds(base, 384)]
        out[...] = pltpu.roll(some, 384 - start % 128, 1)[:, 0 : size // shards]
    for cp in onto:
        cp.wait()


def hand_out(arrays, totals):
    shards = lax.axis_size("dp") * lax.axis_size("seq")
    shapes = [a.shape for a in arrays] + [(1, v // shards) for v in VECTORS]
    return pl.pallas_call(
        functools.partial(hand_out_kernel, shards),
        out_shape=[jax.ShapeDtypeStruct(s, jnp.float32) for s in shapes],
        in_specs=[ANY] * len(arrays) + [VMEM],
        out_specs=[ANY] * len(arrays) + [VMEM] * 3,
        scratch_shapes=[
            *[pltpu.VMEM(a.shape, jnp.float32) for a in arrays],
            pltpu.VMEM((1, max(VECTORS) + 384), jnp.float32),
            pltpu.SemaphoreType.DMA((len(arrays),)),
        ],
        name="hand_out",
    )(*arrays, totals)


def on_device(
    tokens,
    qkv_weight,
    out_weight,
    expand_weight,
    contract_weight,
    bias_vectors,
    gain_vectors,
    ffn_bias,
    random_blocks,
    cotangent,
):
    shards = lax.axis_size("dp") * lax.axis_size("seq")
    me = lax.axis_index("dp") * lax.axis_size("seq") + lax.axis_index("seq")
    planes = kernel_planes()
    rows = tokens.reshape(TOK_SEQ, D)
    weights = (qkv_weight, expand_weight, out_weight, contract_weight)
    vectors = (bias_vectors, gain_vectors, ffn_bias)
    if planes:
        vec = jnp.concatenate(vectors).astype(jnp.float32)
        vec = jnp.pad(vec, (0, -vec.size % 128)).reshape(1, -1)
        qkv, first, out, second = [w.reshape(-1, 128) for w in weights]
    else:
        gather = functools.partial(lax.all_gather, axis_name=("dp", "seq"), axis=0, tiled=True)
        placed = [gather(v).astype(jnp.float32) for v in vectors]
        qkv, first, out, second = [gather(w) for w in weights]
        qkv = qkv.reshape(3 * UNITS, UNIT, D)
        first, out = first.reshape(UNITS, UNIT, FF), out.reshape(UNITS, UNIT, D)
        first = jnp.concatenate([first, out], axis=2)
        second = second.reshape(UNITS, FF // UNITS, D)
        vec = jnp.pad(jnp.concatenate(placed).reshape(-1, D), ((0, 4), (0, 0)))
    (
        result,
        d_sum1,
        kv,
        queries,
        picks,
        lse,
        d_heads,
        d_expand,
        d_contract,
        d_out,
        small,
        d_ffn,
        w_all,
        links,
    ) = front(
        rows, cotangent.reshape(TOK_SEQ, D), random_blocks, vec, qkv, first, out, second, planes
    )
    d_tokens, totals, *grads = back(
        (kv, queries, picks, links, lse, d_heads),
        (rows, w_all, d_sum1, small, d_ffn),
        (d_expand, d_contract, d_out),
        planes,
    )
    if planes:
        result, d_tokens, *grads = hand_out((result, d_tokens, *grads), totals)
        grads, vectors = grads[:4], [v.reshape(-1) for v in grads[4:]]
    else:
        grads = [grads[0], d_out, d_expand, d_contract]
        *vectors, d_qkv, d_out, d_expand, d_contract = [
            lax.psum_scatter(
                g.astype(jnp.float32).reshape(-1),
                ("dp", "seq"),
                scatter_dimension=0,
                tiled=True,
            )
            for g in (totals[0:6], totals[6:8], totals[8 : 8 + FF // D], *grads)
        ]
        grads = (d_qkv, d_out, d_expand, d_contract)
    return (result[None], d_tokens[None], *[g.reshape(-1) for g in grads], *vectors)


def solution(mesh):
    return jax.shard_map(
        on_device,
        mesh=mesh,
        in_specs=(
            P("dp", "seq", None),
            P(("dp", "seq")),
            P(("dp", "seq")),
            P(("dp", "seq")),
            P(("dp", "seq")),
            P(("dp", "seq")),
            P(("dp", "seq")),
            P(("dp", "seq")),
            P("dp", None, "seq", None),
            P("dp", "seq", None),
        ),
        out_specs=(
            P("dp", "seq", None),
            P("dp", "seq", None),
            P(("dp", "seq")),
            P(("dp", "seq")),
            P(("dp", "seq")),
            P(("dp", "seq")),
            P(("dp", "seq")),
            P(("dp", "seq")),
            P(("dp", "seq")),
        ),
        check_vma=False,
    )
```

```python
import functools

import jax
import jax.numpy as jnp
from jax import lax
from jax.experimental import pallas as pl
from jax.experimental.pallas import tpu as pltpu
from jax.sharding import PartitionSpec as P

MESH = pl.DeviceIdType.MESH

D = 768
FF = 3072
H = 12
HD = 64
BLOCK = 64
TOK_SEQ = 256
SEQ_GRP = 1
BPD = 4


norm_eps = 1e-12
masked_score = -1e30


def matmul(left, right):
    return jnp.dot(left, right, preferred_element_type=jnp.float32)


def inner_rows(left, right):
    return lax.dot_general(
        left, right, (((0,), (0,)), ((), ())), preferred_element_type=jnp.float32
    )


def outer_cols(left, right):
    return lax.dot_general(
        left, right, (((1,), (1,)), ((), ())), preferred_element_type=jnp.float32
    )


def normalize(value, gain, shift):
    mean = jnp.mean(value, axis=-1, keepdims=True)
    centred = value - mean
    inverse = lax.rsqrt(jnp.mean(centred * centred, axis=-1, keepdims=True) + norm_eps)
    normed = centred * inverse
    return (normed * gain + shift, normed, inverse)


def normalize_back(grad, normed, inverse, gain):
    scaled = grad * gain
    centred = scaled - jnp.mean(scaled, axis=-1, keepdims=True)
    return inverse * (centred - normed * jnp.mean(scaled * normed, axis=-1, keepdims=True))


def place(nz):
    y = lax.axis_index("dp")
    s = lax.axis_index("seq")
    return {"y": y, "z": s // 4, "x": (s // 2) % 2, "c": s % 2}

def device(p):
    return (p["y"], p["z"] * 4 + p["x"] * 2 + p["c"])

def chip(p, nz):
    return (p["y"] * nz + p["z"]) * 2 + p["x"]

def index(p, nz):
    return chip(p, nz) * 2 + p["c"]

def nearest(m, n, j):
    if n == 2:
        return m if j == 0 else 1 - m
    out = 0
    for i in range(n):
        rank = sorted(range(n), key=lambda s: (abs(s - i), s))
        out = jnp.where(m == i, rank[j], out)
    return out

def combine(dst, srcs):
    rows, cols = dst.shape
    step = min(cols, max(128, (24 * 1024 // rows) // 128 * 128))
    while cols % step:
        step -= 128
    def part(sl):
        total = srcs[0][:, sl].astype(jnp.float32)
        for s in srcs[1:]:
            total = total + s[:, sl].astype(jnp.float32)
        dst[:, sl] = total.astype(dst.dtype)
    if cols == step:
        part(slice(None))
    else:
        def body(i, _):
            part(pl.ds(pl.multiple_of(i * step, 128), step))
            return 0
        lax.fori_loop(0, cols // step, body, 0)

def owner(head, n):
    return head * n // H


def owned(place, n):
    head = (place * H + n - 1) // n
    return jnp.minimum(head, H - 1), jnp.logical_and(head < H, owner(head, n) == place)


def post(place, h, pairs, sems, act, n):
    to = owner(h, n)
    for i, (src, dst) in enumerate(pairs):

        @pl.when(to != place)
        def _():
            act(
                pltpu.make_async_remote_copy(
                    src_ref=src.at[h],
                    dst_ref=dst(place),
                    send_sem=sems[0].at[i, h],
                    recv_sem=sems[1].at[i, place],
                    device_id=(lax.axis_index("dp"), to),
                    device_id_type=MESH,
                )
            )


def walk_to_owners(n, place, head, pairs, sems, act):
    def body(k, _):
        post(place, (head + 1 + k) % H, pairs, sems, act, n)
        return 0

    lax.fori_loop(0, H, body, 0)


def finish_to_owners(n, place, head, pairs, sems):
    walk_to_owners(n, place, head, pairs, sems, lambda cp: cp.wait_send())


def wait_to_owner(n, place, head, mine, pairs, sems):
    @pl.when(mine)
    def _():
        for i, (src, dst) in enumerate(pairs):
            cp = pltpu.make_async_copy(src.at[head], dst(place), sems[2].at[i])
            cp.start()
            cp.wait()

        def body(k, _):
            s = (place + 1 + k) % n
            for i, (src, dst) in enumerate(pairs):
                pltpu.make_async_remote_copy(
                    src_ref=src.at[0],
                    dst_ref=dst(s),
                    send_sem=sems[0].at[i, 0],
                    recv_sem=sems[1].at[i, s],
                    device_id=(lax.axis_index("dp"), place),
                    device_id_type=MESH,
                ).wait_recv()
            return 0

        lax.fori_loop(0, n - 1, body, 0)


def send_to_owners(n, place, head, mine, pairs, sems, meanwhile):
    walk_to_owners(n, place, head, pairs, sems, lambda cp: cp.start())
    meanwhile()
    wait_to_owner(n, place, head, mine, pairs, sems)
    finish_to_owners(n, place, head, pairs, sems)


def walk_from_owners(n, place, head, src, dst, sems, act):
    row = lax.axis_index("dp")

    def body(k, _):
        to = (place + 1 + k) % n
        act(
            pltpu.make_async_remote_copy(
                src_ref=src.at[to],
                dst_ref=dst.at[head],
                send_sem=sems[0].at[0, to],
                recv_sem=sems[1].at[0, head],
                device_id=(row, to),
                device_id_type=MESH,
            )
        )
        return 0

    lax.fori_loop(0, n - 1, body, 0)


def start_from_owners(n, place, head, mine, src, dst, sems):
    @pl.when(mine)
    def _():
        walk_from_owners(n, place, head, src, dst, sems, lambda cp: cp.start())
        cp = pltpu.make_async_copy(src.at[place], dst.at[head], sems[2].at[0])
        cp.start()
        cp.wait()


def wait_head(n, place, h, src, dst, sems):
    @pl.when(owner(h, n) != place)
    def _():
        pltpu.make_async_remote_copy(
            src_ref=src.at[0],
            dst_ref=dst.at[h],
            send_sem=sems[0].at[0, 0],
            recv_sem=sems[1].at[0, h],
            device_id=(lax.axis_index("dp"), place),
            device_id_type=MESH,
        ).wait_recv()


def wait_from_owners(n, place, head, src, dst, sems):
    def body(k, _):
        wait_head(n, place, (head + k) % H, src, dst, sems)
        return 0

    lax.fori_loop(0, H, body, 0)


def finish_from_owners(n, place, head, mine, src, dst, sems):
    @pl.when(mine)
    def _():
        walk_from_owners(n, place, head, src, dst, sems, lambda cp: cp.wait_send())


def swap_halves(tile):
    return pltpu.roll(tile, HD, tile.ndim - 1)


def low_lanes(shape):
    return lax.broadcasted_iota(jnp.int32, shape, len(shape) - 1) < HD


def exchange_sems(n, pairs=1):
    return [
        pltpu.SemaphoreType.DMA((pairs, max(n, H))),
        pltpu.SemaphoreType.DMA((pairs, max(n, H))),
        pltpu.SemaphoreType.DMA((pairs,)),
    ]


ANY = pl.BlockSpec(memory_space=pl.ANY)
VMEM = pl.BlockSpec(memory_space=pltpu.VMEM)
SMEM = pl.BlockSpec(memory_space=pltpu.SMEM)
MSG = TOK_SEQ + TOK_SEQ // 2


def key_list(i, n, picks_ref):
    last = n * BPD - 1

    def of(b):
        s, r = b // BPD, b % BPD
        picked = [picks_ref[s, 0, r * 3 + j] for j in range(3)]
        return [jnp.maximum(b - 1, 0), b, jnp.minimum(b + 1, last), 0, last] + picked

    return [of(2 * i), of(2 * i + 1)]


def fill_pair(lists, kv_ref, vk_ref, keys, values):
    for j in range(8):
        a, b = lists[0][j], lists[1][j]
        to = slice(j * BLOCK, (j + 1) * BLOCK)
        keys[to, 0:HD] = kv_ref[a][:, 0:HD]
        keys[to, HD:128] = vk_ref[b][:, HD:128]
        values[to, 0:HD] = vk_ref[a][:, 0:HD]
        values[to, HD:128] = kv_ref[b][:, HD:128]


def two_blocks(tile):
    left = low_lanes(tile.shape)
    zero = jnp.zeros_like(tile)
    return jnp.concatenate([jnp.where(left, tile, zero), jnp.where(left, zero, tile)], axis=0)


def pair_scores(i, n, keys, query):
    scores = outer_cols(keys, query)
    left = low_lanes((BLOCK, 128))
    right = jnp.logical_not(left)
    end = n * BPD // 2 - 1
    hide_first = jnp.logical_and(left, i == 0)
    hide_last = jnp.logical_and(right, i == end)
    return jnp.concatenate(
        [
            jnp.where(hide_first, masked_score, scores[0:BLOCK]),
            scores[BLOCK : 2 * BLOCK],
            jnp.where(hide_last, masked_score, scores[2 * BLOCK : 3 * BLOCK]),
            scores[3 * BLOCK :],
        ],
        axis=0,
    )


def turn_pairs(n, kv_ref, vk_ref):
    def body(b, _):
        for t in range(BPD):
            tile = kv_ref[b * BPD + t].astype(jnp.float32)
            vk_ref[b * BPD + t] = swap_halves(tile).astype(jnp.bfloat16)
        return 0

    lax.fori_loop(0, n, body, 0)


def chain_table(n, place, picks_vmem, picks_smem, links_ref):
    none = PICKS * n
    lane = lax.broadcasted_iota(jnp.int32, (n, 128), 1)
    turn = (lax.broadcasted_iota(jnp.int32, (n, 128), 0) + 2 * n - place - 1) % n
    order = jnp.where(lane < PICKS, turn * PICKS + lane, -1)
    picks = picks_vmem[:, 0, :]
    blocks = lax.broadcasted_iota(jnp.int32, (8, 128), 1)

    def body(k, tables):
        before, final = tables
        s = (place + 1 + k) % n
        for j in range(PICKS):
            pick, e = picks_smem[s, 0, j], k * PICKS + j
            before = jnp.where(jnp.logical_and(picks == pick, order > e), e, before)
            final = jnp.where(blocks == pick, e, final)
        return before, final

    start = (jnp.full((n, 128), none, jnp.int32), jnp.full((8, 128), none, jnp.int32))
    before, final = lax.fori_loop(0, n, body, start)
    links_ref[0:n] = before
    links_ref[n : n + 8] = final


PICKS = 3 * BPD
UNITS = 32
WIDE = 768


def greet_row(n, place, mine):
    row = lax.axis_index("dp")
    bar = pltpu.get_barrier_semaphore()

    def body(s, _):
        there = owned(s, n)[1]

        @pl.when(jnp.logical_and(s != place, jnp.logical_or(mine, there)))
        def _():
            pl.semaphore_signal(bar, inc=1, device_id=(row, s), device_id_type=MESH)

        return 0

    lax.fori_loop(0, n, body, 0)
    pl.semaphore_wait(bar, jnp.where(mine, n - 1, H))


def unpack_pair(tiles, odd, shape):
    left = low_lanes(shape)
    a, b = tiles.astype(jnp.float32), odd.astype(jnp.float32)
    return (jnp.where(left, a, swap_halves(b)), jnp.where(left, swap_halves(a), b))


def add_flat(out_ref, base, srcs, width=None):
    rows, cols = srcs[0].shape
    width = width or cols
    for k in range(cols // 128):
        lanes = slice(k * 128, (k + 1) * 128)
        total = srcs[0][:, lanes].astype(jnp.float32)
        for s in srcs[1:]:
            total = total + s[:, lanes].astype(jnp.float32)
        out_ref[pl.ds(base + k, rows, stride=width // 128), :] = total


class Reduction:
    def __init__(self, nz, me, links, direct, own, give, emit, bufs, sems, pending):
        self.nz, self.me, self.links, self.direct = nz, me, links, direct
        self.own, self.give, self.emit = own, give, emit
        self.rc, self.ra, self.rb, self.below, self.above = bufs
        self.csend, self.crecv, self.send, self.recv = sems
        self.pending = pending

    @staticmethod
    def buffers(nz, slab):
        counts = (4 * nz, nz, 2 * nz, nz, nz)
        return [pltpu.VMEM((c,) + slab, jnp.bfloat16) for c in counts]

    @staticmethod
    def semaphores(nz):
        return [pltpu.SemaphoreType.DMA((c * nz,)) for c in (4, 4, 5, 5)]

    def start(self, src, dst, slot, to, cond=None, there=None):
        cp = pltpu.make_async_remote_copy(
            src_ref=src,
            dst_ref=dst,
            send_sem=self.send.at[slot],
            recv_sem=self.recv.at[slot if there is None else there],
            device_id=device(to),
            device_id_type=MESH,
        )
        if cond is None:
            cp.start()
        else:
            pl.when(cond)(cp.start)
        self.pending.append((cp, cond))

    def arrived(self, ref, sem):
        pltpu.make_async_remote_copy(
            src_ref=ref,
            dst_ref=ref,
            send_sem=self.send.at[0],
            recv_sem=sem,
            device_id=device(dict(self.me, c=1 - self.me["c"])),
            device_id_type=MESH,
        ).wait_recv()

    def flip(self, which, f):
        d = self.links[which]
        return 1 - self.me[d] if f else self.me[d]

    def piece(self, z, a, b):
        c = {self.links[0]: a, self.links[1]: b}
        return (c["y"] * self.nz + z) * 2 + c["x"]

    def across(self, which):
        d = self.links[which]
        return dict(self.me, **{d: 1 - self.me[d]})

    def hand_over(self):
        nz = self.nz
        zs = sorted(range(nz), key=lambda z: -abs(2 * z - nz + 1))
        order = [(z, fa, fb) for fb in (1, 0) for fa in (1, 0) for z in zs]

        def one(z, fa, fb):
            def run():
                p = self.piece(z, self.flip(0, fa), self.flip(1, fb))
                cp = pltpu.make_async_remote_copy(
                    src_ref=self.give(p),
                    dst_ref=self.rc.at[p],
                    send_sem=self.csend.at[p],
                    recv_sem=self.crecv.at[p],
                    device_id=device(dict(self.me, c=1 - self.me["c"])),
                    device_id_type=MESH,
                )
                cp.start()
                self.pending.append((cp, None))

            return run

        return [one(*o) for o in order]

    def mine(self, p):
        self.arrived(self.rc.at[p], self.crecv.at[p])
        return [self.own(p), self.rc.at[p]]

    def relay(self, z, p, srcs, bref, aref, sb, sa):
        nz, mz, acc = self.nz, self.me["z"], self.rc.at[p]
        if z > 0:

            @pl.when(mz == 0)
            def _():
                combine(acc, srcs)

            @pl.when(jnp.logical_and(mz > 0, mz < z))
            def _():
                self.arrived(bref, self.recv.at[sb])
                combine(acc, srcs + [bref])

            self.start(acc, bref, sb, dict(self.me, z=jnp.minimum(mz + 1, nz - 1)), mz < z)
        if z < nz - 1:

            @pl.when(mz == nz - 1)
            def _():
                combine(acc, srcs)

            @pl.when(jnp.logical_and(mz < nz - 1, mz > z))
            def _():
                self.arrived(aref, self.recv.at[sa])
                combine(acc, srcs + [aref])

            self.start(acc, aref, sa, dict(self.me, z=jnp.maximum(mz - 1, 0)), mz > z)

    def ends(self, z, bref, aref, sb, sa):
        out = []
        if z > 0:
            self.arrived(bref, self.recv.at[sb])
            out.append(bref)
        if z < self.nz - 1:
            self.arrived(aref, self.recv.at[sa])
            out.append(aref)
        return out

    def steps(self):
        nz, me = self.nz, self.me
        zs = sorted(range(nz), key=lambda z: -abs(2 * z - nz + 1))

        def along_b(z, fa):
            def run():
                a = self.flip(0, fa)
                p = self.piece(z, a, self.flip(1, 1))
                combine(self.rc.at[p], self.mine(p))
                s = z * 2 + a
                self.start(self.rc.at[p], self.rb.at[s], s, self.across(1))

            return run

        def along_a(z):
            def run():
                a = self.flip(0, 1)
                p = self.piece(z, a, self.flip(1, 0))
                s = z * 2 + a
                srcs = self.mine(p)
                self.arrived(self.rb.at[s], self.recv.at[s])
                combine(self.rc.at[p], srcs + [self.rb.at[s]])
                self.start(self.rc.at[p], self.ra.at[z], 2 * nz + z, self.across(0))

            return run

        def chain(z):
            def run():
                p = self.piece(z, self.flip(0, 0), self.flip(1, 0))
                s = z * 2 + self.flip(0, 0)
                srcs = self.mine(p)
                self.arrived(self.rb.at[s], self.recv.at[s])
                self.arrived(self.ra.at[z], self.recv.at[2 * nz + z])
                srcs += [self.rb.at[s], self.ra.at[z]]
                if self.direct:
                    mz = me["z"]

                    @pl.when(mz != z)
                    def _():
                        combine(self.rc.at[p], srcs)

                    to = dict(me, z=z)
                    self.start(
                        self.rc.at[p], self.below.at[mz], 3 * nz + z, to, mz != z, 3 * nz + mz
                    )
                    return
                bref, aref = self.below.at[z], self.above.at[z]
                self.relay(z, p, srcs, bref, aref, 3 * nz + z, 4 * nz + z)

            return run

        def last():
            for z in range(nz):

                @pl.when(me["z"] == z)
                def _():
                    p = self.piece(z, self.flip(0, 0), self.flip(1, 0))
                    s = z * 2 + self.flip(0, 0)
                    srcs = [self.own(p), self.rc.at[p], self.rb.at[s], self.ra.at[z]]
                    if self.direct:
                        for other in range(nz):
                            if other != z:
                                ref = self.below.at[other]
                                self.arrived(ref, self.recv.at[3 * nz + other])
                                srcs.append(ref)
                        self.emit(srcs)
                        return
                    bref, aref = self.below.at[z], self.above.at[z]
                    self.emit(srcs + self.ends(z, bref, aref, 3 * nz + z, 4 * nz + z))

        out = [(1 + i, along_b(z, 1)) for i, z in enumerate(zs)]
        out += [(5 + i, along_b(z, 0)) for i, z in enumerate(zs)]
        out += [(5.5 + i, along_a(z)) for i, z in enumerate(zs)]
        out += [(9.5 + i, chain(z)) for i, z in enumerate(zs)]
        return out + [(20, last)]


class Spread:
    def __init__(self, nz, me, order, at, sems, pending):
        self.nz, self.me, self.order, self.at = nz, me, order, at
        self.send, self.recv, self.csend, self.crecv = sems
        self.pending = pending

    @staticmethod
    def semaphores(nz):
        chips = 4 * nz
        return [pltpu.SemaphoreType.DMA((chips, 4))] + [pltpu.SemaphoreType.DMA((chips,))] * 3

    def copy(self, slot, send, recv, to):
        ref = self.at(slot)
        return pltpu.make_async_remote_copy(
            src_ref=ref,
            dst_ref=ref,
            send_sem=send,
            recv_sem=recv,
            device_id=device(to),
            device_id_type=MESH,
        )

    def start(self, cp, cond=None):
        if cond is None:
            cp.start()
        else:
            pl.when(cond)(cp.start)
        self.pending.append((cp, cond))

    def one(self, steps):
        nz, me = self.nz, self.me
        size = {"y": 2, "z": nz, "x": 2}
        own = not any(steps)

        def run():
            src = dict(me)
            for d, i in zip(self.order, steps):
                src[d] = nearest(me[d], size[d], i)
            c = chip(src, nz)
            slot = c * 2 + me["c"]
            if not own:
                self.copy(slot, self.send.at[c, 0], self.recv.at[c], me).wait_recv()
            stage = 2 if steps[2] else (1 if steps[1] else 0)
            for t in range(stage, 3):
                d = self.order[t]
                onward = t == stage and not own
                if d == "z":
                    up, down = me["z"] < nz - 1, me["z"] > 0
                    if onward:
                        up = jnp.logical_and(up, src["z"] <= me["z"])
                        down = jnp.logical_and(down, src["z"] >= me["z"])
                    above = dict(me, z=jnp.minimum(me["z"] + 1, nz - 1))
                    below = dict(me, z=jnp.maximum(me["z"] - 1, 0))
                    self.start(self.copy(slot, self.send.at[c, 0], self.recv.at[c], above), up)
                    self.start(self.copy(slot, self.send.at[c, 1], self.recv.at[c], below), down)
                elif not (onward and steps[t]):
                    way = 2 if d == "x" else 3
                    to = dict(me, **{d: 1 - me[d]})
                    self.start(self.copy(slot, self.send.at[c, way], self.recv.at[c], to))
            sibling = dict(me, c=1 - me["c"])
            self.start(self.copy(slot, self.csend.at[c], self.crecv.at[c], sibling))

        return run

    def steps(self):
        size = {"y": 2, "z": self.nz, "x": 2}
        n0, n1, n2 = (size[d] for d in self.order)
        return [
            (i0 + i1 + i2, self.one((i0, i1, i2)))
            for i2 in range(n2)
            for i1 in range(n1)
            for i0 in range(n0)
        ]

    def finish(self):
        def body(c, _):
            slot = c * 2 + 1 - self.me["c"]
            self.copy(slot, self.csend.at[c], self.crecv.at[c], self.me).wait_recv()
            return 0

        lax.fori_loop(0, 4 * self.nz, body, 0)


def run_in_order(items, low, high):
    steps = [(w, i, f) for i, item in enumerate(items) for w, f in item.steps()]
    for w, _, f in sorted(steps, key=lambda s: s[:2]):
        if low <= w < high:
            f()


def exchange_partners(me, nz):
    partners = [dict(me, **{d: 1 - me[d]}) for d in ("c", "x", "y")]
    step = 1
    while step < nz:
        partners.append(dict(me, z=me["z"] + step - 2 * step * ((me["z"] // step) % 2)))
        step *= 2
    return partners


def vector_copy(i, value, land, sems, partners):
    return pltpu.make_async_remote_copy(
        src_ref=value.at[i],
        dst_ref=land.at[i],
        send_sem=sems[0].at[i],
        recv_sem=sems[1].at[i],
        device_id=device(partners[i]),
        device_id_type=MESH,
    )


def greet_row_and_y(n, me, place_row):
    bar = pltpu.get_barrier_semaphore()

    def greet(k, _):
        to = (place_row + 1 + k) % n
        pl.semaphore_signal(bar, inc=1, device_id=(me["y"], to), device_id_type=MESH)
        return 0

    lax.fori_loop(0, n - 1, greet, 0)
    pl.semaphore_signal(bar, inc=1, device_id=(1 - me["y"], place_row), device_id_type=MESH)
    return lambda: pl.semaphore_wait(bar, n)


UNIT = D // UNITS
THIRD = FF // UNITS // 3
QKV_ORDERS = (("z", "x", "y"), ("z", "y", "x"), ("x", "y", "z"))
REST = (
    ("first", 0, UNIT, ("z", "x", "y")),
    ("second", THIRD, FF // UNITS, ("z", "y", "x")),
    ("second", 0, THIRD, ("z", "x", "y")),
)


EARLY = {1: (0, 1), 4: (1, 2), 5: (2, 3)}
LATE = ((3, 4), (4, 5), (99, 99), (99, 99), (99, 99))


def from_flat(flat, cols, rows):
    step = cols // 128
    return [flat[pl.ds(k, rows, stride=step), :] for k in range(step)]


def as_matrix(units):
    count, rows, cols = units.shape
    return units.astype(jnp.float32).reshape(count * rows, cols).astype(jnp.bfloat16)


def kernel_planes():
    seq = lax.axis_size("seq")
    if lax.axis_size("dp") != 2 or 2 * seq != UNITS or seq % 4:
        return 0
    return seq // 4


def place_vectors(me, shards, pieces, line, value):
    packed = pieces[...]
    at, row = 0, 0
    value[0] = jnp.zeros_like(value[0])
    for size in VECTORS:
        width = size // shards
        start = me * width
        inside = lax.broadcasted_iota(jnp.int32, packed.shape, 1)
        inside = jnp.logical_and(inside >= at, inside < at + width)
        moved = jnp.where(inside, packed, 0.0)
        line[...] = jnp.zeros_like(line)
        base = pl.multiple_of(start // 128 * 128, 128)
        line[:, pl.ds(base, 384)] = pltpu.roll(moved, (start % 128 - at) % 384, 1)
        for r in range(size // D):
            value[0, row + r : row + r + 1] = line[:, r * D : (r + 1) * D]
        row += size // D
        at += width


def front_kernel(n, nz, *refs):
    rows_ref, cot_ref, picks_ref, vec_in, qkv_in, first_in, out_in, second_in = refs[:8]
    (
        result_ref,
        d_sum1_ref,
        kv_hbm,
        q_hbm,
        picks_hbm,
        lse_ref,
        d_heads,
        dw1_hbm,
        dw2_hbm,
        dwo_hbm,
        small_ref,
        d_ffn_ref,
        w_hbm,
        links_hbm,
    ) = refs[8:22]
    (
        w_ref,
        first_ref,
        second_ref,
        flat,
        value,
        land,
        box_kv,
        box_q,
        kv_ref,
        q_ref,
        vk_ref,
        picks_smem,
        keys,
        values,
        attended,
        inbox,
        grad_box,
        slope_ref,
        active_ref,
        dw1_ref,
        dw2_ref,
        dwo_ref,
        mixed_ref,
        load_sem,
        store_sem,
        keep_sem,
        vsend,
        vrecv,
        links_ref,
        picks_vmem,
        line,
        d_up_ref,
    ) = refs[22:54]
    sems_qkv, sems_in, sems_out = refs[54:57], refs[57:60], refs[60:63]
    rest = list(refs[63:])
    place_row = lax.axis_index("seq")
    head, mine = owned(place_row, n)
    pending = []

    if nz:
        me = place(nz)
        slot = index(me, nz)
        hold = greet_row_and_y(n, me, place_row)
        stages = 3 + (nz - 1).bit_length()

        def take():
            out = rest[:4]
            del rest[:4]
            return out

        def widen(src):
            count = src.shape[0]
            flat[0:count] = src[...].astype(jnp.float32)

        widen(qkv_in)
        for j in range(3):
            step = D // 128
            for k in range(step):
                col = flat[pl.ds(j * UNIT * step + k, UNIT, stride=step), :]
                w_ref[slot * 3 + j, :, k * 128 : (k + 1) * 128] = col.astype(jnp.bfloat16)
        place_vectors(slot, 8 * nz, vec_in, line, value)
        hold()
        qkv_items = [
            Spread(nz, me, order, lambda s, j=j: w_ref.at[s * 3 + j], take(), pending)
            for j, order in enumerate(QKV_ORDERS)
        ]
        buffers = {"first": first_ref, "second": second_ref}

        def part(kind, lo, hi):
            ref = buffers[kind]
            if hi - lo == ref.shape[1]:
                return lambda s: ref.at[s]
            return lambda s: ref.at[s, lo:hi]

        rest_items = [
            Spread(nz, me, order, part(kind, lo, hi), take(), pending)
            for kind, lo, hi, order in REST
        ]
        partners = exchange_partners(me, nz)
        vsems = (vsend, vrecv)
        vector_copy(0, value, land, vsems, partners).start()
        run_in_order(qkv_items, 0, 1)
        for src, dst, at, cols, count in (
            (first_in, first_ref, 0, FF, UNIT),
            (out_in, first_ref, FF, D, UNIT),
            (second_in, second_ref, 0, D, FF // UNITS),
        ):
            widen(src)
            for k, col in enumerate(from_flat(flat, cols, count)):
                dst[slot, :, at + k * 128 : at + (k + 1) * 128] = col.astype(jnp.bfloat16)

        def vector_stage(i):
            vector_copy(i, value, land, vsems, partners).wait_recv()
            value[i + 1] = value[i] + land[i]
            if i + 1 < stages:
                vector_copy(i + 1, value, land, vsems, partners).start()

        for depth in range(1, nz + 2):
            vector_stage(min(depth - 1, stages)) if depth <= stages else None
            run_in_order(qkv_items, depth, depth + 1)
            if depth in EARLY:
                run_in_order(rest_items, *EARLY[depth])
        for i in range(nz + 1, stages):
            vector_stage(i)
        for item in qkv_items:
            item.finish()
        vec = value.at[stages]
    else:
        greet_row(n, place_row, mine)
        loads = [
            pltpu.make_async_copy(src, dst, load_sem.at[i])
            for i, (src, dst) in enumerate(
                ((qkv_in, w_ref), (first_in, first_ref), (second_in, second_ref))
            )
        ]
        for cp in loads:
            cp.start()
        for cp in loads:
            cp.wait()
        vec = vec_in

    def rest_steps(low, high, part=slice(None)):
        if nz:
            run_in_order(rest_items[part], low, high)

    rows = rows_ref[...]
    left = low_lanes((TOK_SEQ, 128))
    left_q = low_lanes((BLOCK, 128))
    wide = 256
    parcels = (
        (box_kv, lambda s: kv_ref.at[pl.ds(s * BPD, BPD)]),
        (box_q, lambda s: q_ref.at[s]),
        (picks_ref, lambda s: picks_hbm.at[s]),
    )

    def project_some(step, _):
        g = (place_row + step) % (D // wide)
        cols = pl.ds(pl.multiple_of(g * wide, wide), wide)

        def project(e):
            return matmul(rows, as_matrix(w_ref[e * UNITS : (e + 1) * UNITS, :, cols]))

        q = (project(0) + vec[0:1, cols]) * HD ** (-0.5)
        k = project(1)
        v = project(2) + vec[1:2, cols]
        for p in range(wide // 128):
            h = g * (wide // HD) + p * 2
            lanes = slice(p * 128, (p + 1) * 128)
            kp, vp, qp = k[:, lanes], v[:, lanes], q[:, lanes]
            even, odd = jnp.where(left, kp, swap_halves(vp)), jnp.where(left, swap_halves(kp), vp)
            for t in range(BPD):
                part = slice(t * BLOCK, (t + 1) * BLOCK)
                box_kv[h, t] = even[part].astype(jnp.bfloat16)
                box_kv[h + 1, t] = odd[part].astype(jnp.bfloat16)
            turned = swap_halves(qp)
            for t in range(BPD // 2):
                a = slice(2 * t * BLOCK, (2 * t + 1) * BLOCK)
                b = slice((2 * t + 1) * BLOCK, (2 * t + 2) * BLOCK)
                to = slice(t * BLOCK, (t + 1) * BLOCK)
                box_q[h, to, :] = jnp.where(left_q, qp[a], turned[b]).astype(jnp.bfloat16)
                box_q[h + 1, to, :] = jnp.where(left_q, turned[a], qp[b]).astype(jnp.bfloat16)
            for u in range(2):
                post(place_row, h + u, parcels, sems_qkv, lambda cp: cp.start(), n)
        return 0

    lax.fori_loop(0, D // wide, project_some, 0)
    rest_steps(*LATE[0])
    wait_to_owner(n, place_row, head, mine, parcels, sems_qkv)

    keep = (
        pltpu.make_async_copy(kv_ref, kv_hbm, keep_sem.at[0]),
        pltpu.make_async_copy(q_ref, q_hbm, keep_sem.at[3]),
    )
    keep_w = pltpu.make_async_copy(w_ref, w_hbm, keep_sem.at[2])
    keep_w.start()
    keep_links = pltpu.make_async_copy(links_ref, links_hbm, keep_sem.at[4])
    groups = 4

    @pl.when(mine)
    def _():
        for copy in keep:
            copy.start()
        copies = (
            pltpu.make_async_copy(picks_hbm, picks_smem, keep_sem.at[1]),
            pltpu.make_async_copy(picks_hbm, picks_vmem, keep_sem.at[5]),
        )
        for cp in copies:
            cp.start()
        for cp in copies:
            cp.wait()
        turn_pairs(n, kv_ref, vk_ref)
        chain_table(n, place_row, picks_vmem, picks_smem, links_ref)
        keep_links.start()

    def attend_some(k, _):
        s = (place_row + 1 + k) % n
        for t in range(BPD // 2):
            i = s * (BPD // 2) + t
            fill_pair(key_list(i, n, picks_smem), kv_ref, vk_ref, keys.at[t], values.at[t])
        for t in range(BPD // 2):
            i = s * (BPD // 2) + t
            part = slice(t * BLOCK, (t + 1) * BLOCK)
            query = two_blocks(q_ref[s, part, :])
            scores = pair_scores(i, n, keys[t], query)
            top = jnp.max(scores, axis=0, keepdims=True)
            weights = jnp.exp(scores - top)
            total = jnp.sum(weights, axis=0, keepdims=True)
            probs = (weights * (1.0 / total)).astype(jnp.bfloat16)
            full = inner_rows(probs, values[t])
            attended[s, part, :] = jnp.where(left_q, full[:BLOCK], full[BLOCK:]).astype(
                jnp.bfloat16
            )
            lse_ref[i] = top + jnp.log(total)

        @pl.when(s != place_row)
        def _():
            pltpu.make_async_remote_copy(
                src_ref=attended.at[s],
                dst_ref=inbox.at[head],
                send_sem=sems_in[0].at[0, s],
                recv_sem=sems_in[1].at[0, head],
                device_id=(lax.axis_index("dp"), s),
                device_id_type=MESH,
            ).start()

        return 0

    for g in range(groups):

        @pl.when(mine)
        def _():
            lax.fori_loop(g * (n // groups), (g + 1) * (n // groups), attend_some, 0)

        rest_steps(*LATE[1 + g])

    @pl.when(mine)
    def _():
        cp = pltpu.make_async_copy(attended.at[place_row], inbox.at[head], sems_in[2].at[0])
        cp.start()
        cp.wait()

    rest_steps(5, 99, slice(0, 1))
    if nz:
        rest_items[0].finish()
    wait_from_owners(n, place_row, head, attended, inbox, sems_in)

    for h in range(0, H, 2):
        for t in range(BPD // 2):
            part = slice(t * BLOCK, (t + 1) * BLOCK)
            a, b = unpack_pair(inbox[h, part, :], inbox[h + 1, part, :], (BLOCK, 128))
            lanes = slice(h * HD, (h + 2) * HD)
            mixed_ref[2 * t * BLOCK : (2 * t + 1) * BLOCK, lanes] = a.astype(jnp.bfloat16)
            mixed_ref[(2 * t + 1) * BLOCK : (2 * t + 2) * BLOCK, lanes] = b.astype(jnp.bfloat16)
    out_w = as_matrix(first_ref[:, :, FF : FF + D])
    hidden1 = rows_ref[...].astype(jnp.float32) + matmul(mixed_ref[...], out_w) + vec[2:3]
    normed_out1, normed1, inverse1 = normalize(hidden1, vec[6:7], vec[3:4])
    lowered = normed_out1.astype(jnp.bfloat16)
    per = UNITS * WIDE // FF

    def second_rows(c):
        return second_ref[pl.ds(c * per, per)].reshape(WIDE, D)

    def up_step(c, _):
        cols = pl.ds(pl.multiple_of(c * WIDE, WIDE), WIDE)
        up = matmul(lowered, as_matrix(first_ref[:, :, cols])) + vec[pl.ds(8 + c, 1)]
        square = up * up
        inner = (2 / jnp.pi) ** 0.5 * (up + 0.044715 * up * square)
        curve = jnp.tanh(inner)
        active = (0.5 * up * (1 + curve)).astype(jnp.bfloat16)
        slope_ref[:, cols] = 0.5 * (1 + curve) + 0.5 * up * (1 - curve * curve) * (
            (2 / jnp.pi) ** 0.5 * (1 + 3 * 0.044715 * square)
        )
        active_ref[:, cols] = active
        return 0

    def down_step(c, hidden):
        cols = pl.ds(pl.multiple_of(c * WIDE, WIDE), WIDE)
        return hidden + matmul(active_ref[:, cols], second_rows(c))

    rest_steps(5, 99, slice(1, 3))
    lax.fori_loop(0, FF // WIDE, up_step, 0)
    if nz:
        for item in rest_items[1:]:
            item.finish()
    hidden2 = lax.fori_loop(0, FF // WIDE, down_step, normed_out1 + vec[4:5])
    result, normed2, inverse2 = normalize(hidden2, vec[7:8], vec[5:6])
    result_ref[...] = result
    grad = cot_ref[...].astype(jnp.float32)
    d_sum2 = normalize_back(grad, normed2, inverse2, vec[7:8])
    d_down = d_sum2.astype(jnp.bfloat16)

    def add_rows(x):
        return jnp.sum(x, axis=0, keepdims=True)

    small_ref[2:3] = add_rows(d_down.astype(jnp.float32))
    small_ref[3:4] = add_rows(grad)
    small_ref[5:6] = add_rows(grad * normed2)

    def stores(c):
        cols = pl.ds(pl.multiple_of(c * WIDE, WIDE), WIDE)
        slabs = pl.ds(c * per, per)
        return (
            pltpu.make_async_copy(dw1_ref.at[:, :, cols], dw1_hbm.at[:, :, cols], store_sem.at[0, c]),
            pltpu.make_async_copy(dw2_ref.at[slabs], dw2_hbm.at[slabs], store_sem.at[1, c]),
        )

    def back_step(c, d_norm1):
        cols = pl.ds(pl.multiple_of(c * WIDE, WIDE), WIDE)
        d_active = outer_cols(d_down, second_rows(c))
        d_up = (d_active * slope_ref[:, cols]).astype(jnp.bfloat16)
        d_ffn_ref[:, cols] = add_rows(d_up.astype(jnp.float32))
        d_up_ref[:, cols] = d_up
        return d_norm1 + outer_cols(d_up, as_matrix(first_ref[:, :, cols]))

    d_norm1 = lax.fori_loop(0, FF // WIDE, back_step, d_sum2)
    small_ref[1:2] = add_rows(d_norm1)
    small_ref[4:5] = add_rows(d_norm1 * normed1)
    d_sum1 = normalize_back(d_norm1, normed1, inverse1, vec[6:7])
    d_sum1_ref[...] = d_sum1
    d_attn = d_sum1.astype(jnp.bfloat16)
    small_ref[0:1] = add_rows(d_attn.astype(jnp.float32))
    d_mixed = outer_cols(d_attn, as_matrix(first_ref[:, :, FF : FF + D]))
    for h in range(0, H, 2):
        for t in range(BPD // 2):
            part = slice(t * BLOCK, (t + 1) * BLOCK)
            lanes = slice(h * HD, (h + 2) * HD)
            a, b = unpack_pair(
                d_mixed[2 * t * BLOCK : (2 * t + 1) * BLOCK, lanes],
                d_mixed[(2 * t + 1) * BLOCK : (2 * t + 2) * BLOCK, lanes],
                (BLOCK, 128),
            )
            grad_box[h, part, :] = a.astype(jnp.bfloat16)
            grad_box[h + 1, part, :] = b.astype(jnp.bfloat16)

    store_out = pltpu.make_async_copy(dwo_ref, dwo_hbm, load_sem.at[0])

    def weight_grads(c, _):
        cols = pl.ds(pl.multiple_of(c * WIDE, WIDE), WIDE)
        dw2 = inner_rows(active_ref[:, cols], d_down)
        dw2_ref[pl.ds(c * per, per)] = dw2.reshape(per, FF // UNITS, D).astype(jnp.bfloat16)
        dw1 = inner_rows(lowered, d_up_ref[:, cols])
        dw1_ref[:, :, cols] = dw1.reshape(UNITS, UNIT, WIDE).astype(jnp.bfloat16)
        for cp in stores(c):
            cp.start()
        return 0

    def late():
        lax.fori_loop(0, FF // WIDE, weight_grads, 0)
        dwo = inner_rows(mixed_ref[...], d_attn).reshape(UNITS, UNIT, D)
        dwo_ref[...] = dwo.astype(jnp.bfloat16)
        store_out.start()

    send_to_owners(n, place_row, head, mine, ((grad_box, lambda s: d_heads.at[s]),), sems_out, late)
    store_out.wait()

    def drain(c, _):
        for cp in stores(c):
            cp.wait()
        return 0

    lax.fori_loop(0, FF // WIDE, drain, 0)

    @pl.when(mine)
    def _():
        for copy in keep:
            copy.wait()
        keep_links.wait()

    keep_w.wait()
    finish_from_owners(n, place_row, head, mine, attended, inbox, sems_in)
    finish_to_owners(n, place_row, head, parcels, sems_qkv)
    if nz:
        for i in range(stages):
            vector_copy(i, value, land, vsems, partners).wait_send()
    for cp, cond in pending:
        if cond is None:
            cp.wait_send()
        else:
            pl.when(cond)(cp.wait_send)


def front(rows, cotangent, picks, vec, qkv, first, out, second, nz):
    n = lax.axis_size("seq")
    low, full = jnp.bfloat16, jnp.float32
    picks = jnp.pad(picks.reshape(H, 1, BPD * 3), ((0, 0), (0, 7), (0, 128 - BPD * 3)))
    part = (TOK_SEQ // 2, 128)
    pairs = n * BPD // 2
    units = [(UNITS, UNIT, FF), (UNITS, FF // UNITS, D), (UNITS, UNIT, D)]
    shapes = [((TOK_SEQ, D), full), ((TOK_SEQ, D), full)]
    shapes += [((n * BPD, BLOCK, 128), low), ((n,) + part, low)]
    shapes += [((n, 8, 128), jnp.int32), ((pairs, 1, 128), full), ((n,) + part, low)]
    shapes += [(u, low) for u in units] + [((8, D), full), ((1, FF), full)]
    shapes += [((3 * UNITS, UNIT, D), low), ((n + 8, 128), jnp.int32)]
    stages = 3 + (max(nz, 1) - 1).bit_length()
    where = VMEM if nz else ANY
    extra = []
    for _ in range(6 if nz else 0):
        extra += Spread.semaphores(nz)
    return pl.pallas_call(
        functools.partial(front_kernel, n, nz),
        out_shape=[jax.ShapeDtypeStruct(s, d) for s, d in shapes],
        in_specs=[VMEM, VMEM, ANY, VMEM, where, where, where, where],
        out_specs=[VMEM, VMEM, ANY, ANY, ANY, VMEM, ANY, ANY, ANY, ANY, VMEM, VMEM, ANY, ANY],
        scratch_shapes=[
            pltpu.VMEM((3 * UNITS, UNIT, D), low),
            pltpu.VMEM((UNITS, UNIT, FF + D), low),
            pltpu.VMEM((UNITS, FF // UNITS, D), low),
            pltpu.VMEM((UNIT * FF // 128, 128), full),
            pltpu.VMEM((stages + 1, 16, D), full),
            pltpu.VMEM((stages, 16, D), full),
            pltpu.VMEM((H, BPD, BLOCK, 128), low),
            pltpu.VMEM((H,) + part, low),
            pltpu.VMEM((n * BPD, BLOCK, 128), low),
            pltpu.VMEM((n,) + part, low),
            pltpu.VMEM((n * BPD, BLOCK, 128), low),
            pltpu.SMEM((n, 8, 128), jnp.int32),
            pltpu.VMEM((BPD // 2, 8 * BLOCK, 128), low),
            pltpu.VMEM((BPD // 2, 8 * BLOCK, 128), low),
            pltpu.VMEM((n,) + part, low),
            pltpu.VMEM((H,) + part, low),
            pltpu.VMEM((H,) + part, low),
            pltpu.VMEM((TOK_SEQ, FF), full),
            pltpu.VMEM((TOK_SEQ, FF), low),
            *[pltpu.VMEM(u, low) for u in units],
            pltpu.VMEM((TOK_SEQ, D), low),
            pltpu.SemaphoreType.DMA((3,)),
            pltpu.SemaphoreType.DMA((2, FF // WIDE)),
            pltpu.SemaphoreType.DMA((6,)),
            pltpu.SemaphoreType.DMA((stages,)),
            pltpu.SemaphoreType.DMA((stages,)),
            pltpu.VMEM((n + 8, 128), jnp.int32),
            pltpu.VMEM((n, 8, 128), jnp.int32),
            pltpu.VMEM((1, max(VECTORS) + 384), full),
            pltpu.VMEM((TOK_SEQ, FF), low),
            *exchange_sems(n, 3),
            *exchange_sems(n),
            *exchange_sems(n),
            *extra,
        ],
        compiler_params=pltpu.CompilerParams(
            collective_id=0, has_side_effects=True, vmem_limit_bytes=60 << 20
        ),
        name="front",
    )(rows, cotangent, picks, vec, qkv, first, out, second)


FFN_KINDS = (
    ("expand", 0, UNIT, ("x", "y")),
    ("contract", 0, FF // UNITS, ("y", "x")),
    ("out", 0, UNIT, ("x", "y")),
)
QKV_KINDS = (
    (0, 0, D, ("x", "y")),
    (1, 0, D, ("y", "x")),
    (2, 0, D // 2, ("x", "y")),
    (2, D // 2, D, ("y", "x")),
)
QKV_UNITS = 3 * UNITS


FFN_WITH = ((1,), (2,), (3,), (4,))
FFN_AFTER = ((5, 5.5, 6, 6.5, 7, 7.5, 8, 8.5), (9.5, 10.5, 11.5, 12.5))


def send_one(sems, src, dst, head, to):
    return pltpu.make_async_remote_copy(
        src_ref=src.at[to],
        dst_ref=dst.at[head],
        send_sem=sems[0].at[0, to],
        recv_sem=sems[1].at[0, head],
        device_id=(lax.axis_index("dp"), to),
        device_id_type=MESH,
    )


def back_kernel(n, nz, *refs):
    kv_ref, q_ref, picks_ref, links_ref, lse_ref, grad_ref = refs[:6]
    rows_ref, w_hbm, d_sum1_ref, small_ref, ffn_ref, dw1, dw2, dwo = refs[6:14]
    d_tokens_ref, vec_out = refs[14:16]
    outs = refs[16 : 20 if nz else 17]
    rest = list(refs[20 if nz else 17 :])
    vk_ref, keys, values, acc, out_q, out_kv, inbox_q, inbox_kv, proj, w_ref, ownq = rest[:11]
    turned_rows, value, land, load_sem, vsend, vrecv = rest[11:17]
    sems_q, sems_kv = rest[17:20], rest[20:23]
    own1, own2, owno = rest[23:26] if nz else (None, None, None)
    rest = rest[26:]
    place_row = lax.axis_index("seq")
    head, mine = owned(place_row, n)
    blocks, none = n * BPD, n * BPD + n * PICKS
    pending = []

    load_w = pltpu.make_async_copy(w_hbm, w_ref, load_sem.at[0])
    load_w.start()
    if nz:
        me = place(nz)
        core = me["c"]
        loads = [
            pltpu.make_async_copy(src, dst, load_sem.at[1 + i])
            for i, (src, dst) in enumerate(((dw1, own1), (dw2, own2), (dwo, owno)))
        ]
        for cp in loads:
            cp.start()
        hold = greet_row_and_y(n, me, place_row)
    else:
        greet_row(n, place_row, mine)

    @pl.when(mine)
    def _():
        turn_pairs(n, kv_ref, vk_ref)

        def clear(b, _):
            acc[b] = jnp.zeros((BLOCK, 128), jnp.float32)
            return 0

        lax.fori_loop(0, blocks, clear, 0)
        clear(none, 0)

    def take(count):
        out = rest[:count]
        del rest[:count]
        return out

    def ffn_item(kind, lo, hi, links):
        far, near = {"expand": (dw1, own1), "contract": (dw2, own2), "out": (dwo, owno)}[kind]
        target = outs[("out", "expand", "contract").index(kind) + 1]
        whole = hi - lo == far.shape[1]

        def at(ref, t):
            return ref.at[t] if whole else ref.at[t, lo:hi]

        return Reduction(
            nz,
            me,
            links,
            False,
            lambda p: at(near, p * 2 + core),
            lambda p: at(far, p * 2 + 1 - core),
            lambda srcs: add_flat(target, lo * (far.shape[2] // 128), srcs),
            take(5),
            take(4),
            pending,
        )

    def qkv_item(j, lo, hi, links):
        def at(t):
            ref = ownq.at[t * 3 + j]
            return ref if hi - lo == D else ref.at[:, lo:hi]

        return Reduction(
            nz,
            me,
            links,
            True,
            lambda p: at(p * 2 + core),
            lambda p: at(p * 2 + 1 - core),
            lambda srcs: add_flat(outs[0], (j * UNIT * D + lo) // 128, srcs, D),
            take(5),
            take(4),
            pending,
        )

    def hand_all(items):
        for group in zip(*[i.hand_over() for i in items]):
            for f in group:
                f()

    def ordered(items):
        steps = [(w + 0.01 * i, f) for i, item in enumerate(items) for w, f in item.steps()]
        return sorted(steps, key=lambda s: s[0])

    turned_rows[...] = rows_ref[...].T
    ffn_steps = []
    if nz:
        ffn = [ffn_item(*k) for k in FFN_KINDS]
        qkv = [qkv_item(*k) for k in QKV_KINDS]
        ffn_steps = ordered(ffn)
        hold()
        hand_all(ffn)
        for cp in loads:
            cp.wait()

    def ffn_run(*wanted):
        for at in wanted:
            for w, f in ffn_steps:
                if abs(w - at) < 0.1:
                    f()

    left = low_lanes((BLOCK, 128))
    both = range(BPD // 2)

    def attend_some(k, _):
        s = (place_row + 1 + k) % n
        lists = [key_list(s * (BPD // 2) + t, n, picks_ref) for t in both]
        for t in both:
            fill_pair(lists[t], kv_ref, vk_ref, keys.at[t], values.at[t])
        parts = []
        for t in both:
            i = s * (BPD // 2) + t
            part = slice(t * BLOCK, (t + 1) * BLOCK)
            query = two_blocks(q_ref[s, part, :])
            grad = two_blocks(grad_ref[s, part, :])
            probs = jnp.exp(pair_scores(i, n, keys[t], query) - lse_ref[i])
            d_probs = outer_cols(values[t], grad)
            rows = jnp.sum(probs * d_probs, axis=0, keepdims=True)
            d_scores = (probs * (d_probs - rows)).astype(jnp.bfloat16)
            d_values = matmul(probs.astype(jnp.bfloat16), grad)
            d_keys = matmul(d_scores, query)
            full = inner_rows(d_scores, keys[t]) * HD ** (-0.5)
            out_q[s, part, :] = jnp.where(left, full[:BLOCK], full[BLOCK:]).astype(jnp.bfloat16)
            parts.append((d_keys, d_values))

        @pl.when(s != place_row)
        def _():
            send_one(sems_q, out_q, inbox_q, head, s).start()

        for t in both:
            tiles = []
            for j in range(8):
                part = slice(j * BLOCK, (j + 1) * BLOCK)
                dk, dv = parts[t][0][part], parts[t][1][part]
                a = jnp.where(left, dk, swap_halves(dv))
                b = jnp.where(left, swap_halves(dk), dv)
                tiles.append((a, b))
            a = (s * (BPD // 2) + t) * 2
            acc[jnp.maximum(a - 1, 0)] += tiles[0][0]
            acc[a] += tiles[1][0] + tiles[0][1]
            acc[a + 1] += tiles[2][0] + tiles[1][1]
            acc[jnp.minimum(a + 2, blocks - 1)] += tiles[2][1]
            acc[0] += tiles[3][0] + tiles[3][1]
            acc[blocks - 1] += tiles[4][0] + tiles[4][1]
            for u in range(2):
                for j in range(3):
                    e = (2 * t + u) * 3 + j
                    acc[blocks + k * PICKS + e] = tiles[5 + j][u] + acc[blocks + links_ref[s, e]]
        return 0

    groups = 4
    for g in range(groups):

        @pl.when(mine)
        def _():
            lax.fori_loop(g * (n // groups), (g + 1) * (n // groups), attend_some, 0)

        ffn_run(*FFN_WITH[g])

    @pl.when(mine)
    def _():
        def close(k, _):
            s = (place_row + 1 + k) % n
            for t in range(BPD):
                b = s * BPD + t
                total = acc[b] + acc[blocks + links_ref[n, b]]
                out_kv[s, t * BLOCK : (t + 1) * BLOCK, :] = total.astype(jnp.bfloat16)

            @pl.when(s != place_row)
            def _():
                send_one(sems_kv, out_kv, inbox_kv, head, s).start()

            return 0

        lax.fori_loop(0, n, close, 0)
        copies = (
            pltpu.make_async_copy(out_q.at[place_row], inbox_q.at[head], sems_q[2].at[0]),
            pltpu.make_async_copy(out_kv.at[place_row], inbox_kv.at[head], sems_kv[2].at[0]),
        )
        for cp in copies:
            cp.start()
        for cp in copies:
            cp.wait()

    ffn_run(*FFN_AFTER[0])

    def head_pair(k, _):
        p = (place_row + k) % (H // 2)
        for u in range(2):
            wait_head(n, place_row, 2 * p + u, out_q, inbox_q, sems_q)
            wait_head(n, place_row, 2 * p + u, out_kv, inbox_kv, sems_kv)
        lanes = pl.ds(pl.multiple_of(p * 128, 128), 128)
        keys_values = unpack_pair(inbox_kv[2 * p], inbox_kv[2 * p + 1], (TOK_SEQ, 128))
        queries = []
        for t in both:
            part = slice(t * BLOCK, (t + 1) * BLOCK)
            queries += unpack_pair(inbox_q[2 * p, part, :], inbox_q[2 * p + 1, part, :], (BLOCK, 128))
        grads = (jnp.concatenate(queries, axis=0), *keys_values)
        for e in range(3):
            proj[e, :, lanes] = grads[e].astype(jnp.bfloat16)
        joined = jnp.concatenate(grads, axis=1).astype(jnp.bfloat16)
        grad = matmul(turned_rows[...], joined).reshape(UNITS, UNIT, 3 * 128).astype(jnp.bfloat16)
        for e in range(3):
            ownq[pl.ds(e * UNITS, UNITS), :, lanes] = grad[:, :, e * 128 : (e + 1) * 128]
        return 0

    lax.fori_loop(0, H // 2, head_pair, 0)
    qkv_steps = []
    if nz:
        hand_all(qkv)
        qkv_steps = ordered(qkv)

    def qkv_run(low, high):
        for w, f in qkv_steps:
            if low <= w < high:
                f()

    def add_rows(x):
        return jnp.sum(x.astype(jnp.float32), axis=0, keepdims=True)

    value[0, 0:1] = add_rows(proj[0])
    value[0, 1:2] = add_rows(proj[2])
    value[0, 2:8] = small_ref[0:6]
    for c in range(FF // D):
        value[0, 8 + c : 9 + c] = ffn_ref[:, c * D : (c + 1) * D]
    partners = exchange_partners(me, nz) if nz else []
    vsems = (vsend, vrecv)
    if nz:
        vector_copy(0, value, land, vsems, partners).start()

    def vector_stage(i):
        if i < len(partners):
            vector_copy(i, value, land, vsems, partners).wait_recv()
            total = value[i] + land[i]
            if i + 1 < len(partners):
                value[i + 1] = total
                vector_copy(i + 1, value, land, vsems, partners).start()
            else:
                vec_out[...] = total

    load_w.wait()
    d_tokens = d_sum1_ref[...]
    for e in range(3):
        d_tokens = d_tokens + outer_cols(proj[e], as_matrix(w_ref[e * UNITS : (e + 1) * UNITS]))
    d_tokens_ref[...] = d_tokens
    qkv_run(1, 5)
    ffn_run(*FFN_AFTER[1])
    vector_stage(0)
    qkv_run(5, 9)
    vector_stage(1)
    ffn_run(20)
    vector_stage(2)
    qkv_run(9, 20)
    vector_stage(3)
    vector_stage(4)
    qkv_run(20, 99)
    if not nz:
        vec_out[...] = value[0]
        outs[0][...] = ownq[...]
    for i in range(len(partners)):
        vector_copy(i, value, land, vsems, partners).wait_send()
    finish_from_owners(n, place_row, head, mine, out_q, inbox_q, sems_q)
    finish_from_owners(n, place_row, head, mine, out_kv, inbox_kv, sems_kv)
    for cp, cond in pending:
        if cond is None:
            cp.wait_send()
        else:
            pl.when(cond)(cp.wait_send)


def back(heads, local, weight_grads, nz):
    n = lax.axis_size("seq")
    low, full = jnp.bfloat16, jnp.float32
    rows, w_all, d_sum1, small, d_ffn = local
    outs = [((TOK_SEQ, D), full), ((16, D), full)]
    if nz:
        outs += [((3 * UNIT * D // 128, 128), full), ((UNIT * D // 128, 128), full)]
        outs += [((UNIT * FF // 128, 128), full)] * 2
    else:
        outs += [((QKV_UNITS, UNIT, D), low)]
    stages = 3 + (max(nz, 1) - 1).bit_length()
    part = (TOK_SEQ // 2, 128)
    extra = [pltpu.VMEM(g.shape, low) for g in weight_grads] if nz else []
    slabs = [(hi - lo, FF if kind == "expand" else D) for kind, lo, hi, _ in FFN_KINDS]
    slabs += [(UNIT, hi - lo) for _, lo, hi, _ in QKV_KINDS]
    for slab in slabs if nz else ():
        extra += Reduction.buffers(nz, slab)
        extra += Reduction.semaphores(nz)
    return pl.pallas_call(
        functools.partial(back_kernel, n, nz),
        out_shape=[jax.ShapeDtypeStruct(s, d) for s, d in outs],
        in_specs=[VMEM, VMEM, SMEM, SMEM, VMEM, VMEM]
        + [VMEM, ANY, VMEM, VMEM, VMEM, ANY, ANY, ANY],
        out_specs=[VMEM] * len(outs),
        scratch_shapes=[
            pltpu.VMEM((n * BPD, BLOCK, 128), low),
            pltpu.VMEM((BPD // 2, 8 * BLOCK, 128), low),
            pltpu.VMEM((BPD // 2, 8 * BLOCK, 128), low),
            pltpu.VMEM((n * (BPD + PICKS) + 1, BLOCK, 128), full),
            pltpu.VMEM((n,) + part, low),
            pltpu.VMEM((n, TOK_SEQ, 128), low),
            pltpu.VMEM((H,) + part, low),
            pltpu.VMEM((H, TOK_SEQ, 128), low),
            pltpu.VMEM((3, TOK_SEQ, D), low),
            pltpu.VMEM((QKV_UNITS, UNIT, D), low),
            pltpu.VMEM((QKV_UNITS, UNIT, D), low),
            pltpu.VMEM((D, TOK_SEQ), low),
            pltpu.VMEM((stages, 16, D), full),
            pltpu.VMEM((stages, 16, D), full),
            pltpu.SemaphoreType.DMA((4,)),
            pltpu.SemaphoreType.DMA((stages,)),
            pltpu.SemaphoreType.DMA((stages,)),
            *exchange_sems(n),
            *exchange_sems(n),
            *extra,
        ],
        compiler_params=pltpu.CompilerParams(
            collective_id=5, has_side_effects=True, vmem_limit_bytes=61 << 20
        ),
        name="back",
    )(*heads, *local, *weight_grads)


VECTORS = (6 * D, 2 * D, FF)


def hand_out_kernel(shards, *refs):
    count = (len(refs) - 6) // 3
    arrays, totals, outs = refs[:count], refs[count], refs[count + 1 : 2 * count + 1]
    pieces = refs[2 * count + 1 : 2 * count + 4]
    held, (line, sem) = refs[2 * count + 4 : -2], refs[-2:]
    into = [pltpu.make_async_copy(*pair, sem.at[i]) for i, pair in enumerate(zip(arrays, held))]
    onto = [pltpu.make_async_copy(*pair, sem.at[i]) for i, pair in enumerate(zip(held, outs))]
    for cp in into:
        cp.start()
    for first, second in zip(into, onto):
        first.wait()
        second.start()
    me = lax.axis_index("dp") * lax.axis_size("seq") + lax.axis_index("seq")
    row = 0
    for size, out in zip(VECTORS, pieces):
        for r in range(size // D):
            line[:, r * D : (r + 1) * D] = totals[row + r : row + r + 1]
        row += size // D
        start = me * (size // shards)
        base = pl.multiple_of(start // 128 * 128, 128)
        some = line[:, pl.ds(base, 384)]
        out[...] = pltpu.roll(some, 384 - start % 128, 1)[:, 0 : size // shards]
    for cp in onto:
        cp.wait()


def hand_out(arrays, totals):
    shards = lax.axis_size("dp") * lax.axis_size("seq")
    shapes = [a.shape for a in arrays] + [(1, v // shards) for v in VECTORS]
    return pl.pallas_call(
        functools.partial(hand_out_kernel, shards),
        out_shape=[jax.ShapeDtypeStruct(s, jnp.float32) for s in shapes],
        in_specs=[ANY] * len(arrays) + [VMEM],
        out_specs=[ANY] * len(arrays) + [VMEM] * 3,
        scratch_shapes=[
            *[pltpu.VMEM(a.shape, jnp.float32) for a in arrays],
            pltpu.VMEM((1, max(VECTORS) + 384), jnp.float32),
            pltpu.SemaphoreType.DMA((len(arrays),)),
        ],
        name="hand_out",
    )(*arrays, totals)


def on_device(
    tokens,
    qkv_weight,
    out_weight,
    expand_weight,
    contract_weight,
    bias_vectors,
    gain_vectors,
    ffn_bias,
    random_blocks,
    cotangent,
):
    shards = lax.axis_size("dp") * lax.axis_size("seq")
    me = lax.axis_index("dp") * lax.axis_size("seq") + lax.axis_index("seq")
    planes = kernel_planes()
    rows = tokens.reshape(TOK_SEQ, D)
    weights = (qkv_weight, expand_weight, out_weight, contract_weight)
    vectors = (bias_vectors, gain_vectors, ffn_bias)
    if planes:
        vec = jnp.concatenate(vectors).astype(jnp.float32)
        vec = jnp.pad(vec, (0, -vec.size % 128)).reshape(1, -1)
        qkv, first, out, second = [w.reshape(-1, 128) for w in weights]
    else:
        gather = functools.partial(lax.all_gather, axis_name=("dp", "seq"), axis=0, tiled=True)
        placed = [gather(v).astype(jnp.float32) for v in vectors]
        qkv, first, out, second = [gather(w) for w in weights]
        qkv = qkv.reshape(3 * UNITS, UNIT, D)
        first, out = first.reshape(UNITS, UNIT, FF), out.reshape(UNITS, UNIT, D)
        first = jnp.concatenate([first, out], axis=2)
        second = second.reshape(UNITS, FF // UNITS, D)
        vec = jnp.pad(jnp.concatenate(placed).reshape(-1, D), ((0, 4), (0, 0)))
    (
        result,
        d_sum1,
        kv,
        queries,
        picks,
        lse,
        d_heads,
        d_expand,
        d_contract,
        d_out,
        small,
        d_ffn,
        w_all,
        links,
    ) = front(
        rows, cotangent.reshape(TOK_SEQ, D), random_blocks, vec, qkv, first, out, second, planes
    )
    d_tokens, totals, *grads = back(
        (kv, queries, picks, links, lse, d_heads),
        (rows, w_all, d_sum1, small, d_ffn),
        (d_expand, d_contract, d_out),
        planes,
    )
    if planes:
        result, d_tokens, *grads = hand_out((result, d_tokens, *grads), totals)
        grads, vectors = grads[:4], [v.reshape(-1) for v in grads[4:]]
    else:
        grads = [grads[0], d_out, d_expand, d_contract]
        *vectors, d_qkv, d_out, d_expand, d_contract = [
            lax.psum_scatter(
                g.astype(jnp.float32).reshape(-1),
                ("dp", "seq"),
                scatter_dimension=0,
                tiled=True,
            )
            for g in (totals[0:6], totals[6:8], totals[8 : 8 + FF // D], *grads)
        ]
        grads = (d_qkv, d_out, d_expand, d_contract)
    return (result[None], d_tokens[None], *[g.reshape(-1) for g in grads], *vectors)


def solution(mesh):
    return jax.shard_map(
        on_device,
        mesh=mesh,
        in_specs=(
            P("dp", "seq", None),
            P(("dp", "seq")),
            P(("dp", "seq")),
            P(("dp", "seq")),
            P(("dp", "seq")),
            P(("dp", "seq")),
            P(("dp", "seq")),
            P(("dp", "seq")),
            P("dp", None, "seq", None),
            P("dp", "seq", None),
        ),
        out_specs=(
            P("dp", "seq", None),
            P("dp", "seq", None),
            P(("dp", "seq")),
            P(("dp", "seq")),
            P(("dp", "seq")),
            P(("dp", "seq")),
            P(("dp", "seq")),
            P(("dp", "seq")),
            P(("dp", "seq")),
        ),
        check_vma=False,
    )
```

```python
import functools

import jax
import jax.numpy as jnp
from jax import lax
from jax.experimental import pallas as pl
from jax.experimental.pallas import tpu as pltpu
from jax.sharding import PartitionSpec as P

MESH = pl.DeviceIdType.MESH

D = 768
FF = 3072
H = 12
HD = 64
BLOCK = 64
TOK_SEQ = 256
SEQ_GRP = 1
BPD = 4


norm_eps = 1e-12
masked_score = -1e30


def matmul(left, right):
    return jnp.dot(left, right, preferred_element_type=jnp.float32)


def inner_rows(left, right):
    return lax.dot_general(
        left, right, (((0,), (0,)), ((), ())), preferred_element_type=jnp.float32
    )


def outer_cols(left, right):
    return lax.dot_general(
        left, right, (((1,), (1,)), ((), ())), preferred_element_type=jnp.float32
    )


def normalize(value, gain, shift):
    mean = jnp.mean(value, axis=-1, keepdims=True)
    centred = value - mean
    inverse = lax.rsqrt(jnp.mean(centred * centred, axis=-1, keepdims=True) + norm_eps)
    normed = centred * inverse
    return (normed * gain + shift, normed, inverse)


def normalize_back(grad, normed, inverse, gain):
    scaled = grad * gain
    centred = scaled - jnp.mean(scaled, axis=-1, keepdims=True)
    return inverse * (centred - normed * jnp.mean(scaled * normed, axis=-1, keepdims=True))


def place(nz):
    y = lax.axis_index("dp")
    s = lax.axis_index("seq")
    return {"y": y, "z": s // 4, "x": (s // 2) % 2, "c": s % 2}

def device(p):
    return (p["y"], p["z"] * 4 + p["x"] * 2 + p["c"])

def chip(p, nz):
    return (p["y"] * nz + p["z"]) * 2 + p["x"]

def index(p, nz):
    return chip(p, nz) * 2 + p["c"]

def nearest(m, n, j):
    if n == 2:
        return m if j == 0 else 1 - m
    out = 0
    for i in range(n):
        rank = sorted(range(n), key=lambda s: (abs(s - i), s))
        out = jnp.where(m == i, rank[j], out)
    return out

def combine(dst, srcs):
    rows, cols = dst.shape
    step = min(cols, max(128, (24 * 1024 // rows) // 128 * 128))
    while cols % step:
        step -= 128
    def part(sl):
        total = srcs[0][:, sl].astype(jnp.float32)
        for s in srcs[1:]:
            total = total + s[:, sl].astype(jnp.float32)
        dst[:, sl] = total.astype(dst.dtype)
    if cols == step:
        part(slice(None))
    else:
        def body(i, _):
            part(pl.ds(pl.multiple_of(i * step, 128), step))
            return 0
        lax.fori_loop(0, cols // step, body, 0)

def owner(head, n):
    return head * n // H


def owned(place, n):
    head = (place * H + n - 1) // n
    return jnp.minimum(head, H - 1), jnp.logical_and(head < H, owner(head, n) == place)


def post(place, h, pairs, sems, act, n):
    to = owner(h, n)
    for i, (src, dst) in enumerate(pairs):

        @pl.when(to != place)
        def _():
            act(
                pltpu.make_async_remote_copy(
                    src_ref=src.at[h],
                    dst_ref=dst(place),
                    send_sem=sems[0].at[i, h],
                    recv_sem=sems[1].at[i, place],
                    device_id=(lax.axis_index("dp"), to),
                    device_id_type=MESH,
                )
            )


def walk_to_owners(n, place, head, pairs, sems, act):
    def body(k, _):
        post(place, (head + 1 + k) % H, pairs, sems, act, n)
        return 0

    lax.fori_loop(0, H, body, 0)


def finish_to_owners(n, place, head, pairs, sems):
    walk_to_owners(n, place, head, pairs, sems, lambda cp: cp.wait_send())


def wait_to_owner(n, place, head, mine, pairs, sems):
    @pl.when(mine)
    def _():
        for i, (src, dst) in enumerate(pairs):
            cp = pltpu.make_async_copy(src.at[head], dst(place), sems[2].at[i])
            cp.start()
            cp.wait()

        def body(k, _):
            s = (place + 1 + k) % n
            for i, (src, dst) in enumerate(pairs):
                pltpu.make_async_remote_copy(
                    src_ref=src.at[0],
                    dst_ref=dst(s),
                    send_sem=sems[0].at[i, 0],
                    recv_sem=sems[1].at[i, s],
                    device_id=(lax.axis_index("dp"), place),
                    device_id_type=MESH,
                ).wait_recv()
            return 0

        lax.fori_loop(0, n - 1, body, 0)


def send_to_owners(n, place, head, mine, pairs, sems, meanwhile):
    walk_to_owners(n, place, head, pairs, sems, lambda cp: cp.start())
    meanwhile()
    wait_to_owner(n, place, head, mine, pairs, sems)
    finish_to_owners(n, place, head, pairs, sems)


def walk_from_owners(n, place, head, src, dst, sems, act):
    row = lax.axis_index("dp")

    def body(k, _):
        to = (place + 1 + k) % n
        act(
            pltpu.make_async_remote_copy(
                src_ref=src.at[to],
                dst_ref=dst.at[head],
                send_sem=sems[0].at[0, to],
                recv_sem=sems[1].at[0, head],
                device_id=(row, to),
                device_id_type=MESH,
            )
        )
        return 0

    lax.fori_loop(0, n - 1, body, 0)


def start_from_owners(n, place, head, mine, src, dst, sems):
    @pl.when(mine)
    def _():
        walk_from_owners(n, place, head, src, dst, sems, lambda cp: cp.start())
        cp = pltpu.make_async_copy(src.at[place], dst.at[head], sems[2].at[0])
        cp.start()
        cp.wait()


def wait_head(n, place, h, src, dst, sems):
    @pl.when(owner(h, n) != place)
    def _():
        pltpu.make_async_remote_copy(
            src_ref=src.at[0],
            dst_ref=dst.at[h],
            send_sem=sems[0].at[0, 0],
            recv_sem=sems[1].at[0, h],
            device_id=(lax.axis_index("dp"), place),
            device_id_type=MESH,
        ).wait_recv()


def wait_from_owners(n, place, head, src, dst, sems):
    def body(k, _):
        wait_head(n, place, (head + k) % H, src, dst, sems)
        return 0

    lax.fori_loop(0, H, body, 0)


def finish_from_owners(n, place, head, mine, src, dst, sems):
    @pl.when(mine)
    def _():
        walk_from_owners(n, place, head, src, dst, sems, lambda cp: cp.wait_send())


def swap_halves(tile):
    return pltpu.roll(tile, HD, tile.ndim - 1)


def low_lanes(shape):
    return lax.broadcasted_iota(jnp.int32, shape, len(shape) - 1) < HD


def exchange_sems(n, pairs=1):
    return [
        pltpu.SemaphoreType.DMA((pairs, max(n, H))),
        pltpu.SemaphoreType.DMA((pairs, max(n, H))),
        pltpu.SemaphoreType.DMA((pairs,)),
    ]


ANY = pl.BlockSpec(memory_space=pl.ANY)
VMEM = pl.BlockSpec(memory_space=pltpu.VMEM)
SMEM = pl.BlockSpec(memory_space=pltpu.SMEM)
MSG = TOK_SEQ + TOK_SEQ // 2


def key_list(i, n, picks_ref):
    last = n * BPD - 1

    def of(b):
        s, r = b // BPD, b % BPD
        picked = [picks_ref[s, 0, r * 3 + j] for j in range(3)]
        return [jnp.maximum(b - 1, 0), b, jnp.minimum(b + 1, last), 0, last] + picked

    return [of(2 * i), of(2 * i + 1)]


def fill_pair(lists, kv_ref, vk_ref, keys, values):
    for j in range(8):
        a, b = lists[0][j], lists[1][j]
        to = slice(j * BLOCK, (j + 1) * BLOCK)
        keys[to, 0:HD] = kv_ref[a][:, 0:HD]
        keys[to, HD:128] = vk_ref[b][:, HD:128]
        values[to, 0:HD] = vk_ref[a][:, 0:HD]
        values[to, HD:128] = kv_ref[b][:, HD:128]


def two_blocks(tile):
    left = low_lanes(tile.shape)
    zero = jnp.zeros_like(tile)
    return jnp.concatenate([jnp.where(left, tile, zero), jnp.where(left, zero, tile)], axis=0)


def pair_scores(i, n, keys, query):
    scores = outer_cols(keys, query)
    left = low_lanes((BLOCK, 128))
    right = jnp.logical_not(left)
    end = n * BPD // 2 - 1
    hide_first = jnp.logical_and(left, i == 0)
    hide_last = jnp.logical_and(right, i == end)
    return jnp.concatenate(
        [
            jnp.where(hide_first, masked_score, scores[0:BLOCK]),
            scores[BLOCK : 2 * BLOCK],
            jnp.where(hide_last, masked_score, scores[2 * BLOCK : 3 * BLOCK]),
            scores[3 * BLOCK :],
        ],
        axis=0,
    )


def turn_pairs(n, kv_ref, vk_ref):
    def body(b, _):
        for t in range(BPD):
            tile = kv_ref[b * BPD + t].astype(jnp.float32)
            vk_ref[b * BPD + t] = swap_halves(tile).astype(jnp.bfloat16)
        return 0

    lax.fori_loop(0, n, body, 0)


def chain_table(n, place, picks_vmem, picks_smem, links_ref):
    none = PICKS * n
    lane = lax.broadcasted_iota(jnp.int32, (n, 128), 1)
    turn = (lax.broadcasted_iota(jnp.int32, (n, 128), 0) + 2 * n - place - 1) % n
    order = jnp.where(lane < PICKS, turn * PICKS + lane, -1)
    picks = picks_vmem[:, 0, :]
    blocks = lax.broadcasted_iota(jnp.int32, (8, 128), 1)

    def body(k, tables):
        before, final = tables
        s = (place + 1 + k) % n
        for j in range(PICKS):
            pick, e = picks_smem[s, 0, j], k * PICKS + j
            before = jnp.where(jnp.logical_and(picks == pick, order > e), e, before)
            final = jnp.where(blocks == pick, e, final)
        return before, final

    start = (jnp.full((n, 128), none, jnp.int32), jnp.full((8, 128), none, jnp.int32))
    before, final = lax.fori_loop(0, n, body, start)
    links_ref[0:n] = before
    links_ref[n : n + 8] = final


PICKS = 3 * BPD
UNITS = 32
WIDE = 768


def greet_row(n, place, mine):
    row = lax.axis_index("dp")
    bar = pltpu.get_barrier_semaphore()

    def body(s, _):
        there = owned(s, n)[1]

        @pl.when(jnp.logical_and(s != place, jnp.logical_or(mine, there)))
        def _():
            pl.semaphore_signal(bar, inc=1, device_id=(row, s), device_id_type=MESH)

        return 0

    lax.fori_loop(0, n, body, 0)
    pl.semaphore_wait(bar, jnp.where(mine, n - 1, H))


def unpack_pair(tiles, odd, shape):
    left = low_lanes(shape)
    a, b = tiles.astype(jnp.float32), odd.astype(jnp.float32)
    return (jnp.where(left, a, swap_halves(b)), jnp.where(left, swap_halves(a), b))


def add_flat(out_ref, base, srcs, width=None):
    rows, cols = srcs[0].shape
    width = width or cols
    for k in range(cols // 128):
        lanes = slice(k * 128, (k + 1) * 128)
        total = srcs[0][:, lanes].astype(jnp.float32)
        for s in srcs[1:]:
            total = total + s[:, lanes].astype(jnp.float32)
        out_ref[pl.ds(base + k, rows, stride=width // 128), :] = total


class Reduction:
    def __init__(self, nz, me, links, direct, own, give, emit, bufs, sems, pending):
        self.nz, self.me, self.links, self.direct = nz, me, links, direct
        self.own, self.give, self.emit = own, give, emit
        self.rc, self.ra, self.rb, self.below, self.above = bufs
        self.csend, self.crecv, self.send, self.recv = sems
        self.pending = pending

    @staticmethod
    def buffers(nz, slab):
        counts = (4 * nz, nz, 2 * nz, nz, nz)
        return [pltpu.VMEM((c,) + slab, jnp.bfloat16) for c in counts]

    @staticmethod
    def semaphores(nz):
        return [pltpu.SemaphoreType.DMA((c * nz,)) for c in (4, 4, 5, 5)]

    def start(self, src, dst, slot, to, cond=None, there=None):
        cp = pltpu.make_async_remote_copy(
            src_ref=src,
            dst_ref=dst,
            send_sem=self.send.at[slot],
            recv_sem=self.recv.at[slot if there is None else there],
            device_id=device(to),
            device_id_type=MESH,
        )
        if cond is None:
            cp.start()
        else:
            pl.when(cond)(cp.start)
        self.pending.append((cp, cond))

    def arrived(self, ref, sem):
        pltpu.make_async_remote_copy(
            src_ref=ref,
            dst_ref=ref,
            send_sem=self.send.at[0],
            recv_sem=sem,
            device_id=device(dict(self.me, c=1 - self.me["c"])),
            device_id_type=MESH,
        ).wait_recv()

    def flip(self, which, f):
        d = self.links[which]
        return 1 - self.me[d] if f else self.me[d]

    def piece(self, z, a, b):
        c = {self.links[0]: a, self.links[1]: b}
        return (c["y"] * self.nz + z) * 2 + c["x"]

    def across(self, which):
        d = self.links[which]
        return dict(self.me, **{d: 1 - self.me[d]})

    def hand_over(self):
        nz = self.nz
        zs = sorted(range(nz), key=lambda z: -abs(2 * z - nz + 1))
        order = [(z, fa, fb) for fb in (1, 0) for fa in (1, 0) for z in zs]

        def one(z, fa, fb):
            def run():
                p = self.piece(z, self.flip(0, fa), self.flip(1, fb))
                cp = pltpu.make_async_remote_copy(
                    src_ref=self.give(p),
                    dst_ref=self.rc.at[p],
                    send_sem=self.csend.at[p],
                    recv_sem=self.crecv.at[p],
                    device_id=device(dict(self.me, c=1 - self.me["c"])),
                    device_id_type=MESH,
                )
                cp.start()
                self.pending.append((cp, None))

            return run

        return [one(*o) for o in order]

    def mine(self, p):
        self.arrived(self.rc.at[p], self.crecv.at[p])
        return [self.own(p), self.rc.at[p]]

    def relay(self, z, p, srcs, bref, aref, sb, sa):
        nz, mz, acc = self.nz, self.me["z"], self.rc.at[p]
        if z > 0:

            @pl.when(mz == 0)
            def _():
                combine(acc, srcs)

            @pl.when(jnp.logical_and(mz > 0, mz < z))
            def _():
                self.arrived(bref, self.recv.at[sb])
                combine(acc, srcs + [bref])

            self.start(acc, bref, sb, dict(self.me, z=jnp.minimum(mz + 1, nz - 1)), mz < z)
        if z < nz - 1:

            @pl.when(mz == nz - 1)
            def _():
                combine(acc, srcs)

            @pl.when(jnp.logical_and(mz < nz - 1, mz > z))
            def _():
                self.arrived(aref, self.recv.at[sa])
                combine(acc, srcs + [aref])

            self.start(acc, aref, sa, dict(self.me, z=jnp.maximum(mz - 1, 0)), mz > z)

    def ends(self, z, bref, aref, sb, sa):
        out = []
        if z > 0:
            self.arrived(bref, self.recv.at[sb])
            out.append(bref)
        if z < self.nz - 1:
            self.arrived(aref, self.recv.at[sa])
            out.append(aref)
        return out

    def steps(self):
        nz, me = self.nz, self.me
        zs = sorted(range(nz), key=lambda z: -abs(2 * z - nz + 1))

        def along_b(z, fa):
            def run():
                a = self.flip(0, fa)
                p = self.piece(z, a, self.flip(1, 1))
                combine(self.rc.at[p], self.mine(p))
                s = z * 2 + a
                self.start(self.rc.at[p], self.rb.at[s], s, self.across(1))

            return run

        def along_a(z):
            def run():
                a = self.flip(0, 1)
                p = self.piece(z, a, self.flip(1, 0))
                s = z * 2 + a
                srcs = self.mine(p)
                self.arrived(self.rb.at[s], self.recv.at[s])
                combine(self.rc.at[p], srcs + [self.rb.at[s]])
                self.start(self.rc.at[p], self.ra.at[z], 2 * nz + z, self.across(0))

            return run

        def chain(z):
            def run():
                p = self.piece(z, self.flip(0, 0), self.flip(1, 0))
                s = z * 2 + self.flip(0, 0)
                srcs = self.mine(p)
                self.arrived(self.rb.at[s], self.recv.at[s])
                self.arrived(self.ra.at[z], self.recv.at[2 * nz + z])
                srcs += [self.rb.at[s], self.ra.at[z]]
                if self.direct:
                    mz = me["z"]

                    @pl.when(mz != z)
                    def _():
                        combine(self.rc.at[p], srcs)

                    to = dict(me, z=z)
                    self.start(
                        self.rc.at[p], self.below.at[mz], 3 * nz + z, to, mz != z, 3 * nz + mz
                    )
                    return
                bref, aref = self.below.at[z], self.above.at[z]
                self.relay(z, p, srcs, bref, aref, 3 * nz + z, 4 * nz + z)

            return run

        def last():
            for z in range(nz):

                @pl.when(me["z"] == z)
                def _():
                    p = self.piece(z, self.flip(0, 0), self.flip(1, 0))
                    s = z * 2 + self.flip(0, 0)
                    srcs = [self.own(p), self.rc.at[p], self.rb.at[s], self.ra.at[z]]
                    if self.direct:
                        for other in range(nz):
                            if other != z:
                                ref = self.below.at[other]
                                self.arrived(ref, self.recv.at[3 * nz + other])
                                srcs.append(ref)
                        self.emit(srcs)
                        return
                    bref, aref = self.below.at[z], self.above.at[z]
                    self.emit(srcs + self.ends(z, bref, aref, 3 * nz + z, 4 * nz + z))

        out = [(1 + i, along_b(z, 1)) for i, z in enumerate(zs)]
        out += [(5 + i, along_b(z, 0)) for i, z in enumerate(zs)]
        out += [(5.5 + i, along_a(z)) for i, z in enumerate(zs)]
        out += [(9.5 + i, chain(z)) for i, z in enumerate(zs)]
        return out + [(20, last)]


class Spread:
    def __init__(self, nz, me, order, at, sems, pending):
        self.nz, self.me, self.order, self.at = nz, me, order, at
        self.send, self.recv, self.csend, self.crecv = sems
        self.pending = pending

    @staticmethod
    def semaphores(nz):
        chips = 4 * nz
        return [pltpu.SemaphoreType.DMA((chips, 4))] + [pltpu.SemaphoreType.DMA((chips,))] * 3

    def copy(self, slot, send, recv, to):
        ref = self.at(slot)
        return pltpu.make_async_remote_copy(
            src_ref=ref,
            dst_ref=ref,
            send_sem=send,
            recv_sem=recv,
            device_id=device(to),
            device_id_type=MESH,
        )

    def start(self, cp, cond=None):
        if cond is None:
            cp.start()
        else:
            pl.when(cond)(cp.start)
        self.pending.append((cp, cond))

    def one(self, steps):
        nz, me = self.nz, self.me
        size = {"y": 2, "z": nz, "x": 2}
        own = not any(steps)

        def run():
            src = dict(me)
            for d, i in zip(self.order, steps):
                src[d] = nearest(me[d], size[d], i)
            c = chip(src, nz)
            slot = c * 2 + me["c"]
            if not own:
                self.copy(slot, self.send.at[c, 0], self.recv.at[c], me).wait_recv()
            stage = 2 if steps[2] else (1 if steps[1] else 0)
            for t in range(stage, 3):
                d = self.order[t]
                onward = t == stage and not own
                if d == "z":
                    up, down = me["z"] < nz - 1, me["z"] > 0
                    if onward:
                        up = jnp.logical_and(up, src["z"] <= me["z"])
                        down = jnp.logical_and(down, src["z"] >= me["z"])
                    above = dict(me, z=jnp.minimum(me["z"] + 1, nz - 1))
                    below = dict(me, z=jnp.maximum(me["z"] - 1, 0))
                    self.start(self.copy(slot, self.send.at[c, 0], self.recv.at[c], above), up)
                    self.start(self.copy(slot, self.send.at[c, 1], self.recv.at[c], below), down)
                elif not (onward and steps[t]):
                    way = 2 if d == "x" else 3
                    to = dict(me, **{d: 1 - me[d]})
                    self.start(self.copy(slot, self.send.at[c, way], self.recv.at[c], to))
            sibling = dict(me, c=1 - me["c"])
            self.start(self.copy(slot, self.csend.at[c], self.crecv.at[c], sibling))

        return run

    def steps(self):
        size = {"y": 2, "z": self.nz, "x": 2}
        n0, n1, n2 = (size[d] for d in self.order)
        return [
            (i0 + i1 + i2, self.one((i0, i1, i2)))
            for i2 in range(n2)
            for i1 in range(n1)
            for i0 in range(n0)
        ]

    def finish(self):
        def body(c, _):
            slot = c * 2 + 1 - self.me["c"]
            self.copy(slot, self.csend.at[c], self.crecv.at[c], self.me).wait_recv()
            return 0

        lax.fori_loop(0, 4 * self.nz, body, 0)


def run_in_order(items, low, high):
    steps = [(w, i, f) for i, item in enumerate(items) for w, f in item.steps()]
    for w, _, f in sorted(steps, key=lambda s: s[:2]):
        if low <= w < high:
            f()


def exchange_partners(me, nz):
    partners = [dict(me, **{d: 1 - me[d]}) for d in ("c", "x", "y")]
    step = 1
    while step < nz:
        partners.append(dict(me, z=me["z"] + step - 2 * step * ((me["z"] // step) % 2)))
        step *= 2
    return partners


def vector_copy(i, value, land, sems, partners):
    return pltpu.make_async_remote_copy(
        src_ref=value.at[i],
        dst_ref=land.at[i],
        send_sem=sems[0].at[i],
        recv_sem=sems[1].at[i],
        device_id=device(partners[i]),
        device_id_type=MESH,
    )


def greet_row_and_y(n, me, place_row):
    bar = pltpu.get_barrier_semaphore()

    def greet(k, _):
        to = (place_row + 1 + k) % n
        pl.semaphore_signal(bar, inc=1, device_id=(me["y"], to), device_id_type=MESH)
        return 0

    lax.fori_loop(0, n - 1, greet, 0)
    pl.semaphore_signal(bar, inc=1, device_id=(1 - me["y"], place_row), device_id_type=MESH)
    return lambda: pl.semaphore_wait(bar, n)


UNIT = D // UNITS
THIRD = FF // UNITS // 3
QKV_ORDERS = (("z", "x", "y"), ("z", "y", "x"), ("x", "y", "z"))
REST = (
    ("first", 0, UNIT, ("z", "x", "y")),
    ("second", THIRD, FF // UNITS, ("z", "y", "x")),
    ("second", 0, THIRD, ("z", "x", "y")),
)


EARLY = {1: (0, 1), 4: (1, 2), 5: (2, 3)}
LATE = ((3, 4), (4, 5), (99, 99), (99, 99), (99, 99))


def from_flat(flat, cols, rows):
    step = cols // 128
    return [flat[pl.ds(k, rows, stride=step), :] for k in range(step)]


def as_matrix(units):
    count, rows, cols = units.shape
    return units.astype(jnp.float32).reshape(count * rows, cols).astype(jnp.bfloat16)


def kernel_planes():
    seq = lax.axis_size("seq")
    if lax.axis_size("dp") != 2 or 2 * seq != UNITS or seq % 4:
        return 0
    return seq // 4


def place_vectors(me, shards, pieces, line, value):
    packed = pieces[...]
    at, row = 0, 0
    value[0] = jnp.zeros_like(value[0])
    for size in VECTORS:
        width = size // shards
        start = me * width
        inside = lax.broadcasted_iota(jnp.int32, packed.shape, 1)
        inside = jnp.logical_and(inside >= at, inside < at + width)
        moved = jnp.where(inside, packed, 0.0)
        line[...] = jnp.zeros_like(line)
        base = pl.multiple_of(start // 128 * 128, 128)
        line[:, pl.ds(base, 384)] = pltpu.roll(moved, (start % 128 - at) % 384, 1)
        for r in range(size // D):
            value[0, row + r : row + r + 1] = line[:, r * D : (r + 1) * D]
        row += size // D
        at += width


def front_kernel(n, nz, *refs):
    rows_ref, cot_ref, picks_ref, vec_in, qkv_in, first_in, out_in, second_in = refs[:8]
    (
        result_ref,
        d_sum1_ref,
        kv_hbm,
        q_hbm,
        picks_hbm,
        lse_ref,
        d_heads,
        dw1_hbm,
        dw2_hbm,
        dwo_hbm,
        small_ref,
        d_ffn_ref,
        w_hbm,
        links_hbm,
    ) = refs[8:22]
    (
        w_ref,
        first_ref,
        second_ref,
        flat,
        value,
        land,
        box_kv,
        box_q,
        kv_ref,
        q_ref,
        vk_ref,
        picks_smem,
        keys,
        values,
        attended,
        inbox,
        grad_box,
        slope_ref,
        active_ref,
        dw1_ref,
        dw2_ref,
        dwo_ref,
        mixed_ref,
        load_sem,
        store_sem,
        keep_sem,
        vsend,
        vrecv,
        links_ref,
        picks_vmem,
        line,
        d_up_ref,
    ) = refs[22:54]
    sems_qkv, sems_in, sems_out = refs[54:57], refs[57:60], refs[60:63]
    rest = list(refs[63:])
    place_row = lax.axis_index("seq")
    head, mine = owned(place_row, n)
    pending = []

    if nz:
        me = place(nz)
        slot = index(me, nz)
        hold = greet_row_and_y(n, me, place_row)
        stages = 3 + (nz - 1).bit_length()

        def take():
            out = rest[:4]
            del rest[:4]
            return out

        def widen(src):
            count = src.shape[0]
            flat[0:count] = src[...].astype(jnp.float32)

        widen(qkv_in)
        for j in range(3):
            step = D // 128
            for k in range(step):
                col = flat[pl.ds(j * UNIT * step + k, UNIT, stride=step), :]
                w_ref[slot * 3 + j, :, k * 128 : (k + 1) * 128] = col.astype(jnp.bfloat16)
        place_vectors(slot, 8 * nz, vec_in, line, value)
        hold()
        qkv_items = [
            Spread(nz, me, order, lambda s, j=j: w_ref.at[s * 3 + j], take(), pending)
            for j, order in enumerate(QKV_ORDERS)
        ]
        buffers = {"first": first_ref, "second": second_ref}

        def part(kind, lo, hi):
            ref = buffers[kind]
            if hi - lo == ref.shape[1]:
                return lambda s: ref.at[s]
            return lambda s: ref.at[s, lo:hi]

        rest_items = [
            Spread(nz, me, order, part(kind, lo, hi), take(), pending)
            for kind, lo, hi, order in REST
        ]
        partners = exchange_partners(me, nz)
        vsems = (vsend, vrecv)
        vector_copy(0, value, land, vsems, partners).start()
        run_in_order(qkv_items, 0, 1)
        for src, dst, at, cols, count in (
            (first_in, first_ref, 0, FF, UNIT),
            (out_in, first_ref, FF, D, UNIT),
            (second_in, second_ref, 0, D, FF // UNITS),
        ):
            widen(src)
            for k, col in enumerate(from_flat(flat, cols, count)):
                dst[slot, :, at + k * 128 : at + (k + 1) * 128] = col.astype(jnp.bfloat16)

        def vector_stage(i):
            vector_copy(i, value, land, vsems, partners).wait_recv()
            value[i + 1] = value[i] + land[i]
            if i + 1 < stages:
                vector_copy(i + 1, value, land, vsems, partners).start()

        for depth in range(1, nz + 2):
            vector_stage(min(depth - 1, stages)) if depth <= stages else None
            run_in_order(qkv_items, depth, depth + 1)
            if depth in EARLY:
                run_in_order(rest_items, *EARLY[depth])
        for i in range(nz + 1, stages):
            vector_stage(i)
        for item in qkv_items:
            item.finish()
        vec = value.at[stages]
    else:
        greet_row(n, place_row, mine)
        loads = [
            pltpu.make_async_copy(src, dst, load_sem.at[i])
            for i, (src, dst) in enumerate(
                ((qkv_in, w_ref), (first_in, first_ref), (second_in, second_ref))
            )
        ]
        for cp in loads:
            cp.start()
        for cp in loads:
            cp.wait()
        vec = vec_in

    def rest_steps(low, high, part=slice(None)):
        if nz:
            run_in_order(rest_items[part], low, high)

    rows = rows_ref[...]
    left = low_lanes((TOK_SEQ, 128))
    left_q = low_lanes((BLOCK, 128))
    wide = 256
    parcels = (
        (box_kv, lambda s: kv_ref.at[pl.ds(s * BPD, BPD)]),
        (box_q, lambda s: q_ref.at[s]),
        (picks_ref, lambda s: picks_hbm.at[s]),
    )

    def project_some(step, _):
        g = (place_row + step) % (D // wide)
        cols = pl.ds(pl.multiple_of(g * wide, wide), wide)

        def project(e):
            return matmul(rows, as_matrix(w_ref[e * UNITS : (e + 1) * UNITS, :, cols]))

        q = (project(0) + vec[0:1, cols]) * HD ** (-0.5)
        k = project(1)
        v = project(2) + vec[1:2, cols]
        for p in range(wide // 128):
            h = g * (wide // HD) + p * 2
            lanes = slice(p * 128, (p + 1) * 128)
            kp, vp, qp = k[:, lanes], v[:, lanes], q[:, lanes]
            even, odd = jnp.where(left, kp, swap_halves(vp)), jnp.where(left, swap_halves(kp), vp)
            for t in range(BPD):
                part = slice(t * BLOCK, (t + 1) * BLOCK)
                box_kv[h, t] = even[part].astype(jnp.bfloat16)
                box_kv[h + 1, t] = odd[part].astype(jnp.bfloat16)
            turned = swap_halves(qp)
            for t in range(BPD // 2):
                a = slice(2 * t * BLOCK, (2 * t + 1) * BLOCK)
                b = slice((2 * t + 1) * BLOCK, (2 * t + 2) * BLOCK)
                to = slice(t * BLOCK, (t + 1) * BLOCK)
                box_q[h, to, :] = jnp.where(left_q, qp[a], turned[b]).astype(jnp.bfloat16)
                box_q[h + 1, to, :] = jnp.where(left_q, turned[a], qp[b]).astype(jnp.bfloat16)
            for u in range(2):
                post(place_row, h + u, parcels, sems_qkv, lambda cp: cp.start(), n)
        return 0

    lax.fori_loop(0, D // wide, project_some, 0)
    rest_steps(*LATE[0])
    wait_to_owner(n, place_row, head, mine, parcels, sems_qkv)

    keep = (
        pltpu.make_async_copy(kv_ref, kv_hbm, keep_sem.at[0]),
        pltpu.make_async_copy(q_ref, q_hbm, keep_sem.at[3]),
    )
    keep_w = pltpu.make_async_copy(w_ref, w_hbm, keep_sem.at[2])
    keep_w.start()
    keep_links = pltpu.make_async_copy(links_ref, links_hbm, keep_sem.at[4])
    groups = 4

    @pl.when(mine)
    def _():
        for copy in keep:
            copy.start()
        copies = (
            pltpu.make_async_copy(picks_hbm, picks_smem, keep_sem.at[1]),
            pltpu.make_async_copy(picks_hbm, picks_vmem, keep_sem.at[5]),
        )
        for cp in copies:
            cp.start()
        for cp in copies:
            cp.wait()
        turn_pairs(n, kv_ref, vk_ref)
        chain_table(n, place_row, picks_vmem, picks_smem, links_ref)
        keep_links.start()

    def attend_some(k, _):
        s = (place_row + 1 + k) % n
        for t in range(BPD // 2):
            i = s * (BPD // 2) + t
            fill_pair(key_list(i, n, picks_smem), kv_ref, vk_ref, keys.at[t], values.at[t])
        for t in range(BPD // 2):
            i = s * (BPD // 2) + t
            part = slice(t * BLOCK, (t + 1) * BLOCK)
            query = two_blocks(q_ref[s, part, :])
            scores = pair_scores(i, n, keys[t], query)
            top = jnp.max(scores, axis=0, keepdims=True)
            weights = jnp.exp(scores - top)
            total = jnp.sum(weights, axis=0, keepdims=True)
            probs = (weights * (1.0 / total)).astype(jnp.bfloat16)
            full = inner_rows(probs, values[t])
            attended[s, part, :] = jnp.where(left_q, full[:BLOCK], full[BLOCK:]).astype(
                jnp.bfloat16
            )
            lse_ref[i] = top + jnp.log(total)

        @pl.when(s != place_row)
        def _():
            pltpu.make_async_remote_copy(
                src_ref=attended.at[s],
                dst_ref=inbox.at[head],
                send_sem=sems_in[0].at[0, s],
                recv_sem=sems_in[1].at[0, head],
                device_id=(lax.axis_index("dp"), s),
                device_id_type=MESH,
            ).start()

        return 0

    for g in range(groups):

        @pl.when(mine)
        def _():
            lax.fori_loop(g * (n // groups), (g + 1) * (n // groups), attend_some, 0)

        rest_steps(*LATE[1 + g])

    @pl.when(mine)
    def _():
        cp = pltpu.make_async_copy(attended.at[place_row], inbox.at[head], sems_in[2].at[0])
        cp.start()
        cp.wait()

    rest_steps(5, 99, slice(0, 1))
    if nz:
        rest_items[0].finish()
    wait_from_owners(n, place_row, head, attended, inbox, sems_in)

    for h in range(0, H, 2):
        for t in range(BPD // 2):
            part = slice(t * BLOCK, (t + 1) * BLOCK)
            a, b = unpack_pair(inbox[h, part, :], inbox[h + 1, part, :], (BLOCK, 128))
            lanes = slice(h * HD, (h + 2) * HD)
            mixed_ref[2 * t * BLOCK : (2 * t + 1) * BLOCK, lanes] = a.astype(jnp.bfloat16)
            mixed_ref[(2 * t + 1) * BLOCK : (2 * t + 2) * BLOCK, lanes] = b.astype(jnp.bfloat16)
    out_w = as_matrix(first_ref[:, :, FF : FF + D])
    hidden1 = rows_ref[...].astype(jnp.float32) + matmul(mixed_ref[...], out_w) + vec[2:3]
    normed_out1, normed1, inverse1 = normalize(hidden1, vec[6:7], vec[3:4])
    lowered = normed_out1.astype(jnp.bfloat16)
    per = UNITS * WIDE // FF

    def second_rows(c):
        return second_ref[pl.ds(c * per, per)].reshape(WIDE, D)

    def up_step(c, _):
        cols = pl.ds(pl.multiple_of(c * WIDE, WIDE), WIDE)
        up = matmul(lowered, as_matrix(first_ref[:, :, cols])) + vec[pl.ds(8 + c, 1)]
        square = up * up
        inner = (2 / jnp.pi) ** 0.5 * (up + 0.044715 * up * square)
        curve = jnp.tanh(inner)
        active = (0.5 * up * (1 + curve)).astype(jnp.bfloat16)
        slope_ref[:, cols] = 0.5 * (1 + curve) + 0.5 * up * (1 - curve * curve) * (
            (2 / jnp.pi) ** 0.5 * (1 + 3 * 0.044715 * square)
        )
        active_ref[:, cols] = active
        return 0

    def down_step(c, hidden):
        cols = pl.ds(pl.multiple_of(c * WIDE, WIDE), WIDE)
        return hidden + matmul(active_ref[:, cols], second_rows(c))

    rest_steps(5, 99, slice(1, 3))
    lax.fori_loop(0, FF // WIDE, up_step, 0)
    if nz:
        for item in rest_items[1:]:
            item.finish()
    hidden2 = lax.fori_loop(0, FF // WIDE, down_step, normed_out1 + vec[4:5])
    result, normed2, inverse2 = normalize(hidden2, vec[7:8], vec[5:6])
    result_ref[...] = result
    grad = cot_ref[...].astype(jnp.float32)
    d_sum2 = normalize_back(grad, normed2, inverse2, vec[7:8])
    d_down = d_sum2.astype(jnp.bfloat16)

    def add_rows(x):
        return jnp.sum(x, axis=0, keepdims=True)

    small_ref[2:3] = add_rows(d_down.astype(jnp.float32))
    small_ref[3:4] = add_rows(grad)
    small_ref[5:6] = add_rows(grad * normed2)

    def stores(c):
        cols = pl.ds(pl.multiple_of(c * WIDE, WIDE), WIDE)
        slabs = pl.ds(c * per, per)
        return (
            pltpu.make_async_copy(dw1_ref.at[:, :, cols], dw1_hbm.at[:, :, cols], store_sem.at[0, c]),
            pltpu.make_async_copy(dw2_ref.at[slabs], dw2_hbm.at[slabs], store_sem.at[1, c]),
        )

    def back_step(c, d_norm1):
        cols = pl.ds(pl.multiple_of(c * WIDE, WIDE), WIDE)
        d_active = outer_cols(d_down, second_rows(c))
        d_up = (d_active * slope_ref[:, cols]).astype(jnp.bfloat16)
        d_ffn_ref[:, cols] = add_rows(d_up.astype(jnp.float32))
        d_up_ref[:, cols] = d_up
        return d_norm1 + outer_cols(d_up, as_matrix(first_ref[:, :, cols]))

    d_norm1 = lax.fori_loop(0, FF // WIDE, back_step, d_sum2)
    small_ref[1:2] = add_rows(d_norm1)
    small_ref[4:5] = add_rows(d_norm1 * normed1)
    d_sum1 = normalize_back(d_norm1, normed1, inverse1, vec[6:7])
    d_sum1_ref[...] = d_sum1
    d_attn = d_sum1.astype(jnp.bfloat16)
    small_ref[0:1] = add_rows(d_attn.astype(jnp.float32))
    d_mixed = outer_cols(d_attn, as_matrix(first_ref[:, :, FF : FF + D]))
    for h in range(0, H, 2):
        for t in range(BPD // 2):
            part = slice(t * BLOCK, (t + 1) * BLOCK)
            lanes = slice(h * HD, (h + 2) * HD)
            a, b = unpack_pair(
                d_mixed[2 * t * BLOCK : (2 * t + 1) * BLOCK, lanes],
                d_mixed[(2 * t + 1) * BLOCK : (2 * t + 2) * BLOCK, lanes],
                (BLOCK, 128),
            )
            grad_box[h, part, :] = a.astype(jnp.bfloat16)
            grad_box[h + 1, part, :] = b.astype(jnp.bfloat16)

    store_out = pltpu.make_async_copy(dwo_ref, dwo_hbm, load_sem.at[0])

    def weight_grads(c, _):
        cols = pl.ds(pl.multiple_of(c * WIDE, WIDE), WIDE)
        dw2 = inner_rows(active_ref[:, cols], d_down)
        dw2_ref[pl.ds(c * per, per)] = dw2.reshape(per, FF // UNITS, D).astype(jnp.bfloat16)
        dw1 = inner_rows(lowered, d_up_ref[:, cols])
        dw1_ref[:, :, cols] = dw1.reshape(UNITS, UNIT, WIDE).astype(jnp.bfloat16)
        for cp in stores(c):
            cp.start()
        return 0

    def late():
        lax.fori_loop(0, FF // WIDE, weight_grads, 0)
        dwo = inner_rows(mixed_ref[...], d_attn).reshape(UNITS, UNIT, D)
        dwo_ref[...] = dwo.astype(jnp.bfloat16)
        store_out.start()

    send_to_owners(n, place_row, head, mine, ((grad_box, lambda s: d_heads.at[s]),), sems_out, late)
    store_out.wait()

    def drain(c, _):
        for cp in stores(c):
            cp.wait()
        return 0

    lax.fori_loop(0, FF // WIDE, drain, 0)

    @pl.when(mine)
    def _():
        for copy in keep:
            copy.wait()
        keep_links.wait()

    keep_w.wait()
    finish_from_owners(n, place_row, head, mine, attended, inbox, sems_in)
    finish_to_owners(n, place_row, head, parcels, sems_qkv)
    if nz:
        for i in range(stages):
            vector_copy(i, value, land, vsems, partners).wait_send()
    for cp, cond in pending:
        if cond is None:
            cp.wait_send()
        else:
            pl.when(cond)(cp.wait_send)


def front(rows, cotangent, picks, vec, qkv, first, out, second, nz):
    n = lax.axis_size("seq")
    low, full = jnp.bfloat16, jnp.float32
    picks = jnp.pad(picks.reshape(H, 1, BPD * 3), ((0, 0), (0, 7), (0, 128 - BPD * 3)))
    part = (TOK_SEQ // 2, 128)
    pairs = n * BPD // 2
    units = [(UNITS, UNIT, FF), (UNITS, FF // UNITS, D), (UNITS, UNIT, D)]
    shapes = [((TOK_SEQ, D), full), ((TOK_SEQ, D), full)]
    shapes += [((n * BPD, BLOCK, 128), low), ((n,) + part, low)]
    shapes += [((n, 8, 128), jnp.int32), ((pairs, 1, 128), full), ((n,) + part, low)]
    shapes += [(u, low) for u in units] + [((8, D), full), ((1, FF), full)]
    shapes += [((3 * UNITS, UNIT, D), low), ((n + 8, 128), jnp.int32)]
    stages = 3 + (max(nz, 1) - 1).bit_length()
    where = VMEM if nz else ANY
    extra = []
    for _ in range(6 if nz else 0):
        extra += Spread.semaphores(nz)
    return pl.pallas_call(
        functools.partial(front_kernel, n, nz),
        out_shape=[jax.ShapeDtypeStruct(s, d) for s, d in shapes],
        in_specs=[VMEM, VMEM, ANY, VMEM, where, where, where, where],
        out_specs=[VMEM, VMEM, ANY, ANY, ANY, VMEM, ANY, ANY, ANY, ANY, VMEM, VMEM, ANY, ANY],
        scratch_shapes=[
            pltpu.VMEM((3 * UNITS, UNIT, D), low),
            pltpu.VMEM((UNITS, UNIT, FF + D), low),
            pltpu.VMEM((UNITS, FF // UNITS, D), low),
            pltpu.VMEM((UNIT * FF // 128, 128), full),
            pltpu.VMEM((stages + 1, 16, D), full),
            pltpu.VMEM((stages, 16, D), full),
            pltpu.VMEM((H, BPD, BLOCK, 128), low),
            pltpu.VMEM((H,) + part, low),
            pltpu.VMEM((n * BPD, BLOCK, 128), low),
            pltpu.VMEM((n,) + part, low),
            pltpu.VMEM((n * BPD, BLOCK, 128), low),
            pltpu.SMEM((n, 8, 128), jnp.int32),
            pltpu.VMEM((BPD // 2, 8 * BLOCK, 128), low),
            pltpu.VMEM((BPD // 2, 8 * BLOCK, 128), low),
            pltpu.VMEM((n,) + part, low),
            pltpu.VMEM((H,) + part, low),
            pltpu.VMEM((H,) + part, low),
            pltpu.VMEM((TOK_SEQ, FF), full),
            pltpu.VMEM((TOK_SEQ, FF), low),
            *[pltpu.VMEM(u, low) for u in units],
            pltpu.VMEM((TOK_SEQ, D), low),
            pltpu.SemaphoreType.DMA((3,)),
            pltpu.SemaphoreType.DMA((2, FF // WIDE)),
            pltpu.SemaphoreType.DMA((6,)),
            pltpu.SemaphoreType.DMA((stages,)),
            pltpu.SemaphoreType.DMA((stages,)),
            pltpu.VMEM((n + 8, 128), jnp.int32),
            pltpu.VMEM((n, 8, 128), jnp.int32),
            pltpu.VMEM((1, max(VECTORS) + 384), full),
            pltpu.VMEM((TOK_SEQ, FF), low),
            *exchange_sems(n, 3),
            *exchange_sems(n),
            *exchange_sems(n),
            *extra,
        ],
        compiler_params=pltpu.CompilerParams(
            collective_id=0, has_side_effects=True, vmem_limit_bytes=60 << 20
        ),
        name="front",
    )(rows, cotangent, picks, vec, qkv, first, out, second)


FFN_KINDS = (
    ("expand", 0, UNIT, ("x", "y")),
    ("contract", 0, FF // UNITS, ("y", "x")),
    ("out", 0, UNIT, ("x", "y")),
)
QKV_KINDS = (
    (0, 0, D, ("x", "y")),
    (1, 0, D, ("y", "x")),
    (2, 0, D // 2, ("x", "y")),
    (2, D // 2, D, ("y", "x")),
)
QKV_UNITS = 3 * UNITS


FFN_WITH = ((1,), (2,), (3,), (4,), (), (), (), ())
FFN_AFTER = ((5, 5.5, 6, 6.5, 7, 7.5, 8, 8.5), (9.5, 10.5, 11.5, 12.5))


def send_one(sems, src, dst, head, to):
    return pltpu.make_async_remote_copy(
        src_ref=src.at[to],
        dst_ref=dst.at[head],
        send_sem=sems[0].at[0, to],
        recv_sem=sems[1].at[0, head],
        device_id=(lax.axis_index("dp"), to),
        device_id_type=MESH,
    )


def back_kernel(n, nz, *refs):
    kv_ref, q_ref, picks_ref, links_ref, lse_ref, grad_ref = refs[:6]
    rows_ref, w_hbm, d_sum1_ref, small_ref, ffn_ref, dw1, dw2, dwo = refs[6:14]
    d_tokens_ref, vec_out = refs[14:16]
    outs = refs[16 : 20 if nz else 17]
    rest = list(refs[20 if nz else 17 :])
    vk_ref, keys, values, acc, out_q, out_kv, inbox_q, inbox_kv, proj, w_ref, ownq = rest[:11]
    turned_rows, value, land, load_sem, vsend, vrecv = rest[11:17]
    sems_q, sems_kv = rest[17:20], rest[20:23]
    own1, own2, owno = rest[23:26] if nz else (None, None, None)
    rest = rest[26:]
    place_row = lax.axis_index("seq")
    head, mine = owned(place_row, n)
    blocks, none = n * BPD, n * BPD + n * PICKS
    pending = []

    load_w = pltpu.make_async_copy(w_hbm, w_ref, load_sem.at[0])
    load_w.start()
    if nz:
        me = place(nz)
        core = me["c"]
        loads = [
            pltpu.make_async_copy(src, dst, load_sem.at[1 + i])
            for i, (src, dst) in enumerate(((dw1, own1), (dw2, own2), (dwo, owno)))
        ]
        for cp in loads:
            cp.start()
        hold = greet_row_and_y(n, me, place_row)
    else:
        greet_row(n, place_row, mine)

    @pl.when(mine)
    def _():
        turn_pairs(n, kv_ref, vk_ref)

        def clear(b, _):
            acc[b] = jnp.zeros((BLOCK, 128), jnp.float32)
            return 0

        lax.fori_loop(0, blocks, clear, 0)
        clear(none, 0)

    def take(count):
        out = rest[:count]
        del rest[:count]
        return out

    def ffn_item(kind, lo, hi, links):
        far, near = {"expand": (dw1, own1), "contract": (dw2, own2), "out": (dwo, owno)}[kind]
        target = outs[("out", "expand", "contract").index(kind) + 1]
        whole = hi - lo == far.shape[1]

        def at(ref, t):
            return ref.at[t] if whole else ref.at[t, lo:hi]

        return Reduction(
            nz,
            me,
            links,
            False,
            lambda p: at(near, p * 2 + core),
            lambda p: at(far, p * 2 + 1 - core),
            lambda srcs: add_flat(target, lo * (far.shape[2] // 128), srcs),
            take(5),
            take(4),
            pending,
        )

    def qkv_item(j, lo, hi, links):
        def at(t):
            ref = ownq.at[t * 3 + j]
            return ref if hi - lo == D else ref.at[:, lo:hi]

        return Reduction(
            nz,
            me,
            links,
            True,
            lambda p: at(p * 2 + core),
            lambda p: at(p * 2 + 1 - core),
            lambda srcs: add_flat(outs[0], (j * UNIT * D + lo) // 128, srcs, D),
            take(5),
            take(4),
            pending,
        )

    def hand_all(items):
        for group in zip(*[i.hand_over() for i in items]):
            for f in group:
                f()

    def ordered(items):
        steps = [(w + 0.01 * i, f) for i, item in enumerate(items) for w, f in item.steps()]
        return sorted(steps, key=lambda s: s[0])

    turned_rows[...] = rows_ref[...].T
    ffn_steps = []
    if nz:
        ffn = [ffn_item(*k) for k in FFN_KINDS]
        qkv = [qkv_item(*k) for k in QKV_KINDS]
        ffn_steps = ordered(ffn)
        hold()
        hand_all(ffn)
        for cp in loads:
            cp.wait()

    def ffn_run(*wanted):
        for at in wanted:
            for w, f in ffn_steps:
                if abs(w - at) < 0.1:
                    f()

    left = low_lanes((BLOCK, 128))
    both = range(BPD // 2)

    def attend_some(k, _):
        s = (place_row + 1 + k) % n
        lists = [key_list(s * (BPD // 2) + t, n, picks_ref) for t in both]
        for t in both:
            fill_pair(lists[t], kv_ref, vk_ref, keys.at[t], values.at[t])
        parts = []
        for t in both:
            i = s * (BPD // 2) + t
            part = slice(t * BLOCK, (t + 1) * BLOCK)
            query = two_blocks(q_ref[s, part, :])
            grad = two_blocks(grad_ref[s, part, :])
            probs = jnp.exp(pair_scores(i, n, keys[t], query) - lse_ref[i])
            d_probs = outer_cols(values[t], grad)
            rows = jnp.sum(probs * d_probs, axis=0, keepdims=True)
            d_scores = (probs * (d_probs - rows)).astype(jnp.bfloat16)
            d_values = matmul(probs.astype(jnp.bfloat16), grad)
            d_keys = matmul(d_scores, query)
            full = inner_rows(d_scores, keys[t]) * HD ** (-0.5)
            out_q[s, part, :] = jnp.where(left, full[:BLOCK], full[BLOCK:]).astype(jnp.bfloat16)
            parts.append((d_keys, d_values))

        @pl.when(s != place_row)
        def _():
            send_one(sems_q, out_q, inbox_q, head, s).start()

        for t in both:
            tiles = []
            for j in range(8):
                part = slice(j * BLOCK, (j + 1) * BLOCK)
                dk, dv = parts[t][0][part], parts[t][1][part]
                a = jnp.where(left, dk, swap_halves(dv))
                b = jnp.where(left, swap_halves(dk), dv)
                tiles.append((a, b))
            a = (s * (BPD // 2) + t) * 2
            acc[jnp.maximum(a - 1, 0)] += tiles[0][0]
            acc[a] += tiles[1][0] + tiles[0][1]
            acc[a + 1] += tiles[2][0] + tiles[1][1]
            acc[jnp.minimum(a + 2, blocks - 1)] += tiles[2][1]
            acc[0] += tiles[3][0] + tiles[3][1]
            acc[blocks - 1] += tiles[4][0] + tiles[4][1]
            for u in range(2):
                for j in range(3):
                    e = (2 * t + u) * 3 + j
                    acc[blocks + k * PICKS + e] = tiles[5 + j][u] + acc[blocks + links_ref[s, e]]
        return 0

    groups = 8
    for g in range(groups):

        @pl.when(mine)
        def _():
            lax.fori_loop(g * (n // groups), (g + 1) * (n // groups), attend_some, 0)

        ffn_run(*FFN_WITH[g])

    @pl.when(mine)
    def _():
        def close(k, _):
            s = (place_row + 1 + k) % n
            for t in range(BPD):
                b = s * BPD + t
                total = acc[b] + acc[blocks + links_ref[n, b]]
                out_kv[s, t * BLOCK : (t + 1) * BLOCK, :] = total.astype(jnp.bfloat16)

            @pl.when(s != place_row)
            def _():
                send_one(sems_kv, out_kv, inbox_kv, head, s).start()

            return 0

        lax.fori_loop(0, n, close, 0)
        copies = (
            pltpu.make_async_copy(out_q.at[place_row], inbox_q.at[head], sems_q[2].at[0]),
            pltpu.make_async_copy(out_kv.at[place_row], inbox_kv.at[head], sems_kv[2].at[0]),
        )
        for cp in copies:
            cp.start()
        for cp in copies:
            cp.wait()

    ffn_run(*FFN_AFTER[0])

    def head_pair(k, _):
        p = (place_row + k) % (H // 2)
        for u in range(2):
            wait_head(n, place_row, 2 * p + u, out_q, inbox_q, sems_q)
            wait_head(n, place_row, 2 * p + u, out_kv, inbox_kv, sems_kv)
        lanes = pl.ds(pl.multiple_of(p * 128, 128), 128)
        keys_values = unpack_pair(inbox_kv[2 * p], inbox_kv[2 * p + 1], (TOK_SEQ, 128))
        queries = []
        for t in both:
            part = slice(t * BLOCK, (t + 1) * BLOCK)
            queries += unpack_pair(inbox_q[2 * p, part, :], inbox_q[2 * p + 1, part, :], (BLOCK, 128))
        grads = (jnp.concatenate(queries, axis=0), *keys_values)
        for e in range(3):
            proj[e, :, lanes] = grads[e].astype(jnp.bfloat16)
        joined = jnp.concatenate(grads, axis=1).astype(jnp.bfloat16)
        grad = matmul(turned_rows[...], joined).reshape(UNITS, UNIT, 3 * 128).astype(jnp.bfloat16)
        for e in range(3):
            ownq[pl.ds(e * UNITS, UNITS), :, lanes] = grad[:, :, e * 128 : (e + 1) * 128]
        return 0

    lax.fori_loop(0, H // 2, head_pair, 0)
    qkv_steps = []
    if nz:
        hand_all(qkv)
        qkv_steps = ordered(qkv)

    def qkv_run(low, high):
        for w, f in qkv_steps:
            if low <= w < high:
                f()

    def add_rows(x):
        return jnp.sum(x.astype(jnp.float32), axis=0, keepdims=True)

    value[0, 0:1] = add_rows(proj[0])
    value[0, 1:2] = add_rows(proj[2])
    value[0, 2:8] = small_ref[0:6]
    for c in range(FF // D):
        value[0, 8 + c : 9 + c] = ffn_ref[:, c * D : (c + 1) * D]
    partners = exchange_partners(me, nz) if nz else []
    vsems = (vsend, vrecv)
    if nz:
        vector_copy(0, value, land, vsems, partners).start()

    def vector_stage(i):
        if i < len(partners):
            vector_copy(i, value, land, vsems, partners).wait_recv()
            total = value[i] + land[i]
            if i + 1 < len(partners):
                value[i + 1] = total
                vector_copy(i + 1, value, land, vsems, partners).start()
            else:
                vec_out[...] = total

    load_w.wait()
    d_tokens = d_sum1_ref[...]
    for e in range(3):
        d_tokens = d_tokens + outer_cols(proj[e], as_matrix(w_ref[e * UNITS : (e + 1) * UNITS]))
    d_tokens_ref[...] = d_tokens
    qkv_run(1, 5)
    ffn_run(*FFN_AFTER[1])
    vector_stage(0)
    qkv_run(5, 9)
    vector_stage(1)
    ffn_run(20)
    vector_stage(2)
    qkv_run(9, 20)
    vector_stage(3)
    vector_stage(4)
    qkv_run(20, 99)
    if not nz:
        vec_out[...] = value[0]
        outs[0][...] = ownq[...]
    for i in range(len(partners)):
        vector_copy(i, value, land, vsems, partners).wait_send()
    finish_from_owners(n, place_row, head, mine, out_q, inbox_q, sems_q)
    finish_from_owners(n, place_row, head, mine, out_kv, inbox_kv, sems_kv)
    for cp, cond in pending:
        if cond is None:
            cp.wait_send()
        else:
            pl.when(cond)(cp.wait_send)


def back(heads, local, weight_grads, nz):
    n = lax.axis_size("seq")
    low, full = jnp.bfloat16, jnp.float32
    rows, w_all, d_sum1, small, d_ffn = local
    outs = [((TOK_SEQ, D), full), ((16, D), full)]
    if nz:
        outs += [((3 * UNIT * D // 128, 128), full), ((UNIT * D // 128, 128), full)]
        outs += [((UNIT * FF // 128, 128), full)] * 2
    else:
        outs += [((QKV_UNITS, UNIT, D), low)]
    stages = 3 + (max(nz, 1) - 1).bit_length()
    part = (TOK_SEQ // 2, 128)
    extra = [pltpu.VMEM(g.shape, low) for g in weight_grads] if nz else []
    slabs = [(hi - lo, FF if kind == "expand" else D) for kind, lo, hi, _ in FFN_KINDS]
    slabs += [(UNIT, hi - lo) for _, lo, hi, _ in QKV_KINDS]
    for slab in slabs if nz else ():
        extra += Reduction.buffers(nz, slab)
        extra += Reduction.semaphores(nz)
    return pl.pallas_call(
        functools.partial(back_kernel, n, nz),
        out_shape=[jax.ShapeDtypeStruct(s, d) for s, d in outs],
        in_specs=[VMEM, VMEM, SMEM, SMEM, VMEM, VMEM]
        + [VMEM, ANY, VMEM, VMEM, VMEM, ANY, ANY, ANY],
        out_specs=[VMEM] * len(outs),
        scratch_shapes=[
            pltpu.VMEM((n * BPD, BLOCK, 128), low),
            pltpu.VMEM((BPD // 2, 8 * BLOCK, 128), low),
            pltpu.VMEM((BPD // 2, 8 * BLOCK, 128), low),
            pltpu.VMEM((n * (BPD + PICKS) + 1, BLOCK, 128), full),
            pltpu.VMEM((n,) + part, low),
            pltpu.VMEM((n, TOK_SEQ, 128), low),
            pltpu.VMEM((H,) + part, low),
            pltpu.VMEM((H, TOK_SEQ, 128), low),
            pltpu.VMEM((3, TOK_SEQ, D), low),
            pltpu.VMEM((QKV_UNITS, UNIT, D), low),
            pltpu.VMEM((QKV_UNITS, UNIT, D), low),
            pltpu.VMEM((D, TOK_SEQ), low),
            pltpu.VMEM((stages, 16, D), full),
            pltpu.VMEM((stages, 16, D), full),
            pltpu.SemaphoreType.DMA((4,)),
            pltpu.SemaphoreType.DMA((stages,)),
            pltpu.SemaphoreType.DMA((stages,)),
            *exchange_sems(n),
            *exchange_sems(n),
            *extra,
        ],
        compiler_params=pltpu.CompilerParams(
            collective_id=5, has_side_effects=True, vmem_limit_bytes=61 << 20
        ),
        name="back",
    )(*heads, *local, *weight_grads)


VECTORS = (6 * D, 2 * D, FF)


def hand_out_kernel(shards, *refs):
    count = (len(refs) - 6) // 3
    arrays, totals, outs = refs[:count], refs[count], refs[count + 1 : 2 * count + 1]
    pieces = refs[2 * count + 1 : 2 * count + 4]
    held, (line, sem) = refs[2 * count + 4 : -2], refs[-2:]
    into = [pltpu.make_async_copy(*pair, sem.at[i]) for i, pair in enumerate(zip(arrays, held))]
    onto = [pltpu.make_async_copy(*pair, sem.at[i]) for i, pair in enumerate(zip(held, outs))]
    for cp in into:
        cp.start()
    for first, second in zip(into, onto):
        first.wait()
        second.start()
    me = lax.axis_index("dp") * lax.axis_size("seq") + lax.axis_index("seq")
    row = 0
    for size, out in zip(VECTORS, pieces):
        for r in range(size // D):
            line[:, r * D : (r + 1) * D] = totals[row + r : row + r + 1]
        row += size // D
        start = me * (size // shards)
        base = pl.multiple_of(start // 128 * 128, 128)
        some = line[:, pl.ds(base, 384)]
        out[...] = pltpu.roll(some, 384 - start % 128, 1)[:, 0 : size // shards]
    for cp in onto:
        cp.wait()


def hand_out(arrays, totals):
    shards = lax.axis_size("dp") * lax.axis_size("seq")
    shapes = [a.shape for a in arrays] + [(1, v // shards) for v in VECTORS]
    return pl.pallas_call(
        functools.partial(hand_out_kernel, shards),
        out_shape=[jax.ShapeDtypeStruct(s, jnp.float32) for s in shapes],
        in_specs=[ANY] * len(arrays) + [VMEM],
        out_specs=[ANY] * len(arrays) + [VMEM] * 3,
        scratch_shapes=[
            *[pltpu.VMEM(a.shape, jnp.float32) for a in arrays],
            pltpu.VMEM((1, max(VECTORS) + 384), jnp.float32),
            pltpu.SemaphoreType.DMA((len(arrays),)),
        ],
        name="hand_out",
    )(*arrays, totals)


def on_device(
    tokens,
    qkv_weight,
    out_weight,
    expand_weight,
    contract_weight,
    bias_vectors,
    gain_vectors,
    ffn_bias,
    random_blocks,
    cotangent,
):
    shards = lax.axis_size("dp") * lax.axis_size("seq")
    me = lax.axis_index("dp") * lax.axis_size("seq") + lax.axis_index("seq")
    planes = kernel_planes()
    rows = tokens.reshape(TOK_SEQ, D)
    weights = (qkv_weight, expand_weight, out_weight, contract_weight)
    vectors = (bias_vectors, gain_vectors, ffn_bias)
    if planes:
        vec = jnp.concatenate(vectors).astype(jnp.float32)
        vec = jnp.pad(vec, (0, -vec.size % 128)).reshape(1, -1)
        qkv, first, out, second = [w.reshape(-1, 128) for w in weights]
    else:
        gather = functools.partial(lax.all_gather, axis_name=("dp", "seq"), axis=0, tiled=True)
        placed = [gather(v).astype(jnp.float32) for v in vectors]
        qkv, first, out, second = [gather(w) for w in weights]
        qkv = qkv.reshape(3 * UNITS, UNIT, D)
        first, out = first.reshape(UNITS, UNIT, FF), out.reshape(UNITS, UNIT, D)
        first = jnp.concatenate([first, out], axis=2)
        second = second.reshape(UNITS, FF // UNITS, D)
        vec = jnp.pad(jnp.concatenate(placed).reshape(-1, D), ((0, 4), (0, 0)))
    (
        result,
        d_sum1,
        kv,
        queries,
        picks,
        lse,
        d_heads,
        d_expand,
        d_contract,
        d_out,
        small,
        d_ffn,
        w_all,
        links,
    ) = front(
        rows, cotangent.reshape(TOK_SEQ, D), random_blocks, vec, qkv, first, out, second, planes
    )
    d_tokens, totals, *grads = back(
        (kv, queries, picks, links, lse, d_heads),
        (rows, w_all, d_sum1, small, d_ffn),
        (d_expand, d_contract, d_out),
        planes,
    )
    if planes:
        result, d_tokens, *grads = hand_out((result, d_tokens, *grads), totals)
        grads, vectors = grads[:4], [v.reshape(-1) for v in grads[4:]]
    else:
        grads = [grads[0], d_out, d_expand, d_contract]
        *vectors, d_qkv, d_out, d_expand, d_contract = [
            lax.psum_scatter(
                g.astype(jnp.float32).reshape(-1),
                ("dp", "seq"),
                scatter_dimension=0,
                tiled=True,
            )
            for g in (totals[0:6], totals[6:8], totals[8 : 8 + FF // D], *grads)
        ]
        grads = (d_qkv, d_out, d_expand, d_contract)
    return (result[None], d_tokens[None], *[g.reshape(-1) for g in grads], *vectors)


def solution(mesh):
    return jax.shard_map(
        on_device,
        mesh=mesh,
        in_specs=(
            P("dp", "seq", None),
            P(("dp", "seq")),
            P(("dp", "seq")),
            P(("dp", "seq")),
            P(("dp", "seq")),
            P(("dp", "seq")),
            P(("dp", "seq")),
            P(("dp", "seq")),
            P("dp", None, "seq", None),
            P("dp", "seq", None),
        ),
        out_specs=(
            P("dp", "seq", None),
            P("dp", "seq", None),
            P(("dp", "seq")),
            P(("dp", "seq")),
            P(("dp", "seq")),
            P(("dp", "seq")),
            P(("dp", "seq")),
            P(("dp", "seq")),
            P(("dp", "seq")),
        ),
        check_vma=False,
    )
```
